32 devices in a mesh: grp: 2 (over x), leaf: 16 (over z, y, core).
Axes of the slice: x: 2, y: 2, z: 4, core: 2. Of those that a mesh axis runs over, the one named last changes fastest.
Arguments:
- probes: bfloat16 [65, 32768], P(None, ('grp', 'leaf')), parts along dimension 1, may hold values from -6 to 6
- basis: bfloat16 [256, 64, 128], P(('grp', 'leaf')), parts along dimension 0, may hold values from -0.5 to 0.5
- transfer: bfloat16 [256, 64, 64], P(('grp', 'leaf')), parts along dimension 0, may hold values from -0.75 to 0.75
- local_blocks: bfloat16 [256, 8, 128, 128], P(('grp', 'leaf')), parts along dimension 0, may hold values from -0.1875 to 0.1875
- remote_blocks: bfloat16 [256, 4, 128, 128], P(('grp', 'leaf')), parts along dimension 0, may hold values from -0.25 to 0.25
- near_dest: int32 [256, 4], P(('grp', 'leaf')), parts along dimension 0, may hold values from 0 to 15, as said below
- near_leaf: int32 [256, 4], P(('grp', 'leaf')), parts along dimension 0, may hold values from 0 to 7, as said below
- couplings: bfloat16 [32, 12, 64, 64], P(('grp', 'leaf')), parts along dimension 0, may hold values from -0.078125 to 0.078125
- far_list: int32 [32, 12], P(('grp', 'leaf')), parts along dimension 0, may hold values from 0 to 15, as said below
Outputs:
- mean_and_probes: float32 [65, 32768], P(None, ('grp', 'leaf')), parts along dimension 1
The draws below stay inside these ranges and needn't reach their ends.
There are 2 independent parts, one for each index of `grp`. The reference program is written for one: setup_inputs(seed, part) draws one part's arguments, and reference() takes and returns one part's arrays. A program takes and returns all parts, laid end to end along the dimension named above; each array names one. Nothing has to cross between parts.
Inputs may be any that keep to these rules, and one draw needn't show every extreme that they name: `near_dest`: among the rows of one device, exactly 8 distinct devices appear, each exactly 4 times; some device appears in the rows of every device. Within the rows of one device no pair of near_dest and near_leaf repeats. `far_list`: each row names 12 distinct boxes, never its own box.
All inputs are finite; a program needn't handle non-finite values.
Results may differ from the reference program's by a relative error of at most 0.0031.
Values may be sent and summed in bfloat16 or wider, within the bound.
No kernel may reach another device: no remote copies, remote signals or barrier semaphores. Data moves between devices by JAX's collectives and lax.ppermute only.
A program may use at most 128 MiB of HBM per device.

```python
import jax
import jax.numpy as jnp
from jax import lax

P_SIZE = 128
K = 64
R = 65
LEAF_DEV = 8
CAP = 4
FAR = 12
FAN = 8
RB = 4
LEAVES = 128
POINTS = 16384
N_LEAF = 16


def near_routes(key):
    hot_device = jax.random.randint(jax.random.fold_in(key, 11), (), 0, N_LEAF)

    def sender(subkey):
        first_key, second_key, third_key = jax.random.split(subkey, 3)
        ordering = jax.random.permutation(first_key, N_LEAF)
        leading = ordering[0]
        ordering = jnp.where(ordering == hot_device, leading, ordering)
        ordering = ordering.at[0].set(hot_device)
        chosen_dest = ordering[:FAN]
        leaf_keys = jax.random.split(second_key, FAN)
        slot_sets = jax.vmap(lambda single: jax.random.permutation(single, LEAF_DEV)[:CAP])(leaf_keys)
        targets = jnp.repeat(chosen_dest, CAP)
        slots = slot_sets.reshape(FAN * CAP)
        shuffle = jax.random.permutation(third_key, FAN * CAP)
        return (targets[shuffle], slots[shuffle])
    sender_keys = jax.random.split(jax.random.fold_in(key, 12), N_LEAF)
    targets, slots = jax.vmap(sender)(sender_keys)
    return (targets.reshape(N_LEAF * LEAF_DEV, RB), slots.reshape(N_LEAF * LEAF_DEV, RB))


def draw_near_dest(key, part):
    targets, slots = near_routes(key)
    return targets.astype(jnp.int32)


def draw_near_leaf(key, part):
    targets, slots = near_routes(key)
    return slots.astype(jnp.int32)


def draw_far_list(key, part):
    key = jax.random.fold_in(key, 3)

    def one_row(subkey, owner_box):
        others = jax.random.permutation(subkey, N_LEAF - 1)[:FAR]
        return jnp.where(others >= owner_box, others + 1, others)
    return jax.vmap(one_row)(jax.random.split(key, N_LEAF), jnp.arange(N_LEAF)).astype(jnp.int32)


def block_levels(rng, shape, shards, smallest, largest):
    def one(position, parts):
        steps = jax.random.uniform(jax.random.fold_in(jax.random.fold_in(rng, 6), position), (parts,), jnp.float32, smallest / len(shards), largest / len(shards))
        return jnp.repeat(jnp.exp(steps), shape[position] // parts).reshape((-1,) + (1,) * (len(shape) - position - 1))

    level = one(*shards[0])
    for cut in shards[1:]:
        level = level * one(*cut)
    return level


def centred(rng, extent, scale, bound, cuts=(), dtype=jnp.bfloat16):
    gain = block_levels(rng, extent, cuts, -0.22, 0.18) if cuts else 1.0
    entries = jax.random.normal(rng, extent, jnp.float32) * scale * gain
    return jnp.minimum(jnp.maximum(entries, -bound), bound).astype(dtype)


def setup_inputs(seed: int = 0, part: int = 0) -> dict:
    arg_keys = jax.random.split(jax.random.key(seed), 10)
    part_keys = jax.random.split(jax.random.fold_in(arg_keys[9], part), 10)
    probes = centred(part_keys[0], (R, POINTS), 1.0, 6.0, ((1, 16),))
    basis = centred(part_keys[1], (LEAVES, K, P_SIZE), P_SIZE ** -0.5, 0.5, ((0, 16),))
    transfer = centred(part_keys[2], (LEAVES, K, K), K ** -0.5, 0.75, ((0, 16),))
    local_blocks = centred(part_keys[3], (LEAVES, LEAF_DEV, P_SIZE, P_SIZE), (P_SIZE * LEAF_DEV) ** -0.5, 0.1875, ((0, 16),))
    remote_blocks = centred(part_keys[4], (LEAVES, RB, P_SIZE, P_SIZE), (P_SIZE * RB) ** -0.5, 0.25, ((0, 16),))
    near_dest = draw_near_dest(jax.random.fold_in(jax.random.fold_in(arg_keys[9], part), 71), part)
    near_leaf = draw_near_leaf(jax.random.fold_in(jax.random.fold_in(arg_keys[9], part), 71), part)
    couplings = centred(part_keys[7], (N_LEAF, FAR, K, K), (K * FAR * LEAF_DEV) ** -0.5, 0.078125, ((0, 16),))
    far_list = draw_far_list(jax.random.fold_in(jax.random.fold_in(arg_keys[9], part), 71), part)
    return {"probes": probes, "basis": basis, "transfer": transfer, "local_blocks": local_blocks, "remote_blocks": remote_blocks, "near_dest": near_dest, "near_leaf": near_leaf, "couplings": couplings, "far_list": far_list}


def settle(array):
    return lax.optimization_barrier(array.astype(jnp.bfloat16)).astype(jnp.float32)


def reference(probes, basis, transfer, local_blocks, remote_blocks, near_dest, near_leaf, couplings, far_list):
    leaves = LEAF_DEV * N_LEAF
    values = probes.astype(jnp.float32).reshape(R, leaves, P_SIZE)
    per_device = jnp.transpose(values.reshape(R, N_LEAF, LEAF_DEV, P_SIZE), (1, 0, 2, 3))
    grouped_local = local_blocks.reshape(N_LEAF, LEAF_DEV, LEAF_DEV, P_SIZE, P_SIZE)

    def local_one(operands):
        blocks, inputs = operands
        return jnp.einsum("icpq,rcq->irp", blocks.astype(jnp.float32), inputs)

    local_part = lax.map(local_one, (grouped_local, per_device)).reshape(leaves, R, P_SIZE)

    grouped_remote = remote_blocks.reshape(N_LEAF, LEAF_DEV, RB, P_SIZE, P_SIZE)
    places = (near_dest.astype(jnp.int32) * LEAF_DEV + near_leaf.astype(jnp.int32)).reshape(N_LEAF, LEAF_DEV * RB)

    def remote_step(accum, operands):
        blocks, inputs, where_to = operands
        products = jnp.einsum("jbpq,rjq->jbrp", blocks.astype(jnp.float32), inputs)
        products = settle(products).reshape(LEAF_DEV * RB, R, P_SIZE)
        return accum.at[where_to].add(products), None

    remote_part = lax.scan(remote_step, jnp.zeros((leaves, R, P_SIZE), jnp.float32), (grouped_remote, per_device, places))[0]

    basis_wide = basis.astype(jnp.float32)
    transfer_wide = transfer.astype(jnp.float32).reshape(N_LEAF, LEAF_DEV, K, K)
    leaf_coef = settle(jnp.einsum("jkp,rjp->jrk", basis_wide, values))
    box_coef = settle(jnp.einsum("djkl,djrl->drk", transfer_wide, leaf_coef.reshape(N_LEAF, LEAF_DEV, R, K)))
    chosen = box_coef[far_list.astype(jnp.int32)]
    far_box = settle(jnp.einsum("dfkl,dfrl->drk", couplings.astype(jnp.float32), chosen))
    down_coef = settle(jnp.einsum("djkl,drk->djrl", transfer_wide, far_box))
    far_part = jnp.einsum("jlp,jrl->jrp", basis_wide, down_coef.reshape(leaves, R, K))
    combined = local_part + remote_part + far_part
    return jnp.transpose(combined, (1, 0, 2)).reshape(R, leaves * P_SIZE)
```

```python
import functools

import jax
import jax.numpy as jnp
from jax import lax
from jax.experimental import pallas as pl
from jax.experimental.pallas import tpu as pltpu
from jax.sharding import PartitionSpec as P

CAP = 4
TILE = 16
HALF = 64
VMEM_BYTES = 48 * 2**20

F32 = jnp.float32
BF16 = jnp.bfloat16

VMEM = pl.BlockSpec(memory_space=pltpu.VMEM)
SMEM = pl.BlockSpec(memory_space=pltpu.SMEM)


def dot_t(lhs, rhs):
    return lax.dot_general(lhs, rhs, (((1,), (1,)), ((), ())), preferred_element_type=F32)


def dot(lhs, rhs):
    return lax.dot_general(lhs, rhs, (((1,), (0,)), ((), ())), preferred_element_type=F32)


def products_kernel(main, dest_ref, probes_ref, blocks_ref, send_ref, tails, count):
    devices = send_ref.shape[0]
    leaves, per_leaf, size = blocks_ref.shape[:3]

    @pl.loop(0, devices)
    def _(i):
        count[i] = 0
        tails[i] = jnp.zeros_like(tails[i])

    for j in range(leaves):
        x = probes_ref[:, j * size : (j + 1) * size]
        for first in range(0, per_leaf, 4):
            many = min(4, per_leaf - first)
            rhs = blocks_ref[j, first : first + many].reshape(many * size, size)
            product = dot_t(x, rhs)
            for b in range(many):
                target = dest_ref[j, first + b]
                slot = count[target]
                count[target] = slot + 1
                block = product[:, b * size : (b + 1) * size]
                send_ref[target, pl.ds(pl.multiple_of(slot * main, TILE), main), :] = block[:main].astype(BF16)
                tails[target, pl.ds(slot, 1), :] = block[main:]

    @pl.loop(0, devices)
    def _(i):
        send_ref[i, CAP * main :, :] = tails[i].astype(BF16)


def near_kernel(
    devices, dest_ref, leaf_ref, probes_ref, basis_ref, transfer_ref, local_ref, pay_ref, base_ref, count
):
    leaves, rank, size = basis_ref.shape
    columns = probes_ref.shape[0]
    per_leaf = dest_ref.shape[1]
    box = jnp.zeros((columns, rank), F32)
    for j in range(leaves):
        coef = dot_t(probes_ref[:, j * size : (j + 1) * size], basis_ref[j]).astype(BF16)
        box += dot_t(coef, transfer_ref[j])
    pay_ref[:, :HALF] = box.astype(BF16)

    @pl.loop(0, devices)
    def _(i):
        count[i] = 0

    where = HALF * lax.broadcasted_iota(jnp.int32, (columns, HALF), 0) + lax.broadcasted_iota(
        jnp.int32, (columns, HALF), 1
    )
    rows = -(-devices * CAP // HALF)
    rows = min(columns, -(-rows // 8) * 8)
    where = where[:rows]
    table = jnp.full((rows, HALF), leaves, jnp.int32)
    for j in range(leaves):
        for b in range(per_leaf):
            target = dest_ref[j, b]
            slot = count[target]
            count[target] = slot + 1
            table = jnp.where(where == target * CAP + slot, leaf_ref[j, b], table)
    pay_ref[:rows, HALF:] = table.astype(F32).astype(BF16)
    pay_ref[rows:, HALF:] = jnp.zeros((columns - rows, HALF), BF16)

    for i in range(leaves):
        total = dot_t(probes_ref[:, :size], local_ref[i, 0])
        for c in range(1, leaves):
            total += dot_t(probes_ref[:, c * size : (c + 1) * size], local_ref[i, c])
        base_ref[:, i * size : (i + 1) * size] = total


def far_kernel(partner_ref, pay_ref, couplings_ref, transfer_ref, basis_ref, base_ref, out_ref):
    leaves, rank, size = basis_ref.shape
    columns = base_ref.shape[0]
    far = jnp.zeros((columns, rank), F32)
    for f in range(couplings_ref.shape[1]):
        far += dot_t(pay_ref[partner_ref[0, f]][:, :HALF], couplings_ref[0, f])
    far = far.astype(BF16)
    for j in range(leaves):
        down = dot(far, transfer_ref[j]).astype(BF16)
        cols = slice(j * size, (j + 1) * size)
        out_ref[:, cols] = base_ref[:, cols] + dot(down, basis_ref[j])


def gather_kernel(main, leaf_ref, base_ref, incoming_ref, out_ref, total):
    columns, points = base_ref.shape
    size = incoming_ref.shape[2]
    total[:, :points] = base_ref[...]
    total[:, points:] = jnp.zeros((columns, size), F32)

    @pl.loop(0, incoming_ref.shape[0])
    def _(source):
        tail = incoming_ref[source, CAP * main :, :].astype(F32)
        for slot in range(CAP):
            cols = pl.ds(pl.multiple_of(leaf_ref[source * CAP + slot] * size, size), size)
            total[:main, cols] += incoming_ref[source, slot * main : (slot + 1) * main, :].astype(F32)
            total[main:, cols] += tail[slot : slot + 1]

    out_ref[...] = total[:, :points]


def call(kernel, out_shape, in_specs, scratch, flops, nbytes):
    return pl.pallas_call(
        kernel,
        out_shape=out_shape,
        in_specs=in_specs,
        out_specs=jax.tree.map(lambda _: VMEM, out_shape),
        scratch_shapes=scratch,
        compiler_params=pltpu.CompilerParams(vmem_limit_bytes=VMEM_BYTES),
        cost_estimate=pl.CostEstimate(flops=flops, bytes_accessed=nbytes, transcendentals=0),
    )


def per_device(
    probes, basis, transfer, local_blocks, remote_blocks, near_dest, near_leaf, couplings, far_list
):
    columns, points = probes.shape
    leaves, rank, size = basis.shape
    devices = lax.axis_size("leaf")
    main = columns // TILE * TILE
    depth = CAP * main + TILE
    blocks = remote_blocks.shape[0] * remote_blocks.shape[1]
    unit = 2 * columns * size * size

    send = call(
        functools.partial(products_kernel, main),
        jax.ShapeDtypeStruct((devices, depth, size), BF16),
        [SMEM, VMEM, VMEM],
        [pltpu.VMEM((devices, TILE, size), F32), pltpu.SMEM((devices,), jnp.int32)],
        blocks * unit,
        remote_blocks.size * 2 + devices * depth * size * 2,
    )(near_dest, probes, remote_blocks)
    incoming = lax.all_to_all(send, "leaf", split_axis=0, concat_axis=0, tiled=True)

    pay, base = call(
        functools.partial(near_kernel, devices),
        (
            jax.ShapeDtypeStruct((columns, 2 * HALF), BF16),
            jax.ShapeDtypeStruct((columns, points), F32),
        ),
        [SMEM, SMEM, VMEM, VMEM, VMEM, VMEM],
        [pltpu.SMEM((devices,), jnp.int32)],
        leaves * leaves * unit,
        local_blocks.size * 2,
    )(near_dest, near_leaf, probes, basis, transfer, local_blocks)
    every = lax.all_gather(pay[None], "leaf", axis=0, tiled=True)
    first = lax.axis_index("leaf") * CAP
    mine = lax.dynamic_slice(every, (0, first // HALF, HALF + first % HALF), (devices, 1, CAP))
    slots = mine.reshape(devices * CAP).astype(jnp.int32)

    base = call(
        far_kernel,
        jax.ShapeDtypeStruct((columns, points), F32),
        [SMEM, VMEM, VMEM, VMEM, VMEM, VMEM],
        [],
        4 * leaves * unit,
        couplings.size * 2 + every.size * 2,
    )(far_list, every, couplings, transfer, basis, base)

    return call(
        functools.partial(gather_kernel, main),
        jax.ShapeDtypeStruct((columns, points), F32),
        [SMEM, VMEM, VMEM],
        [pltpu.VMEM((columns, points + size), F32)],
        devices * CAP * columns * size,
        devices * depth * size * 2,
    )(slots, base, incoming)


def solution(mesh):
    placed = (
        P(None, ("grp", "leaf")),
        P(("grp", "leaf"), None, None),
        P(("grp", "leaf"), None, None),
        P(("grp", "leaf"), None, None, None),
        P(("grp", "leaf"), None, None, None),
        P(("grp", "leaf"), None),
        P(("grp", "leaf"), None),
        P(("grp", "leaf"), None, None, None),
        P(("grp", "leaf"), None),
    )
    return jax.shard_map(
        per_device, mesh=mesh, in_specs=placed, out_specs=P(None, ("grp", "leaf")), check_vma=False
    )
```

```python
import functools

import jax
import jax.numpy as jnp
from jax import lax
from jax.experimental import pallas as pl
from jax.experimental.pallas import tpu as pltpu
from jax.sharding import PartitionSpec as P

CAP = 4
TILE = 16

F32 = jnp.float32
BF16 = jnp.bfloat16

VMEM = pl.BlockSpec(memory_space=pltpu.VMEM)
SMEM = pl.BlockSpec(memory_space=pltpu.SMEM)
ANY = pl.BlockSpec(memory_space=pl.ANY)


def dot_t(lhs, rhs):
    return lax.dot_general(lhs, rhs, (((1,), (1,)), ((), ())), preferred_element_type=F32)


def dot(lhs, rhs):
    return lax.dot_general(lhs, rhs, (((1,), (0,)), ((), ())), preferred_element_type=F32)


def products_kernel(
    main,
    dest_ref,
    leaf_ref,
    probes_hbm,
    basis_hbm,
    transfer_hbm,
    blocks_hbm,
    send_ref,
    probes_ref,
    basis_ref,
    transfer_ref,
    blocks_ref,
    tails,
    count,
    sems,
):
    devices = send_ref.shape[0]
    leaves, per_leaf, size = blocks_ref.shape[:3]
    columns, rank = probes_ref.shape[0], basis_ref.shape[1]
    copies = [
        pltpu.make_async_copy(probes_hbm, probes_ref, sems.at[0]),
        pltpu.make_async_copy(basis_hbm, basis_ref, sems.at[1]),
        pltpu.make_async_copy(transfer_hbm, transfer_ref, sems.at[2]),
    ] + [pltpu.make_async_copy(blocks_hbm.at[j], blocks_ref.at[j], sems.at[3 + j]) for j in range(leaves)]
    for copy in copies:
        copy.start()

    @pl.loop(0, devices)
    def _(i):
        count[i] = 0
        tails[i] = jnp.full(tails.shape[1:], leaves, F32)

    for copy in copies[:3]:
        copy.wait()
    box = jnp.zeros((columns, rank), F32)
    for j in range(leaves):
        coef = dot_t(probes_ref[:, j * size : (j + 1) * size], basis_ref[j]).astype(BF16)
        box += dot_t(coef, transfer_ref[j])
    half = main // 2
    packed = jnp.concatenate([box[:half], box[half:main]], axis=1).astype(BF16)
    last = jnp.concatenate([box[main:], jnp.zeros_like(box[main:])], axis=1)

    for j in range(leaves):
        copies[3 + j].wait()
        x = probes_ref[:, j * size : (j + 1) * size]
        for first in range(0, per_leaf, 4):
            many = min(4, per_leaf - first)
            rhs = blocks_ref[j, first : first + many].reshape(many * size, size)
            product = dot_t(x, rhs)
            for b in range(many):
                target = dest_ref[first + b, j]
                slot = count[target]
                count[target] = slot + 1
                block = product[:, b * size : (b + 1) * size]
                send_ref[target, pl.ds(pl.multiple_of(slot * main, TILE), main), :] = block[:main].astype(BF16)
                tails[target, pl.ds(slot, 1), :] = block[main:]
                tails[target, pl.ds(CAP + slot, 1), :] = jnp.full((1, size), leaf_ref[first + b, j], F32)

    @pl.loop(0, devices)
    def _(i):
        tails[i, 2 * CAP : 2 * CAP + 1, :] = last
        send_ref[i, CAP * main : CAP * main + TILE, :] = tails[i].astype(BF16)
        send_ref[i, CAP * main + TILE :, :] = packed


def local_kernel(probes_ref, local_ref, base_ref):
    leaves, size = local_ref.shape[0], local_ref.shape[2]
    for i in range(leaves):
        total = dot_t(probes_ref[:, :size], local_ref[i, 0])
        for c in range(1, leaves):
            total += dot_t(probes_ref[:, c * size : (c + 1) * size], local_ref[i, c])
        base_ref[:, i * size : (i + 1) * size] = total


def gather_kernel(
    main,
    leaf_ref,
    partner_ref,
    base_ref,
    incoming_ref,
    couplings_ref,
    transfer_ref,
    basis_ref,
    out_ref,
    total,
):
    columns, points = base_ref.shape
    leaves, rank, size = basis_ref.shape
    far = jnp.zeros((columns, rank), F32)
    for f in range(couplings_ref.shape[1]):
        source = partner_ref[0, f]
        packed = incoming_ref[source, CAP * main + TILE :, :]
        last = incoming_ref[source, CAP * main : CAP * main + TILE, :].astype(F32)[2 * CAP : 2 * CAP + 1, :rank]
        box = jnp.concatenate(
            [packed[:, :rank].astype(F32), packed[:, rank:].astype(F32), last], axis=0
        ).astype(BF16)
        far += dot_t(box, couplings_ref[0, f])
    far = far.astype(BF16)
    for j in range(leaves):
        down = dot(far, transfer_ref[j]).astype(BF16)
        cols = slice(j * size, (j + 1) * size)
        total[:, cols] = base_ref[:, cols] + dot(down, basis_ref[j])
    total[:, points:] = jnp.zeros((columns, size), F32)

    @pl.loop(0, incoming_ref.shape[0])
    def _(source):
        tail = incoming_ref[source, CAP * main : CAP * main + TILE, :].astype(F32)
        for slot in range(CAP):
            cols = pl.ds(pl.multiple_of(leaf_ref[source * CAP + slot] * size, size), size)
            total[:main, cols] += incoming_ref[source, slot * main : (slot + 1) * main, :].astype(F32)
            total[main:, cols] += tail[slot : slot + 1]

    out_ref[...] = total[:, :points]


def call(kernel, out_shape, in_specs, scratch, flops, nbytes, vmem):
    return pl.pallas_call(
        kernel,
        out_shape=out_shape,
        in_specs=in_specs,
        out_specs=VMEM,
        scratch_shapes=scratch,
        compiler_params=pltpu.CompilerParams(vmem_limit_bytes=vmem + 4 * 2**20),
        cost_estimate=pl.CostEstimate(flops=flops, bytes_accessed=nbytes, transcendentals=0),
    )


def per_device(
    probes, basis, transfer, local_blocks, remote_blocks, near_dest, near_leaf, couplings, far_list
):
    columns, points = probes.shape
    leaves, rank, size = basis.shape
    devices = lax.axis_size("leaf")
    main = columns // TILE * TILE
    depth = CAP * main + TILE + main // 2
    blocks = remote_blocks.shape[0] * remote_blocks.shape[1]
    unit = 2 * columns * size * size
    send_bytes = devices * depth * size * 2

    send = call(
        functools.partial(products_kernel, main),
        jax.ShapeDtypeStruct((devices, depth, size), BF16),
        [SMEM, SMEM, ANY, ANY, ANY, ANY],
        [
            pltpu.VMEM(probes.shape, BF16),
            pltpu.VMEM(basis.shape, BF16),
            pltpu.VMEM(transfer.shape, BF16),
            pltpu.VMEM(remote_blocks.shape, BF16),
            pltpu.VMEM((devices, TILE, size), F32),
            pltpu.SMEM((devices,), jnp.int32),
            pltpu.SemaphoreType.DMA((3 + leaves,)),
        ],
        blocks * unit,
        remote_blocks.size * 2 + send_bytes,
        remote_blocks.size * 2 + 2 * send_bytes,
    )(near_dest.T, near_leaf.T, probes, basis, transfer, remote_blocks)
    incoming = lax.all_to_all(send, "leaf", split_axis=0, concat_axis=0, tiled=True)

    base = call(
        local_kernel,
        jax.ShapeDtypeStruct((columns, points), F32),
        [VMEM, VMEM],
        [],
        leaves * leaves * unit,
        local_blocks.size * 2,
        2 * local_blocks.size,
    )(probes, local_blocks)

    slots = incoming[:, CAP * main + CAP : CAP * main + 2 * CAP, 0].astype(jnp.int32)
    return call(
        functools.partial(gather_kernel, main),
        jax.ShapeDtypeStruct((columns, points), F32),
        [SMEM, SMEM, VMEM, VMEM, VMEM, VMEM, VMEM],
        [pltpu.VMEM((columns, points + size), F32)],
        devices * CAP * columns * size,
        send_bytes,
        send_bytes + 4 * 2**20,
    )(slots.reshape(devices * CAP), far_list, base, incoming, couplings, transfer, basis)


def solution(mesh):
    placed = (
        P(None, ("grp", "leaf")),
        P(("grp", "leaf"), None, None),
        P(("grp", "leaf"), None, None),
        P(("grp", "leaf"), None, None, None),
        P(("grp", "leaf"), None, None, None),
        P(("grp", "leaf"), None),
        P(("grp", "leaf"), None),
        P(("grp", "leaf"), None, None, None),
        P(("grp", "leaf"), None),
    )
    return jax.shard_map(
        per_device, mesh=mesh, in_specs=placed, out_specs=P(None, ("grp", "leaf")), check_vma=False
    )
```

```python
import functools

import jax
import jax.numpy as jnp
from jax import lax
from jax.experimental import pallas as pl
from jax.experimental.pallas import tpu as pltpu
from jax.sharding import PartitionSpec as P

TILE = 16

F32 = jnp.float32
BF16 = jnp.bfloat16

VMEM = pl.BlockSpec(memory_space=pltpu.VMEM)
SMEM = pl.BlockSpec(memory_space=pltpu.SMEM)
HBM = pl.BlockSpec(memory_space=pl.ANY)


def dot_t(lhs, rhs):
    return lax.dot_general(lhs, rhs, (((1,), (1,)), ((), ())), preferred_element_type=F32)


def dot(lhs, rhs):
    return lax.dot_general(lhs, rhs, (((1,), (0,)), ((), ())), preferred_element_type=F32)


def fetch(pairs, sems):
    copies = [pltpu.make_async_copy(src, dst, sems.at[i]) for i, (src, dst) in enumerate(pairs)]
    for copy in copies:
        copy.start()
    return copies


def box_kernel(probes_hbm, basis_hbm, transfer_hbm, box_ref, probes_ref, basis_ref, transfer_ref, sems):
    copies = fetch(
        [(probes_hbm, probes_ref), (basis_hbm, basis_ref), (transfer_hbm, transfer_ref)], sems
    )
    for copy in copies:
        copy.wait()
    leaves, rank, size = basis_ref.shape
    box = jnp.zeros(box_ref.shape, F32)
    for j in range(leaves):
        coef = dot_t(probes_ref[:, j * size : (j + 1) * size], basis_ref[j]).astype(BF16)
        box += dot_t(coef, transfer_ref[j])
    box_ref[...] = box.astype(BF16)


def products_kernel(
    main, dest_ref, leaf_ref, probes_hbm, blocks_hbm, send_ref, probes_ref, blocks_ref, tails, sems
):
    devices = send_ref.shape[0]
    leaves, per_leaf, size = blocks_ref.shape[:3]
    copies = fetch(
        [(probes_hbm, probes_ref)] + [(blocks_hbm.at[j], blocks_ref.at[j]) for j in range(leaves)], sems
    )

    @pl.loop(0, devices)
    def _(i):
        send_ref[i] = jnp.zeros(send_ref.shape[1:], BF16)
        tails[i] = jnp.zeros(tails.shape[1:], F32)

    copies[0].wait()
    for j in range(leaves):
        copies[1 + j].wait()
        x = probes_ref[:, j * size : (j + 1) * size]
        for first in range(0, per_leaf, 4):
            many = min(4, per_leaf - first)
            rhs = blocks_ref[j, first : first + many].reshape(many * size, size)
            product = dot_t(x, rhs)
            for b in range(many):
                target = dest_ref[first + b, j]
                row = leaf_ref[first + b, j]
                block = product[:, b * size : (b + 1) * size]
                send_ref[target, pl.ds(pl.multiple_of(row * main, TILE), main), :] = block[:main].astype(BF16)
                tails[target, pl.ds(row, 1), :] = block[main:]

    @pl.loop(0, devices)
    def _(i):
        send_ref[i, leaves * main :, :] = tails[i].astype(BF16)


def local_kernel(probes_hbm, local_hbm, base_ref, probes_ref, local_ref, sems):
    leaves, size = local_ref.shape[0], local_ref.shape[2]
    copies = fetch(
        [(probes_hbm, probes_ref)] + [(local_hbm.at[i], local_ref.at[i]) for i in range(leaves)], sems
    )
    copies[0].wait()
    for i in range(leaves):
        copies[1 + i].wait()
        total = dot_t(probes_ref[:, :size], local_ref[i, 0])
        for c in range(1, leaves):
            total += dot_t(probes_ref[:, c * size : (c + 1) * size], local_ref[i, c])
        base_ref[:, i * size : (i + 1) * size] = total


def far_kernel(
    partner_ref,
    base_ref,
    boxes_ref,
    couplings_hbm,
    transfer_hbm,
    basis_hbm,
    out_ref,
    couplings_ref,
    transfer_ref,
    basis_ref,
    sems,
):
    copies = fetch(
        [(couplings_hbm, couplings_ref), (transfer_hbm, transfer_ref), (basis_hbm, basis_ref)], sems
    )
    for copy in copies:
        copy.wait()
    leaves, rank, size = basis_ref.shape
    columns = base_ref.shape[0]
    far = jnp.zeros((columns, rank), F32)
    for f in range(couplings_ref.shape[1]):
        far += dot_t(boxes_ref[partner_ref[0, f]], couplings_ref[0, f])
    far = far.astype(BF16)
    for j in range(leaves):
        down = dot(far, transfer_ref[j]).astype(BF16)
        cols = slice(j * size, (j + 1) * size)
        out_ref[:, cols] = base_ref[:, cols] + dot(down, basis_ref[j])


def add_kernel(main, base_ref, near_ref, out_ref):
    columns, points = base_ref.shape
    size = near_ref.shape[1]
    leaves = points // size
    tail = near_ref[leaves * main :, :].astype(F32)
    for j in range(leaves):
        cols = slice(j * size, (j + 1) * size)
        out_ref[:main, cols] = base_ref[:main, cols] + near_ref[j * main : (j + 1) * main, :].astype(F32)
        out_ref[main:, cols] = base_ref[main:, cols] + tail[j : j + 1]


def call(kernel, out_shape, in_specs, scratch, flops, nbytes):
    return pl.pallas_call(
        kernel,
        out_shape=out_shape,
        in_specs=in_specs,
        out_specs=VMEM,
        scratch_shapes=scratch,
        cost_estimate=pl.CostEstimate(flops=flops, bytes_accessed=nbytes, transcendentals=0),
    )


def per_device(
    probes, basis, transfer, local_blocks, remote_blocks, near_dest, near_leaf, couplings, far_list
):
    columns, points = probes.shape
    leaves, rank, size = basis.shape
    devices = lax.axis_size("leaf")
    main = columns // TILE * TILE
    depth = leaves * main + TILE
    blocks = remote_blocks.shape[0] * remote_blocks.shape[1]
    unit = 2 * columns * size * size
    send_bytes = devices * depth * size * 2
    scratch = lambda *arrays: [pltpu.VMEM(a.shape, a.dtype) for a in arrays]

    box = call(
        box_kernel,
        jax.ShapeDtypeStruct((columns, rank), BF16),
        [HBM, HBM, HBM],
        scratch(probes, basis, transfer) + [pltpu.SemaphoreType.DMA((3,))],
        2 * leaves * unit,
        basis.size * 2 + transfer.size * 2,
    )(probes, basis, transfer)
    boxes = lax.all_gather(box[None], "leaf", axis=0, tiled=True)

    send = call(
        functools.partial(products_kernel, main),
        jax.ShapeDtypeStruct((devices, depth, size), BF16),
        [SMEM, SMEM, HBM, HBM],
        scratch(probes, remote_blocks)
        + [pltpu.VMEM((devices, TILE, size), F32), pltpu.SemaphoreType.DMA((1 + leaves,))],
        blocks * unit,
        remote_blocks.size * 2 + send_bytes,
    )(near_dest.T, near_leaf.T, probes, remote_blocks)
    near = lax.psum_scatter(send, "leaf", scatter_dimension=0, tiled=True)[0]

    base = call(
        local_kernel,
        jax.ShapeDtypeStruct((columns, points), F32),
        [HBM, HBM],
        scratch(probes, local_blocks) + [pltpu.SemaphoreType.DMA((1 + leaves,))],
        leaves * leaves * unit,
        local_blocks.size * 2,
    )(probes, local_blocks)
    base = call(
        far_kernel,
        jax.ShapeDtypeStruct((columns, points), F32),
        [SMEM, VMEM, VMEM, HBM, HBM, HBM],
        scratch(couplings, transfer, basis) + [pltpu.SemaphoreType.DMA((3,))],
        4 * leaves * unit,
        couplings.size * 2 + boxes.size * 2,
    )(far_list, base, boxes, couplings, transfer, basis)

    return call(
        functools.partial(add_kernel, main),
        jax.ShapeDtypeStruct((columns, points), F32),
        [VMEM, VMEM],
        [],
        columns * points,
        depth * size * 2,
    )(base, near)


def solution(mesh):
    placed = (
        P(None, ("grp", "leaf")),
        P(("grp", "leaf"), None, None),
        P(("grp", "leaf"), None, None),
        P(("grp", "leaf"), None, None, None),
        P(("grp", "leaf"), None, None, None),
        P(("grp", "leaf"), None),
        P(("grp", "leaf"), None),
        P(("grp", "leaf"), None, None, None),
        P(("grp", "leaf"), None),
    )
    return jax.shard_map(
        per_device, mesh=mesh, in_specs=placed, out_specs=P(None, ("grp", "leaf")), check_vma=False
    )
```

```python
import functools

import jax
import jax.numpy as jnp
from jax import lax
from jax.experimental import pallas as pl
from jax.experimental.pallas import tpu as pltpu
from jax.sharding import PartitionSpec as P

CAP = 4
TILE = 16
LANES = 128
DIRECT = 16

F32 = jnp.float32
BF16 = jnp.bfloat16
I32 = jnp.int32

ANY = pl.BlockSpec(memory_space=pl.ANY)
VMEM = pl.BlockSpec(memory_space=pltpu.VMEM)


def dot_t(lhs, rhs):
    return lax.dot_general(lhs, rhs, (((1,), (1,)), ((), ())), preferred_element_type=F32)


def dot(lhs, rhs):
    return lax.dot_general(lhs, rhs, (((1,), (0,)), ((), ())), preferred_element_type=F32)


class Copies:
    def __init__(self, sems):
        self.sems, self.used = sems, 0

    def start(self, src, dst):
        copy = pltpu.make_async_copy(src, dst, self.sems.at[self.used])
        self.used += 1
        copy.start()
        return copy


def relative(devices):
    return devices <= DIRECT


def place(device, devices):
    return jnp.bitwise_xor(device, lax.axis_index("leaf")) if relative(devices) else device


def products_kernel(main, devices, *refs):
    dest_hbm, leaf_hbm, probes_hbm, basis_hbm, transfer_hbm, blocks_hbm = refs[:6]
    outs = refs[6:-10]
    dest_ref, leaf_ref, probes_ref, basis_ref, transfer_ref, blocks_ref, send_ref, tails, count, sems = refs[-10:]
    leaves, per_leaf, size = blocks_ref.shape[:3]
    columns, rank = probes_ref.shape[0], basis_ref.shape[1]
    copies = Copies(sems)
    early = [
        copies.start(probes_hbm, probes_ref),
        copies.start(basis_hbm, basis_ref),
        copies.start(transfer_hbm, transfer_ref),
        copies.start(dest_hbm, dest_ref),
        copies.start(leaf_hbm, leaf_ref),
    ]
    arrivals = [copies.start(blocks_hbm.at[j], blocks_ref.at[j]) for j in range(leaves)]

    @pl.loop(0, devices)
    def _(i):
        count[i] = 0
        tails[i] = jnp.full(tails.shape[1:], leaves, F32)

    for copy in early:
        copy.wait()
    box = jnp.zeros((columns, rank), F32)
    for j in range(leaves):
        coef = dot_t(probes_ref[:, j * size : (j + 1) * size], basis_ref[j]).astype(BF16)
        box += dot_t(coef, transfer_ref[j])
    half = main // 2
    packed = jnp.concatenate([box[:half], box[half:main]], axis=1).astype(BF16)
    last = jnp.concatenate([box[main:], jnp.zeros_like(box[main:])], axis=1)

    lane = lax.broadcasted_iota(I32, (1, size), 1)
    for j in range(leaves):
        arrivals[j].wait()
        x = probes_ref[:, j * size : (j + 1) * size]
        for first in range(0, per_leaf, 4):
            many = min(4, per_leaf - first)
            rhs = blocks_ref[j, first : first + many].reshape(many * size, size)
            product = dot_t(x, rhs)
            for b in range(many):
                target = place(dest_ref[first + b, j], devices)
                slot = count[target]
                count[target] = slot + 1
                block = product[:, b * size : (b + 1) * size]
                send_ref[target, pl.ds(pl.multiple_of(slot * main, TILE), main), :] = block[:main].astype(BF16)
                tails[target, pl.ds(slot, 1), :] = block[main:]
                number = leaf_ref[first + b, j].astype(F32)
                tails[target, CAP : CAP + 1, :] = jnp.where(lane == slot, number, tails[target, CAP : CAP + 1, :])

    @pl.loop(0, devices)
    def _(i):
        tails[i, CAP + 1 : CAP + 2, :] = last
        send_ref[i, CAP * main : CAP * main + TILE, :] = tails[i].astype(BF16)
        send_ref[i, CAP * main + TILE :, :] = packed

    leaving = []
    for m in order(devices):
        out = outs[m] if relative(devices) else outs[0].at[m]
        leaving.append(copies.start(send_ref.at[m], out))
    for copy in leaving:
        copy.wait()


def order(devices):
    return sorted(range(devices), reverse=True)


def local_kernel(probes_hbm, local_hbm, base_ref, probes_ref, local_ref, sems):
    leaves, size = local_ref.shape[0], local_ref.shape[2]
    copies = Copies(sems)
    early = copies.start(probes_hbm, probes_ref)
    arrivals = [copies.start(local_hbm.at[i], local_ref.at[i]) for i in range(leaves)]
    early.wait()
    for i in range(leaves):
        arrivals[i].wait()
        total = dot_t(probes_ref[:, :size], local_ref[i, 0])
        for c in range(1, leaves):
            total += dot_t(probes_ref[:, c * size : (c + 1) * size], local_ref[i, c])
        base_ref[:, i * size : (i + 1) * size] = total


def gather_kernel(main, devices, *refs):
    partner_hbm, base_hbm, couplings_hbm, transfer_hbm, basis_hbm = refs[:5]
    parts = refs[5:-11]
    out_ref, partner_ref, couplings_ref, transfer_ref, basis_ref, incoming_ref, meta, leaf_ref, total, sems, late = (
        refs[-11:]
    )
    columns = out_ref.shape[0]
    leaves, rank, size = basis_ref.shape
    points = leaves * size
    edge = CAP * main
    copies = Copies(sems)
    part = lambda m: parts[m] if relative(devices) else parts[0].at[m]
    small = [
        copies.start(part(m).at[pl.ds(edge, incoming_ref.shape[1] - edge)], incoming_ref.at[m, pl.ds(edge, incoming_ref.shape[1] - edge)])
        for m in range(devices)
    ]
    weights = [
        copies.start(partner_hbm, partner_ref),
        copies.start(couplings_hbm, couplings_ref),
        copies.start(transfer_hbm, transfer_ref),
        copies.start(basis_hbm, basis_ref),
        copies.start(base_hbm, total.at[:, pl.ds(0, points)]),
    ]
    large = [copies.start(part(m).at[pl.ds(0, edge)], incoming_ref.at[m, pl.ds(0, edge)]) for m in range(devices)]

    for m in range(devices):
        small[m].wait()
        meta[m : m + 1, :] = incoming_ref[m, edge : edge + TILE, :].astype(F32)[CAP : CAP + 1].astype(I32)
    numbers = pltpu.make_async_copy(meta, leaf_ref, late)
    numbers.start()

    for copy in weights:
        copy.wait()
    total[:, points:] = jnp.zeros((columns, size), F32)
    far = jnp.zeros((columns, rank), F32)
    for f in range(couplings_ref.shape[1]):
        source = place(partner_ref[0, f], devices)
        packed = incoming_ref[source, edge + TILE :, :]
        last = incoming_ref[source, edge : edge + TILE, :].astype(F32)[CAP + 1 : CAP + 2, :rank]
        box = jnp.concatenate(
            [packed[:, :rank].astype(F32), packed[:, rank:].astype(F32), last], axis=0
        ).astype(BF16)
        far += dot_t(box, couplings_ref[0, f])
    far = far.astype(BF16)
    for j in range(leaves):
        down = dot(far, transfer_ref[j]).astype(BF16)
        total[:, j * size : (j + 1) * size] += dot(down, basis_ref[j])

    numbers.wait()
    for copy in large:
        copy.wait()

    @pl.loop(0, devices)
    def _(m):
        tail = incoming_ref[m, edge : edge + TILE, :].astype(F32)
        for slot in range(CAP):
            cols = pl.ds(pl.multiple_of(leaf_ref[m, slot] * size, size), size)
            total[:main, cols] += incoming_ref[m, slot * main : (slot + 1) * main, :].astype(F32)
            total[main:, cols] += tail[slot : slot + 1]

    out_ref[...] = total[:, :points]


def call(kernel, out_shape, out_specs, operands, scratch, flops, nbytes):
    return pl.pallas_call(
        kernel,
        out_shape=out_shape,
        in_specs=[ANY] * len(operands),
        out_specs=out_specs,
        scratch_shapes=scratch,
        cost_estimate=pl.CostEstimate(flops=flops, bytes_accessed=nbytes, transcendentals=0),
    )(*operands)


def per_device(
    probes, basis, transfer, local_blocks, remote_blocks, near_dest, near_leaf, couplings, far_list
):
    columns, points = probes.shape
    leaves, rank, size = basis.shape
    devices = lax.axis_size("leaf")
    main = columns // TILE * TILE
    depth = CAP * main + TILE + main // 2
    blocks = remote_blocks.shape[0] * remote_blocks.shape[1]
    unit = 2 * columns * size * size
    send_bytes = devices * depth * size * 2
    like = lambda *arrays: [pltpu.VMEM(a.shape, a.dtype) for a in arrays]
    numbers = lambda *arrays: [pltpu.SMEM(a.shape, a.dtype) for a in arrays]
    sems = lambda count: [pltpu.SemaphoreType.DMA((count,))]

    if relative(devices):
        outgoing = [jax.ShapeDtypeStruct((depth, size), BF16)] * devices
    else:
        outgoing = [jax.ShapeDtypeStruct((devices, depth, size), BF16)]
    dest, leaf = near_dest.T, near_leaf.T
    send = call(
        functools.partial(products_kernel, main, devices),
        outgoing,
        [ANY] * len(outgoing),
        (dest, leaf, probes, basis, transfer, remote_blocks),
        numbers(dest, leaf)
        + like(probes, basis, transfer, remote_blocks)
        + [
            pltpu.VMEM((devices, depth, size), BF16),
            pltpu.VMEM((devices, TILE, size), F32),
            pltpu.SMEM((devices,), I32),
        ]
        + sems(5 + leaves + devices),
        blocks * unit,
        remote_blocks.size * 2 + send_bytes,
    )
    if relative(devices):
        incoming = list(send)
        for m in order(devices)[:-1]:
            incoming[m] = lax.ppermute(send[m], "leaf", [(i, i ^ m) for i in range(devices)])
    else:
        incoming = [lax.all_to_all(send[0], "leaf", split_axis=0, concat_axis=0, tiled=True)]

    base = call(
        local_kernel,
        jax.ShapeDtypeStruct((columns, points), F32),
        VMEM,
        (probes, local_blocks),
        like(probes, local_blocks) + sems(1 + leaves),
        leaves * leaves * unit,
        local_blocks.size * 2,
    )

    return call(
        functools.partial(gather_kernel, main, devices),
        jax.ShapeDtypeStruct((columns, points), F32),
        VMEM,
        (far_list, base, couplings, transfer, basis, *incoming),
        numbers(far_list)
        + like(couplings, transfer, basis)
        + [
            pltpu.VMEM((devices, depth, size), BF16),
            pltpu.VMEM((devices, LANES), I32),
            pltpu.SMEM((devices, LANES), I32),
            pltpu.VMEM((columns, points + size), F32),
        ]
        + sems(5 + 2 * devices)
        + [pltpu.SemaphoreType.DMA(())],
        devices * CAP * columns * size,
        send_bytes,
    )


def solution(mesh):
    placed = (
        P(None, ("grp", "leaf")),
        P(("grp", "leaf"), None, None),
        P(("grp", "leaf"), None, None),
        P(("grp", "leaf"), None, None, None),
        P(("grp", "leaf"), None, None, None),
        P(("grp", "leaf"), None),
        P(("grp", "leaf"), None),
        P(("grp", "leaf"), None, None, None),
        P(("grp", "leaf"), None),
    )
    return jax.shard_map(
        per_device, mesh=mesh, in_specs=placed, out_specs=P(None, ("grp", "leaf")), check_vma=False
    )
```

```python
import functools

import jax
import jax.numpy as jnp
from jax import lax
from jax.experimental import pallas as pl
from jax.experimental.pallas import tpu as pltpu
from jax.sharding import PartitionSpec as P

CAP = 4
TILE = 16
LANES = 128
DIRECT = 16
AHEAD = 5

F32 = jnp.float32
BF16 = jnp.bfloat16
I32 = jnp.int32

ANY = pl.BlockSpec(memory_space=pl.ANY)
VMEM = pl.BlockSpec(memory_space=pltpu.VMEM)


def dot_t(lhs, rhs):
    return lax.dot_general(lhs, rhs, (((1,), (1,)), ((), ())), preferred_element_type=F32)


def dot(lhs, rhs):
    return lax.dot_general(lhs, rhs, (((1,), (0,)), ((), ())), preferred_element_type=F32)


class Copies:
    def __init__(self, sems):
        self.sems, self.used = sems, 0

    def start(self, src, dst):
        copy = pltpu.make_async_copy(src, dst, self.sems.at[self.used])
        self.used += 1
        copy.start()
        return copy


def relative(devices):
    return devices <= DIRECT


def place(device, devices):
    return jnp.bitwise_xor(device, lax.axis_index("leaf")) if relative(devices) else device


def products_kernel(main, devices, *refs):
    dest_hbm, leaf_hbm, probes_hbm, basis_hbm, transfer_hbm, blocks_hbm = refs[:6]
    outs = refs[6:-10]
    dest_ref, leaf_ref, probes_ref, basis_ref, transfer_ref, blocks_ref, send_ref, tails, count, sems = refs[-10:]
    leaves, per_leaf, size = blocks_ref.shape[:3]
    columns, rank = probes_ref.shape[0], basis_ref.shape[1]
    copies = Copies(sems)
    early = [
        copies.start(probes_hbm, probes_ref),
        copies.start(basis_hbm, basis_ref),
        copies.start(transfer_hbm, transfer_ref),
        copies.start(dest_hbm, dest_ref),
        copies.start(leaf_hbm, leaf_ref),
    ]
    chunk = leaves // 2
    arrivals = [
        copies.start(blocks_hbm.at[pl.ds(j, chunk)], blocks_ref.at[pl.ds(j, chunk)])
        for j in range(0, leaves, chunk)
    ]

    @pl.loop(0, devices)
    def _(i):
        count[i] = 0
        tails[i] = jnp.full(tails.shape[1:], leaves, F32)

    for copy in early:
        copy.wait()
    box = jnp.zeros((columns, rank), F32)
    for j in range(leaves):
        coef = dot_t(probes_ref[:, j * size : (j + 1) * size], basis_ref[j]).astype(BF16)
        box += dot_t(coef, transfer_ref[j])
    half = main // 2
    packed = jnp.concatenate([box[:half], box[half:main]], axis=1).astype(BF16)
    last = jnp.concatenate([box[main:], jnp.zeros_like(box[main:])], axis=1)

    lane = lax.broadcasted_iota(I32, (1, size), 1)
    for j in range(leaves):
        if j % chunk == 0:
            arrivals[j // chunk].wait()
        x = probes_ref[:, j * size : (j + 1) * size]
        for first in range(0, per_leaf, 4):
            many = min(4, per_leaf - first)
            rhs = blocks_ref[j, first : first + many].reshape(many * size, size)
            product = dot_t(x, rhs)
            for b in range(many):
                target = place(dest_ref[first + b, j], devices)
                slot = count[target]
                count[target] = slot + 1
                block = product[:, b * size : (b + 1) * size]
                send_ref[target, pl.ds(pl.multiple_of(slot * main, TILE), main), :] = block[:main].astype(BF16)
                tails[target, pl.ds(slot, 1), :] = block[main:]
                number = leaf_ref[first + b, j].astype(F32)
                tails[target, CAP : CAP + 1, :] = jnp.where(lane == slot, number, tails[target, CAP : CAP + 1, :])

    @pl.loop(0, devices)
    def _(i):
        tails[i, CAP + 1 : CAP + 2, :] = last
        send_ref[i, CAP * main : CAP * main + TILE, :] = tails[i].astype(BF16)
        send_ref[i, CAP * main + TILE :, :] = packed

    leaving = []
    for m in order(devices):
        out = outs[m] if relative(devices) else outs[0].at[m]
        leaving.append(copies.start(send_ref.at[m], out))
    for copy in leaving:
        copy.wait()


def order(devices):
    half = devices // 2
    far, near = list(range(half, devices)), list(range(1, half)) + [0]
    return [m for pair in zip(far, near) for m in pair]


def local_part(probes_ref, local_ref, out_ref):
    leaves, size = local_ref.shape[0], local_ref.shape[2]
    for i in range(leaves):
        total = dot_t(probes_ref[:, :size], local_ref[i, 0])
        for c in range(1, leaves):
            total += dot_t(probes_ref[:, c * size : (c + 1) * size], local_ref[i, c])
        out_ref[:, i * size : (i + 1) * size] = total


def local_kernel(probes_hbm, local_hbm, base_ref, probes_ref, local_ref, sems):
    copies = Copies(sems)
    for copy in [copies.start(probes_hbm, probes_ref), copies.start(local_hbm, local_ref)]:
        copy.wait()
    local_part(probes_ref, local_ref, base_ref)


def add_slots(main, members, parts, incoming_ref, meta, leaf_ref, total, copies, late, between):
    size = incoming_ref.shape[2]
    points = total.shape[1] - size
    edge = CAP * main
    tiles = [
        copies.start(parts(m).at[pl.ds(edge, TILE)], incoming_ref.at[i, pl.ds(edge, TILE)])
        for i, m in enumerate(members)
    ]
    large = [
        copies.start(parts(m).at[pl.ds(0, edge)], incoming_ref.at[i, pl.ds(0, edge)])
        for i, m in enumerate(members)
    ]
    total[:, points:] = jnp.zeros((total.shape[0], size), F32)
    for i, copy in enumerate(tiles):
        copy.wait()
        meta[i : i + 1, :] = incoming_ref[i, edge : edge + TILE, :].astype(F32)[CAP : CAP + 1].astype(I32)
    numbers = pltpu.make_async_copy(meta, leaf_ref, late)
    numbers.start()
    between()
    numbers.wait()
    for copy in large:
        copy.wait()

    @pl.loop(0, len(members))
    def _(i):
        tail = incoming_ref[i, edge : edge + TILE, :].astype(F32)
        for slot in range(CAP):
            cols = pl.ds(pl.multiple_of(leaf_ref[i, slot] * size, size), size)
            total[:main, cols] += incoming_ref[i, slot * main : (slot + 1) * main, :].astype(F32)
            total[main:, cols] += tail[slot : slot + 1]


def early_kernel(main, devices, members, probes_hbm, local_hbm, *refs):
    parts = refs[:-9]
    out_ref, probes_ref, local_ref, incoming_ref, meta, leaf_ref, total, sems, late = refs[-9:]
    part = lambda m: parts[members.index(m)]
    copies = Copies(sems)
    arrivals = [copies.start(probes_hbm, probes_ref), copies.start(local_hbm, local_ref)]

    def between():
        for copy in arrivals:
            copy.wait()
        local_part(probes_ref, local_ref, total)

    add_slots(main, members, part, incoming_ref, meta, leaf_ref, total, copies, late, between)
    out_ref[...] = total[:, : out_ref.shape[1]]


def last_kernel(main, devices, members, *refs):
    partner_hbm, base_hbm, couplings_hbm, transfer_hbm, basis_hbm = refs[:5]
    parts = refs[5:-12]
    (
        out_ref, partner_ref, couplings_ref, transfer_ref, basis_ref,
        boxes_ref, incoming_ref, meta, leaf_ref, total, sems, late,
    ) = refs[-12:]
    columns = out_ref.shape[0]
    leaves, rank, size = basis_ref.shape
    edge = CAP * main
    copies = Copies(sems)
    part = lambda m: parts[m] if relative(devices) else parts[0].at[m]
    arrivals = [
        copies.start(part(m).at[pl.ds(edge, boxes_ref.shape[1])], boxes_ref.at[m]) for m in range(devices)
    ] + [
        copies.start(partner_hbm, partner_ref),
        copies.start(couplings_hbm, couplings_ref),
        copies.start(transfer_hbm, transfer_ref),
        copies.start(basis_hbm, basis_ref),
        copies.start(base_hbm, total.at[:, pl.ds(0, leaves * size)]),
    ]

    def far_part():
        for copy in arrivals:
            copy.wait()
        far = jnp.zeros((columns, rank), F32)
        for f in range(couplings_ref.shape[1]):
            source = place(partner_ref[0, f], devices)
            packed = boxes_ref[source, TILE:, :]
            last = boxes_ref[source, :TILE, :].astype(F32)[CAP + 1 : CAP + 2, :rank]
            box = jnp.concatenate(
                [packed[:, :rank].astype(F32), packed[:, rank:].astype(F32), last], axis=0
            ).astype(BF16)
            far += dot_t(box, couplings_ref[0, f])
        far = far.astype(BF16)
        for j in range(leaves):
            down = dot(far, transfer_ref[j]).astype(BF16)
            total[:, j * size : (j + 1) * size] += dot(down, basis_ref[j])

    add_slots(main, members, part, incoming_ref, meta, leaf_ref, total, copies, late, far_part)
    out_ref[...] = total[:, : out_ref.shape[1]]


def call(kernel, out_shape, out_specs, operands, scratch, flops, nbytes):
    return pl.pallas_call(
        kernel,
        out_shape=out_shape,
        in_specs=[ANY] * len(operands),
        out_specs=out_specs,
        scratch_shapes=scratch,
        cost_estimate=pl.CostEstimate(flops=flops, bytes_accessed=nbytes, transcendentals=0),
    )(*operands)


def per_device(
    probes, basis, transfer, local_blocks, remote_blocks, near_dest, near_leaf, couplings, far_list
):
    columns, points = probes.shape
    leaves, rank, size = basis.shape
    devices = lax.axis_size("leaf")
    main = columns // TILE * TILE
    depth = CAP * main + TILE + main // 2
    blocks = remote_blocks.shape[0] * remote_blocks.shape[1]
    unit = 2 * columns * size * size
    send_bytes = devices * depth * size * 2
    like = lambda *arrays: [pltpu.VMEM(a.shape, a.dtype) for a in arrays]
    numbers = lambda *arrays: [pltpu.SMEM(a.shape, a.dtype) for a in arrays]
    sems = lambda count: [pltpu.SemaphoreType.DMA((count,))]

    if relative(devices):
        outgoing = [jax.ShapeDtypeStruct((depth, size), BF16)] * devices
    else:
        outgoing = [jax.ShapeDtypeStruct((devices, depth, size), BF16)]
    dest, leaf = near_dest.T, near_leaf.T
    send = call(
        functools.partial(products_kernel, main, devices),
        outgoing,
        [ANY] * len(outgoing),
        (dest, leaf, probes, basis, transfer, remote_blocks),
        numbers(dest, leaf)
        + like(probes, basis, transfer, remote_blocks)
        + [
            pltpu.VMEM((devices, depth, size), BF16),
            pltpu.VMEM((devices, TILE, size), F32),
            pltpu.SMEM((devices,), I32),
        ]
        + sems(7 + devices),
        blocks * unit,
        remote_blocks.size * 2 + send_bytes,
    )
    gathering = lambda members: [
        pltpu.VMEM((len(members), depth, size), BF16),
        pltpu.VMEM((len(members), LANES), I32),
        pltpu.SMEM((len(members), LANES), I32),
        pltpu.VMEM((columns, points + size), F32),
    ]

    late = list(range(devices))
    if relative(devices):
        ways = order(devices)[:-1]
        send = list(send)
        incoming = [send[0]] + [None] * (devices - 1)
        for m in ways:
            incoming[m] = lax.ppermute(send[m], "leaf", [(i, i ^ m) for i in range(devices)])
        late = ways[-AHEAD:]
        early = [0] + ways[:-AHEAD]
        base = call(
            functools.partial(early_kernel, main, devices, early),
            jax.ShapeDtypeStruct((columns, points), F32),
            VMEM,
            (probes, local_blocks, *[incoming[m] for m in early]),
            like(probes, local_blocks)
            + gathering(early)
            + sems(2 + 2 * len(early))
            + [pltpu.SemaphoreType.DMA(())],
            leaves * leaves * unit,
            local_blocks.size * 2 + len(early) * depth * size * 2,
        )
    else:
        incoming = [lax.all_to_all(send[0], "leaf", split_axis=0, concat_axis=0, tiled=True)]
        base = call(
            local_kernel,
            jax.ShapeDtypeStruct((columns, points), F32),
            VMEM,
            (probes, local_blocks),
            like(probes, local_blocks) + sems(2),
            leaves * leaves * unit,
            local_blocks.size * 2,
        )

    return call(
        functools.partial(last_kernel, main, devices, late),
        jax.ShapeDtypeStruct((columns, points), F32),
        VMEM,
        (far_list, base, couplings, transfer, basis, *incoming),
        numbers(far_list)
        + like(couplings, transfer, basis)
        + [pltpu.VMEM((devices, depth - CAP * main, size), BF16)]
        + gathering(late)
        + sems(5 + devices + 2 * len(late))
        + [pltpu.SemaphoreType.DMA(())],
        len(late) * CAP * columns * size,
        send_bytes,
    )


def solution(mesh):
    placed = (
        P(None, ("grp", "leaf")),
        P(("grp", "leaf"), None, None),
        P(("grp", "leaf"), None, None),
        P(("grp", "leaf"), None, None, None),
        P(("grp", "leaf"), None, None, None),
        P(("grp", "leaf"), None),
        P(("grp", "leaf"), None),
        P(("grp", "leaf"), None, None, None),
        P(("grp", "leaf"), None),
    )
    return jax.shard_map(
        per_device, mesh=mesh, in_specs=placed, out_specs=P(None, ("grp", "leaf")), check_vma=False
    )
```

```python
import functools

import jax
import jax.numpy as jnp
from jax import lax
from jax.experimental import pallas as pl
from jax.experimental.pallas import tpu as pltpu
from jax.sharding import PartitionSpec as P

CAP = 4
TILE = 16
LANES = 128
F32 = jnp.float32
BF16 = jnp.bfloat16
I32 = jnp.int32

ANY = pl.BlockSpec(memory_space=pl.ANY)
VMEM = pl.BlockSpec(memory_space=pltpu.VMEM)


def dot_t(lhs, rhs):
    return lax.dot_general(lhs, rhs, (((1,), (1,)), ((), ())), preferred_element_type=F32)


def dot(lhs, rhs):
    return lax.dot_general(lhs, rhs, (((1,), (0,)), ((), ())), preferred_element_type=F32)


class Copies:
    def __init__(self, sems):
        self.sems, self.used = sems, 0

    def start(self, src, dst):
        copy = pltpu.make_async_copy(src, dst, self.sems.at[self.used])
        self.used += 1
        copy.start()
        return copy


def grid_of(devices):
    low = 1 << (devices.bit_length() // 2)
    return devices // low, low


def up(rows):
    return -(-rows // TILE) * TILE


class Route:
    def __init__(self, first, last, fan, extra, main, columns, leaves, sources):
        self.first, self.rows, self.fan, self.extra, self.main = first, last - first, fan, extra, main
        self.leaves, self.half = leaves, main // 2
        slots = fan * CAP
        self.tails = slots * self.rows
        self.meta = self.tails + (up(slots) if extra else 0)
        self.box = self.meta + TILE
        self.depth = self.box + (self.half if extra else 0)
        self.dense_tails = leaves * self.rows
        self.dense_box = self.dense_tails + (up(leaves + sources) if extra else 0)
        self.dense_depth = self.dense_box + (sources * self.half if extra else 0)


def routes_of(devices, main, columns, leaves):
    high, low = grid_of(devices)
    split = main // 4 * 3
    return (
        Route(0, split, high, False, main, columns, leaves, low),
        Route(split, main, low, True, main, columns, leaves, high),
    )


def products_kernel(routes, devices, *refs):
    dest_hbm, leaf_hbm, probes_hbm, basis_hbm, transfer_hbm, blocks_hbm = refs[:6]
    (
        outs_low, outs_high, dest_ref, leaf_ref, probes_ref, basis_ref, transfer_ref, blocks_ref,
        send_low, send_high, tails, meta_low, meta_high, count, sems,
    ) = refs[6:]
    by_low, by_high = routes
    high, low = grid_of(devices)
    main = by_high.main
    leaves, per_leaf, size = blocks_ref.shape[:3]
    columns, rank = probes_ref.shape[0], basis_ref.shape[1]
    copies = Copies(sems)
    early = [
        copies.start(probes_hbm, probes_ref),
        copies.start(basis_hbm, basis_ref),
        copies.start(transfer_hbm, transfer_ref),
        copies.start(dest_hbm, dest_ref),
        copies.start(leaf_hbm, leaf_ref),
    ]
    chunk = leaves // 2
    arrivals = [
        copies.start(blocks_hbm.at[pl.ds(j, chunk)], blocks_ref.at[pl.ds(j, chunk)])
        for j in range(0, leaves, chunk)
    ]

    @pl.loop(0, devices)
    def _(i):
        count[i] = 0

    tails[...] = jnp.zeros(tails.shape, F32)
    meta_low[...] = jnp.full(meta_low.shape, leaves, F32)
    meta_high[...] = jnp.full(meta_high.shape, leaves, F32)
    for copy in early:
        copy.wait()
    box = jnp.zeros((columns, rank), F32)
    for j in range(leaves):
        coef = dot_t(probes_ref[:, j * size : (j + 1) * size], basis_ref[j]).astype(BF16)
        box += dot_t(coef, transfer_ref[j])
    half = by_high.half
    packed = jnp.concatenate([box[:half], box[half:main]], axis=1).astype(BF16)
    last = jnp.concatenate([box[main:], jnp.zeros_like(box[main:])], axis=1)

    lane = lax.broadcasted_iota(I32, (1, size), 1)
    for j in range(leaves):
        if j % chunk == 0:
            arrivals[j // chunk].wait()
        x = probes_ref[:, j * size : (j + 1) * size]
        for first in range(0, per_leaf, 4):
            many = min(4, per_leaf - first)
            rhs = blocks_ref[j, first : first + many].reshape(many * size, size)
            product = dot_t(x, rhs)
            for b in range(many):
                target = dest_ref[first + b, j]
                slot = count[target]
                count[target] = slot + 1
                to_high, to_low = target // low, target % low
                block = product[:, b * size : (b + 1) * size]
                piece = block[:main].astype(BF16)
                number = leaf_ref[first + b, j].astype(F32)

                at = to_high * CAP + slot
                rows = pl.ds(pl.multiple_of(at * by_low.rows, TILE), by_low.rows)
                send_low[to_low, rows, :] = piece[: by_low.rows]
                meta_low[to_low, 0:1, :] = jnp.where(lane == at, number, meta_low[to_low, 0:1, :])

                at = to_low * CAP + slot
                rows = pl.ds(pl.multiple_of(at * by_high.rows, TILE), by_high.rows)
                send_high[to_high, rows, :] = piece[by_low.rows :]
                tails[to_high, pl.ds(at, 1), :] = block[main:]
                meta_high[to_high, 0:1, :] = jnp.where(lane == at, number, meta_high[to_high, 0:1, :])

    for i in range(low):
        send_low[i, by_low.meta : by_low.box, :] = meta_low[i].astype(BF16)
    for i in range(high):
        meta_high[i, 1:2, :] = last
        send_high[i, by_high.tails : by_high.meta, :] = tails[i].astype(BF16)
        send_high[i, by_high.meta : by_high.box, :] = meta_high[i].astype(BF16)
        send_high[i, by_high.box :, :] = packed
    for copy in [copies.start(send_low, outs_low), copies.start(send_high, outs_high)]:
        copy.wait()


def sum_kernel(routes, devices, *refs):
    came_low, came_high, outs_high, outs_low = refs[:4]
    in_low, in_high, meta, leaf_ref, total_low, total_high, total_tails, send_high, send_low, sems, late = refs[4:]
    by_low, by_high = routes
    high, low = grid_of(devices)
    leaves = by_low.leaves
    copies = Copies(sems)
    arrivals = [
        [
            copies.start(came.at[i, pl.ds(route.meta, TILE)], ref.at[i, pl.ds(route.meta, TILE)])
            for i in range(ways)
        ]
        for came, ref, route, ways in ((came_low, in_low, by_low, low), (came_high, in_high, by_high, high))
    ]
    large = [
        copies.start(came_low.at[:, pl.ds(0, by_low.meta)], in_low.at[:, pl.ds(0, by_low.meta)]),
        copies.start(came_high.at[:, pl.ds(0, by_high.meta)], in_high.at[:, pl.ds(0, by_high.meta)]),
        copies.start(
            came_high.at[:, pl.ds(by_high.box, by_high.half)], in_high.at[:, pl.ds(by_high.box, by_high.half)]
        ),
    ]
    at = 0
    for ref, route, group in ((in_low, by_low, arrivals[0]), (in_high, by_high, arrivals[1])):
        for i, copy in enumerate(group):
            copy.wait()
            tile = ref[i, route.meta : route.box, :].astype(F32)
            meta[at : at + 1, :] = tile[:1].astype(I32)
            at += 1
    numbers = pltpu.make_async_copy(meta, leaf_ref, late)
    numbers.start()
    total_low[...] = jnp.zeros(total_low.shape, F32)
    total_high[...] = jnp.zeros(total_high.shape, F32)
    total_tails[...] = jnp.zeros(total_tails.shape, F32)
    numbers.wait()
    for copy in large:
        copy.wait()

    @pl.loop(0, low)
    def _(i):
        for k in range(high):
            for slot in range(CAP):
                at = k * CAP + slot
                leaf = leaf_ref[i, at]
                rows = pl.ds(pl.multiple_of(leaf * by_low.rows, TILE), by_low.rows)
                total_low[k, rows, :] += in_low[i, at * by_low.rows : (at + 1) * by_low.rows, :].astype(F32)

    @pl.loop(0, high)
    def _(i):
        tail = in_high[i, by_high.tails : by_high.meta, :].astype(F32)
        for k in range(low):
            for slot in range(CAP):
                at = k * CAP + slot
                leaf = leaf_ref[low + i, at]
                rows = pl.ds(pl.multiple_of(leaf * by_high.rows, TILE), by_high.rows)
                total_high[k, rows, :] += in_high[i, at * by_high.rows : (at + 1) * by_high.rows, :].astype(F32)
                total_tails[k, pl.ds(leaf, 1), :] += tail[at : at + 1]

    for k in range(high):
        send_high[k] = total_low[k, : by_low.dense_tails, :].astype(BF16)
    lasts = [in_high[i, by_high.meta : by_high.box, :].astype(F32)[1:2] for i in range(high)]
    for k in range(low):
        send_low[k, : by_high.dense_tails, :] = total_high[k, : by_high.dense_tails, :].astype(BF16)
        for i in range(high):
            total_tails[k, leaves + i : leaves + i + 1, :] = lasts[i]
            start = by_high.dense_box + i * by_high.half
            send_low[k, start : start + by_high.half, :] = in_high[i, by_high.box :, :]
        send_low[k, by_high.dense_tails : by_high.dense_box, :] = total_tails[k].astype(BF16)
    for copy in [copies.start(send_high, outs_high), copies.start(send_low, outs_low)]:
        copy.wait()


def local_part(probes_ref, local_ref, out_ref):
    leaves, size = local_ref.shape[0], local_ref.shape[2]
    for i in range(leaves):
        total = dot_t(probes_ref[:, :size], local_ref[i, 0])
        for c in range(1, leaves):
            total += dot_t(probes_ref[:, c * size : (c + 1) * size], local_ref[i, c])
        out_ref[:, i * size : (i + 1) * size] = total


def local_kernel(probes_hbm, local_hbm, base_ref, probes_ref, local_ref, sems):
    copies = Copies(sems)
    for copy in [copies.start(probes_hbm, probes_ref), copies.start(local_hbm, local_ref)]:
        copy.wait()
    local_part(probes_ref, local_ref, base_ref)


def last_kernel(routes, devices, *refs):
    (
        partner_hbm, base_hbm, couplings_hbm, transfer_hbm, basis_hbm, came_high, came_low,
        out_ref, partner_ref, base_ref, couplings_ref, transfer_ref, basis_ref, in_high, in_low, sems,
    ) = refs
    by_low, by_high = routes
    high, low = grid_of(devices)
    columns = out_ref.shape[0]
    leaves, rank, size = basis_ref.shape
    split, main = by_low.rows, by_low.main
    copies = Copies(sems)
    early = [
        copies.start(came_low, in_low),
        copies.start(partner_hbm, partner_ref),
        copies.start(couplings_hbm, couplings_ref),
        copies.start(transfer_hbm, transfer_ref),
        copies.start(basis_hbm, basis_ref),
    ]
    later = [copies.start(came_high, in_high), copies.start(base_hbm, base_ref)]
    for copy in early:
        copy.wait()
    far = jnp.zeros((columns, rank), F32)
    for f in range(couplings_ref.shape[1]):
        source = partner_ref[0, f]
        to_high, to_low = source // low, source % low
        start = pl.multiple_of(by_high.dense_box + to_high * by_high.half, TILE)
        packed = in_low[to_low, pl.ds(start, by_high.half), :]
        tile = in_low[to_low, by_high.dense_tails : by_high.dense_box, :].astype(F32)
        row = lax.broadcasted_iota(I32, tile.shape, 0)
        last = jnp.sum(jnp.where(row == leaves + to_high, tile, 0.0), axis=0, keepdims=True)[:, :rank]
        box = jnp.concatenate(
            [packed[:, :rank].astype(F32), packed[:, rank:].astype(F32), last], axis=0
        ).astype(BF16)
        far += dot_t(box, couplings_ref[0, f])
    far = far.astype(BF16)
    down = [dot(far, transfer_ref[j]).astype(BF16) for j in range(leaves)]
    far_part = [dot(down[j], basis_ref[j]) for j in range(leaves)]
    for copy in later:
        copy.wait()
    tails = sum(in_low[k, by_high.dense_tails : by_high.dense_box, :].astype(F32) for k in range(low))
    for j in range(leaves):
        cols = slice(j * size, (j + 1) * size)
        upper = sum(in_high[k, j * by_low.rows : (j + 1) * by_low.rows, :].astype(F32) for k in range(high))
        lower = sum(in_low[k, j * by_high.rows : (j + 1) * by_high.rows, :].astype(F32) for k in range(low))
        out_ref[:split, cols] = base_ref[:split, cols] + far_part[j][:split] + upper
        out_ref[split:main, cols] = base_ref[split:main, cols] + far_part[j][split:main] + lower
        out_ref[main:, cols] = base_ref[main:, cols] + far_part[j][main:] + tails[j : j + 1]


def call(kernel, out_shape, out_specs, operands, scratch, flops, nbytes):
    return pl.pallas_call(
        kernel,
        out_shape=out_shape,
        in_specs=[ANY] * len(operands),
        out_specs=out_specs,
        scratch_shapes=scratch,
        cost_estimate=pl.CostEstimate(flops=flops, bytes_accessed=nbytes, transcendentals=0),
    )(*operands)


def per_device(
    probes, basis, transfer, local_blocks, remote_blocks, near_dest, near_leaf, couplings, far_list
):
    columns, points = probes.shape
    leaves, rank, size = basis.shape
    devices = lax.axis_size("leaf")
    main = columns // TILE * TILE
    routes = by_low, by_high = routes_of(devices, main, columns, leaves)
    high, low = grid_of(devices)
    blocks = remote_blocks.shape[0] * remote_blocks.shape[1]
    unit = 2 * columns * size * size
    like = lambda *arrays: [pltpu.VMEM(a.shape, a.dtype) for a in arrays]
    numbers = lambda *arrays: [pltpu.SMEM(a.shape, a.dtype) for a in arrays]
    sems = lambda count: [pltpu.SemaphoreType.DMA((count,))]
    same_high = [[h * low + l for l in range(low)] for h in range(high)]
    same_low = [[h * low + l for h in range(high)] for l in range(low)]
    exchange = lambda x, groups: lax.all_to_all(
        x, "leaf", split_axis=0, concat_axis=0, tiled=True, axis_index_groups=groups
    )

    to_low = jax.ShapeDtypeStruct((low, by_low.depth, size), BF16)
    to_high = jax.ShapeDtypeStruct((high, by_high.depth, size), BF16)
    dest, leaf = near_dest.T, near_leaf.T
    send_low, send_high = call(
        functools.partial(products_kernel, routes, devices),
        [to_low, to_high],
        [ANY, ANY],
        (dest, leaf, probes, basis, transfer, remote_blocks),
        numbers(dest, leaf)
        + like(probes, basis, transfer, remote_blocks, to_low, to_high)
        + [
            pltpu.VMEM((high, by_high.meta - by_high.tails, size), F32),
            pltpu.VMEM((low, TILE, size), F32),
            pltpu.VMEM((high, TILE, size), F32),
            pltpu.SMEM((devices,), I32),
        ]
        + sems(9),
        blocks * unit,
        remote_blocks.size * 2 + to_low.size * 2 + to_high.size * 2,
    )
    came_low = exchange(send_low, same_high)
    came_high = exchange(send_high, same_low)

    base = call(
        local_kernel,
        jax.ShapeDtypeStruct((columns, points), F32),
        VMEM,
        (probes, local_blocks),
        like(probes, local_blocks) + sems(2),
        leaves * leaves * unit,
        local_blocks.size * 2,
    )

    dense_high = jax.ShapeDtypeStruct((high, by_low.dense_depth, size), BF16)
    dense_low = jax.ShapeDtypeStruct((low, by_high.dense_depth, size), BF16)
    send_high, send_low = call(
        functools.partial(sum_kernel, routes, devices),
        [dense_high, dense_low],
        [ANY, ANY],
        (came_low, came_high),
        like(came_low, came_high)
        + [
            pltpu.VMEM((low + high, size), I32),
            pltpu.SMEM((low + high, size), I32),
            pltpu.VMEM((high, (leaves + 1) * by_low.rows, size), F32),
            pltpu.VMEM((low, (leaves + 1) * by_high.rows, size), F32),
            pltpu.VMEM((low, by_high.dense_box - by_high.dense_tails, size), F32),
        ]
        + like(dense_high, dense_low)
        + sems(5 + low + high)
        + [pltpu.SemaphoreType.DMA(())],
        devices * CAP * columns * size,
        4 * (to_low.size + to_high.size),
    )
    came_high = exchange(send_high, same_low)
    came_low = exchange(send_low, same_high)

    return call(
        functools.partial(last_kernel, routes, devices),
        jax.ShapeDtypeStruct((columns, points), F32),
        VMEM,
        (far_list, base, couplings, transfer, basis, came_high, came_low),
        numbers(far_list) + like(base, couplings, transfer, basis, came_high, came_low) + sems(7),
        devices * columns * size,
        2 * (dense_high.size + dense_low.size),
    )


def solution(mesh):
    placed = (
        P(None, ("grp", "leaf")),
        P(("grp", "leaf"), None, None),
        P(("grp", "leaf"), None, None),
        P(("grp", "leaf"), None, None, None),
        P(("grp", "leaf"), None, None, None),
        P(("grp", "leaf"), None),
        P(("grp", "leaf"), None),
        P(("grp", "leaf"), None, None, None),
        P(("grp", "leaf"), None),
    )
    return jax.shard_map(
        per_device, mesh=mesh, in_specs=placed, out_specs=P(None, ("grp", "leaf")), check_vma=False
    )
```

```python
import functools

import jax
import jax.numpy as jnp
from jax import lax
from jax.experimental import pallas as pl
from jax.experimental.pallas import tpu as pltpu
from jax.sharding import PartitionSpec as P

CAP = 4
TILE = 16
LANES = 128
F32 = jnp.float32
BF16 = jnp.bfloat16
I32 = jnp.int32

ANY = pl.BlockSpec(memory_space=pl.ANY)
VMEM = pl.BlockSpec(memory_space=pltpu.VMEM)


def dot_t(lhs, rhs):
    return lax.dot_general(lhs, rhs, (((1,), (1,)), ((), ())), preferred_element_type=F32)


def dot(lhs, rhs):
    return lax.dot_general(lhs, rhs, (((1,), (0,)), ((), ())), preferred_element_type=F32)


class Copies:
    def __init__(self, sems):
        self.sems, self.used = sems, 0

    def start(self, src, dst):
        copy = pltpu.make_async_copy(src, dst, self.sems.at[self.used])
        self.used += 1
        copy.start()
        return copy


def grid_of(devices):
    low = 1 << (devices.bit_length() // 2)
    return devices // low, low


def up(rows):
    return -(-rows // TILE) * TILE


class Route:
    def __init__(self, first, last, fan, extra, main, columns, leaves, sources):
        self.first, self.rows, self.fan, self.extra, self.main = first, last - first, fan, extra, main
        self.leaves, self.half = leaves, main // 2
        slots = fan * CAP
        self.tails = slots * self.rows
        self.meta = self.tails + (up(slots) if extra else 0)
        self.box = self.meta + TILE
        self.depth = self.box + (self.half if extra else 0)
        self.dense_tails = leaves * self.rows
        self.dense_box = self.dense_tails + (up(leaves + sources) if extra else 0)
        self.dense_depth = self.dense_box + (sources * self.half if extra else 0)


def routes_of(devices, main, columns, leaves):
    high, low = grid_of(devices)
    split = up(main // 2)
    return (
        Route(0, split, high, False, main, columns, leaves, low),
        Route(split, main, low, True, main, columns, leaves, high),
    )


def products_kernel(routes, devices, *refs):
    dest_hbm, leaf_hbm, probes_hbm, basis_hbm, transfer_hbm, blocks_hbm = refs[:6]
    outs = refs[6:-13]
    (
        dest_ref, leaf_ref, probes_ref, basis_ref, transfer_ref, blocks_ref,
        send_low, send_high, tails, meta_low, meta_high, count, sems,
    ) = refs[-13:]
    by_low, by_high = routes
    high, low = grid_of(devices)
    me = lax.axis_index("leaf")
    main = by_high.main
    leaves, per_leaf, size = blocks_ref.shape[:3]
    columns, rank = probes_ref.shape[0], basis_ref.shape[1]
    copies = Copies(sems)
    early = [
        copies.start(probes_hbm, probes_ref),
        copies.start(basis_hbm, basis_ref),
        copies.start(transfer_hbm, transfer_ref),
        copies.start(dest_hbm, dest_ref),
        copies.start(leaf_hbm, leaf_ref),
    ]
    chunk = leaves // 2
    arrivals = [
        copies.start(blocks_hbm.at[pl.ds(j, chunk)], blocks_ref.at[pl.ds(j, chunk)])
        for j in range(0, leaves, chunk)
    ]

    @pl.loop(0, devices)
    def _(i):
        count[i] = 0

    tails[...] = jnp.zeros(tails.shape, F32)
    meta_low[...] = jnp.full(meta_low.shape, leaves, F32)
    meta_high[...] = jnp.full(meta_high.shape, leaves, F32)
    for copy in early:
        copy.wait()
    box = jnp.zeros((columns, rank), F32)
    for j in range(leaves):
        coef = dot_t(probes_ref[:, j * size : (j + 1) * size], basis_ref[j]).astype(BF16)
        box += dot_t(coef, transfer_ref[j])
    half = by_high.half
    packed = jnp.concatenate([box[:half], box[half:main]], axis=1).astype(BF16)
    last = jnp.concatenate([box[main:], jnp.zeros_like(box[main:])], axis=1)

    lane = lax.broadcasted_iota(I32, (1, size), 1)
    for j in range(leaves):
        if j % chunk == 0:
            arrivals[j // chunk].wait()
        x = probes_ref[:, j * size : (j + 1) * size]
        for first in range(0, per_leaf, 4):
            many = min(4, per_leaf - first)
            rhs = blocks_ref[j, first : first + many].reshape(many * size, size)
            product = dot_t(x, rhs)
            for b in range(many):
                target = jnp.bitwise_xor(dest_ref[first + b, j], me)
                slot = count[target]
                count[target] = slot + 1
                to_high, to_low = target // low, target % low
                block = product[:, b * size : (b + 1) * size]
                piece = block[:main].astype(BF16)
                number = leaf_ref[first + b, j].astype(F32)

                at = to_high * CAP + slot
                rows = pl.ds(pl.multiple_of(at * by_low.rows, TILE), by_low.rows)
                send_low[to_low, rows, :] = piece[: by_low.rows]
                meta_low[to_low, 0:1, :] = jnp.where(lane == at, number, meta_low[to_low, 0:1, :])

                at = to_low * CAP + slot
                rows = pl.ds(pl.multiple_of(at * by_high.rows, TILE), by_high.rows)
                send_high[to_high, rows, :] = piece[by_low.rows :]
                tails[to_high, pl.ds(at, 1), :] = block[main:]
                meta_high[to_high, 0:1, :] = jnp.where(lane == at, number, meta_high[to_high, 0:1, :])

    for i in range(low):
        send_low[i, by_low.meta : by_low.box, :] = meta_low[i].astype(BF16)
    for i in range(high):
        meta_high[i, 1:2, :] = last
        send_high[i, by_high.tails : by_high.meta, :] = tails[i].astype(BF16)
        send_high[i, by_high.meta : by_high.box, :] = meta_high[i].astype(BF16)
        send_high[i, by_high.box :, :] = packed
    leaving = [copies.start(send_low.at[i], outs[i]) for i in range(low)]
    leaving += [copies.start(send_high.at[i], outs[low + i]) for i in range(high)]
    for copy in leaving:
        copy.wait()


def sum_kernel(route, ways, *refs):
    came, outs = refs[:ways], refs[ways : ways + route.fan]
    in_ref, meta, leaf_ref, total, tails, send_ref, sems, late = refs[ways + route.fan :]
    leaves, half = route.leaves, route.half
    copies = Copies(sems)
    small = [
        copies.start(came[i].at[pl.ds(route.meta, TILE)], in_ref.at[i, pl.ds(route.meta, TILE)])
        for i in range(ways)
    ]
    large = [
        copies.start(came[i].at[pl.ds(0, route.meta)], in_ref.at[i, pl.ds(0, route.meta)]) for i in range(ways)
    ]
    if route.extra:
        large += [
            copies.start(came[i].at[pl.ds(route.box, half)], in_ref.at[i, pl.ds(route.box, half)])
            for i in range(ways)
        ]
    lasts = []
    for i in range(ways):
        small[i].wait()
        tile = in_ref[i, route.meta : route.box, :].astype(F32)
        meta[i : i + 1, :] = tile[:1].astype(I32)
        lasts.append(tile[1:2])
    numbers = pltpu.make_async_copy(meta, leaf_ref, late)
    numbers.start()
    total[...] = jnp.zeros(total.shape, F32)
    tails[...] = jnp.zeros(tails.shape, F32)
    numbers.wait()
    for copy in large:
        copy.wait()

    @pl.loop(0, ways)
    def _(i):
        if route.extra:
            tail = in_ref[i, route.tails : route.meta, :].astype(F32)
        for k in range(route.fan):
            for slot in range(CAP):
                at = k * CAP + slot
                leaf = leaf_ref[i, at]
                rows = pl.ds(pl.multiple_of(leaf * route.rows, TILE), route.rows)
                total[k, rows, :] += in_ref[i, at * route.rows : (at + 1) * route.rows, :].astype(F32)
                if route.extra:
                    tails[k, pl.ds(leaf, 1), :] += tail[at : at + 1]

    leaving = []
    for k in range(route.fan):
        send_ref[k, : route.dense_tails, :] = total[k, : route.dense_tails, :].astype(BF16)
        if route.extra:
            for i in range(ways):
                tails[k, leaves + i : leaves + i + 1, :] = lasts[i]
                start = route.dense_box + i * half
                send_ref[k, start : start + half, :] = in_ref[i, route.box :, :]
            send_ref[k, route.dense_tails : route.dense_box, :] = tails[k].astype(BF16)
        leaving.append(copies.start(send_ref.at[k], outs[k]))
    for copy in leaving:
        copy.wait()


def local_part(probes_ref, local_ref, out_ref):
    leaves, size = local_ref.shape[0], local_ref.shape[2]
    for i in range(leaves):
        total = dot_t(probes_ref[:, :size], local_ref[i, 0])
        for c in range(1, leaves):
            total += dot_t(probes_ref[:, c * size : (c + 1) * size], local_ref[i, c])
        out_ref[:, i * size : (i + 1) * size] = total


def local_kernel(probes_hbm, local_hbm, base_ref, probes_ref, local_ref, sems):
    copies = Copies(sems)
    for copy in [copies.start(probes_hbm, probes_ref), copies.start(local_hbm, local_ref)]:
        copy.wait()
    local_part(probes_ref, local_ref, base_ref)


def last_kernel(routes, devices, *refs):
    partner_hbm, base_hbm, couplings_hbm, transfer_hbm, basis_hbm = refs[:5]
    by_low, by_high = routes
    high, low = grid_of(devices)
    came_high, came_low = refs[5 : 5 + high], refs[5 + high : 5 + high + low]
    (
        out_ref, partner_ref, base_ref, couplings_ref, transfer_ref, basis_ref, in_high, in_low, sems,
    ) = refs[5 + high + low :]
    me = lax.axis_index("leaf")
    columns = out_ref.shape[0]
    leaves, rank, size = basis_ref.shape
    split, main = by_low.rows, by_low.main
    copies = Copies(sems)
    early = [copies.start(came_low[k], in_low.at[k]) for k in range(low)]
    early += [
        copies.start(partner_hbm, partner_ref),
        copies.start(couplings_hbm, couplings_ref),
        copies.start(transfer_hbm, transfer_ref),
        copies.start(basis_hbm, basis_ref),
    ]
    later = [copies.start(came_high[k], in_high.at[k]) for k in range(high)]
    later += [copies.start(base_hbm, base_ref)]
    for copy in early:
        copy.wait()
    far = jnp.zeros((columns, rank), F32)
    for f in range(couplings_ref.shape[1]):
        source = jnp.bitwise_xor(partner_ref[0, f], me)
        to_high, to_low = source // low, source % low
        start = pl.multiple_of(by_high.dense_box + to_high * by_high.half, TILE)
        packed = in_low[to_low, pl.ds(start, by_high.half), :]
        tile = in_low[to_low, by_high.dense_tails : by_high.dense_box, :].astype(F32)
        row = lax.broadcasted_iota(I32, tile.shape, 0)
        last = jnp.sum(jnp.where(row == leaves + to_high, tile, 0.0), axis=0, keepdims=True)[:, :rank]
        box = jnp.concatenate(
            [packed[:, :rank].astype(F32), packed[:, rank:].astype(F32), last], axis=0
        ).astype(BF16)
        far += dot_t(box, couplings_ref[0, f])
    far = far.astype(BF16)
    down = [dot(far, transfer_ref[j]).astype(BF16) for j in range(leaves)]
    far_part = [dot(down[j], basis_ref[j]) for j in range(leaves)]
    for copy in later:
        copy.wait()
    tails = sum(in_low[k, by_high.dense_tails : by_high.dense_box, :].astype(F32) for k in range(low))
    for j in range(leaves):
        cols = slice(j * size, (j + 1) * size)
        upper = sum(in_high[k, j * by_low.rows : (j + 1) * by_low.rows, :].astype(F32) for k in range(high))
        lower = sum(in_low[k, j * by_high.rows : (j + 1) * by_high.rows, :].astype(F32) for k in range(low))
        out_ref[:split, cols] = base_ref[:split, cols] + far_part[j][:split] + upper
        out_ref[split:main, cols] = base_ref[split:main, cols] + far_part[j][split:main] + lower
        out_ref[main:, cols] = base_ref[main:, cols] + far_part[j][main:] + tails[j : j + 1]


def call(kernel, out_shape, out_specs, operands, scratch, flops, nbytes):
    return pl.pallas_call(
        kernel,
        out_shape=out_shape,
        in_specs=[ANY] * len(operands),
        out_specs=out_specs,
        scratch_shapes=scratch,
        cost_estimate=pl.CostEstimate(flops=flops, bytes_accessed=nbytes, transcendentals=0),
    )(*operands)


def per_device(
    probes, basis, transfer, local_blocks, remote_blocks, near_dest, near_leaf, couplings, far_list
):
    columns, points = probes.shape
    leaves, rank, size = basis.shape
    devices = lax.axis_size("leaf")
    main = columns // TILE * TILE
    routes = by_low, by_high = routes_of(devices, main, columns, leaves)
    high, low = grid_of(devices)
    blocks = remote_blocks.shape[0] * remote_blocks.shape[1]
    unit = 2 * columns * size * size
    like = lambda *arrays: [pltpu.VMEM(a.shape, a.dtype) for a in arrays]
    numbers = lambda *arrays: [pltpu.SMEM(a.shape, a.dtype) for a in arrays]
    sems = lambda count: [pltpu.SemaphoreType.DMA((count,))]
    relative = lambda x, way: lax.ppermute(x, "leaf", [(i, i ^ way) for i in range(devices)])
    message = lambda route: jax.ShapeDtypeStruct((route.depth, size), BF16)
    dense = lambda route: jax.ShapeDtypeStruct((route.dense_depth, size), BF16)

    def stacked(count, like_this):
        return pltpu.VMEM((count, *like_this.shape), like_this.dtype)

    def summed(route, ways, came):
        return call(
            functools.partial(sum_kernel, route, ways),
            [dense(route)] * route.fan,
            [ANY] * route.fan,
            came,
            [
                stacked(ways, message(route)),
                pltpu.VMEM((ways, size), I32),
                pltpu.SMEM((ways, size), I32),
                pltpu.VMEM((route.fan, (leaves + 1) * route.rows, size), F32),
                pltpu.VMEM((route.fan, max(TILE, route.dense_box - route.dense_tails), size), F32),
                stacked(route.fan, dense(route)),
            ]
            + sems(3 * ways + route.fan)
            + [pltpu.SemaphoreType.DMA(())],
            devices * CAP * route.rows * size,
            2 * ways * message(route).size,
        )

    dest, leaf = near_dest.T, near_leaf.T
    sent = call(
        functools.partial(products_kernel, routes, devices),
        [message(by_low)] * low + [message(by_high)] * high,
        [ANY] * (low + high),
        (dest, leaf, probes, basis, transfer, remote_blocks),
        numbers(dest, leaf)
        + like(probes, basis, transfer, remote_blocks)
        + [
            stacked(low, message(by_low)),
            stacked(high, message(by_high)),
            pltpu.VMEM((high, by_high.meta - by_high.tails, size), F32),
            pltpu.VMEM((low, TILE, size), F32),
            pltpu.VMEM((high, TILE, size), F32),
            pltpu.SMEM((devices,), I32),
        ]
        + sems(7 + low + high),
        blocks * unit,
        remote_blocks.size * 2 + 2 * low * message(by_low).size + 2 * high * message(by_high).size,
    )
    came_low, came_high = list(sent[:low]), list(sent[low:])
    came_low[1] = relative(came_low[1], 1)
    for k in range(high - 1, 1, -1):
        came_high[k] = relative(came_high[k], k * low)
    for k in range(low - 1, 1, -1):
        came_low[k] = relative(came_low[k], k)
    came_high[1] = relative(came_high[1], low)

    to_high = list(summed(by_low, low, came_low))
    for k in range(high - 1, 0, -1):
        to_high[k] = relative(to_high[k], k * low)
    to_low = list(summed(by_high, high, came_high))
    probes_then, to_low[0] = lax.optimization_barrier((probes, to_low[0]))
    for k in range(low - 1, 0, -1):
        to_low[k] = relative(to_low[k], k)

    base = call(
        local_kernel,
        jax.ShapeDtypeStruct((columns, points), F32),
        VMEM,
        (probes_then, local_blocks),
        like(probes, local_blocks) + sems(2),
        leaves * leaves * unit,
        local_blocks.size * 2,
    )
    return call(
        functools.partial(last_kernel, routes, devices),
        jax.ShapeDtypeStruct((columns, points), F32),
        VMEM,
        (far_list, base, couplings, transfer, basis, *to_high, *to_low),
        numbers(far_list)
        + like(base, couplings, transfer, basis)
        + [stacked(high, dense(by_low)), stacked(low, dense(by_high))]
        + sems(5 + low + high),
        devices * columns * size,
        2 * (high * dense(by_low).size + low * dense(by_high).size),
    )


def solution(mesh):
    placed = (
        P(None, ("grp", "leaf")),
        P(("grp", "leaf"), None, None),
        P(("grp", "leaf"), None, None),
        P(("grp", "leaf"), None, None, None),
        P(("grp", "leaf"), None, None, None),
        P(("grp", "leaf"), None),
        P(("grp", "leaf"), None),
        P(("grp", "leaf"), None, None, None),
        P(("grp", "leaf"), None),
    )
    return jax.shard_map(
        per_device, mesh=mesh, in_specs=placed, out_specs=P(None, ("grp", "leaf")), check_vma=False
    )
```

```python
import functools

import jax
import jax.numpy as jnp
from jax import lax
from jax.experimental import pallas as pl
from jax.experimental.pallas import tpu as pltpu
from jax.sharding import PartitionSpec as P

CAP = 4
TILE = 16
LANES = 128
F32 = jnp.float32
BF16 = jnp.bfloat16
I32 = jnp.int32

ANY = pl.BlockSpec(memory_space=pl.ANY)
VMEM = pl.BlockSpec(memory_space=pltpu.VMEM)
SMEM = pl.BlockSpec(memory_space=pltpu.SMEM)


def dot_t(lhs, rhs):
    return lax.dot_general(lhs, rhs, (((1,), (1,)), ((), ())), preferred_element_type=F32)


def dot(lhs, rhs):
    return lax.dot_general(lhs, rhs, (((1,), (0,)), ((), ())), preferred_element_type=F32)


class Copies:
    def __init__(self, sems):
        self.sems, self.used = sems, 0

    def start(self, src, dst):
        copy = pltpu.make_async_copy(src, dst, self.sems.at[self.used])
        self.used += 1
        copy.start()
        return copy


def grid_of(devices):
    low = 1 << (devices.bit_length() // 2)
    return devices // low, low


def up(rows):
    return -(-rows // TILE) * TILE


class Route:
    def __init__(self, first, last, fan, extra, main, columns, leaves, sources):
        self.first, self.rows, self.fan, self.extra, self.main = first, last - first, fan, extra, main
        self.leaves, self.half = leaves, main // 2
        slots = fan * CAP
        self.tails = slots * self.rows
        self.meta = self.tails + (up(slots) if extra else 0)
        self.box = self.meta + TILE
        self.depth = self.box + (self.half if extra else 0)
        self.dense_tails = leaves * self.rows
        self.dense_box = self.dense_tails + (up(leaves + sources) if extra else 0)
        self.dense_depth = self.dense_box + (sources * self.half if extra else 0)


def routes_of(devices, main, columns, leaves):
    high, low = grid_of(devices)
    split = up(main * 3 // 4)
    return (
        Route(0, split, high, False, main, columns, leaves, low),
        Route(split, main, low, True, main, columns, leaves, high),
    )


def products_kernel(routes, devices, *refs):
    dest_hbm, leaf_hbm, probes_hbm, basis_hbm, transfer_hbm, blocks_hbm = refs[:6]
    outs = refs[6:-13]
    (
        dest_ref, leaf_ref, probes_ref, basis_ref, transfer_ref, blocks_ref,
        send_low, send_high, tails, meta_low, meta_high, count, sems,
    ) = refs[-13:]
    by_low, by_high = routes
    high, low = grid_of(devices)
    me = lax.axis_index("leaf")
    main = by_high.main
    leaves, per_leaf, size = blocks_ref.shape[:3]
    columns, rank = probes_ref.shape[0], basis_ref.shape[1]
    copies = Copies(sems)
    early = [
        copies.start(probes_hbm, probes_ref),
        copies.start(basis_hbm, basis_ref),
        copies.start(transfer_hbm, transfer_ref),
        copies.start(dest_hbm, dest_ref),
        copies.start(leaf_hbm, leaf_ref),
    ]
    chunk = leaves // 2
    arrivals = [
        copies.start(blocks_hbm.at[pl.ds(j, chunk)], blocks_ref.at[pl.ds(j, chunk)])
        for j in range(0, leaves, chunk)
    ]

    @pl.loop(0, devices)
    def _(i):
        count[i] = 0

    tails[...] = jnp.zeros(tails.shape, F32)
    meta_low[...] = jnp.full(meta_low.shape, leaves, F32)
    meta_high[...] = jnp.full(meta_high.shape, leaves, F32)
    for copy in early:
        copy.wait()
    box = jnp.zeros((columns, rank), F32)
    for j in range(leaves):
        coef = dot_t(probes_ref[:, j * size : (j + 1) * size], basis_ref[j]).astype(BF16)
        box += dot_t(coef, transfer_ref[j])
    half = by_high.half
    packed = jnp.concatenate([box[:half], box[half:main]], axis=1).astype(BF16)
    last = jnp.concatenate([box[main:], jnp.zeros_like(box[main:])], axis=1)

    lane = lax.broadcasted_iota(I32, (1, size), 1)
    for j in range(leaves):
        if j % chunk == 0:
            arrivals[j // chunk].wait()
        x = probes_ref[:, j * size : (j + 1) * size]
        for first in range(0, per_leaf, 4):
            many = min(4, per_leaf - first)
            rhs = blocks_ref[j, first : first + many].reshape(many * size, size)
            product = dot_t(x, rhs)
            for b in range(many):
                target = jnp.bitwise_xor(dest_ref[first + b, j], me)
                slot = count[target]
                count[target] = slot + 1
                to_high, to_low = target // low, target % low
                block = product[:, b * size : (b + 1) * size]
                piece = block[:main].astype(BF16)
                number = leaf_ref[first + b, j].astype(F32)

                at = to_high * CAP + slot
                rows = pl.ds(pl.multiple_of(at * by_low.rows, TILE), by_low.rows)
                send_low[to_low, rows, :] = piece[: by_low.rows]
                meta_low[to_low, 0:1, :] = jnp.where(lane == at, number, meta_low[to_low, 0:1, :])

                at = to_low * CAP + slot
                rows = pl.ds(pl.multiple_of(at * by_high.rows, TILE), by_high.rows)
                send_high[to_high, rows, :] = piece[by_low.rows :]
                tails[to_high, pl.ds(at, 1), :] = block[main:]
                meta_high[to_high, 0:1, :] = jnp.where(lane == at, number, meta_high[to_high, 0:1, :])

    for i in range(low):
        send_low[i, by_low.meta : by_low.box, :] = meta_low[i].astype(BF16)
    for i in range(high):
        meta_high[i, 1:2, :] = last
        send_high[i, by_high.tails : by_high.meta, :] = tails[i].astype(BF16)
        send_high[i, by_high.meta : by_high.box, :] = meta_high[i].astype(BF16)
        send_high[i, by_high.box :, :] = packed
    leaving = [copies.start(send_low.at[i], outs[i]) for i in range(low)]
    leaving += [copies.start(send_high.at[i], outs[low + i]) for i in range(high)]
    for copy in leaving:
        copy.wait()


def sum_kernel(route, ways, *refs):
    came, outs = refs[:ways], refs[ways : ways + route.fan]
    meta, leaf_ref, total, tails, late = refs[ways + route.fan :]
    leaves, half = route.leaves, route.half
    lasts = []
    for i in range(ways):
        tile = came[i][route.meta : route.box, :].astype(F32)
        meta[i : i + 1, :] = tile[:1].astype(I32)
        lasts.append(tile[1:2])
    numbers = pltpu.make_async_copy(meta, leaf_ref, late)
    numbers.start()
    total[...] = jnp.zeros(total.shape, F32)
    tails[...] = jnp.zeros(tails.shape, F32)
    numbers.wait()
    for i in range(ways):
        if route.extra:
            tail = came[i][route.tails : route.meta, :].astype(F32)
        for k in range(route.fan):
            for slot in range(CAP):
                at = k * CAP + slot
                leaf = leaf_ref[i, at]
                rows = pl.ds(pl.multiple_of(leaf * route.rows, TILE), route.rows)
                total[k, rows, :] += came[i][at * route.rows : (at + 1) * route.rows, :].astype(F32)
                if route.extra:
                    tails[k, pl.ds(leaf, 1), :] += tail[at : at + 1]

    for k in range(route.fan):
        outs[k][: route.dense_tails, :] = total[k, : route.dense_tails, :].astype(BF16)
        if route.extra:
            for i in range(ways):
                tails[k, leaves + i : leaves + i + 1, :] = lasts[i]
                start = route.dense_box + i * half
                outs[k][start : start + half, :] = came[i][route.box :, :]
            outs[k][route.dense_tails : route.dense_box, :] = tails[k].astype(BF16)


def local_kernel(probes_ref, local_ref, out_ref):
    leaves, size = local_ref.shape[0], local_ref.shape[2]
    for i in range(leaves):
        total = dot_t(probes_ref[:, :size], local_ref[i, 0])
        for c in range(1, leaves):
            total += dot_t(probes_ref[:, c * size : (c + 1) * size], local_ref[i, c])
        out_ref[:, i * size : (i + 1) * size] = total


def far_kernel(by_high, low, partner_ref, base_ref, couplings_ref, transfer_ref, basis_ref, *refs):
    came, out_ref, boxes = refs[:low], refs[low], refs[low + 1]
    columns = out_ref.shape[0]
    leaves, rank, size = basis_ref.shape
    high = boxes.shape[0] // low
    me = lax.axis_index("leaf")
    for k in range(low):
        tile = came[k][by_high.dense_tails : by_high.dense_box, :].astype(F32)
        for i in range(high):
            start = by_high.dense_box + i * by_high.half
            packed = came[k][start : start + by_high.half, :]
            last = tile[leaves + i : leaves + i + 1, :rank]
            boxes[i * low + k] = jnp.concatenate(
                [packed[:, :rank].astype(F32), packed[:, rank:].astype(F32), last], axis=0
            ).astype(BF16)
    far = jnp.zeros((columns, rank), F32)
    for f in range(couplings_ref.shape[1]):
        source = jnp.bitwise_xor(partner_ref[0, f], me)
        far += dot_t(boxes[source], couplings_ref[0, f])
    far = far.astype(BF16)
    down = [dot(far, transfer_ref[j]).astype(BF16) for j in range(leaves)]
    for j in range(leaves):
        cols = slice(j * size, (j + 1) * size)
        out_ref[:, cols] = base_ref[:, cols] + dot(down[j], basis_ref[j])


def last_kernel(routes, devices, base_ref, *refs):
    by_low, by_high = routes
    high, low = grid_of(devices)
    came_high, came_low, out_ref = refs[:high], refs[high : high + low], refs[high + low]
    leaves, split, main = by_low.leaves, by_low.rows, by_low.main
    size = base_ref.shape[1] // leaves
    tails = sum(came_low[k][by_high.dense_tails : by_high.dense_box, :].astype(F32) for k in range(low))
    for j in range(leaves):
        cols = slice(j * size, (j + 1) * size)
        upper = sum(came_high[k][j * by_low.rows : (j + 1) * by_low.rows, :].astype(F32) for k in range(high))
        lower = sum(came_low[k][j * by_high.rows : (j + 1) * by_high.rows, :].astype(F32) for k in range(low))
        out_ref[:split, cols] = base_ref[:split, cols] + upper
        out_ref[split:main, cols] = base_ref[split:main, cols] + lower
        out_ref[main:, cols] = base_ref[main:, cols] + tails[j : j + 1]


def call(kernel, out_shape, specs, operands, scratch, flops, room=None):
    outs = jax.tree.leaves(out_shape)
    nbytes = sum(a.size * a.dtype.itemsize for a in (*operands, *outs))
    limit = None if room is None else nbytes + room + 2**21
    return pl.pallas_call(
        kernel,
        out_shape=out_shape,
        in_specs=specs[0],
        out_specs=specs[1],
        scratch_shapes=scratch,
        compiler_params=pltpu.CompilerParams(vmem_limit_bytes=limit),
        cost_estimate=pl.CostEstimate(flops=flops, bytes_accessed=nbytes, transcendentals=0),
    )(*operands)


def per_device(
    probes, basis, transfer, local_blocks, remote_blocks, near_dest, near_leaf, couplings, far_list
):
    columns, points = probes.shape
    leaves, rank, size = basis.shape
    devices = lax.axis_size("leaf")
    main = columns // TILE * TILE
    routes = by_low, by_high = routes_of(devices, main, columns, leaves)
    high, low = grid_of(devices)
    blocks = remote_blocks.shape[0] * remote_blocks.shape[1]
    unit = 2 * columns * size * size
    like = lambda *arrays: [pltpu.VMEM(a.shape, a.dtype) for a in arrays]
    numbers = lambda *arrays: [pltpu.SMEM(a.shape, a.dtype) for a in arrays]
    sems = lambda count: [pltpu.SemaphoreType.DMA((count,))]
    relative = lambda x, way: lax.ppermute(x, "leaf", [(i, i ^ way) for i in range(devices)])
    message = lambda route: jax.ShapeDtypeStruct((route.depth, size), BF16)
    dense = lambda route: jax.ShapeDtypeStruct((route.dense_depth, size), BF16)

    def stacked(count, like_this):
        return pltpu.VMEM((count, *like_this.shape), like_this.dtype)

    def summed(route, ways, came):
        total = jax.ShapeDtypeStruct((route.fan, (leaves + 1) * route.rows, size), F32)
        tails = jax.ShapeDtypeStruct((route.fan, max(TILE, route.dense_box - route.dense_tails), size), F32)
        return call(
            functools.partial(sum_kernel, route, ways),
            [dense(route)] * route.fan,
            ([VMEM] * ways, [VMEM] * route.fan),
            came,
            [pltpu.VMEM((ways, size), I32), pltpu.SMEM((ways, size), I32)]
            + like(total, tails)
            + [pltpu.SemaphoreType.DMA(())],
            devices * CAP * route.rows * size,
            4 * (total.size + tails.size),
        )

    dest, leaf = near_dest.T, near_leaf.T
    sent = call(
        functools.partial(products_kernel, routes, devices),
        [message(by_low)] * low + [message(by_high)] * high,
        ([ANY] * 6, [ANY] * (low + high)),
        (dest, leaf, probes, basis, transfer, remote_blocks),
        numbers(dest, leaf)
        + like(probes, basis, transfer, remote_blocks)
        + [
            stacked(low, message(by_low)),
            stacked(high, message(by_high)),
            pltpu.VMEM((high, by_high.meta - by_high.tails, size), F32),
            pltpu.VMEM((low, TILE, size), F32),
            pltpu.VMEM((high, TILE, size), F32),
            pltpu.SMEM((devices,), I32),
        ]
        + sems(7 + low + high),
        blocks * unit,
    )
    came_low, came_high = list(sent[:low]), list(sent[low:])
    came_low[1] = relative(came_low[1], 1)
    for k in range(high - 1, 1, -1):
        came_high[k] = relative(came_high[k], k * low)
    for k in range(low - 1, 1, -1):
        came_low[k] = relative(came_low[k], k)
    came_high[1] = relative(came_high[1], low)

    probes_then, came_low[0] = lax.optimization_barrier((probes, came_low[0]))
    base_shape = jax.ShapeDtypeStruct((columns, points), F32)
    base = call(
        local_kernel, base_shape, ([VMEM] * 2, VMEM), (probes_then, local_blocks), [], leaves * leaves * unit, 0
    )

    to_high = list(summed(by_low, low, came_low))
    for k in range(high - 1, 0, -1):
        to_high[k] = relative(to_high[k], k * low)
    came_high[0], to_high[0] = lax.optimization_barrier((came_high[0], to_high[0]))
    to_low = list(summed(by_high, high, came_high))
    for k in range(low - 1, 0, -1):
        to_low[k] = relative(to_low[k], k)

    boxes = jax.ShapeDtypeStruct((devices, columns, rank), BF16)
    base = call(
        functools.partial(far_kernel, by_high, low),
        base_shape,
        ([SMEM] + [VMEM] * (4 + low), VMEM),
        (far_list, base, couplings, transfer, basis, *to_low),
        like(boxes),
        4 * leaves * unit,
        4 * boxes.size,
    )
    return call(
        functools.partial(last_kernel, routes, devices),
        base_shape,
        ([VMEM] * (1 + high + low), VMEM),
        (base, *to_high, *to_low),
        [],
        devices * columns * size,
        0,
    )


def solution(mesh):
    placed = (
        P(None, ("grp", "leaf")),
        P(("grp", "leaf"), None, None),
        P(("grp", "leaf"), None, None),
        P(("grp", "leaf"), None, None, None),
        P(("grp", "leaf"), None, None, None),
        P(("grp", "leaf"), None),
        P(("grp", "leaf"), None),
        P(("grp", "leaf"), None, None, None),
        P(("grp", "leaf"), None),
    )
    return jax.shard_map(
        per_device, mesh=mesh, in_specs=placed, out_specs=P(None, ("grp", "leaf")), check_vma=False
    )
```

```python
import functools

import jax
import jax.numpy as jnp
from jax import lax
from jax.experimental import pallas as pl
from jax.experimental.pallas import tpu as pltpu
from jax.sharding import PartitionSpec as P

CAP = 4
TILE = 16
LANES = 128
F32 = jnp.float32
BF16 = jnp.bfloat16
I32 = jnp.int32

ANY = pl.BlockSpec(memory_space=pl.ANY)
VMEM = pl.BlockSpec(memory_space=pltpu.VMEM)
SMEM = pl.BlockSpec(memory_space=pltpu.SMEM)


def dot_t(lhs, rhs):
    return lax.dot_general(lhs, rhs, (((1,), (1,)), ((), ())), preferred_element_type=F32)


def dot(lhs, rhs):
    return lax.dot_general(lhs, rhs, (((1,), (0,)), ((), ())), preferred_element_type=F32)


class Copies:
    def __init__(self, sems):
        self.sems, self.used = sems, 0

    def start(self, src, dst):
        copy = pltpu.make_async_copy(src, dst, self.sems.at[self.used])
        self.used += 1
        copy.start()
        return copy


def grid_of(devices):
    low = 1 << (devices.bit_length() // 2)
    return devices // low, low


def up(rows):
    return -(-rows // TILE) * TILE


class Route:
    def __init__(self, first, last, fan, extra, main, columns, leaves, sources):
        self.first, self.rows, self.fan, self.extra, self.main = first, last - first, fan, extra, main
        self.leaves, self.half = leaves, main // 2
        slots = fan * CAP
        self.tails = slots * self.rows
        self.meta = self.tails + (up(slots) if extra else 0)
        self.box = self.meta + TILE
        self.depth = self.box + (self.half if extra else 0)
        self.dense_tails = leaves * self.rows
        self.dense_box = self.dense_tails + (up(leaves + sources) if extra else 0)
        self.dense_depth = self.dense_box + (sources * self.half if extra else 0)


def routes_of(devices, main, columns, leaves):
    high, low = grid_of(devices)
    split = up(main * 3 // 4)
    return (
        Route(0, split, high, False, main, columns, leaves, low),
        Route(split, main, low, True, main, columns, leaves, high),
    )


def products_kernel(routes, devices, *refs):
    dest_hbm, leaf_hbm, probes_hbm, basis_hbm, transfer_hbm, blocks_hbm = refs[:6]
    outs = refs[6:-13]
    (
        dest_ref, leaf_ref, probes_ref, basis_ref, transfer_ref, blocks_ref,
        send_low, send_high, tails, meta_low, meta_high, count, sems,
    ) = refs[-13:]
    by_low, by_high = routes
    high, low = grid_of(devices)
    me = lax.axis_index("leaf")
    main = by_high.main
    leaves, per_leaf, size = blocks_ref.shape[:3]
    columns, rank = probes_ref.shape[0], basis_ref.shape[1]
    copies = Copies(sems)
    early = [
        copies.start(probes_hbm, probes_ref),
        copies.start(basis_hbm, basis_ref),
        copies.start(transfer_hbm, transfer_ref),
        copies.start(dest_hbm, dest_ref),
        copies.start(leaf_hbm, leaf_ref),
    ]
    chunk = leaves // 2
    arrivals = [
        copies.start(blocks_hbm.at[pl.ds(j, chunk)], blocks_ref.at[pl.ds(j, chunk)])
        for j in range(0, leaves, chunk)
    ]

    @pl.loop(0, devices)
    def _(i):
        count[i] = 0

    tails[...] = jnp.zeros(tails.shape, F32)
    meta_low[...] = jnp.full(meta_low.shape, leaves, F32)
    meta_high[...] = jnp.full(meta_high.shape, leaves, F32)
    for copy in early:
        copy.wait()
    box = jnp.zeros((columns, rank), F32)
    for j in range(leaves):
        coef = dot_t(probes_ref[:, j * size : (j + 1) * size], basis_ref[j]).astype(BF16)
        box += dot_t(coef, transfer_ref[j])
    half = by_high.half
    packed = jnp.concatenate([box[:half], box[half:main]], axis=1).astype(BF16)
    last = jnp.concatenate([box[main:], jnp.zeros_like(box[main:])], axis=1)

    lane = lax.broadcasted_iota(I32, (1, size), 1)
    for j in range(leaves):
        if j % chunk == 0:
            arrivals[j // chunk].wait()
        x = probes_ref[:, j * size : (j + 1) * size]
        for first in range(0, per_leaf, 4):
            many = min(4, per_leaf - first)
            rhs = blocks_ref[j, first : first + many].reshape(many * size, size)
            product = dot_t(x, rhs)
            for b in range(many):
                target = jnp.bitwise_xor(dest_ref[first + b, j], me)
                slot = count[target]
                count[target] = slot + 1
                to_high, to_low = target // low, target % low
                block = product[:, b * size : (b + 1) * size]
                piece = block[:main].astype(BF16)
                number = leaf_ref[first + b, j].astype(F32)

                at = to_high * CAP + slot
                rows = pl.ds(pl.multiple_of(at * by_low.rows, TILE), by_low.rows)
                send_low[to_low, rows, :] = piece[: by_low.rows]
                meta_low[to_low, 0:1, :] = jnp.where(lane == at, number, meta_low[to_low, 0:1, :])

                at = to_low * CAP + slot
                rows = pl.ds(pl.multiple_of(at * by_high.rows, TILE), by_high.rows)
                send_high[to_high, rows, :] = piece[by_low.rows :]
                tails[to_high, pl.ds(at, 1), :] = block[main:]
                meta_high[to_high, 0:1, :] = jnp.where(lane == at, number, meta_high[to_high, 0:1, :])

    for i in range(low):
        send_low[i, by_low.meta : by_low.box, :] = meta_low[i].astype(BF16)
    for i in range(high):
        meta_high[i, 1:2, :] = last
        send_high[i, by_high.tails : by_high.meta, :] = tails[i].astype(BF16)
        send_high[i, by_high.meta : by_high.box, :] = meta_high[i].astype(BF16)
        send_high[i, by_high.box :, :] = packed
    leaving = [copies.start(send_low.at[i], outs[i]) for i in range(low)]
    leaving += [copies.start(send_high.at[i], outs[low + i]) for i in range(high)]
    for copy in leaving:
        copy.wait()


def sum_kernel(route, ways, *refs):
    came, outs = refs[:ways], refs[ways : ways + route.fan]
    meta, leaf_ref, total, tails, late = refs[ways + route.fan :]
    leaves, half = route.leaves, route.half
    lasts = []
    for i in range(ways):
        tile = came[i][route.meta : route.box, :].astype(F32)
        meta[i : i + 1, :] = tile[:1].astype(I32)
        lasts.append(tile[1:2])
    numbers = pltpu.make_async_copy(meta, leaf_ref, late)
    numbers.start()
    total[...] = jnp.zeros(total.shape, F32)
    tails[...] = jnp.zeros(tails.shape, F32)
    numbers.wait()
    for i in range(ways):
        if route.extra:
            tail = came[i][route.tails : route.meta, :].astype(F32)
        for k in range(route.fan):
            for slot in range(CAP):
                at = k * CAP + slot
                leaf = leaf_ref[i, at]
                rows = pl.ds(pl.multiple_of(leaf * route.rows, TILE), route.rows)
                total[k, rows, :] += came[i][at * route.rows : (at + 1) * route.rows, :].astype(F32)
                if route.extra:
                    tails[k, pl.ds(leaf, 1), :] += tail[at : at + 1]

    for k in range(route.fan):
        outs[k][: route.dense_tails, :] = total[k, : route.dense_tails, :].astype(BF16)
        if route.extra:
            for i in range(ways):
                tails[k, leaves + i : leaves + i + 1, :] = lasts[i]
                start = route.dense_box + i * half
                outs[k][start : start + half, :] = came[i][route.box :, :]
            outs[k][route.dense_tails : route.dense_box, :] = tails[k].astype(BF16)


def local_kernel(probes_ref, local_ref, own_low, own_high, out_ref, kept_low, kept_high):
    kept_low[...] = own_low[...]
    kept_high[...] = own_high[...]
    leaves, size = local_ref.shape[0], local_ref.shape[2]
    for i in range(leaves):
        total = dot_t(probes_ref[:, :size], local_ref[i, 0])
        for c in range(1, leaves):
            total += dot_t(probes_ref[:, c * size : (c + 1) * size], local_ref[i, c])
        out_ref[:, i * size : (i + 1) * size] = total


def far_kernel(by_high, low, partner_ref, base_ref, couplings_ref, transfer_ref, basis_ref, *refs):
    came, out_ref, boxes = refs[:low], refs[low], refs[low + 1]
    columns = out_ref.shape[0]
    leaves, rank, size = basis_ref.shape
    high = boxes.shape[0] // low
    me = lax.axis_index("leaf")
    for k in range(low):
        tile = came[k][by_high.dense_tails : by_high.dense_box, :].astype(F32)
        for i in range(high):
            start = by_high.dense_box + i * by_high.half
            packed = came[k][start : start + by_high.half, :]
            last = tile[leaves + i : leaves + i + 1, :rank]
            boxes[i * low + k] = jnp.concatenate(
                [packed[:, :rank].astype(F32), packed[:, rank:].astype(F32), last], axis=0
            ).astype(BF16)
    far = jnp.zeros((columns, rank), F32)
    for f in range(couplings_ref.shape[1]):
        source = jnp.bitwise_xor(partner_ref[0, f], me)
        far += dot_t(boxes[source], couplings_ref[0, f])
    far = far.astype(BF16)
    down = [dot(far, transfer_ref[j]).astype(BF16) for j in range(leaves)]
    for j in range(leaves):
        cols = slice(j * size, (j + 1) * size)
        out_ref[:, cols] = base_ref[:, cols] + dot(down[j], basis_ref[j])


def last_kernel(routes, devices, base_ref, *refs):
    by_low, by_high = routes
    high, low = grid_of(devices)
    came_high, came_low, out_ref = refs[:high], refs[high : high + low], refs[high + low]
    leaves, split, main = by_low.leaves, by_low.rows, by_low.main
    size = base_ref.shape[1] // leaves
    tails = sum(came_low[k][by_high.dense_tails : by_high.dense_box, :].astype(F32) for k in range(low))
    for j in range(leaves):
        cols = slice(j * size, (j + 1) * size)
        upper = sum(came_high[k][j * by_low.rows : (j + 1) * by_low.rows, :].astype(F32) for k in range(high))
        lower = sum(came_low[k][j * by_high.rows : (j + 1) * by_high.rows, :].astype(F32) for k in range(low))
        out_ref[:split, cols] = base_ref[:split, cols] + upper
        out_ref[split:main, cols] = base_ref[split:main, cols] + lower
        out_ref[main:, cols] = base_ref[main:, cols] + tails[j : j + 1]


def call(kernel, out_shape, specs, operands, scratch, flops, room=None):
    outs = jax.tree.leaves(out_shape)
    nbytes = sum(a.size * a.dtype.itemsize for a in (*operands, *outs))
    limit = None if room is None else nbytes + room + 2**21
    return pl.pallas_call(
        kernel,
        out_shape=out_shape,
        in_specs=specs[0],
        out_specs=specs[1],
        scratch_shapes=scratch,
        compiler_params=pltpu.CompilerParams(vmem_limit_bytes=limit),
        cost_estimate=pl.CostEstimate(flops=flops, bytes_accessed=nbytes, transcendentals=0),
    )(*operands)


def per_device(
    probes, basis, transfer, local_blocks, remote_blocks, near_dest, near_leaf, couplings, far_list
):
    columns, points = probes.shape
    leaves, rank, size = basis.shape
    devices = lax.axis_size("leaf")
    main = columns // TILE * TILE
    routes = by_low, by_high = routes_of(devices, main, columns, leaves)
    high, low = grid_of(devices)
    blocks = remote_blocks.shape[0] * remote_blocks.shape[1]
    unit = 2 * columns * size * size
    like = lambda *arrays: [pltpu.VMEM(a.shape, a.dtype) for a in arrays]
    numbers = lambda *arrays: [pltpu.SMEM(a.shape, a.dtype) for a in arrays]
    sems = lambda count: [pltpu.SemaphoreType.DMA((count,))]
    relative = lambda x, way: lax.ppermute(x, "leaf", [(i, i ^ way) for i in range(devices)])
    message = lambda route: jax.ShapeDtypeStruct((route.depth, size), BF16)
    dense = lambda route: jax.ShapeDtypeStruct((route.dense_depth, size), BF16)

    def stacked(count, like_this):
        return pltpu.VMEM((count, *like_this.shape), like_this.dtype)

    def summed(route, ways, came):
        total = jax.ShapeDtypeStruct((route.fan, (leaves + 1) * route.rows, size), F32)
        tails = jax.ShapeDtypeStruct((route.fan, max(TILE, route.dense_box - route.dense_tails), size), F32)
        return call(
            functools.partial(sum_kernel, route, ways),
            [dense(route)] * route.fan,
            ([VMEM] * ways, [VMEM] * route.fan),
            came,
            [pltpu.VMEM((ways, size), I32), pltpu.SMEM((ways, size), I32)]
            + like(total, tails)
            + [pltpu.SemaphoreType.DMA(())],
            devices * CAP * route.rows * size,
            4 * (total.size + tails.size),
        )

    dest, leaf = near_dest.T, near_leaf.T
    sent = call(
        functools.partial(products_kernel, routes, devices),
        [message(by_low)] * low + [message(by_high)] * high,
        ([ANY] * 6, [ANY] * (low + high)),
        (dest, leaf, probes, basis, transfer, remote_blocks),
        numbers(dest, leaf)
        + like(probes, basis, transfer, remote_blocks)
        + [
            stacked(low, message(by_low)),
            stacked(high, message(by_high)),
            pltpu.VMEM((high, by_high.meta - by_high.tails, size), F32),
            pltpu.VMEM((low, TILE, size), F32),
            pltpu.VMEM((high, TILE, size), F32),
            pltpu.SMEM((devices,), I32),
        ]
        + sems(7 + low + high),
        blocks * unit,
    )
    came_low, came_high = list(sent[:low]), list(sent[low:])
    came_low[1] = relative(came_low[1], 1)
    for k in range(high - 1, 1, -1):
        came_high[k] = relative(came_high[k], k * low)
    for k in range(low - 1, 1, -1):
        came_low[k] = relative(came_low[k], k)
    came_high[1] = relative(came_high[1], low)

    base_shape = jax.ShapeDtypeStruct((columns, points), F32)
    base, came_low[0], came_high[0] = call(
        local_kernel,
        (base_shape, message(by_low), message(by_high)),
        ([VMEM] * 4, (VMEM,) * 3),
        (probes, local_blocks, came_low[0], came_high[0]),
        [],
        leaves * leaves * unit,
        0,
    )

    to_high = list(summed(by_low, low, came_low))
    for k in range(high - 1, 0, -1):
        to_high[k] = relative(to_high[k], k * low)
    came_high[0], to_high[0] = lax.optimization_barrier((came_high[0], to_high[0]))
    to_low = list(summed(by_high, high, came_high))
    for k in range(1, low):
        to_low[k] = relative(to_low[k], k)

    boxes = jax.ShapeDtypeStruct((devices, columns, rank), BF16)
    base = call(
        functools.partial(far_kernel, by_high, low),
        base_shape,
        ([SMEM] + [VMEM] * (4 + low), VMEM),
        (far_list, base, couplings, transfer, basis, *to_low),
        like(boxes),
        4 * leaves * unit,
        4 * boxes.size,
    )
    return call(
        functools.partial(last_kernel, routes, devices),
        base_shape,
        ([VMEM] * (1 + high + low), VMEM),
        (base, *to_high, *to_low),
        [],
        devices * columns * size,
        0,
    )


def solution(mesh):
    placed = (
        P(None, ("grp", "leaf")),
        P(("grp", "leaf"), None, None),
        P(("grp", "leaf"), None, None),
        P(("grp", "leaf"), None, None, None),
        P(("grp", "leaf"), None, None, None),
        P(("grp", "leaf"), None),
        P(("grp", "leaf"), None),
        P(("grp", "leaf"), None, None, None),
        P(("grp", "leaf"), None),
    )
    return jax.shard_map(
        per_device, mesh=mesh, in_specs=placed, out_specs=P(None, ("grp", "leaf")), check_vma=False
    )
```

```python
import functools

import jax
import jax.numpy as jnp
from jax import lax
from jax.experimental import pallas as pl
from jax.experimental.pallas import tpu as pltpu
from jax.sharding import PartitionSpec as P

CAP = 4
TILE = 16
LANES = 128
F32 = jnp.float32
BF16 = jnp.bfloat16
I32 = jnp.int32

ANY = pl.BlockSpec(memory_space=pl.ANY)
VMEM = pl.BlockSpec(memory_space=pltpu.VMEM)
SMEM = pl.BlockSpec(memory_space=pltpu.SMEM)


def dot_t(lhs, rhs):
    return lax.dot_general(lhs, rhs, (((1,), (1,)), ((), ())), preferred_element_type=F32)


def dot(lhs, rhs):
    return lax.dot_general(lhs, rhs, (((1,), (0,)), ((), ())), preferred_element_type=F32)


class Copies:
    def __init__(self, sems):
        self.sems, self.used = sems, 0

    def start(self, src, dst):
        copy = pltpu.make_async_copy(src, dst, self.sems.at[self.used])
        self.used += 1
        copy.start()
        return copy


def grid_of(devices):
    low = 1 << (devices.bit_length() // 2)
    return devices // low, low


def up(rows):
    return -(-rows // TILE) * TILE


class Route:
    def __init__(self, first, last, fan, extra, main, columns, leaves, sources):
        self.first, self.rows, self.fan, self.extra, self.main = first, last - first, fan, extra, main
        self.leaves, self.half = leaves, main // 2
        slots = fan * CAP
        self.tails = slots * self.rows
        self.meta = self.tails + (up(slots) if extra else 0)
        self.box = self.meta + TILE
        self.depth = self.box + (self.half if extra else 0)
        self.dense_tails = leaves * self.rows
        self.dense_box = self.dense_tails + (up(leaves + sources) if extra else 0)
        self.dense_depth = self.dense_box + (sources * self.half if extra else 0)


def routes_of(devices, main, columns, leaves):
    high, low = grid_of(devices)
    split = up(main * 3 // 4)
    return (
        Route(0, split, high, False, main, columns, leaves, low),
        Route(split, main, low, True, main, columns, leaves, high),
    )


def products_kernel(routes, devices, *refs):
    dest_hbm, leaf_hbm, probes_hbm, basis_hbm, transfer_hbm, blocks_hbm = refs[:6]
    outs = refs[6:-13]
    (
        dest_ref, leaf_ref, probes_ref, basis_ref, transfer_ref, blocks_ref,
        send_low, send_high, tails, meta_low, meta_high, count, sems,
    ) = refs[-13:]
    by_low, by_high = routes
    high, low = grid_of(devices)
    me = lax.axis_index("leaf")
    main = by_high.main
    leaves, per_leaf, size = blocks_ref.shape[:3]
    columns, rank = probes_ref.shape[0], basis_ref.shape[1]
    copies = Copies(sems)
    early = [
        copies.start(probes_hbm, probes_ref),
        copies.start(basis_hbm, basis_ref),
        copies.start(transfer_hbm, transfer_ref),
        copies.start(dest_hbm, dest_ref),
        copies.start(leaf_hbm, leaf_ref),
    ]
    chunk = leaves // 2
    arrivals = [
        copies.start(blocks_hbm.at[pl.ds(j, chunk)], blocks_ref.at[pl.ds(j, chunk)])
        for j in range(0, leaves, chunk)
    ]

    @pl.loop(0, devices)
    def _(i):
        count[i] = 0

    tails[...] = jnp.zeros(tails.shape, F32)
    meta_low[...] = jnp.full(meta_low.shape, leaves, F32)
    meta_high[...] = jnp.full(meta_high.shape, leaves, F32)
    for copy in early:
        copy.wait()
    box = jnp.zeros((columns, rank), F32)
    for j in range(leaves):
        coef = dot_t(probes_ref[:, j * size : (j + 1) * size], basis_ref[j]).astype(BF16)
        box += dot_t(coef, transfer_ref[j])
    half = by_high.half
    packed = jnp.concatenate([box[:half], box[half:main]], axis=1).astype(BF16)
    last = jnp.concatenate([box[main:], jnp.zeros_like(box[main:])], axis=1)

    lane = lax.broadcasted_iota(I32, (1, size), 1)
    for j in range(leaves):
        if j % chunk == 0:
            arrivals[j // chunk].wait()
        x = probes_ref[:, j * size : (j + 1) * size]
        for first in range(0, per_leaf, 4):
            many = min(4, per_leaf - first)
            rhs = blocks_ref[j, first : first + many].reshape(many * size, size)
            product = dot_t(x, rhs)
            for b in range(many):
                target = jnp.bitwise_xor(dest_ref[first + b, j], me)
                slot = count[target]
                count[target] = slot + 1
                to_high, to_low = target // low, target % low
                block = product[:, b * size : (b + 1) * size]
                piece = block[:main].astype(BF16)
                number = leaf_ref[first + b, j].astype(F32)

                at = to_high * CAP + slot
                rows = pl.ds(pl.multiple_of(at * by_low.rows, TILE), by_low.rows)
                send_low[to_low, rows, :] = piece[: by_low.rows]
                meta_low[to_low, 0:1, :] = jnp.where(lane == at, number, meta_low[to_low, 0:1, :])

                at = to_low * CAP + slot
                rows = pl.ds(pl.multiple_of(at * by_high.rows, TILE), by_high.rows)
                send_high[to_high, rows, :] = piece[by_low.rows :]
                tails[to_high, pl.ds(at, 1), :] = block[main:]
                meta_high[to_high, 0:1, :] = jnp.where(lane == at, number, meta_high[to_high, 0:1, :])

    for i in range(low):
        send_low[i, by_low.meta : by_low.box, :] = meta_low[i].astype(BF16)
    for i in range(high):
        meta_high[i, 1:2, :] = last
        send_high[i, by_high.tails : by_high.meta, :] = tails[i].astype(BF16)
        send_high[i, by_high.meta : by_high.box, :] = meta_high[i].astype(BF16)
        send_high[i, by_high.box :, :] = packed
    leaving = [copies.start(send_low.at[i], outs[i]) for i in range(low)]
    leaving += [copies.start(send_high.at[i], outs[low + i]) for i in range(high)]
    for copy in leaving:
        copy.wait()


def sum_route(route, came, outs, base, leaf_ref, total, tails):
    leaves, half, ways = route.leaves, route.half, len(came)
    for i in range(ways):
        if route.extra:
            tail = came[i][route.tails : route.meta, :].astype(F32)
        for k in range(route.fan):
            for slot in range(CAP):
                at = k * CAP + slot
                leaf = leaf_ref[base + i, at]
                rows = pl.ds(pl.multiple_of(leaf * route.rows, TILE), route.rows)
                total[k, rows, :] += came[i][at * route.rows : (at + 1) * route.rows, :].astype(F32)
                if route.extra:
                    tails[k, pl.ds(leaf, 1), :] += tail[at : at + 1]

    for k in range(route.fan):
        outs[k][: route.dense_tails, :] = total[k, : route.dense_tails, :].astype(BF16)
        if route.extra:
            for i in range(ways):
                last = came[i][route.meta : route.box, :].astype(F32)[1:2]
                tails[k, leaves + i : leaves + i + 1, :] = last
                start = route.dense_box + i * half
                outs[k][start : start + half, :] = came[i][route.box :, :]
            outs[k][route.dense_tails : route.dense_box, :] = tails[k].astype(BF16)


def sum_kernel(routes, devices, *refs):
    by_low, by_high = routes
    high, low = grid_of(devices)
    ways = low + high
    came, outs, scratch = refs[:ways], refs[ways : 2 * ways], refs[2 * ways :]
    meta, leaf_ref, total_low, total_high, tails, late = scratch
    for i, route in enumerate([by_low] * low + [by_high] * high):
        meta[i : i + 1, :] = came[i][route.meta : route.box, :].astype(F32)[:1].astype(I32)
    numbers = pltpu.make_async_copy(meta, leaf_ref, late)
    numbers.start()
    for ref in (total_low, total_high, tails):
        ref[...] = jnp.zeros(ref.shape, F32)
    numbers.wait()
    sum_route(by_low, came[:low], outs[:high], 0, leaf_ref, total_low, None)
    sum_route(by_high, came[low:], outs[high:], low, leaf_ref, total_high, tails)


def keep_kernel(own_low, own_high, kept_low, kept_high):
    kept_low[...] = own_low[...]
    kept_high[...] = own_high[...]


def local_kernel(probes_ref, local_ref, out_ref):
    leaves, size = local_ref.shape[0], local_ref.shape[2]
    for i in range(leaves):
        total = dot_t(probes_ref[:, :size], local_ref[i, 0])
        for c in range(1, leaves):
            total += dot_t(probes_ref[:, c * size : (c + 1) * size], local_ref[i, c])
        out_ref[:, i * size : (i + 1) * size] = total


def far_kernel(by_high, low, partner_ref, base_ref, couplings_ref, transfer_ref, basis_ref, *refs):
    came, out_ref, boxes = refs[:low], refs[low], refs[low + 1]
    columns = out_ref.shape[0]
    leaves, rank, size = basis_ref.shape
    high = boxes.shape[0] // low
    me = lax.axis_index("leaf")
    for k in range(low):
        tile = came[k][by_high.dense_tails : by_high.dense_box, :].astype(F32)
        for i in range(high):
            start = by_high.dense_box + i * by_high.half
            packed = came[k][start : start + by_high.half, :]
            last = tile[leaves + i : leaves + i + 1, :rank]
            boxes[i * low + k] = jnp.concatenate(
                [packed[:, :rank].astype(F32), packed[:, rank:].astype(F32), last], axis=0
            ).astype(BF16)
    far = jnp.zeros((columns, rank), F32)
    for f in range(couplings_ref.shape[1]):
        source = jnp.bitwise_xor(partner_ref[0, f], me)
        far += dot_t(boxes[source], couplings_ref[0, f])
    far = far.astype(BF16)
    down = [dot(far, transfer_ref[j]).astype(BF16) for j in range(leaves)]
    for j in range(leaves):
        cols = slice(j * size, (j + 1) * size)
        out_ref[:, cols] = base_ref[:, cols] + dot(down[j], basis_ref[j])


def last_kernel(routes, devices, base_ref, *refs):
    by_low, by_high = routes
    high, low = grid_of(devices)
    came_high, came_low, out_ref = refs[:high], refs[high : high + low], refs[high + low]
    leaves, split, main = by_low.leaves, by_low.rows, by_low.main
    size = base_ref.shape[1] // leaves
    tails = sum(came_low[k][by_high.dense_tails : by_high.dense_box, :].astype(F32) for k in range(low))
    for j in range(leaves):
        cols = slice(j * size, (j + 1) * size)
        upper = sum(came_high[k][j * by_low.rows : (j + 1) * by_low.rows, :].astype(F32) for k in range(high))
        lower = sum(came_low[k][j * by_high.rows : (j + 1) * by_high.rows, :].astype(F32) for k in range(low))
        out_ref[:split, cols] = base_ref[:split, cols] + upper
        out_ref[split:main, cols] = base_ref[split:main, cols] + lower
        out_ref[main:, cols] = base_ref[main:, cols] + tails[j : j + 1]


def call(kernel, out_shape, specs, operands, scratch, flops, room=None):
    outs = jax.tree.leaves(out_shape)
    nbytes = sum(a.size * a.dtype.itemsize for a in (*operands, *outs))
    limit = None if room is None else nbytes + room + 2**21
    return pl.pallas_call(
        kernel,
        out_shape=out_shape,
        in_specs=specs[0],
        out_specs=specs[1],
        scratch_shapes=scratch,
        compiler_params=pltpu.CompilerParams(vmem_limit_bytes=limit),
        cost_estimate=pl.CostEstimate(flops=flops, bytes_accessed=nbytes, transcendentals=0),
    )(*operands)


def per_device(
    probes, basis, transfer, local_blocks, remote_blocks, near_dest, near_leaf, couplings, far_list
):
    columns, points = probes.shape
    leaves, rank, size = basis.shape
    devices = lax.axis_size("leaf")
    main = columns // TILE * TILE
    routes = by_low, by_high = routes_of(devices, main, columns, leaves)
    high, low = grid_of(devices)
    blocks = remote_blocks.shape[0] * remote_blocks.shape[1]
    unit = 2 * columns * size * size
    like = lambda *arrays: [pltpu.VMEM(a.shape, a.dtype) for a in arrays]
    numbers = lambda *arrays: [pltpu.SMEM(a.shape, a.dtype) for a in arrays]
    sems = lambda count: [pltpu.SemaphoreType.DMA((count,))]
    relative = lambda x, way: lax.ppermute(x, "leaf", [(i, i ^ way) for i in range(devices)])
    message = lambda route: jax.ShapeDtypeStruct((route.depth, size), BF16)
    dense = lambda route: jax.ShapeDtypeStruct((route.dense_depth, size), BF16)

    def stacked(count, like_this):
        return pltpu.VMEM((count, *like_this.shape), like_this.dtype)

    dest, leaf = near_dest.T, near_leaf.T
    sent = call(
        functools.partial(products_kernel, routes, devices),
        [message(by_low)] * low + [message(by_high)] * high,
        ([ANY] * 6, [ANY] * (low + high)),
        (dest, leaf, probes, basis, transfer, remote_blocks),
        numbers(dest, leaf)
        + like(probes, basis, transfer, remote_blocks)
        + [
            stacked(low, message(by_low)),
            stacked(high, message(by_high)),
            pltpu.VMEM((high, by_high.meta - by_high.tails, size), F32),
            pltpu.VMEM((low, TILE, size), F32),
            pltpu.VMEM((high, TILE, size), F32),
            pltpu.SMEM((devices,), I32),
        ]
        + sems(7 + low + high),
        blocks * unit,
    )
    came_low, came_high = list(sent[:low]), list(sent[low:])
    came_low[1] = relative(came_low[1], 1)
    for k in range(max(low, high) - 1, 0, -1):
        if 1 < k < low:
            came_low[k] = relative(came_low[k], k)
        if k < high:
            came_high[k] = relative(came_high[k], k * low)
    came_low[0], came_high[0] = call(
        keep_kernel,
        (message(by_low), message(by_high)),
        ([VMEM] * 2, (VMEM,) * 2),
        (came_low[0], came_high[0]),
        [],
        0,
        0,
    )

    total = lambda route: jax.ShapeDtypeStruct((route.fan, (leaves + 1) * route.rows, size), F32)
    tails = jax.ShapeDtypeStruct((low, by_high.dense_box - by_high.dense_tails, size), F32)
    sums = call(
        functools.partial(sum_kernel, routes, devices),
        [dense(by_low)] * high + [dense(by_high)] * low,
        ([VMEM] * (low + high), [VMEM] * (low + high)),
        (*came_low, *came_high),
        [pltpu.VMEM((low + high, size), I32), pltpu.SMEM((low + high, size), I32)]
        + like(total(by_low), total(by_high), tails)
        + [pltpu.SemaphoreType.DMA(())],
        devices * CAP * columns * size,
        4 * (total(by_low).size + total(by_high).size + tails.size),
    )
    to_high, to_low = list(sums[:high]), list(sums[high:])
    probes_then, to_low[0] = lax.optimization_barrier((probes, to_low[0]))
    for k in range(max(low, high) - 1, 0, -1):
        if k < high:
            to_high[k] = relative(to_high[k], k * low)
        if k < low:
            to_low[k] = relative(to_low[k], k)

    base_shape = jax.ShapeDtypeStruct((columns, points), F32)
    base = call(
        local_kernel, base_shape, ([VMEM] * 2, VMEM), (probes_then, local_blocks), [], leaves * leaves * unit, 0
    )
    boxes = jax.ShapeDtypeStruct((devices, columns, rank), BF16)
    base = call(
        functools.partial(far_kernel, by_high, low),
        base_shape,
        ([SMEM] + [VMEM] * (4 + low), VMEM),
        (far_list, base, couplings, transfer, basis, *to_low),
        like(boxes),
        4 * leaves * unit,
        4 * boxes.size,
    )
    return call(
        functools.partial(last_kernel, routes, devices),
        base_shape,
        ([VMEM] * (1 + high + low), VMEM),
        (base, *to_high, *to_low),
        [],
        devices * columns * size,
        0,
    )


def solution(mesh):
    placed = (
        P(None, ("grp", "leaf")),
        P(("grp", "leaf"), None, None),
        P(("grp", "leaf"), None, None),
        P(("grp", "leaf"), None, None, None),
        P(("grp", "leaf"), None, None, None),
        P(("grp", "leaf"), None),
        P(("grp", "leaf"), None),
        P(("grp", "leaf"), None, None, None),
        P(("grp", "leaf"), None),
    )
    return jax.shard_map(
        per_device, mesh=mesh, in_specs=placed, out_specs=P(None, ("grp", "leaf")), check_vma=False
    )
```

```python
import functools

import jax
import jax.numpy as jnp
from jax import lax
from jax.experimental import pallas as pl
from jax.experimental.pallas import tpu as pltpu
from jax.sharding import PartitionSpec as P

CAP = 4
TILE = 16
FIRST_FAR = 2
F32 = jnp.float32
BF16 = jnp.bfloat16
I32 = jnp.int32

ANY = pl.BlockSpec(memory_space=pl.ANY)
VMEM = pl.BlockSpec(memory_space=pltpu.VMEM)
SMEM = pl.BlockSpec(memory_space=pltpu.SMEM)


def dot_t(lhs, rhs):
    return lax.dot_general(lhs, rhs, (((1,), (1,)), ((), ())), preferred_element_type=F32)


def dot(lhs, rhs):
    return lax.dot_general(lhs, rhs, (((1,), (0,)), ((), ())), preferred_element_type=F32)


class Copies:
    def __init__(self, sems):
        self.sems, self.used = sems, 0

    def start(self, src, dst):
        copy = pltpu.make_async_copy(src, dst, self.sems.at[self.used])
        self.used += 1
        copy.start()
        return copy


def grid_of(devices):
    low = 1 << (devices.bit_length() // 2)
    return devices // low, low


def up(rows):
    return -(-rows // TILE) * TILE


class Message:
    def __init__(self, fan, box, main):
        self.fan, self.slots, self.main, self.half = fan, fan * CAP, main, main // 2
        self.tile = self.slots * main
        self.leaf, self.last = self.slots, self.slots + 1
        self.box = self.tile + up(self.slots + 2)
        self.depth = self.box + (self.half if box else 0)


class Dense:
    def __init__(self, leaves, boxes, main):
        self.leaves, self.main, self.half = leaves, main, main // 2
        self.tile = leaves * main
        self.box = self.tile + up(leaves + boxes)
        self.depth = self.box + boxes * self.half


class Plan:
    def __init__(self, devices, main, leaves):
        self.high, self.low = grid_of(devices)
        self.far = range(FIRST_FAR, self.high)
        self.plane = Message(len(self.far), False, main)
        self.near = Message(self.low, True, main)
        self.along = Dense(leaves, 0, main)
        self.within = Dense(leaves, self.high, main)
        self.parts = self.low + FIRST_FAR


def products_kernel(plan, *refs):
    dest_hbm, leaf_hbm, probes_hbm, basis_hbm, transfer_hbm, blocks_hbm = refs[:6]
    outs = refs[6:-11]
    (
        dest_ref, leaf_ref, probes_ref, basis_ref, transfer_ref, blocks_ref, send_ref, box_ref, tails, count, sems,
    ) = refs[-11:]
    low, plane, near = plan.low, plan.plane, plan.near
    me = lax.axis_index("leaf")
    main, half = plane.main, plane.half
    leaves, per_leaf, size = blocks_ref.shape[:3]
    columns, rank = probes_ref.shape[0], basis_ref.shape[1]
    copies = Copies(sems)
    early = [
        copies.start(probes_hbm, probes_ref),
        copies.start(basis_hbm, basis_ref),
        copies.start(transfer_hbm, transfer_ref),
        copies.start(dest_hbm, dest_ref),
        copies.start(leaf_hbm, leaf_ref),
    ]
    chunk = leaves // 2
    arrivals = [
        copies.start(blocks_hbm.at[pl.ds(j, chunk)], blocks_ref.at[pl.ds(j, chunk)])
        for j in range(0, leaves, chunk)
    ]

    @pl.loop(0, count.shape[0])
    def _(i):
        count[i] = 0

    kinds = [plane] * low + [near] * FIRST_FAR
    starts = [sum(kind.depth for kind in kinds[:i]) for i in range(len(kinds))]
    tails[...] = jnp.zeros(tails.shape, F32)
    for i, kind in enumerate(kinds):
        tails[i, kind.leaf : kind.leaf + 1, :] = jnp.full((1, size), leaves, F32)
    for copy in early:
        copy.wait()
    box = jnp.zeros((columns, rank), F32)
    for j in range(leaves):
        coef = dot_t(probes_ref[:, j * size : (j + 1) * size], basis_ref[j]).astype(BF16)
        box += dot_t(coef, transfer_ref[j])
    packed = jnp.concatenate([box[:half], box[half:main]], axis=1).astype(BF16)
    last = jnp.concatenate([box[main:], jnp.zeros_like(box[main:])], axis=1)

    lane = lax.broadcasted_iota(I32, (1, size), 1)
    for j in range(leaves):
        if j % chunk == 0:
            arrivals[j // chunk].wait()
        x = probes_ref[:, j * size : (j + 1) * size]
        for first in range(0, per_leaf, 4):
            many = min(4, per_leaf - first)
            rhs = blocks_ref[j, first : first + many].reshape(many * size, size)
            product = dot_t(x, rhs)
            for b in range(many):
                target = jnp.bitwise_xor(dest_ref[first + b, j], me)
                slot = count[target]
                count[target] = slot + 1
                to_high, to_low = target // low, target % low
                is_near = to_high < FIRST_FAR
                part = jnp.where(is_near, low + to_high, to_low)
                at = jnp.where(is_near, to_low, to_high - FIRST_FAR) * CAP + slot
                start = jnp.where(is_near, low * plane.depth + to_high * near.depth, to_low * plane.depth)
                rows = pl.ds(pl.multiple_of(start + at * main, TILE), main)
                block = product[:, b * size : (b + 1) * size]
                send_ref[rows, :] = block[:main].astype(BF16)
                tails[part, pl.ds(at, 1), :] = block[main:]
                row = pl.ds(jnp.where(is_near, near.leaf, plane.leaf), 1)
                number = leaf_ref[first + b, j].astype(F32)
                tails[part, row, :] = jnp.where(lane == at, number, tails[part, row, :])

    leaving = []
    for i, kind in enumerate(kinds):
        tails[i, kind.last : kind.last + 1, :] = last
        start = starts[i]
        send_ref[start + kind.tile : start + kind.box, :] = tails[i, : kind.box - kind.tile, :].astype(BF16)
        if kind.depth > kind.box:
            send_ref[start + kind.box : start + kind.depth, :] = packed
        leaving.append(copies.start(send_ref.at[pl.ds(start, kind.depth)], outs[i]))
    box_ref[:half, :] = packed
    box_ref[half:, :] = jnp.broadcast_to(last, (TILE, size)).astype(BF16)
    leaving.append(copies.start(box_ref, outs[-1]))
    for copy in leaving:
        copy.wait()


def read_leaves(kind, came, meta, leaf_ref, late, meanwhile):
    for i, ref in enumerate(came):
        tile = ref[kind.tile : kind.box, :].astype(F32)
        meta[i : i + 1, :] = tile[kind.leaf : kind.leaf + 1].astype(I32)
    numbers = pltpu.make_async_copy(meta, leaf_ref, late)
    numbers.start()
    for ref in meanwhile:
        ref[...] = jnp.zeros(ref.shape, F32)
    numbers.wait()


def add_slots(kind, came, leaf_ref, total, tails):
    main = kind.main
    for i, ref in enumerate(came):
        tile = ref[kind.tile : kind.box, :].astype(F32)
        for k in range(kind.fan):
            for at in range(k * CAP, (k + 1) * CAP):
                leaf = leaf_ref[i, at]
                rows = pl.ds(pl.multiple_of(leaf * main, TILE), main)
                total[k, rows, :] += ref[at * main : (at + 1) * main, :].astype(F32)
                tails[k, pl.ds(leaf, 1), :] += tile[at : at + 1]


def far_sum_kernel(plan, *refs):
    came, outs = refs[: plan.low], refs[plan.low : -5]
    meta, leaf_ref, total, tails, late = refs[-5:]
    to = plan.along
    read_leaves(plan.plane, came, meta, leaf_ref, late, (total, tails))
    add_slots(plan.plane, came, leaf_ref, total, tails)
    for k, out in enumerate(outs):
        out[: to.tile, :] = total[k, : to.tile, :].astype(BF16)
        out[to.tile : to.box, :] = tails[k, : to.box - to.tile, :].astype(BF16)


def near_sum_kernel(plan, *refs):
    came, boxes = refs[:FIRST_FAR], refs[FIRST_FAR : plan.high]
    outs = refs[plan.high : -5]
    meta, leaf_ref, total, tails, late = refs[-5:]
    kind, to = plan.near, plan.within
    read_leaves(kind, came, meta, leaf_ref, late, (total, tails))
    add_slots(kind, came, leaf_ref, total, tails)
    lasts = [ref[kind.tile : kind.box, :].astype(F32)[kind.last : kind.last + 1] for ref in came]
    lasts += [ref[kind.half :, :].astype(F32)[:1] for ref in boxes]
    packed = [ref[kind.box :, :] for ref in came] + [ref[: kind.half, :] for ref in boxes]
    for p, out in enumerate(outs):
        out[: to.tile, :] = total[p, : to.tile, :].astype(BF16)
        for k, last in enumerate(lasts):
            tails[p, to.leaves + k : to.leaves + k + 1, :] = last
        out[to.tile : to.box, :] = tails[p, : to.box - to.tile, :].astype(BF16)
        for k, rows in enumerate(packed):
            out[to.box + k * to.half : to.box + (k + 1) * to.half, :] = rows


def keep_kernel(*refs):
    for came, kept in zip(refs[: len(refs) // 2], refs[len(refs) // 2 :]):
        kept[...] = came[...]


def local_kernel(probes_ref, local_ref, out_ref):
    leaves, size = local_ref.shape[0], local_ref.shape[2]
    for i in range(leaves):
        total = dot_t(probes_ref[:, :size], local_ref[i, 0])
        for c in range(1, leaves):
            total += dot_t(probes_ref[:, c * size : (c + 1) * size], local_ref[i, c])
        out_ref[:, i * size : (i + 1) * size] = total


def far_kernel(plan, partner_ref, base_ref, couplings_ref, transfer_ref, basis_ref, *refs):
    high, low, came_as = plan.high, plan.low, plan.within
    came, out_ref, boxes = refs[:low], refs[low], refs[low + 1]
    columns = out_ref.shape[0]
    leaves, rank, size = basis_ref.shape
    me = lax.axis_index("leaf")
    for p in range(low):
        tile = came[p][came_as.tile : came_as.box, :].astype(F32)
        for k in range(high):
            start = came_as.box + k * came_as.half
            packed = came[p][start : start + came_as.half, :]
            last = tile[leaves + k : leaves + k + 1, :rank]
            boxes[k * low + p] = jnp.concatenate(
                [packed[:, :rank].astype(F32), packed[:, rank:].astype(F32), last], axis=0
            ).astype(BF16)
    far = jnp.zeros((columns, rank), F32)
    for f in range(couplings_ref.shape[1]):
        source = jnp.bitwise_xor(partner_ref[0, f], me)
        far += dot_t(boxes[source], couplings_ref[0, f])
    far = far.astype(BF16)
    down = [dot(far, transfer_ref[j]).astype(BF16) for j in range(leaves)]
    for j in range(leaves):
        cols = slice(j * size, (j + 1) * size)
        out_ref[:, cols] = base_ref[:, cols] + dot(down[j], basis_ref[j])


def last_kernel(leaves, main, base_ref, *refs):
    came, out_ref = refs[:-1], refs[-1]
    size = base_ref.shape[1] // leaves
    tile = leaves * main
    tails = sum(ref[tile : tile + TILE, :].astype(F32) for ref in came)
    for j in range(leaves):
        cols = slice(j * size, (j + 1) * size)
        rows = slice(j * main, (j + 1) * main)
        out_ref[:main, cols] = base_ref[:main, cols] + sum(ref[rows, :].astype(F32) for ref in came)
        out_ref[main:, cols] = base_ref[main:, cols] + tails[j : j + 1]


def call(kernel, out_shape, specs, operands, scratch, flops, room=None):
    outs = jax.tree.leaves(out_shape)
    nbytes = sum(a.size * a.dtype.itemsize for a in (*operands, *outs))
    limit = None if room is None else nbytes + room + 2**21
    return pl.pallas_call(
        kernel,
        out_shape=out_shape,
        in_specs=specs[0],
        out_specs=specs[1],
        scratch_shapes=scratch,
        compiler_params=pltpu.CompilerParams(vmem_limit_bytes=limit),
        cost_estimate=pl.CostEstimate(flops=flops, bytes_accessed=nbytes, transcendentals=0),
    )(*operands)


def per_device(
    probes, basis, transfer, local_blocks, remote_blocks, near_dest, near_leaf, couplings, far_list
):
    columns, points = probes.shape
    leaves, rank, size = basis.shape
    devices = lax.axis_size("leaf")
    main = columns // TILE * TILE
    plan = Plan(devices, main, leaves)
    high, low = plan.high, plan.low
    blocks = remote_blocks.shape[0] * remote_blocks.shape[1]
    unit = 2 * columns * size * size
    array = lambda rows, dtype=BF16: jax.ShapeDtypeStruct((*rows, size), dtype)
    like = lambda *arrays: [pltpu.VMEM(a.shape, a.dtype) for a in arrays]
    numbers = lambda *arrays: [pltpu.SMEM(a.shape, a.dtype) for a in arrays]
    sems = lambda count: [pltpu.SemaphoreType.DMA((count,))]
    relative = lambda x, way: lax.ppermute(x, "leaf", [(i, i ^ way) for i in range(devices)])

    dest, leaf = near_dest.T, near_leaf.T
    sizes = [plan.plane.depth] * low + [plan.near.depth] * FIRST_FAR + [main // 2 + TILE]
    sent = call(
        functools.partial(products_kernel, plan),
        [array((rows,)) for rows in sizes],
        ([ANY] * 6, [ANY] * len(sizes)),
        (dest, leaf, probes, basis, transfer, remote_blocks),
        numbers(dest, leaf)
        + like(probes, basis, transfer, remote_blocks)
        + like(array((sum(sizes[:-1]),)), array(sizes[-1:]))
        + [
            pltpu.VMEM((plan.parts, max(k.box - k.tile for k in (plan.plane, plan.near)), size), F32),
            pltpu.SMEM((devices,), I32),
        ]
        + sems(7 + len(sizes)),
        blocks * unit,
    )
    plane, near, box = list(sent[:low]), list(sent[low:-1]), sent[-1]
    for p in range(1, low):
        plane[p] = relative(plane[p], p)
    for k in range(1, FIRST_FAR):
        near[k] = relative(near[k], k * low)
    boxes = [relative(box, k * low) for k in plan.far]
    plane[0], near[0] = call(
        keep_kernel, (array(sizes[:1]), array(sizes[low : low + 1])), ([VMEM] * 2, (VMEM,) * 2), (plane[0], near[0]), [], 0, 0
    )

    def summed(kernel, kind, dense, came, others):
        count = kind.fan
        total = array((count, (leaves + 1) * main), F32)
        tails = array((count, max(TILE, dense.box - dense.tile)), F32)
        return call(
            functools.partial(kernel, plan),
            [array((dense.depth,))] * count,
            ([VMEM] * (len(came) + len(others)), [VMEM] * count),
            (*came, *others),
            [pltpu.VMEM((len(came), size), I32), pltpu.SMEM((len(came), size), I32)]
            + like(total, tails)
            + [pltpu.SemaphoreType.DMA(())],
            len(came) * kind.slots * columns * size,
            4 * (total.size + tails.size),
        )

    along = summed(far_sum_kernel, plan.plane, plan.along, plane, [])
    near[0], *along = lax.optimization_barrier((near[0], *along))
    along = [relative(x, k * low) for k, x in zip(plan.far, along)]
    within = list(summed(near_sum_kernel, plan.near, plan.within, near, boxes))
    probes_then, within[0] = lax.optimization_barrier((probes, within[0]))
    for p in range(1, low):
        within[p] = relative(within[p], p)

    base_shape = jax.ShapeDtypeStruct((columns, points), F32)
    base = call(
        local_kernel, base_shape, ([VMEM] * 2, VMEM), (probes_then, local_blocks), [], leaves * leaves * unit, 0
    )
    every = jax.ShapeDtypeStruct((devices, columns, rank), BF16)
    base = call(
        functools.partial(far_kernel, plan),
        base_shape,
        ([SMEM] + [VMEM] * (4 + low), VMEM),
        (far_list, base, couplings, transfer, basis, *within),
        like(every),
        4 * leaves * unit,
        4 * every.size,
    )
    came = (*within, *along)
    return call(
        functools.partial(last_kernel, leaves, main),
        base_shape,
        ([VMEM] * (1 + len(came)), VMEM),
        (base, *came),
        [],
        devices * columns * size,
        0,
    )


def solution(mesh):
    placed = (
        P(None, ("grp", "leaf")),
        P(("grp", "leaf"), None, None),
        P(("grp", "leaf"), None, None),
        P(("grp", "leaf"), None, None, None),
        P(("grp", "leaf"), None, None, None),
        P(("grp", "leaf"), None),
        P(("grp", "leaf"), None),
        P(("grp", "leaf"), None, None, None),
        P(("grp", "leaf"), None),
    )
    return jax.shard_map(
        per_device, mesh=mesh, in_specs=placed, out_specs=P(None, ("grp", "leaf")), check_vma=False
    )
```

```python
import functools

import jax
import jax.numpy as jnp
from jax import lax
from jax.experimental import pallas as pl
from jax.experimental.pallas import tpu as pltpu
from jax.sharding import PartitionSpec as P

CAP = 4
TILE = 16
FIRST_FAR = 2
F32 = jnp.float32
BF16 = jnp.bfloat16
I32 = jnp.int32

ANY = pl.BlockSpec(memory_space=pl.ANY)
VMEM = pl.BlockSpec(memory_space=pltpu.VMEM)
SMEM = pl.BlockSpec(memory_space=pltpu.SMEM)


def dot_t(lhs, rhs):
    return lax.dot_general(lhs, rhs, (((1,), (1,)), ((), ())), preferred_element_type=F32)


def dot(lhs, rhs):
    return lax.dot_general(lhs, rhs, (((1,), (0,)), ((), ())), preferred_element_type=F32)


class Copies:
    def __init__(self, sems):
        self.sems, self.used = sems, 0

    def start(self, src, dst):
        copy = pltpu.make_async_copy(src, dst, self.sems.at[self.used])
        self.used += 1
        copy.start()
        return copy


def grid_of(devices):
    low = 1 << (devices.bit_length() // 2)
    return devices // low, low


def up(rows):
    return -(-rows // TILE) * TILE


class Message:
    def __init__(self, fan, box, main):
        self.fan, self.slots, self.main, self.half = fan, fan * CAP, main, main // 2
        self.tile = self.slots * main
        self.leaf, self.last = self.slots, self.slots + 1
        self.box = self.tile + up(self.slots + 2)
        self.depth = self.box + (self.half if box else 0)


class Dense:
    def __init__(self, leaves, boxes, main):
        self.leaves, self.main, self.half = leaves, main, main // 2
        self.tile = leaves * main
        self.box = self.tile + up(leaves + boxes)
        self.depth = self.box + boxes * self.half


class Plan:
    def __init__(self, devices, main, leaves):
        self.high, self.low = grid_of(devices)
        self.far = range(FIRST_FAR, self.high)
        self.plane = Message(len(self.far), False, main)
        self.near = Message(self.low, True, main)
        self.along = Dense(leaves, 0, main)
        self.within = Dense(leaves, self.high, main)
        self.parts = self.low + FIRST_FAR


def products_kernel(plan, *refs):
    dest_hbm, leaf_hbm, probes_hbm, basis_hbm, transfer_hbm, blocks_hbm = refs[:6]
    outs = refs[6:-11]
    (
        dest_ref, leaf_ref, probes_ref, basis_ref, transfer_ref, blocks_ref, send_ref, box_ref, tails, count, sems,
    ) = refs[-11:]
    low, plane, near = plan.low, plan.plane, plan.near
    me = lax.axis_index("leaf")
    main, half = plane.main, plane.half
    leaves, per_leaf, size = blocks_ref.shape[:3]
    columns, rank = probes_ref.shape[0], basis_ref.shape[1]
    copies = Copies(sems)
    early = [
        copies.start(probes_hbm, probes_ref),
        copies.start(basis_hbm, basis_ref),
        copies.start(transfer_hbm, transfer_ref),
        copies.start(dest_hbm, dest_ref),
        copies.start(leaf_hbm, leaf_ref),
    ]
    chunk = leaves // 2
    arrivals = [
        copies.start(blocks_hbm.at[pl.ds(j, chunk)], blocks_ref.at[pl.ds(j, chunk)])
        for j in range(0, leaves, chunk)
    ]

    @pl.loop(0, count.shape[0])
    def _(i):
        count[i] = 0

    kinds = [plane] * low + [near] * FIRST_FAR
    starts = [sum(kind.depth for kind in kinds[:i]) for i in range(len(kinds))]
    tails[...] = jnp.zeros(tails.shape, F32)
    for i, kind in enumerate(kinds):
        tails[i, kind.leaf : kind.leaf + 1, :] = jnp.full((1, size), leaves, F32)
    for copy in early:
        copy.wait()
    box = jnp.zeros((columns, rank), F32)
    for j in range(leaves):
        coef = dot_t(probes_ref[:, j * size : (j + 1) * size], basis_ref[j]).astype(BF16)
        box += dot_t(coef, transfer_ref[j])
    packed = jnp.concatenate([box[:half], box[half:main]], axis=1).astype(BF16)
    last = jnp.concatenate([box[main:], jnp.zeros_like(box[main:])], axis=1)

    lane = lax.broadcasted_iota(I32, (1, size), 1)
    for j in range(leaves):
        if j % chunk == 0:
            arrivals[j // chunk].wait()
        x = probes_ref[:, j * size : (j + 1) * size]
        for first in range(0, per_leaf, 4):
            many = min(4, per_leaf - first)
            rhs = blocks_ref[j, first : first + many].reshape(many * size, size)
            product = dot_t(x, rhs)
            for b in range(many):
                target = jnp.bitwise_xor(dest_ref[first + b, j], me)
                slot = count[target]
                count[target] = slot + 1
                to_high, to_low = target // low, target % low
                is_near = to_high < FIRST_FAR
                part = jnp.where(is_near, low + to_high, to_low)
                at = jnp.where(is_near, to_low, to_high - FIRST_FAR) * CAP + slot
                start = jnp.where(is_near, low * plane.depth + to_high * near.depth, to_low * plane.depth)
                rows = pl.ds(pl.multiple_of(start + at * main, TILE), main)
                block = product[:, b * size : (b + 1) * size]
                send_ref[rows, :] = block[:main].astype(BF16)
                tails[part, pl.ds(at, 1), :] = block[main:]
                row = pl.ds(jnp.where(is_near, near.leaf, plane.leaf), 1)
                number = leaf_ref[first + b, j].astype(F32)
                tails[part, row, :] = jnp.where(lane == at, number, tails[part, row, :])

    leaving = []
    for i, kind in enumerate(kinds):
        tails[i, kind.last : kind.last + 1, :] = last
        start = starts[i]
        send_ref[start + kind.tile : start + kind.box, :] = tails[i, : kind.box - kind.tile, :].astype(BF16)
        if kind.depth > kind.box:
            send_ref[start + kind.box : start + kind.depth, :] = packed
        leaving.append(copies.start(send_ref.at[pl.ds(start, kind.depth)], outs[i]))
    box_ref[:half, :] = packed
    box_ref[half:, :] = jnp.broadcast_to(last, (TILE, size)).astype(BF16)
    leaving.append(copies.start(box_ref, outs[-1]))
    for copy in leaving:
        copy.wait()


def read_leaves(kind, came, meta, leaf_ref, late, meanwhile):
    for i, ref in enumerate(came):
        tile = ref[kind.tile : kind.box, :].astype(F32)
        meta[i : i + 1, :] = tile[kind.leaf : kind.leaf + 1].astype(I32)
    numbers = pltpu.make_async_copy(meta, leaf_ref, late)
    numbers.start()
    for ref in meanwhile:
        ref[...] = jnp.zeros(ref.shape, F32)
    numbers.wait()


def add_slots(kind, came, leaf_ref, total, tails):
    main = kind.main
    for i, ref in enumerate(came):
        tile = ref[kind.tile : kind.box, :].astype(F32)
        for k in range(kind.fan):
            for at in range(k * CAP, (k + 1) * CAP):
                leaf = leaf_ref[i, at]
                rows = pl.ds(pl.multiple_of(leaf * main, TILE), main)
                total[k, rows, :] += ref[at * main : (at + 1) * main, :].astype(F32)
                tails[k, pl.ds(leaf, 1), :] += tile[at : at + 1]


def split(keys, bit):
    return [k for k in keys if k & bit], [k for k in keys if not k & bit]


def far_sum_kernel(plan, *refs):
    came, outs = refs[: plan.low], refs[plan.low : -5]
    meta, leaf_ref, total, tails, late = refs[-5:]
    to = plan.along
    read_leaves(plan.plane, came, meta, leaf_ref, late, (total, tails))
    add_slots(plan.plane, came, leaf_ref, total, tails)
    for out, keys in zip(outs, split(plan.far, 1)):
        for i, k in enumerate(keys):
            out[i, : to.tile, :] = total[k - FIRST_FAR, : to.tile, :].astype(BF16)
            out[i, to.tile :, :] = tails[k - FIRST_FAR, : to.box - to.tile, :].astype(BF16)


def fold_kernel(terms, *refs):
    inputs, outs = refs[: -len(terms)], refs[-len(terms) :]
    for out, entries in zip(outs, terms):
        for i, entry in enumerate(entries):
            out[i] = sum(inputs[n][at].astype(F32) for n, at in entry).astype(BF16)


def near_sum_kernel(plan, *refs):
    came, boxes = refs[:FIRST_FAR], refs[FIRST_FAR : plan.high]
    outs = refs[plan.high : -5]
    meta, leaf_ref, total, tails, late = refs[-5:]
    kind, to = plan.near, plan.within
    read_leaves(kind, came, meta, leaf_ref, late, (total, tails))
    add_slots(kind, came, leaf_ref, total, tails)
    lasts = [ref[kind.tile : kind.box, :].astype(F32)[kind.last : kind.last + 1] for ref in came]
    lasts += [ref[kind.half :, :].astype(F32)[:1] for ref in boxes]
    packed = [ref[kind.box :, :] for ref in came] + [ref[: kind.half, :] for ref in boxes]
    for p, out in enumerate(outs):
        out[: to.tile, :] = total[p, : to.tile, :].astype(BF16)
        for k, last in enumerate(lasts):
            tails[p, to.leaves + k : to.leaves + k + 1, :] = last
        out[to.tile : to.box, :] = tails[p, : to.box - to.tile, :].astype(BF16)
        for k, rows in enumerate(packed):
            out[to.box + k * to.half : to.box + (k + 1) * to.half, :] = rows


def keep_kernel(*refs):
    for came, kept in zip(refs[: len(refs) // 2], refs[len(refs) // 2 :]):
        kept[...] = came[...]


def local_kernel(probes_ref, local_ref, out_ref):
    leaves, size = local_ref.shape[0], local_ref.shape[2]
    for i in range(leaves):
        total = dot_t(probes_ref[:, :size], local_ref[i, 0])
        for c in range(1, leaves):
            total += dot_t(probes_ref[:, c * size : (c + 1) * size], local_ref[i, c])
        out_ref[:, i * size : (i + 1) * size] = total


def far_kernel(plan, partner_ref, base_ref, couplings_ref, transfer_ref, basis_ref, *refs):
    high, low, came_as = plan.high, plan.low, plan.within
    came, out_ref, boxes = refs[:low], refs[low], refs[low + 1]
    columns = out_ref.shape[0]
    leaves, rank, size = basis_ref.shape
    me = lax.axis_index("leaf")
    for p in range(low):
        tile = came[p][came_as.tile : came_as.box, :].astype(F32)
        for k in range(high):
            start = came_as.box + k * came_as.half
            packed = came[p][start : start + came_as.half, :]
            last = tile[leaves + k : leaves + k + 1, :rank]
            boxes[k * low + p] = jnp.concatenate(
                [packed[:, :rank].astype(F32), packed[:, rank:].astype(F32), last], axis=0
            ).astype(BF16)
    far = jnp.zeros((columns, rank), F32)
    for f in range(couplings_ref.shape[1]):
        source = jnp.bitwise_xor(partner_ref[0, f], me)
        far += dot_t(boxes[source], couplings_ref[0, f])
    far = far.astype(BF16)
    down = [dot(far, transfer_ref[j]).astype(BF16) for j in range(leaves)]
    for j in range(leaves):
        cols = slice(j * size, (j + 1) * size)
        out_ref[:, cols] = base_ref[:, cols] + dot(down[j], basis_ref[j])


def last_kernel(leaves, main, picks, base_ref, *refs):
    out_ref = refs[-1]
    came = [ref if at is None else ref.at[at] for ref, at in zip(refs, picks)]
    size = base_ref.shape[1] // leaves
    tile = leaves * main
    tails = sum(ref[tile : tile + TILE, :].astype(F32) for ref in came)
    for j in range(leaves):
        cols = slice(j * size, (j + 1) * size)
        rows = slice(j * main, (j + 1) * main)
        out_ref[:main, cols] = base_ref[:main, cols] + sum(ref[rows, :].astype(F32) for ref in came)
        out_ref[main:, cols] = base_ref[main:, cols] + tails[j : j + 1]


def call(kernel, out_shape, specs, operands, scratch, flops, room=None):
    outs = jax.tree.leaves(out_shape)
    nbytes = sum(a.size * a.dtype.itemsize for a in (*operands, *outs))
    limit = None if room is None else nbytes + room + 2**21
    return pl.pallas_call(
        kernel,
        out_shape=out_shape,
        in_specs=specs[0],
        out_specs=specs[1],
        scratch_shapes=scratch,
        compiler_params=pltpu.CompilerParams(vmem_limit_bytes=limit),
        cost_estimate=pl.CostEstimate(flops=flops, bytes_accessed=nbytes, transcendentals=0),
    )(*operands)


def per_device(
    probes, basis, transfer, local_blocks, remote_blocks, near_dest, near_leaf, couplings, far_list
):
    columns, points = probes.shape
    leaves, rank, size = basis.shape
    devices = lax.axis_size("leaf")
    main = columns // TILE * TILE
    plan = Plan(devices, main, leaves)
    high, low = plan.high, plan.low
    blocks = remote_blocks.shape[0] * remote_blocks.shape[1]
    unit = 2 * columns * size * size
    array = lambda rows, dtype=BF16: jax.ShapeDtypeStruct((*rows, size), dtype)
    like = lambda *arrays: [pltpu.VMEM(a.shape, a.dtype) for a in arrays]
    numbers = lambda *arrays: [pltpu.SMEM(a.shape, a.dtype) for a in arrays]
    sems = lambda count: [pltpu.SemaphoreType.DMA((count,))]
    relative = lambda x, way: lax.ppermute(x, "leaf", [(i, i ^ way) for i in range(devices)])

    dest, leaf = near_dest.T, near_leaf.T
    sizes = [plan.plane.depth] * low + [plan.near.depth] * FIRST_FAR + [main // 2 + TILE]
    sent = call(
        functools.partial(products_kernel, plan),
        [array((rows,)) for rows in sizes],
        ([ANY] * 6, [ANY] * len(sizes)),
        (dest, leaf, probes, basis, transfer, remote_blocks),
        numbers(dest, leaf)
        + like(probes, basis, transfer, remote_blocks)
        + like(array((sum(sizes[:-1]),)), array(sizes[-1:]))
        + [
            pltpu.VMEM((plan.parts, max(k.box - k.tile for k in (plan.plane, plan.near)), size), F32),
            pltpu.SMEM((devices,), I32),
        ]
        + sems(7 + len(sizes)),
        blocks * unit,
    )
    plane, near, box = list(sent[:low]), list(sent[low:-1]), sent[-1]
    for p in range(1, low):
        plane[p] = relative(plane[p], p)
    for k in range(1, FIRST_FAR):
        near[k] = relative(near[k], k * low)
    boxes = [relative(box, k * low) for k in plan.far]
    plane[0], near[0] = call(
        keep_kernel, (array(sizes[:1]), array(sizes[low : low + 1])), ([VMEM] * 2, (VMEM,) * 2), (plane[0], near[0]), [], 0, 0
    )

    def summed(kernel, kind, dense, outs, came, others):
        total = array((kind.fan, (leaves + 1) * main), F32)
        tails = array((kind.fan, max(TILE, dense.box - dense.tile)), F32)
        return call(
            functools.partial(kernel, plan),
            outs,
            ([VMEM] * (len(came) + len(others)), [VMEM] * len(outs)),
            (*came, *others),
            [pltpu.VMEM((len(came), size), I32), pltpu.SMEM((len(came), size), I32)]
            + like(total, tails)
            + [pltpu.SemaphoreType.DMA(())],
            len(came) * kind.slots * columns * size,
            4 * (total.size + tails.size),
        )

    plane[0], *boxes = lax.optimization_barrier((plane[0], *boxes))
    stack = lambda keys: array((len(keys), plan.along.depth))
    leaving, staying = split(plan.far, 1)
    going, kept = summed(far_sum_kernel, plan.plane, plan.along, [stack(leaving), stack(staying)], plane, [])
    near[0], kept = lax.optimization_barrier((near[0], kept))
    finals, bit = [], 1
    while True:
        came = relative(going, bit * low)
        arrived = [k ^ bit for k in leaving]
        finals += [(came, arrived.index(0))] if 0 in arrived else []
        bit *= 2
        if bit >= high:
            break
        leaving, staying_next = split(staying, bit)
        entry = lambda k: [(0, staying.index(k))] + ([(1, arrived.index(k))] if k in arrived else [])
        keys = [group for group in (leaving, staying_next) if group]
        going, *rest = call(
            functools.partial(fold_kernel, [[entry(k) for k in group] for group in keys]),
            [stack(group) for group in keys],
            ([VMEM] * 2, [VMEM] * len(keys)),
            (kept, came),
            [],
            going.size,
            0,
        )
        kept, staying = (rest[0] if rest else None), staying_next

    within = list(summed(near_sum_kernel, plan.near, plan.within, [array((plan.within.depth,))] * low, near, boxes))
    probes_then, within[0] = lax.optimization_barrier((probes, within[0]))
    for p in range(1, low):
        within[p] = relative(within[p], p)

    base_shape = jax.ShapeDtypeStruct((columns, points), F32)
    base = call(
        local_kernel, base_shape, ([VMEM] * 2, VMEM), (probes_then, local_blocks), [], leaves * leaves * unit, 0
    )
    every = jax.ShapeDtypeStruct((devices, columns, rank), BF16)
    base = call(
        functools.partial(far_kernel, plan),
        base_shape,
        ([SMEM] + [VMEM] * (4 + low), VMEM),
        (far_list, base, couplings, transfer, basis, *within),
        like(every),
        4 * leaves * unit,
        4 * every.size,
    )
    came = (*within, *(ref for ref, _ in finals))
    picks = [None] * low + [at for _, at in finals]
    return call(
        functools.partial(last_kernel, leaves, main, picks),
        base_shape,
        ([VMEM] * (1 + len(came)), VMEM),
        (base, *came),
        [],
        devices * columns * size,
        0,
    )


def solution(mesh):
    placed = (
        P(None, ("grp", "leaf")),
        P(("grp", "leaf"), None, None),
        P(("grp", "leaf"), None, None),
        P(("grp", "leaf"), None, None, None),
        P(("grp", "leaf"), None, None, None),
        P(("grp", "leaf"), None),
        P(("grp", "leaf"), None),
        P(("grp", "leaf"), None, None, None),
        P(("grp", "leaf"), None),
    )
    return jax.shard_map(
        per_device, mesh=mesh, in_specs=placed, out_specs=P(None, ("grp", "leaf")), check_vma=False
    )
```

```python
import functools

import jax
import jax.numpy as jnp
from jax import lax
from jax.experimental import pallas as pl
from jax.experimental.pallas import tpu as pltpu
from jax.sharding import PartitionSpec as P

CAP = 4
TILE = 16
HEAVY = 4 * 10**9

F32 = jnp.float32
BF16 = jnp.bfloat16
I32 = jnp.int32

ANY = pl.BlockSpec(memory_space=pl.ANY)
VMEM = pl.BlockSpec(memory_space=pltpu.VMEM)
SMEM = pl.BlockSpec(memory_space=pltpu.SMEM)


def dot_t(lhs, rhs):
    return lax.dot_general(lhs, rhs, (((1,), (1,)), ((), ())), preferred_element_type=F32)


def dot(lhs, rhs):
    return lax.dot_general(lhs, rhs, (((1,), (0,)), ((), ())), preferred_element_type=F32)


class Copies:
    def __init__(self, sems):
        self.sems, self.used = sems, 0

    def start(self, src, dst):
        copy = pltpu.make_async_copy(src, dst, self.sems.at[self.used])
        self.used += 1
        copy.start()
        return copy


def grid_of(devices):
    low = 1 << (devices.bit_length() // 2)
    return devices // low, low


def up(rows):
    return -(-rows // TILE) * TILE


class Route:
    def __init__(self, first, last, fan, extra, main, columns, leaves, sources):
        self.first, self.rows, self.fan, self.extra, self.main = first, last - first, fan, extra, main
        self.leaves, self.half = leaves, main // 2
        slots = fan * CAP
        self.tails = slots * self.rows
        self.meta = self.tails + (up(slots) if extra else 0)
        self.box = self.meta + TILE
        self.depth = self.box + (self.half if extra else 0)
        self.dense_tails = leaves * self.rows
        self.dense_box = self.dense_tails + (up(leaves + sources) if extra else 0)
        self.dense_depth = self.dense_box + (sources * self.half if extra else 0)


def routes_of(devices, main, columns, leaves):
    high, low = grid_of(devices)
    split = up(main * 3 // 4)
    return (
        Route(0, split, high, False, main, columns, leaves, low),
        Route(split, main, low, True, main, columns, leaves, high),
    )


def products_kernel(routes, devices, *refs):
    dest_hbm, leaf_hbm, probes_hbm, basis_hbm, transfer_hbm, blocks_hbm = refs[:6]
    outs = refs[6:-13]
    (
        dest_ref, leaf_ref, probes_ref, basis_ref, transfer_ref, blocks_ref,
        send_low, send_high, tails, meta_low, meta_high, count, sems,
    ) = refs[-13:]
    by_low, by_high = routes
    high, low = grid_of(devices)
    me = lax.axis_index("leaf")
    main = by_high.main
    leaves, per_leaf, size = blocks_ref.shape[:3]
    columns, rank = probes_ref.shape[0], basis_ref.shape[1]
    copies = Copies(sems)
    early = [
        copies.start(probes_hbm, probes_ref),
        copies.start(basis_hbm, basis_ref),
        copies.start(transfer_hbm, transfer_ref),
        copies.start(dest_hbm, dest_ref),
        copies.start(leaf_hbm, leaf_ref),
    ]
    chunk = leaves // 2
    arrivals = [
        copies.start(blocks_hbm.at[pl.ds(j, chunk)], blocks_ref.at[pl.ds(j, chunk)])
        for j in range(0, leaves, chunk)
    ]

    @pl.loop(0, devices)
    def _(i):
        count[i] = 0

    tails[...] = jnp.zeros(tails.shape, F32)
    meta_low[...] = jnp.full(meta_low.shape, leaves, F32)
    meta_high[...] = jnp.full(meta_high.shape, leaves, F32)
    for copy in early:
        copy.wait()
    box = jnp.zeros((columns, rank), F32)
    for j in range(leaves):
        coef = dot_t(probes_ref[:, j * size : (j + 1) * size], basis_ref[j]).astype(BF16)
        box += dot_t(coef, transfer_ref[j])
    half = by_high.half
    packed = jnp.concatenate([box[:half], box[half:main]], axis=1).astype(BF16)
    last = jnp.concatenate([box[main:], jnp.zeros_like(box[main:])], axis=1)

    lane = lax.broadcasted_iota(I32, (1, size), 1)
    for j in range(leaves):
        if j % chunk == 0:
            arrivals[j // chunk].wait()
        x = probes_ref[:, j * size : (j + 1) * size]
        for first in range(0, per_leaf, 4):
            many = min(4, per_leaf - first)
            rhs = blocks_ref[j, first : first + many].reshape(many * size, size)
            product = dot_t(x, rhs)
            for b in range(many):
                target = jnp.bitwise_xor(dest_ref[first + b, j], me)
                slot = count[target]
                count[target] = slot + 1
                to_high, to_low = target // low, target % low
                block = product[:, b * size : (b + 1) * size]
                piece = block[:main].astype(BF16)
                number = leaf_ref[first + b, j].astype(F32)

                at = to_high * CAP + slot
                rows = pl.ds(pl.multiple_of(at * by_low.rows, TILE), by_low.rows)
                send_low[to_low, rows, :] = piece[: by_low.rows]
                meta_low[to_low, 0:1, :] = jnp.where(lane == at, number, meta_low[to_low, 0:1, :])

                at = to_low * CAP + slot
                rows = pl.ds(pl.multiple_of(at * by_high.rows, TILE), by_high.rows)
                send_high[to_high, rows, :] = piece[by_low.rows :]
                tails[to_high, pl.ds(at, 1), :] = block[main:]
                meta_high[to_high, 0:1, :] = jnp.where(lane == at, number, meta_high[to_high, 0:1, :])

    for i in range(low):
        send_low[i, by_low.meta : by_low.box, :] = meta_low[i].astype(BF16)
    for i in range(high):
        meta_high[i, 1:2, :] = last
        send_high[i, by_high.tails : by_high.meta, :] = tails[i].astype(BF16)
        send_high[i, by_high.meta : by_high.box, :] = meta_high[i].astype(BF16)
        send_high[i, by_high.box :, :] = packed
    leaving = [copies.start(send_low.at[i], outs[i]) for i in range(low)]
    leaving += [copies.start(send_high.at[i], outs[low + i]) for i in range(high)]
    for copy in leaving:
        copy.wait()


def split(keys, bit):
    return [k for k in keys if k & bit], [k for k in keys if not k & bit]


def sum_kernel(route, ways, places, *refs):
    came, given = refs[:ways], refs[ways:-5]
    meta, leaf_ref, total, tails, late = refs[-5:]
    outs = [given[n] if at is None else given[n].at[at] for n, at in places]
    leaves, half = route.leaves, route.half
    lasts = []
    for i in range(ways):
        tile = came[i][route.meta : route.box, :].astype(F32)
        meta[i : i + 1, :] = tile[:1].astype(I32)
        lasts.append(tile[1:2])
    numbers = pltpu.make_async_copy(meta, leaf_ref, late)
    numbers.start()
    total[...] = jnp.zeros(total.shape, F32)
    tails[...] = jnp.zeros(tails.shape, F32)
    numbers.wait()
    for i in range(ways):
        if route.extra:
            tail = came[i][route.tails : route.meta, :].astype(F32)
        for k in range(route.fan):
            for slot in range(CAP):
                at = k * CAP + slot
                leaf = leaf_ref[i, at]
                rows = pl.ds(pl.multiple_of(leaf * route.rows, TILE), route.rows)
                total[k, rows, :] += came[i][at * route.rows : (at + 1) * route.rows, :].astype(F32)
                if route.extra:
                    tails[k, pl.ds(leaf, 1), :] += tail[at : at + 1]

    for k in range(route.fan):
        outs[k][: route.dense_tails, :] = total[k, : route.dense_tails, :].astype(BF16)
        if route.extra:
            for i in range(ways):
                tails[k, leaves + i : leaves + i + 1, :] = lasts[i]
                start = route.dense_box + i * half
                outs[k][start : start + half, :] = came[i][route.box :, :]
            outs[k][route.dense_tails : route.dense_box, :] = tails[k].astype(BF16)


def fold_kernel(terms, *refs):
    inputs, outs = refs[: -len(terms)], refs[-len(terms) :]
    for out, entries in zip(outs, terms):
        for i, entry in enumerate(entries):
            out[i] = sum(inputs[n][at].astype(F32) for n, at in entry).astype(BF16)


def keep_kernel(own_low, own_high, kept_low, kept_high):
    kept_low[...] = own_low[...]
    kept_high[...] = own_high[...]


def local_kernel(probes_ref, local_ref, out_ref):
    leaves, size = local_ref.shape[0], local_ref.shape[2]
    for i in range(leaves):
        total = dot_t(probes_ref[:, :size], local_ref[i, 0])
        for c in range(1, leaves):
            total += dot_t(probes_ref[:, c * size : (c + 1) * size], local_ref[i, c])
        out_ref[:, i * size : (i + 1) * size] = total


def far_kernel(by_high, low, partner_ref, base_ref, couplings_ref, transfer_ref, basis_ref, *refs):
    came, out_ref, boxes = refs[:low], refs[low], refs[low + 1]
    columns = out_ref.shape[0]
    leaves, rank, size = basis_ref.shape
    high = boxes.shape[0] // low
    me = lax.axis_index("leaf")
    for k in range(low):
        tile = came[k][by_high.dense_tails : by_high.dense_box, :].astype(F32)
        for i in range(high):
            start = by_high.dense_box + i * by_high.half
            packed = came[k][start : start + by_high.half, :]
            last = tile[leaves + i : leaves + i + 1, :rank]
            boxes[i * low + k] = jnp.concatenate(
                [packed[:, :rank].astype(F32), packed[:, rank:].astype(F32), last], axis=0
            ).astype(BF16)
    far = jnp.zeros((columns, rank), F32)
    for f in range(couplings_ref.shape[1]):
        source = jnp.bitwise_xor(partner_ref[0, f], me)
        far += dot_t(boxes[source], couplings_ref[0, f])
    far = far.astype(BF16)
    down = [dot(far, transfer_ref[j]).astype(BF16) for j in range(leaves)]
    for j in range(leaves):
        cols = slice(j * size, (j + 1) * size)
        out_ref[:, cols] = base_ref[:, cols] + dot(down[j], basis_ref[j])


def last_kernel(routes, devices, picks, base_ref, *refs):
    by_low, by_high = routes
    low = grid_of(devices)[1]
    came_low, out_ref = refs[:low], refs[-1]
    came_high = [refs[low + n].at[at] for n, at in enumerate(picks)]
    leaves, split, main = by_low.leaves, by_low.rows, by_low.main
    size = base_ref.shape[1] // leaves
    tails = sum(came_low[k][by_high.dense_tails : by_high.dense_box, :].astype(F32) for k in range(low))
    for j in range(leaves):
        cols = slice(j * size, (j + 1) * size)
        upper = sum(ref[j * by_low.rows : (j + 1) * by_low.rows, :].astype(F32) for ref in came_high)
        lower = sum(came_low[k][j * by_high.rows : (j + 1) * by_high.rows, :].astype(F32) for k in range(low))
        out_ref[:split, cols] = base_ref[:split, cols] + upper
        out_ref[split:main, cols] = base_ref[split:main, cols] + lower
        out_ref[main:, cols] = base_ref[main:, cols] + tails[j : j + 1]


def call(kernel, out_shape, specs, operands, scratch, flops, room=None):
    outs = jax.tree.leaves(out_shape)
    nbytes = sum(a.size * a.dtype.itemsize for a in (*operands, *outs))
    limit = None if room is None else nbytes + room + 2**21
    return pl.pallas_call(
        kernel,
        out_shape=out_shape,
        in_specs=specs[0],
        out_specs=specs[1],
        scratch_shapes=scratch,
        compiler_params=pltpu.CompilerParams(vmem_limit_bytes=limit),
        cost_estimate=pl.CostEstimate(flops=flops, bytes_accessed=nbytes, transcendentals=0),
    )(*operands)


def per_device(
    probes, basis, transfer, local_blocks, remote_blocks, near_dest, near_leaf, couplings, far_list
):
    columns, points = probes.shape
    leaves, rank, size = basis.shape
    devices = lax.axis_size("leaf")
    main = columns // TILE * TILE
    routes = by_low, by_high = routes_of(devices, main, columns, leaves)
    high, low = grid_of(devices)
    blocks = remote_blocks.shape[0] * remote_blocks.shape[1]
    unit = 2 * columns * size * size
    like = lambda *arrays: [pltpu.VMEM(a.shape, a.dtype) for a in arrays]
    numbers = lambda *arrays: [pltpu.SMEM(a.shape, a.dtype) for a in arrays]
    sems = lambda count: [pltpu.SemaphoreType.DMA((count,))]
    relative = lambda x, way: lax.ppermute(x, "leaf", [(i, i ^ way) for i in range(devices)])
    message = lambda route: jax.ShapeDtypeStruct((route.depth, size), BF16)
    dense = lambda route: jax.ShapeDtypeStruct((route.dense_depth, size), BF16)

    def stacked(count, like_this):
        return pltpu.VMEM((count, *like_this.shape), like_this.dtype)

    def summed(route, ways, came, outs, places):
        total = jax.ShapeDtypeStruct((route.fan, (leaves + 1) * route.rows, size), F32)
        tails = jax.ShapeDtypeStruct((route.fan, max(TILE, route.dense_box - route.dense_tails), size), F32)
        return call(
            functools.partial(sum_kernel, route, ways, places),
            outs,
            ([VMEM] * ways, [VMEM] * len(outs)),
            came,
            [pltpu.VMEM((ways, size), I32), pltpu.SMEM((ways, size), I32)]
            + like(total, tails)
            + [pltpu.SemaphoreType.DMA(())],
            HEAVY,
            4 * (total.size + tails.size),
        )

    dest, leaf = near_dest.T, near_leaf.T
    sent = call(
        functools.partial(products_kernel, routes, devices),
        [message(by_low)] * low + [message(by_high)] * high,
        ([ANY] * 6, [ANY] * (low + high)),
        (dest, leaf, probes, basis, transfer, remote_blocks),
        numbers(dest, leaf)
        + like(probes, basis, transfer, remote_blocks)
        + [
            stacked(low, message(by_low)),
            stacked(high, message(by_high)),
            pltpu.VMEM((high, by_high.meta - by_high.tails, size), F32),
            pltpu.VMEM((low, TILE, size), F32),
            pltpu.VMEM((high, TILE, size), F32),
            pltpu.SMEM((devices,), I32),
        ]
        + sems(7 + low + high),
        blocks * unit,
    )
    came_low, came_high = list(sent[:low]), list(sent[low:])
    came_low[1] = relative(came_low[1], 1)
    for k in range(high - 1, 1, -1):
        came_high[k] = relative(came_high[k], k * low)
    for k in range(low - 1, 1, -1):
        came_low[k] = relative(came_low[k], k)
    came_high[1] = relative(came_high[1], low)

    base_shape = jax.ShapeDtypeStruct((columns, points), F32)
    came_low[0], came_high[0] = call(
        keep_kernel,
        (message(by_low), message(by_high)),
        ([VMEM] * 2, (VMEM,) * 2),
        (came_low[0], came_high[0]),
        [],
        0,
        0,
    )

    stack = lambda keys: jax.ShapeDtypeStruct((len(keys), by_low.dense_depth, size), BF16)
    leaving, staying = split(range(high), 1)
    places = [(0, leaving.index(k)) if k in leaving else (1, staying.index(k)) for k in range(high)]
    going, kept = summed(by_low, low, came_low, [stack(leaving), stack(staying)], places)
    came_high[0], kept = lax.optimization_barrier((came_high[0], kept))
    finals, bit = [(kept, staying.index(0))], 1
    while True:
        came = relative(going, bit * low)
        arrived = [k ^ bit for k in leaving]
        finals += [(came, arrived.index(0))]
        bit *= 2
        if bit >= high:
            break
        leaving, staying_next = split([k for k in staying if k], bit)
        entry = lambda k: [(0, staying.index(k)), (1, arrived.index(k))]
        groups = [group for group in (leaving, staying_next) if group]
        outs = [stack(group) for group in groups]
        going, *rest = call(
            functools.partial(fold_kernel, [[entry(k) for k in group] for group in groups]),
            outs,
            ([VMEM] * 2, [VMEM] * len(outs)),
            (kept, came),
            [],
            going.size,
            0,
        )
        kept, staying = (rest[0] if rest else None), staying_next

    to_low = list(
        summed(by_high, high, came_high, [dense(by_high)] * low, [(p, None) for p in range(low)])
    )
    probes_then, to_low[0] = lax.optimization_barrier((probes, to_low[0]))
    for k in range(1, low):
        to_low[k] = relative(to_low[k], k)
    base = call(
        local_kernel, base_shape, ([VMEM] * 2, VMEM), (probes_then, local_blocks), [], leaves * leaves * unit, 0
    )

    boxes = jax.ShapeDtypeStruct((devices, columns, rank), BF16)
    base = call(
        functools.partial(far_kernel, by_high, low),
        base_shape,
        ([SMEM] + [VMEM] * (4 + low), VMEM),
        (far_list, base, couplings, transfer, basis, *to_low),
        like(boxes),
        HEAVY,
        4 * boxes.size,
    )
    return call(
        functools.partial(last_kernel, routes, devices, [at for _, at in finals]),
        base_shape,
        ([VMEM] * (1 + low + len(finals)), VMEM),
        (base, *to_low, *(ref for ref, _ in finals)),
        [],
        devices * columns * size,
        0,
    )


def solution(mesh):
    placed = (
        P(None, ("grp", "leaf")),
        P(("grp", "leaf"), None, None),
        P(("grp", "leaf"), None, None),
        P(("grp", "leaf"), None, None, None),
        P(("grp", "leaf"), None, None, None),
        P(("grp", "leaf"), None),
        P(("grp", "leaf"), None),
        P(("grp", "leaf"), None, None, None),
        P(("grp", "leaf"), None),
    )
    return jax.shard_map(
        per_device, mesh=mesh, in_specs=placed, out_specs=P(None, ("grp", "leaf")), check_vma=False
    )
```

```python
import functools

import jax
import jax.numpy as jnp
from jax import lax
from jax.experimental import pallas as pl
from jax.experimental.pallas import tpu as pltpu
from jax.sharding import PartitionSpec as P

CAP = 4
TILE = 16
F32 = jnp.float32
BF16 = jnp.bfloat16
I32 = jnp.int32

ANY = pl.BlockSpec(memory_space=pl.ANY)
VMEM = pl.BlockSpec(memory_space=pltpu.VMEM)
SMEM = pl.BlockSpec(memory_space=pltpu.SMEM)


def dot_t(lhs, rhs):
    return lax.dot_general(lhs, rhs, (((1,), (1,)), ((), ())), preferred_element_type=F32)


def dot(lhs, rhs):
    return lax.dot_general(lhs, rhs, (((1,), (0,)), ((), ())), preferred_element_type=F32)


class Copies:
    def __init__(self, sems):
        self.sems, self.used = sems, 0

    def start(self, src, dst):
        copy = pltpu.make_async_copy(src, dst, self.sems.at[self.used])
        self.used += 1
        copy.start()
        return copy


def grid_of(devices):
    low = 1 << (devices.bit_length() // 2)
    return devices // low, low


def up(rows):
    return -(-rows // TILE) * TILE


class Route:
    def __init__(self, first, last, fan, extra, main, columns, leaves, sources):
        self.first, self.rows, self.fan, self.extra, self.main = first, last - first, fan, extra, main
        self.leaves, self.half = leaves, main // 2
        slots = fan * CAP
        self.tails = slots * self.rows
        self.meta = self.tails + (up(slots) if extra else 0)
        self.box = self.meta + TILE
        self.depth = self.box + (self.half if extra else 0)
        self.dense_tails = leaves * self.rows
        self.dense_box = self.dense_tails + (up(leaves + sources) if extra else 0)
        self.dense_depth = self.dense_box + (sources * self.half if extra else 0)


def routes_of(devices, main, columns, leaves):
    high, low = grid_of(devices)
    split = up(main * 3 // 4)
    return (
        Route(0, split, high, False, main, columns, leaves, low),
        Route(split, main, low, True, main, columns, leaves, high),
    )


def products_kernel(routes, devices, *refs):
    dest_hbm, leaf_hbm, probes_hbm, basis_hbm, transfer_hbm, blocks_hbm = refs[:6]
    outs = refs[6:-11]
    (
        dest_ref, leaf_ref, probes_ref, basis_ref, transfer_ref, blocks_ref,
        send_low, send_high, tails, count, sems,
    ) = refs[-11:]
    by_low, by_high = routes
    high, low = grid_of(devices)
    me = lax.axis_index("leaf")
    main = by_high.main
    leaves, per_leaf, size = blocks_ref.shape[:3]
    columns, rank = probes_ref.shape[0], basis_ref.shape[1]
    copies = Copies(sems)
    early = [
        copies.start(probes_hbm, probes_ref),
        copies.start(basis_hbm, basis_ref),
        copies.start(transfer_hbm, transfer_ref),
        copies.start(dest_hbm, dest_ref),
        copies.start(leaf_hbm, leaf_ref),
    ]
    chunk = leaves // 2
    arrivals = [
        copies.start(blocks_hbm.at[pl.ds(j, chunk)], blocks_ref.at[pl.ds(j, chunk)])
        for j in range(0, leaves, chunk)
    ]

    @pl.loop(0, devices)
    def _(i):
        count[i] = 0

    tails[...] = jnp.zeros(tails.shape, F32)
    for copy in early:
        copy.wait()
    box = jnp.zeros((columns, rank), F32)
    for j in range(leaves):
        coef = dot_t(probes_ref[:, j * size : (j + 1) * size], basis_ref[j]).astype(BF16)
        box += dot_t(coef, transfer_ref[j])
    half = by_high.half
    packed = jnp.concatenate([box[:half], box[half:main]], axis=1).astype(BF16)
    last = jnp.concatenate([box[main:], jnp.zeros_like(box[main:])], axis=1)

    numbers = jnp.full((-(-(low + high) // 8) * 8, size), leaves, I32)
    row = lax.broadcasted_iota(I32, numbers.shape, 0)
    lane = lax.broadcasted_iota(I32, numbers.shape, 1)
    for j in range(leaves):
        if j % chunk == 0:
            arrivals[j // chunk].wait()
        x = probes_ref[:, j * size : (j + 1) * size]
        for first in range(0, per_leaf, 4):
            many = min(4, per_leaf - first)
            rhs = blocks_ref[j, first : first + many].reshape(many * size, size)
            product = dot_t(x, rhs)
            for b in range(many):
                target = jnp.bitwise_xor(dest_ref[first + b, j], me)
                slot = count[target]
                count[target] = slot + 1
                to_high = lax.shift_right_logical(target, low.bit_length() - 1)
                to_low = jnp.bitwise_and(target, low - 1)
                block = product[:, b * size : (b + 1) * size]
                piece = block[:main].astype(BF16)
                number = leaf_ref[first + b, j]

                at = to_high * CAP + slot
                rows = pl.ds(pl.multiple_of(at * by_low.rows, TILE), by_low.rows)
                send_low[to_low, rows, :] = piece[: by_low.rows]
                numbers = jnp.where((row == to_low) & (lane == at), number, numbers)

                at = to_low * CAP + slot
                rows = pl.ds(pl.multiple_of(at * by_high.rows, TILE), by_high.rows)
                send_high[to_high, rows, :] = piece[by_low.rows :]
                tails[to_high, pl.ds(at, 1), :] = block[main:]
                numbers = jnp.where((row == low + to_high) & (lane == at), number, numbers)

    numbers = numbers.astype(F32)
    blank = jnp.zeros((TILE - 2, size), F32)
    for i in range(low):
        tile = jnp.concatenate([numbers[i : i + 1], last, blank], axis=0)
        send_low[i, by_low.meta : by_low.box, :] = tile.astype(BF16)
    for i in range(high):
        tile = jnp.concatenate([numbers[low + i : low + i + 1], last, blank], axis=0)
        send_high[i, by_high.tails : by_high.meta, :] = tails[i].astype(BF16)
        send_high[i, by_high.meta : by_high.box, :] = tile.astype(BF16)
        send_high[i, by_high.box :, :] = packed
    leaving = [copies.start(send_low.at[i], outs[i]) for i in range(low)]
    leaving += [copies.start(send_high.at[i], outs[low + i]) for i in range(high)]
    for copy in leaving:
        copy.wait()


def sum_route(route, came, outs, base, leaf_ref, total, tails):
    leaves, half, ways = route.leaves, route.half, len(came)
    for i in range(ways):
        if route.extra:
            tail = came[i][route.tails : route.meta, :].astype(F32)
        for k in range(route.fan):
            for slot in range(CAP):
                at = k * CAP + slot
                leaf = leaf_ref[base + i, at]
                rows = pl.ds(pl.multiple_of(leaf * route.rows, TILE), route.rows)
                total[k, rows, :] += came[i][at * route.rows : (at + 1) * route.rows, :].astype(F32)
                if route.extra:
                    tails[k, pl.ds(leaf, 1), :] += tail[at : at + 1]

    for k in range(route.fan):
        outs[k][: route.dense_tails, :] = total[k, : route.dense_tails, :].astype(BF16)
        if route.extra:
            for i in range(ways):
                last = came[i][route.meta : route.box, :].astype(F32)[1:2]
                tails[k, leaves + i : leaves + i + 1, :] = last
                start = route.dense_box + i * half
                outs[k][start : start + half, :] = came[i][route.box :, :]
            outs[k][route.dense_tails : route.dense_box, :] = tails[k].astype(BF16)


def sum_kernel(routes, devices, *refs):
    by_low, by_high = routes
    high, low = grid_of(devices)
    ways = low + high
    came, outs, scratch = refs[:ways], refs[ways : 2 * ways], refs[2 * ways :]
    meta, leaf_ref, total_low, total_high, tails, late = scratch
    for i, route in enumerate([by_low] * low + [by_high] * high):
        meta[i : i + 1, :] = came[i][route.meta : route.box, :].astype(F32)[:1].astype(I32)
    numbers = pltpu.make_async_copy(meta, leaf_ref, late)
    numbers.start()
    for ref in (total_low, total_high, tails):
        ref[...] = jnp.zeros(ref.shape, F32)
    numbers.wait()
    sum_route(by_low, came[:low], outs[:high], 0, leaf_ref, total_low, None)
    sum_route(by_high, came[low:], outs[high:], low, leaf_ref, total_high, tails)


def keep_kernel(*refs):
    half = len(refs) // 2
    for came, kept in zip(refs[:half], refs[half:]):
        kept[...] = came[...]


def local_kernel(probes_ref, local_ref, out_ref):
    leaves, size = local_ref.shape[0], local_ref.shape[2]
    for i in range(leaves):
        total = dot_t(probes_ref[:, :size], local_ref[i, 0])
        for c in range(1, leaves):
            total += dot_t(probes_ref[:, c * size : (c + 1) * size], local_ref[i, c])
        out_ref[:, i * size : (i + 1) * size] = total


def far_kernel(by_high, low, partner_ref, base_ref, couplings_ref, transfer_ref, basis_ref, *refs):
    came, out_ref, boxes = refs[:low], refs[low], refs[low + 1]
    columns = out_ref.shape[0]
    leaves, rank, size = basis_ref.shape
    high = boxes.shape[0] // low
    me = lax.axis_index("leaf")
    for k in range(low):
        tile = came[k][by_high.dense_tails : by_high.dense_box, :].astype(F32)
        for i in range(high):
            start = by_high.dense_box + i * by_high.half
            packed = came[k][start : start + by_high.half, :]
            last = tile[leaves + i : leaves + i + 1, :rank]
            boxes[i * low + k] = jnp.concatenate(
                [packed[:, :rank].astype(F32), packed[:, rank:].astype(F32), last], axis=0
            ).astype(BF16)
    far = jnp.zeros((columns, rank), F32)
    for f in range(couplings_ref.shape[1]):
        source = jnp.bitwise_xor(partner_ref[0, f], me)
        far += dot_t(boxes[source], couplings_ref[0, f])
    far = far.astype(BF16)
    down = [dot(far, transfer_ref[j]).astype(BF16) for j in range(leaves)]
    for j in range(leaves):
        cols = slice(j * size, (j + 1) * size)
        out_ref[:, cols] = base_ref[:, cols] + dot(down[j], basis_ref[j])


def last_kernel(routes, devices, base_ref, *refs):
    by_low, by_high = routes
    high, low = grid_of(devices)
    came_high, came_low, out_ref = refs[:high], refs[high : high + low], refs[high + low]
    leaves, split, main = by_low.leaves, by_low.rows, by_low.main
    size = base_ref.shape[1] // leaves
    tails = sum(came_low[k][by_high.dense_tails : by_high.dense_box, :].astype(F32) for k in range(low))
    for j in range(leaves):
        cols = slice(j * size, (j + 1) * size)
        upper = sum(came_high[k][j * by_low.rows : (j + 1) * by_low.rows, :].astype(F32) for k in range(high))
        lower = sum(came_low[k][j * by_high.rows : (j + 1) * by_high.rows, :].astype(F32) for k in range(low))
        out_ref[:split, cols] = base_ref[:split, cols] + upper
        out_ref[split:main, cols] = base_ref[split:main, cols] + lower
        out_ref[main:, cols] = base_ref[main:, cols] + tails[j : j + 1]


def call(kernel, out_shape, specs, operands, scratch, flops, room=None):
    outs = jax.tree.leaves(out_shape)
    nbytes = sum(a.size * a.dtype.itemsize for a in (*operands, *outs))
    limit = None if room is None else nbytes + room + 2**21
    return pl.pallas_call(
        kernel,
        out_shape=out_shape,
        in_specs=specs[0],
        out_specs=specs[1],
        scratch_shapes=scratch,
        compiler_params=pltpu.CompilerParams(vmem_limit_bytes=limit),
        cost_estimate=pl.CostEstimate(flops=flops, bytes_accessed=nbytes, transcendentals=0),
    )(*operands)


def per_device(
    probes, basis, transfer, local_blocks, remote_blocks, near_dest, near_leaf, couplings, far_list
):
    columns, points = probes.shape
    leaves, rank, size = basis.shape
    devices = lax.axis_size("leaf")
    main = columns // TILE * TILE
    routes = by_low, by_high = routes_of(devices, main, columns, leaves)
    high, low = grid_of(devices)
    blocks = remote_blocks.shape[0] * remote_blocks.shape[1]
    unit = 2 * columns * size * size
    like = lambda *arrays: [pltpu.VMEM(a.shape, a.dtype) for a in arrays]
    numbers = lambda *arrays: [pltpu.SMEM(a.shape, a.dtype) for a in arrays]
    sems = lambda count: [pltpu.SemaphoreType.DMA((count,))]
    relative = lambda x, way: lax.ppermute(x, "leaf", [(i, i ^ way) for i in range(devices)])
    message = lambda route: jax.ShapeDtypeStruct((route.depth, size), BF16)
    dense = lambda route: jax.ShapeDtypeStruct((route.dense_depth, size), BF16)

    def stacked(count, like_this):
        return pltpu.VMEM((count, *like_this.shape), like_this.dtype)

    dest, leaf = near_dest.T, near_leaf.T
    sent = call(
        functools.partial(products_kernel, routes, devices),
        [message(by_low)] * low + [message(by_high)] * high,
        ([ANY] * 6, [ANY] * (low + high)),
        (dest, leaf, probes, basis, transfer, remote_blocks),
        numbers(dest, leaf)
        + like(probes, basis, transfer, remote_blocks)
        + [
            stacked(low, message(by_low)),
            stacked(high, message(by_high)),
            pltpu.VMEM((high, by_high.meta - by_high.tails, size), F32),
            pltpu.SMEM((devices,), I32),
        ]
        + sems(7 + low + high),
        blocks * unit,
    )
    came_low, came_high = list(sent[:low]), list(sent[low:])
    for k in range(low - 1, 0, -1):
        came_low[k] = relative(came_low[k], k)
    for k in range(high - 1, 0, -1):
        came_high[k] = relative(came_high[k], k * low)
    came_low[0], came_low[1], came_high[0] = call(
        keep_kernel,
        (message(by_low), message(by_low), message(by_high)),
        ([VMEM] * 3, (VMEM,) * 3),
        (came_low[0], came_low[1], came_high[0]),
        [],
        0,
        0,
    )

    total = lambda route: jax.ShapeDtypeStruct((route.fan, (leaves + 1) * route.rows, size), F32)
    tails = jax.ShapeDtypeStruct((low, by_high.dense_box - by_high.dense_tails, size), F32)
    sums = call(
        functools.partial(sum_kernel, routes, devices),
        [dense(by_low)] * high + [dense(by_high)] * low,
        ([VMEM] * (low + high), [VMEM] * (low + high)),
        (*came_low, *came_high),
        [pltpu.VMEM((low + high, size), I32), pltpu.SMEM((low + high, size), I32)]
        + like(total(by_low), total(by_high), tails)
        + [pltpu.SemaphoreType.DMA(())],
        devices * CAP * columns * size,
        4 * (total(by_low).size + total(by_high).size + tails.size),
    )
    to_high, to_low = list(sums[:high]), list(sums[high:])
    probes_then, to_low[0] = lax.optimization_barrier((probes, to_low[0]))
    for k in range(max(low, high) - 1, 0, -1):
        if k < high:
            to_high[k] = relative(to_high[k], k * low)
        if k < low:
            to_low[k] = relative(to_low[k], k)

    base_shape = jax.ShapeDtypeStruct((columns, points), F32)
    base = call(
        local_kernel, base_shape, ([VMEM] * 2, VMEM), (probes_then, local_blocks), [], leaves * leaves * unit, 0
    )
    boxes = jax.ShapeDtypeStruct((devices, columns, rank), BF16)
    base = call(
        functools.partial(far_kernel, by_high, low),
        base_shape,
        ([SMEM] + [VMEM] * (4 + low), VMEM),
        (far_list, base, couplings, transfer, basis, *to_low),
        like(boxes),
        4 * leaves * unit,
        4 * boxes.size,
    )
    return call(
        functools.partial(last_kernel, routes, devices),
        base_shape,
        ([VMEM] * (1 + high + low), VMEM),
        (base, *to_high, *to_low),
        [],
        devices * columns * size,
        0,
    )


def solution(mesh):
    placed = (
        P(None, ("grp", "leaf")),
        P(("grp", "leaf"), None, None),
        P(("grp", "leaf"), None, None),
        P(("grp", "leaf"), None, None, None),
        P(("grp", "leaf"), None, None, None),
        P(("grp", "leaf"), None),
        P(("grp", "leaf"), None),
        P(("grp", "leaf"), None, None, None),
        P(("grp", "leaf"), None),
    )
    return jax.shard_map(
        per_device, mesh=mesh, in_specs=placed, out_specs=P(None, ("grp", "leaf")), check_vma=False
    )
```

```python
import functools

import jax
import jax.numpy as jnp
from jax import lax
from jax.experimental import pallas as pl
from jax.experimental.pallas import tpu as pltpu
from jax.sharding import PartitionSpec as P

CAP = 4
TILE = 16
F32 = jnp.float32
BF16 = jnp.bfloat16
I32 = jnp.int32

ANY = pl.BlockSpec(memory_space=pl.ANY)
VMEM = pl.BlockSpec(memory_space=pltpu.VMEM)
SMEM = pl.BlockSpec(memory_space=pltpu.SMEM)


def dot_t(lhs, rhs):
    return lax.dot_general(lhs, rhs, (((1,), (1,)), ((), ())), preferred_element_type=F32)


def dot(lhs, rhs):
    return lax.dot_general(lhs, rhs, (((1,), (0,)), ((), ())), preferred_element_type=F32)


class Copies:
    def __init__(self, sems):
        self.sems, self.used = sems, 0

    def start(self, src, dst):
        copy = pltpu.make_async_copy(src, dst, self.sems.at[self.used])
        self.used += 1
        copy.start()
        return copy


def grid_of(devices):
    low = 1 << (devices.bit_length() // 2)
    return devices // low, low


def up(rows):
    return -(-rows // TILE) * TILE


class Route:
    def __init__(self, first, last, fan, extra, main, columns, leaves, sources):
        self.first, self.rows, self.fan, self.extra, self.main = first, last - first, fan, extra, main
        self.leaves, self.half = leaves, main // 2
        slots = fan * CAP
        self.tails = slots * self.rows
        self.meta = self.tails + (up(slots) if extra else 0)
        self.box = self.meta + TILE
        self.depth = self.box + (self.half if extra else 0)
        self.dense_tails = leaves * self.rows
        self.dense_box = self.dense_tails + (up(leaves + sources) if extra else 0)
        self.dense_depth = self.dense_box + (sources * self.half if extra else 0)


def routes_of(devices, main, columns, leaves):
    high, low = grid_of(devices)
    split = up(main * 3 // 4)
    return (
        Route(0, split, high, False, main, columns, leaves, low),
        Route(split, main, low, True, main, columns, leaves, high),
    )


def products_kernel(routes, devices, *refs):
    dest_hbm, leaf_hbm, probes_hbm, basis_hbm, transfer_hbm, blocks_hbm = refs[:6]
    outs = refs[6:-11]
    (
        dest_ref, leaf_ref, probes_ref, basis_ref, transfer_ref, blocks_ref,
        send_low, send_high, tails, count, sems,
    ) = refs[-11:]
    by_low, by_high = routes
    high, low = grid_of(devices)
    me = lax.axis_index("leaf")
    main = by_high.main
    leaves, per_leaf, size = blocks_ref.shape[:3]
    columns, rank = probes_ref.shape[0], basis_ref.shape[1]
    copies = Copies(sems)
    early = [
        copies.start(probes_hbm, probes_ref),
        copies.start(basis_hbm, basis_ref),
        copies.start(transfer_hbm, transfer_ref),
        copies.start(dest_hbm, dest_ref),
        copies.start(leaf_hbm, leaf_ref),
    ]
    chunk = leaves // 2
    arrivals = [
        copies.start(blocks_hbm.at[pl.ds(j, chunk)], blocks_ref.at[pl.ds(j, chunk)])
        for j in range(0, leaves, chunk)
    ]

    @pl.loop(0, devices)
    def _(i):
        count[i] = 0

    tails[...] = jnp.zeros(tails.shape, F32)
    for copy in early:
        copy.wait()
    box = jnp.zeros((columns, rank), F32)
    for j in range(leaves):
        coef = dot_t(probes_ref[:, j * size : (j + 1) * size], basis_ref[j]).astype(BF16)
        box += dot_t(coef, transfer_ref[j])
    half = by_high.half
    packed = jnp.concatenate([box[:half], box[half:main]], axis=1).astype(BF16)
    last = jnp.concatenate([box[main:], jnp.zeros_like(box[main:])], axis=1)

    numbers = jnp.full((-(-(low + high) // 8) * 8, size), leaves, I32)
    row = lax.broadcasted_iota(I32, numbers.shape, 0)
    lane = lax.broadcasted_iota(I32, numbers.shape, 1)
    for j in range(leaves):
        if j % chunk == 0:
            arrivals[j // chunk].wait()
        x = probes_ref[:, j * size : (j + 1) * size]
        for first in range(0, per_leaf, 4):
            many = min(4, per_leaf - first)
            rhs = blocks_ref[j, first : first + many].reshape(many * size, size)
            product = dot_t(x, rhs)
            for b in range(many):
                target = jnp.bitwise_xor(dest_ref[first + b, j], me)
                slot = count[target]
                count[target] = slot + 1
                to_high = lax.shift_right_logical(target, low.bit_length() - 1)
                to_low = jnp.bitwise_and(target, low - 1)
                block = product[:, b * size : (b + 1) * size]
                piece = block[:main].astype(BF16)
                number = leaf_ref[first + b, j]

                at = to_high * CAP + slot
                rows = pl.ds(pl.multiple_of(at * by_low.rows, TILE), by_low.rows)
                send_low[to_low, rows, :] = piece[: by_low.rows]
                numbers = jnp.where((row == to_low) & (lane == at), number, numbers)

                at = to_low * CAP + slot
                rows = pl.ds(pl.multiple_of(at * by_high.rows, TILE), by_high.rows)
                send_high[to_high, rows, :] = piece[by_low.rows :]
                tails[to_high, pl.ds(at, 1), :] = block[main:]
                numbers = jnp.where((row == low + to_high) & (lane == at), number, numbers)

    numbers = numbers.astype(F32)
    blank = jnp.zeros((TILE - 2, size), F32)
    for i in range(low):
        tile = jnp.concatenate([numbers[i : i + 1], last, blank], axis=0)
        send_low[i, by_low.meta : by_low.box, :] = tile.astype(BF16)
    for i in range(high):
        tile = jnp.concatenate([numbers[low + i : low + i + 1], last, blank], axis=0)
        send_high[i, by_high.tails : by_high.meta, :] = tails[i].astype(BF16)
        send_high[i, by_high.meta : by_high.box, :] = tile.astype(BF16)
        send_high[i, by_high.box :, :] = packed
    leaving = [copies.start(send_low.at[i], outs[i]) for i in range(low)]
    leaving += [copies.start(send_high.at[i], outs[low + i]) for i in range(high)]
    for copy in leaving:
        copy.wait()


def sum_route(route, came, outs, base, leaf_ref, total, tails):
    leaves, half, ways = route.leaves, route.half, len(came)
    for i in range(ways):
        if route.extra:
            tail = came[i][route.tails : route.meta, :].astype(F32)
        for k in range(route.fan):
            for slot in range(CAP):
                at = k * CAP + slot
                leaf = leaf_ref[base + i, at]
                rows = pl.ds(pl.multiple_of(leaf * route.rows, TILE), route.rows)
                total[k, rows, :] += came[i][at * route.rows : (at + 1) * route.rows, :].astype(F32)
                if route.extra:
                    tails[k, pl.ds(leaf, 1), :] += tail[at : at + 1]

    for k in range(route.fan):
        outs[k][: route.dense_tails, :] = total[k, : route.dense_tails, :].astype(BF16)
        if route.extra:
            for i in range(ways):
                last = came[i][route.meta : route.box, :].astype(F32)[1:2]
                tails[k, leaves + i : leaves + i + 1, :] = last
                start = route.dense_box + i * half
                outs[k][start : start + half, :] = came[i][route.box :, :]
            outs[k][route.dense_tails : route.dense_box, :] = tails[k].astype(BF16)


def sum_kernel(routes, devices, *refs):
    by_low, by_high = routes
    high, low = grid_of(devices)
    ways = low + high
    came, outs, scratch = refs[:ways], refs[ways : 2 * ways], refs[2 * ways :]
    meta, leaf_ref, total_low, total_high, tails, late = scratch
    for i, route in enumerate([by_low] * low + [by_high] * high):
        meta[i : i + 1, :] = came[i][route.meta : route.box, :].astype(F32)[:1].astype(I32)
    numbers = pltpu.make_async_copy(meta, leaf_ref, late)
    numbers.start()
    for ref in (total_low, total_high, tails):
        ref[...] = jnp.zeros(ref.shape, F32)
    numbers.wait()
    sum_route(by_low, came[:low], outs[:high], 0, leaf_ref, total_low, None)
    sum_route(by_high, came[low:], outs[high:], low, leaf_ref, total_high, tails)


def keep_kernel(*refs):
    half = len(refs) // 2
    for came, kept in zip(refs[:half], refs[half:]):
        kept[...] = came[...]


def local_kernel(probes_ref, local_ref, out_ref):
    leaves, size = local_ref.shape[0], local_ref.shape[2]
    for i in range(leaves):
        total = dot_t(probes_ref[:, :size], local_ref[i, 0])
        for c in range(1, leaves):
            total += dot_t(probes_ref[:, c * size : (c + 1) * size], local_ref[i, c])
        out_ref[:, i * size : (i + 1) * size] = total


def far_kernel(by_high, low, partner_ref, base_ref, couplings_ref, transfer_ref, basis_ref, *refs):
    came, out_ref, boxes = refs[:low], refs[low], refs[low + 1]
    columns = out_ref.shape[0]
    leaves, rank, size = basis_ref.shape
    high = boxes.shape[0] // low
    me = lax.axis_index("leaf")
    for k in range(low):
        tile = came[k][by_high.dense_tails : by_high.dense_box, :].astype(F32)
        for i in range(high):
            start = by_high.dense_box + i * by_high.half
            packed = came[k][start : start + by_high.half, :]
            last = tile[leaves + i : leaves + i + 1, :rank]
            boxes[i * low + k] = jnp.concatenate(
                [packed[:, :rank].astype(F32), packed[:, rank:].astype(F32), last], axis=0
            ).astype(BF16)
    far = jnp.zeros((columns, rank), F32)
    for f in range(couplings_ref.shape[1]):
        source = jnp.bitwise_xor(partner_ref[0, f], me)
        far += dot_t(boxes[source], couplings_ref[0, f])
    far = far.astype(BF16)
    down = [dot(far, transfer_ref[j]).astype(BF16) for j in range(leaves)]
    for j in range(leaves):
        cols = slice(j * size, (j + 1) * size)
        out_ref[:, cols] = base_ref[:, cols] + dot(down[j], basis_ref[j])


def last_kernel(routes, devices, base_ref, *refs):
    by_low, by_high = routes
    high, low = grid_of(devices)
    came_high, came_low, out_ref = refs[:high], refs[high : high + low], refs[high + low]
    leaves, split, main = by_low.leaves, by_low.rows, by_low.main
    size = base_ref.shape[1] // leaves
    tails = sum(came_low[k][by_high.dense_tails : by_high.dense_box, :].astype(F32) for k in range(low))
    for j in range(leaves):
        cols = slice(j * size, (j + 1) * size)
        upper = sum(came_high[k][j * by_low.rows : (j + 1) * by_low.rows, :].astype(F32) for k in range(high))
        lower = sum(came_low[k][j * by_high.rows : (j + 1) * by_high.rows, :].astype(F32) for k in range(low))
        out_ref[:split, cols] = base_ref[:split, cols] + upper
        out_ref[split:main, cols] = base_ref[split:main, cols] + lower
        out_ref[main:, cols] = base_ref[main:, cols] + tails[j : j + 1]


def call(kernel, out_shape, specs, operands, scratch, flops, room=None):
    outs = jax.tree.leaves(out_shape)
    nbytes = sum(a.size * a.dtype.itemsize for a in (*operands, *outs))
    limit = None if room is None else nbytes + room + 2**21
    return pl.pallas_call(
        kernel,
        out_shape=out_shape,
        in_specs=specs[0],
        out_specs=specs[1],
        scratch_shapes=scratch,
        compiler_params=pltpu.CompilerParams(vmem_limit_bytes=limit),
        cost_estimate=pl.CostEstimate(flops=flops, bytes_accessed=nbytes, transcendentals=0),
    )(*operands)


def per_device(
    probes, basis, transfer, local_blocks, remote_blocks, near_dest, near_leaf, couplings, far_list
):
    columns, points = probes.shape
    leaves, rank, size = basis.shape
    devices = lax.axis_size("leaf")
    main = columns // TILE * TILE
    routes = by_low, by_high = routes_of(devices, main, columns, leaves)
    high, low = grid_of(devices)
    blocks = remote_blocks.shape[0] * remote_blocks.shape[1]
    unit = 2 * columns * size * size
    like = lambda *arrays: [pltpu.VMEM(a.shape, a.dtype) for a in arrays]
    numbers = lambda *arrays: [pltpu.SMEM(a.shape, a.dtype) for a in arrays]
    sems = lambda count: [pltpu.SemaphoreType.DMA((count,))]
    relative = lambda x, way: lax.ppermute(x, "leaf", [(i, i ^ way) for i in range(devices)])
    message = lambda route: jax.ShapeDtypeStruct((route.depth, size), BF16)
    dense = lambda route: jax.ShapeDtypeStruct((route.dense_depth, size), BF16)

    def stacked(count, like_this):
        return pltpu.VMEM((count, *like_this.shape), like_this.dtype)

    dest, leaf = near_dest.T, near_leaf.T
    sent = call(
        functools.partial(products_kernel, routes, devices),
        [message(by_low)] * low + [message(by_high)] * high,
        ([ANY] * 6, [ANY] * (low + high)),
        (dest, leaf, probes, basis, transfer, remote_blocks),
        numbers(dest, leaf)
        + like(probes, basis, transfer, remote_blocks)
        + [
            stacked(low, message(by_low)),
            stacked(high, message(by_high)),
            pltpu.VMEM((high, by_high.meta - by_high.tails, size), F32),
            pltpu.SMEM((devices,), I32),
        ]
        + sems(7 + low + high),
        blocks * unit,
    )
    came_low, came_high = list(sent[:low]), list(sent[low:])
    ways_low = range(low - 1, 0, -1)
    ways_high = [high - 1, *range(1, 2), *range(high - 2, 1, -1)]
    for k in ways_low:
        came_low[k] = relative(came_low[k], k)
    for k in ways_high:
        came_high[k] = relative(came_high[k], k * low)
    came_low[0], came_low[1], came_high[0] = call(
        keep_kernel,
        (message(by_low), message(by_low), message(by_high)),
        ([VMEM] * 3, (VMEM,) * 3),
        (came_low[0], came_low[1], came_high[0]),
        [],
        0,
        0,
    )

    total = lambda route: jax.ShapeDtypeStruct((route.fan, (leaves + 1) * route.rows, size), F32)
    tails = jax.ShapeDtypeStruct((low, by_high.dense_box - by_high.dense_tails, size), F32)
    sums = call(
        functools.partial(sum_kernel, routes, devices),
        [dense(by_low)] * high + [dense(by_high)] * low,
        ([VMEM] * (low + high), [VMEM] * (low + high)),
        (*came_low, *came_high),
        [pltpu.VMEM((low + high, size), I32), pltpu.SMEM((low + high, size), I32)]
        + like(total(by_low), total(by_high), tails)
        + [pltpu.SemaphoreType.DMA(())],
        devices * CAP * columns * size,
        4 * (total(by_low).size + total(by_high).size + tails.size),
    )
    to_high, to_low = list(sums[:high]), list(sums[high:])
    probes_then, to_low[0] = lax.optimization_barrier((probes, to_low[0]))
    for k in ways_high:
        to_high[k] = relative(to_high[k], k * low)
    for k in ways_low:
        to_low[k] = relative(to_low[k], k)

    base_shape = jax.ShapeDtypeStruct((columns, points), F32)
    base = call(
        local_kernel, base_shape, ([VMEM] * 2, VMEM), (probes_then, local_blocks), [], leaves * leaves * unit, 0
    )
    boxes = jax.ShapeDtypeStruct((devices, columns, rank), BF16)
    base = call(
        functools.partial(far_kernel, by_high, low),
        base_shape,
        ([SMEM] + [VMEM] * (4 + low), VMEM),
        (far_list, base, couplings, transfer, basis, *to_low),
        like(boxes),
        4 * leaves * unit,
        4 * boxes.size,
    )
    return call(
        functools.partial(last_kernel, routes, devices),
        base_shape,
        ([VMEM] * (1 + high + low), VMEM),
        (base, *to_high, *to_low),
        [],
        devices * columns * size,
        0,
    )


def solution(mesh):
    placed = (
        P(None, ("grp", "leaf")),
        P(("grp", "leaf"), None, None),
        P(("grp", "leaf"), None, None),
        P(("grp", "leaf"), None, None, None),
        P(("grp", "leaf"), None, None, None),
        P(("grp", "leaf"), None),
        P(("grp", "leaf"), None),
        P(("grp", "leaf"), None, None, None),
        P(("grp", "leaf"), None),
    )
    return jax.shard_map(
        per_device, mesh=mesh, in_specs=placed, out_specs=P(None, ("grp", "leaf")), check_vma=False
    )
```

```python
import functools

import jax
import jax.numpy as jnp
from jax import lax
from jax.experimental import pallas as pl
from jax.experimental.pallas import tpu as pltpu
from jax.sharding import PartitionSpec as P

CAP = 4
TILE = 16
F32 = jnp.float32
BF16 = jnp.bfloat16
I32 = jnp.int32

ANY = pl.BlockSpec(memory_space=pl.ANY)
VMEM = pl.BlockSpec(memory_space=pltpu.VMEM)
SMEM = pl.BlockSpec(memory_space=pltpu.SMEM)


def dot_t(lhs, rhs):
    return lax.dot_general(lhs, rhs, (((1,), (1,)), ((), ())), preferred_element_type=F32)


def dot(lhs, rhs):
    return lax.dot_general(lhs, rhs, (((1,), (0,)), ((), ())), preferred_element_type=F32)


class Copies:
    def __init__(self, sems):
        self.sems, self.used = sems, 0

    def start(self, src, dst):
        copy = pltpu.make_async_copy(src, dst, self.sems.at[self.used])
        self.used += 1
        copy.start()
        return copy


def grid_of(devices):
    low = 1 << (devices.bit_length() // 2)
    return devices // low, low


def up(rows):
    return -(-rows // TILE) * TILE


class Route:
    def __init__(self, first, last, fan, extra, main, columns, leaves, sources):
        self.first, self.rows, self.fan, self.extra, self.main = first, last - first, fan, extra, main
        self.leaves, self.half = leaves, main // 2
        slots = fan * CAP
        self.tails = slots * self.rows
        self.meta = self.tails + (up(slots) if extra else 0)
        self.box = self.meta + TILE
        self.depth = self.box + (self.half if extra else 0)
        self.dense_tails = leaves * self.rows
        self.dense_box = self.dense_tails + (up(leaves + sources) if extra else 0)
        self.dense_depth = self.dense_box + (sources * self.half if extra else 0)


def routes_of(devices, main, columns, leaves):
    high, low = grid_of(devices)
    split = up(main * 3 // 4)
    return (
        Route(0, split, high, False, main, columns, leaves, low),
        Route(split, main, low, True, main, columns, leaves, high),
    )


def products_kernel(routes, devices, *refs):
    dest_hbm, leaf_hbm, probes_hbm, basis_hbm, transfer_hbm, blocks_hbm = refs[:6]
    outs = refs[6:-11]
    (
        dest_ref, leaf_ref, probes_ref, basis_ref, transfer_ref, blocks_ref,
        send_low, send_high, tails, count, sems,
    ) = refs[-11:]
    by_low, by_high = routes
    high, low = grid_of(devices)
    me = lax.axis_index("leaf")
    main = by_high.main
    leaves, per_leaf, size = blocks_ref.shape[:3]
    columns, rank = probes_ref.shape[0], basis_ref.shape[1]
    copies = Copies(sems)
    early = [
        copies.start(probes_hbm, probes_ref),
        copies.start(basis_hbm, basis_ref),
        copies.start(transfer_hbm, transfer_ref),
        copies.start(dest_hbm, dest_ref),
        copies.start(leaf_hbm, leaf_ref),
    ]
    chunk = leaves // 2
    arrivals = [
        copies.start(blocks_hbm.at[pl.ds(j, chunk)], blocks_ref.at[pl.ds(j, chunk)])
        for j in range(0, leaves, chunk)
    ]

    @pl.loop(0, devices)
    def _(i):
        count[i] = 0

    tails[...] = jnp.zeros(tails.shape, F32)
    for copy in early:
        copy.wait()
    box = jnp.zeros((columns, rank), F32)
    for j in range(leaves):
        coef = dot_t(probes_ref[:, j * size : (j + 1) * size], basis_ref[j]).astype(BF16)
        box += dot_t(coef, transfer_ref[j])
    half = by_high.half
    packed = jnp.concatenate([box[:half], box[half:main]], axis=1).astype(BF16)
    last = jnp.concatenate([box[main:], jnp.zeros_like(box[main:])], axis=1)

    numbers = jnp.full((-(-(low + high) // 8) * 8, size), leaves, I32)
    row = lax.broadcasted_iota(I32, numbers.shape, 0)
    lane = lax.broadcasted_iota(I32, numbers.shape, 1)
    for j in range(leaves):
        if j % chunk == 0:
            arrivals[j // chunk].wait()
        x = probes_ref[:, j * size : (j + 1) * size]
        for first in range(0, per_leaf, 4):
            many = min(4, per_leaf - first)
            rhs = blocks_ref[j, first : first + many].reshape(many * size, size)
            product = dot_t(x, rhs)
            for b in range(many):
                target = jnp.bitwise_xor(dest_ref[first + b, j], me)
                slot = count[target]
                count[target] = slot + 1
                to_high = lax.shift_right_logical(target, low.bit_length() - 1)
                to_low = jnp.bitwise_and(target, low - 1)
                block = product[:, b * size : (b + 1) * size]
                piece = block[:main].astype(BF16)
                number = leaf_ref[first + b, j]

                at = to_high * CAP + slot
                rows = pl.ds(pl.multiple_of(at * by_low.rows, TILE), by_low.rows)
                send_low[to_low, rows, :] = piece[: by_low.rows]
                numbers = jnp.where((row == to_low) & (lane == at), number, numbers)

                at = to_low * CAP + slot
                rows = pl.ds(pl.multiple_of(at * by_high.rows, TILE), by_high.rows)
                send_high[to_high, rows, :] = piece[by_low.rows :]
                tails[to_high, pl.ds(at, 1), :] = block[main:]
                numbers = jnp.where((row == low + to_high) & (lane == at), number, numbers)

    numbers = numbers.astype(F32)
    blank = jnp.zeros((TILE - 2, size), F32)
    for i in range(low):
        tile = jnp.concatenate([numbers[i : i + 1], last, blank], axis=0)
        send_low[i, by_low.meta : by_low.box, :] = tile.astype(BF16)
    for i in range(high):
        tile = jnp.concatenate([numbers[low + i : low + i + 1], last, blank], axis=0)
        send_high[i, by_high.tails : by_high.meta, :] = tails[i].astype(BF16)
        send_high[i, by_high.meta : by_high.box, :] = tile.astype(BF16)
        send_high[i, by_high.box :, :] = packed
    leaving = [copies.start(send_low.at[i], outs[i]) for i in range(low)]
    leaving += [copies.start(send_high.at[i], outs[low + i]) for i in range(high)]
    for copy in leaving:
        copy.wait()


def sum_route(route, came, planes, outs, base, leaf_ref, total, tails):
    leaves, half, ways = route.leaves, route.half, len(came)
    for i in range(ways):
        if route.extra:
            tail = came[i][route.tails : route.meta, :].astype(F32)
        for k in range(route.fan):
            for slot in range(CAP):
                at = k * CAP + slot
                leaf = leaf_ref[base + i, at]
                rows = pl.ds(pl.multiple_of(leaf * route.rows, TILE), route.rows)
                total[k, rows, :] += came[i][at * route.rows : (at + 1) * route.rows, :].astype(F32)
                if route.extra:
                    tails[k, pl.ds(leaf, 1), :] += tail[at : at + 1]

    for k in range(route.fan):
        outs[k][: route.dense_tails, :] = total[k, : route.dense_tails, :].astype(BF16)
        if route.extra:
            for i in range(ways):
                last = came[i][route.meta : route.box, :].astype(F32)[1:2]
                at = planes[i]
                tails[k, leaves + at : leaves + at + 1, :] = last
                start = route.dense_box + at * half
                outs[k][start : start + half, :] = came[i][route.box :, :]
            outs[k][route.dense_tails : route.dense_box, :] = tails[k].astype(BF16)


def across_first(high):
    return [0, *range(2, high), 1]


def sum_kernel(routes, devices, *refs):
    by_low, by_high = routes
    high, low = grid_of(devices)
    ways = low + high
    came, outs, scratch = refs[:ways], refs[ways : 2 * ways], refs[2 * ways :]
    meta, leaf_ref, total_low, total_high, tails, late = scratch
    for i, route in enumerate([by_low] * low + [by_high] * high):
        meta[i : i + 1, :] = came[i][route.meta : route.box, :].astype(F32)[:1].astype(I32)
    numbers = pltpu.make_async_copy(meta, leaf_ref, late)
    numbers.start()
    for ref in (total_low, total_high, tails):
        ref[...] = jnp.zeros(ref.shape, F32)
    numbers.wait()
    sum_route(by_low, came[:low], None, outs[:high], 0, leaf_ref, total_low, None)
    sum_route(by_high, came[low:], across_first(high), outs[high:], low, leaf_ref, total_high, tails)


def keep_kernel(*refs):
    half = len(refs) // 2
    for came, kept in zip(refs[:half], refs[half:]):
        kept[...] = came[...]


def local_kernel(probes_ref, local_ref, out_ref):
    leaves, size = local_ref.shape[0], local_ref.shape[2]
    for i in range(leaves):
        total = dot_t(probes_ref[:, :size], local_ref[i, 0])
        for c in range(1, leaves):
            total += dot_t(probes_ref[:, c * size : (c + 1) * size], local_ref[i, c])
        out_ref[:, i * size : (i + 1) * size] = total


def far_kernel(by_high, low, partner_ref, base_ref, couplings_ref, transfer_ref, basis_ref, *refs):
    came, out_ref, boxes = refs[:low], refs[low], refs[low + 1]
    columns = out_ref.shape[0]
    leaves, rank, size = basis_ref.shape
    high = boxes.shape[0] // low
    me = lax.axis_index("leaf")
    for k in range(low):
        tile = came[k][by_high.dense_tails : by_high.dense_box, :].astype(F32)
        for i in range(high):
            start = by_high.dense_box + i * by_high.half
            packed = came[k][start : start + by_high.half, :]
            last = tile[leaves + i : leaves + i + 1, :rank]
            boxes[i * low + k] = jnp.concatenate(
                [packed[:, :rank].astype(F32), packed[:, rank:].astype(F32), last], axis=0
            ).astype(BF16)
    far = jnp.zeros((columns, rank), F32)
    for f in range(couplings_ref.shape[1]):
        source = jnp.bitwise_xor(partner_ref[0, f], me)
        far += dot_t(boxes[source], couplings_ref[0, f])
    far = far.astype(BF16)
    down = [dot(far, transfer_ref[j]).astype(BF16) for j in range(leaves)]
    for j in range(leaves):
        cols = slice(j * size, (j + 1) * size)
        out_ref[:, cols] = base_ref[:, cols] + dot(down[j], basis_ref[j])


def last_kernel(routes, devices, base_ref, *refs):
    by_low, by_high = routes
    high, low = grid_of(devices)
    came_high, came_low, out_ref = refs[:high], refs[high : high + low], refs[high + low]
    leaves, split, main = by_low.leaves, by_low.rows, by_low.main
    size = base_ref.shape[1] // leaves
    tails = sum(came_low[k][by_high.dense_tails : by_high.dense_box, :].astype(F32) for k in range(low))
    for j in range(leaves):
        cols = slice(j * size, (j + 1) * size)
        upper = sum(came_high[k][j * by_low.rows : (j + 1) * by_low.rows, :].astype(F32) for k in range(high))
        lower = sum(came_low[k][j * by_high.rows : (j + 1) * by_high.rows, :].astype(F32) for k in range(low))
        out_ref[:split, cols] = base_ref[:split, cols] + upper
        out_ref[split:main, cols] = base_ref[split:main, cols] + lower
        out_ref[main:, cols] = base_ref[main:, cols] + tails[j : j + 1]


def call(kernel, out_shape, specs, operands, scratch, flops, room=None):
    outs = jax.tree.leaves(out_shape)
    nbytes = sum(a.size * a.dtype.itemsize for a in (*operands, *outs))
    limit = None if room is None else nbytes + room + 2**21
    return pl.pallas_call(
        kernel,
        out_shape=out_shape,
        in_specs=specs[0],
        out_specs=specs[1],
        scratch_shapes=scratch,
        compiler_params=pltpu.CompilerParams(vmem_limit_bytes=limit),
        cost_estimate=pl.CostEstimate(flops=flops, bytes_accessed=nbytes, transcendentals=0),
    )(*operands)


def per_device(
    probes, basis, transfer, local_blocks, remote_blocks, near_dest, near_leaf, couplings, far_list
):
    columns, points = probes.shape
    leaves, rank, size = basis.shape
    devices = lax.axis_size("leaf")
    main = columns // TILE * TILE
    routes = by_low, by_high = routes_of(devices, main, columns, leaves)
    high, low = grid_of(devices)
    blocks = remote_blocks.shape[0] * remote_blocks.shape[1]
    unit = 2 * columns * size * size
    like = lambda *arrays: [pltpu.VMEM(a.shape, a.dtype) for a in arrays]
    numbers = lambda *arrays: [pltpu.SMEM(a.shape, a.dtype) for a in arrays]
    sems = lambda count: [pltpu.SemaphoreType.DMA((count,))]
    relative = lambda x, way: lax.ppermute(x, "leaf", [(i, i ^ way) for i in range(devices)])
    message = lambda route: jax.ShapeDtypeStruct((route.depth, size), BF16)
    dense = lambda route: jax.ShapeDtypeStruct((route.dense_depth, size), BF16)

    def stacked(count, like_this):
        return pltpu.VMEM((count, *like_this.shape), like_this.dtype)

    dest, leaf = near_dest.T, near_leaf.T
    sent = call(
        functools.partial(products_kernel, routes, devices),
        [message(by_low)] * low + [message(by_high)] * high,
        ([ANY] * 6, [ANY] * (low + high)),
        (dest, leaf, probes, basis, transfer, remote_blocks),
        numbers(dest, leaf)
        + like(probes, basis, transfer, remote_blocks)
        + [
            stacked(low, message(by_low)),
            stacked(high, message(by_high)),
            pltpu.VMEM((high, by_high.meta - by_high.tails, size), F32),
            pltpu.SMEM((devices,), I32),
        ]
        + sems(7 + low + high),
        blocks * unit,
    )
    came_low, came_high = list(sent[:low]), list(sent[low:])
    planes = across_first(high)
    for k in range(1, low):
        came_low[k] = relative(came_low[k], k)
    for k in planes[1:]:
        came_high[k] = relative(came_high[k], k * low)
    came_low[0], came_low[1], came_high[0] = call(
        keep_kernel,
        (message(by_low), message(by_low), message(by_high)),
        ([VMEM] * 3, (VMEM,) * 3),
        (came_low[0], came_low[1], came_high[0]),
        [],
        0,
        0,
    )

    total = lambda route: jax.ShapeDtypeStruct((route.fan, (leaves + 1) * route.rows, size), F32)
    tails = jax.ShapeDtypeStruct((low, by_high.dense_box - by_high.dense_tails, size), F32)
    sums = call(
        functools.partial(sum_kernel, routes, devices),
        [dense(by_low)] * high + [dense(by_high)] * low,
        ([VMEM] * (low + high), [VMEM] * (low + high)),
        (*came_low, *(came_high[k] for k in planes)),
        [pltpu.VMEM((low + high, size), I32), pltpu.SMEM((low + high, size), I32)]
        + like(total(by_low), total(by_high), tails)
        + [pltpu.SemaphoreType.DMA(())],
        devices * CAP * columns * size,
        4 * (total(by_low).size + total(by_high).size + tails.size),
    )
    to_high, to_low = list(sums[:high]), list(sums[high:])
    probes_then, to_low[0] = lax.optimization_barrier((probes, to_low[0]))
    for k in planes[1:]:
        to_high[k] = relative(to_high[k], k * low)
    for k in range(1, low):
        to_low[k] = relative(to_low[k], k)

    base_shape = jax.ShapeDtypeStruct((columns, points), F32)
    base = call(
        local_kernel, base_shape, ([VMEM] * 2, VMEM), (probes_then, local_blocks), [], leaves * leaves * unit, 0
    )
    boxes = jax.ShapeDtypeStruct((devices, columns, rank), BF16)
    base = call(
        functools.partial(far_kernel, by_high, low),
        base_shape,
        ([SMEM] + [VMEM] * (4 + low), VMEM),
        (far_list, base, couplings, transfer, basis, *to_low),
        like(boxes),
        4 * leaves * unit,
        4 * boxes.size,
    )
    return call(
        functools.partial(last_kernel, routes, devices),
        base_shape,
        ([VMEM] * (1 + high + low), VMEM),
        (base, *(to_high[k] for k in planes), *to_low),
        [],
        devices * columns * size,
        0,
    )


def solution(mesh):
    placed = (
        P(None, ("grp", "leaf")),
        P(("grp", "leaf"), None, None),
        P(("grp", "leaf"), None, None),
        P(("grp", "leaf"), None, None, None),
        P(("grp", "leaf"), None, None, None),
        P(("grp", "leaf"), None),
        P(("grp", "leaf"), None),
        P(("grp", "leaf"), None, None, None),
        P(("grp", "leaf"), None),
    )
    return jax.shard_map(
        per_device, mesh=mesh, in_specs=placed, out_specs=P(None, ("grp", "leaf")), check_vma=False
    )
```

```python
import functools

import jax
import jax.numpy as jnp
from jax import lax
from jax.experimental import pallas as pl
from jax.experimental.pallas import tpu as pltpu
from jax.sharding import PartitionSpec as P

CAP = 4
TILE = 16
F32 = jnp.float32
BF16 = jnp.bfloat16
I32 = jnp.int32

ANY = pl.BlockSpec(memory_space=pl.ANY)
VMEM = pl.BlockSpec(memory_space=pltpu.VMEM)
SMEM = pl.BlockSpec(memory_space=pltpu.SMEM)


def dot_t(lhs, rhs):
    return lax.dot_general(lhs, rhs, (((1,), (1,)), ((), ())), preferred_element_type=F32)


def dot(lhs, rhs):
    return lax.dot_general(lhs, rhs, (((1,), (0,)), ((), ())), preferred_element_type=F32)


class Copies:
    def __init__(self, sems):
        self.sems, self.used = sems, 0

    def start(self, src, dst):
        copy = pltpu.make_async_copy(src, dst, self.sems.at[self.used])
        self.used += 1
        copy.start()
        return copy


def grid_of(devices):
    low = 1 << (devices.bit_length() // 2)
    return devices // low, low


def up(rows):
    return -(-rows // TILE) * TILE


class Route:
    def __init__(self, first, last, fan, extra, main, columns, leaves, sources):
        self.first, self.rows, self.fan, self.extra, self.main = first, last - first, fan, extra, main
        self.leaves, self.half = leaves, main // 2
        slots = fan * CAP
        self.tails = slots * self.rows
        self.meta = self.tails + (up(slots) if extra else 0)
        self.box = self.meta + TILE
        self.depth = self.box + (self.half if extra else 0)
        self.dense_tails = leaves * self.rows
        self.dense_box = self.dense_tails + (up(leaves + sources) if extra else 0)
        self.dense_depth = self.dense_box + (sources * self.half if extra else 0)


def routes_of(devices, main, columns, leaves):
    high, low = grid_of(devices)
    split = up(main * 3 // 4)
    return (
        Route(0, split, high, False, main, columns, leaves, low),
        Route(split, main, low, True, main, columns, leaves, high),
    )


def products_kernel(routes, devices, *refs):
    dest_hbm, leaf_hbm, probes_hbm, basis_hbm, transfer_hbm, blocks_hbm = refs[:6]
    outs = refs[6:-11]
    (
        dest_ref, leaf_ref, probes_ref, basis_ref, transfer_ref, blocks_ref,
        send_low, send_high, tails, count, sems,
    ) = refs[-11:]
    by_low, by_high = routes
    high, low = grid_of(devices)
    me = lax.axis_index("leaf")
    main = by_high.main
    leaves, per_leaf, size = blocks_ref.shape[:3]
    columns, rank = probes_ref.shape[0], basis_ref.shape[1]
    copies = Copies(sems)
    chunk = leaves // 2
    arrivals = []
    early = [
        copies.start(probes_hbm, probes_ref),
        copies.start(dest_hbm, dest_ref),
        copies.start(leaf_hbm, leaf_ref),
    ]
    for j in range(0, leaves, chunk):
        arrivals.append(copies.start(blocks_hbm.at[pl.ds(j, chunk)], blocks_ref.at[pl.ds(j, chunk)]))
        if j == 0:
            early += [copies.start(basis_hbm, basis_ref), copies.start(transfer_hbm, transfer_ref)]

    @pl.loop(0, devices)
    def _(i):
        count[i] = 0

    tails[...] = jnp.zeros(tails.shape, F32)
    for copy in early:
        copy.wait()
    box = jnp.zeros((columns, rank), F32)

    numbers = jnp.full((-(-(low + high) // 8) * 8, size), leaves, I32)
    row = lax.broadcasted_iota(I32, numbers.shape, 0)
    lane = lax.broadcasted_iota(I32, numbers.shape, 1)
    for j in range(leaves):
        if j % chunk == 0:
            arrivals[j // chunk].wait()
        x = probes_ref[:, j * size : (j + 1) * size]
        box += dot_t(dot_t(x, basis_ref[j]).astype(BF16), transfer_ref[j])
        for first in range(0, per_leaf, 4):
            many = min(4, per_leaf - first)
            rhs = blocks_ref[j, first : first + many].reshape(many * size, size)
            product = dot_t(x, rhs)
            for b in range(many):
                target = jnp.bitwise_xor(dest_ref[first + b, j], me)
                slot = count[target]
                count[target] = slot + 1
                to_high = lax.shift_right_logical(target, low.bit_length() - 1)
                to_low = jnp.bitwise_and(target, low - 1)
                block = product[:, b * size : (b + 1) * size]
                piece = block[:main].astype(BF16)
                number = leaf_ref[first + b, j]

                at = to_high * CAP + slot
                rows = pl.ds(pl.multiple_of(at * by_low.rows, TILE), by_low.rows)
                send_low[to_low, rows, :] = piece[: by_low.rows]
                numbers = jnp.where((row == to_low) & (lane == at), number, numbers)

                at = to_low * CAP + slot
                rows = pl.ds(pl.multiple_of(at * by_high.rows, TILE), by_high.rows)
                send_high[to_high, rows, :] = piece[by_low.rows :]
                tails[to_high, pl.ds(at, 1), :] = block[main:]
                numbers = jnp.where((row == low + to_high) & (lane == at), number, numbers)

    half = by_high.half
    packed = jnp.concatenate([box[:half], box[half:main]], axis=1).astype(BF16)
    last = jnp.concatenate([box[main:], jnp.zeros_like(box[main:])], axis=1)
    numbers = numbers.astype(F32)
    blank = jnp.zeros((TILE - 2, size), F32)
    for i in range(low):
        tile = jnp.concatenate([numbers[i : i + 1], last, blank], axis=0)
        send_low[i, by_low.meta : by_low.box, :] = tile.astype(BF16)
    for i in range(high):
        tile = jnp.concatenate([numbers[low + i : low + i + 1], last, blank], axis=0)
        send_high[i, by_high.tails : by_high.meta, :] = tails[i].astype(BF16)
        send_high[i, by_high.meta : by_high.box, :] = tile.astype(BF16)
        send_high[i, by_high.box :, :] = packed
    leaving = [copies.start(send_low.at[i], outs[i]) for i in range(low)]
    leaving += [copies.start(send_high.at[i], outs[low + i]) for i in range(high)]
    for copy in leaving:
        copy.wait()


def sum_route(route, came, planes, outs, base, leaf_ref, total, tails):
    leaves, half, ways = route.leaves, route.half, len(came)
    for i in range(ways):
        if route.extra:
            tail = came[i][route.tails : route.meta, :].astype(F32)
        for k in range(route.fan):
            for slot in range(CAP):
                at = k * CAP + slot
                leaf = leaf_ref[base + i, at]
                rows = pl.ds(pl.multiple_of(leaf * route.rows, TILE), route.rows)
                total[k, rows, :] += came[i][at * route.rows : (at + 1) * route.rows, :].astype(F32)
                if route.extra:
                    tails[k, pl.ds(leaf, 1), :] += tail[at : at + 1]

    for k in range(route.fan):
        outs[k][: route.dense_tails, :] = total[k, : route.dense_tails, :].astype(BF16)
        if route.extra:
            for i in range(ways):
                last = came[i][route.meta : route.box, :].astype(F32)[1:2]
                at = planes[i]
                tails[k, leaves + at : leaves + at + 1, :] = last
                start = route.dense_box + at * half
                outs[k][start : start + half, :] = came[i][route.box :, :]
            outs[k][route.dense_tails : route.dense_box, :] = tails[k].astype(BF16)


def across_first(high):
    return [0, *range(2, high), 1]


def sum_kernel(routes, devices, *refs):
    by_low, by_high = routes
    high, low = grid_of(devices)
    ways = low + high
    came, outs, scratch = refs[:ways], refs[ways : 2 * ways], refs[2 * ways :]
    meta, leaf_ref, total_low, total_high, tails, late = scratch
    for i, route in enumerate([by_low] * low + [by_high] * high):
        meta[i : i + 1, :] = came[i][route.meta : route.box, :].astype(F32)[:1].astype(I32)
    numbers = pltpu.make_async_copy(meta, leaf_ref, late)
    numbers.start()
    for ref in (total_low, total_high, tails):
        ref[...] = jnp.zeros(ref.shape, F32)
    numbers.wait()
    sum_route(by_low, came[:low], None, outs[:high], 0, leaf_ref, total_low, None)
    sum_route(by_high, came[low:], across_first(high), outs[high:], low, leaf_ref, total_high, tails)


def keep_kernel(*refs):
    half = len(refs) // 2
    for came, kept in zip(refs[:half], refs[half:]):
        kept[...] = came[...]


def local_kernel(probes_ref, local_ref, out_ref):
    leaves, size = local_ref.shape[0], local_ref.shape[2]
    for i in range(leaves):
        total = dot_t(probes_ref[:, :size], local_ref[i, 0])
        for c in range(1, leaves):
            total += dot_t(probes_ref[:, c * size : (c + 1) * size], local_ref[i, c])
        out_ref[:, i * size : (i + 1) * size] = total


def far_kernel(by_high, low, partner_ref, base_ref, couplings_ref, transfer_ref, basis_ref, *refs):
    came, out_ref, boxes = refs[:low], refs[low], refs[low + 1]
    columns = out_ref.shape[0]
    leaves, rank, size = basis_ref.shape
    high = boxes.shape[0] // low
    me = lax.axis_index("leaf")
    for k in range(low):
        tile = came[k][by_high.dense_tails : by_high.dense_box, :].astype(F32)
        for i in range(high):
            start = by_high.dense_box + i * by_high.half
            packed = came[k][start : start + by_high.half, :]
            last = tile[leaves + i : leaves + i + 1, :rank]
            boxes[i * low + k] = jnp.concatenate(
                [packed[:, :rank].astype(F32), packed[:, rank:].astype(F32), last], axis=0
            ).astype(BF16)
    far = jnp.zeros((columns, rank), F32)
    for f in range(couplings_ref.shape[1]):
        source = jnp.bitwise_xor(partner_ref[0, f], me)
        far += dot_t(boxes[source], couplings_ref[0, f])
    far = far.astype(BF16)
    down = [dot(far, transfer_ref[j]).astype(BF16) for j in range(leaves)]
    for j in range(leaves):
        cols = slice(j * size, (j + 1) * size)
        out_ref[:, cols] = base_ref[:, cols] + dot(down[j], basis_ref[j])


def last_kernel(routes, devices, base_ref, *refs):
    by_low, by_high = routes
    high, low = grid_of(devices)
    came_high, came_low, out_ref = refs[:high], refs[high : high + low], refs[high + low]
    leaves, split, main = by_low.leaves, by_low.rows, by_low.main
    size = base_ref.shape[1] // leaves
    tails = sum(came_low[k][by_high.dense_tails : by_high.dense_box, :].astype(F32) for k in range(low))
    for j in range(leaves):
        cols = slice(j * size, (j + 1) * size)
        upper = sum(came_high[k][j * by_low.rows : (j + 1) * by_low.rows, :].astype(F32) for k in range(high))
        lower = sum(came_low[k][j * by_high.rows : (j + 1) * by_high.rows, :].astype(F32) for k in range(low))
        out_ref[:split, cols] = base_ref[:split, cols] + upper
        out_ref[split:main, cols] = base_ref[split:main, cols] + lower
        out_ref[main:, cols] = base_ref[main:, cols] + tails[j : j + 1]


def call(kernel, out_shape, specs, operands, scratch, flops, room=None):
    outs = jax.tree.leaves(out_shape)
    nbytes = sum(a.size * a.dtype.itemsize for a in (*operands, *outs))
    limit = None if room is None else nbytes + room + 2**21
    return pl.pallas_call(
        kernel,
        out_shape=out_shape,
        in_specs=specs[0],
        out_specs=specs[1],
        scratch_shapes=scratch,
        compiler_params=pltpu.CompilerParams(vmem_limit_bytes=limit),
        cost_estimate=pl.CostEstimate(flops=flops, bytes_accessed=nbytes, transcendentals=0),
    )(*operands)


def per_device(
    probes, basis, transfer, local_blocks, remote_blocks, near_dest, near_leaf, couplings, far_list
):
    columns, points = probes.shape
    leaves, rank, size = basis.shape
    devices = lax.axis_size("leaf")
    main = columns // TILE * TILE
    routes = by_low, by_high = routes_of(devices, main, columns, leaves)
    high, low = grid_of(devices)
    blocks = remote_blocks.shape[0] * remote_blocks.shape[1]
    unit = 2 * columns * size * size
    like = lambda *arrays: [pltpu.VMEM(a.shape, a.dtype) for a in arrays]
    numbers = lambda *arrays: [pltpu.SMEM(a.shape, a.dtype) for a in arrays]
    sems = lambda count: [pltpu.SemaphoreType.DMA((count,))]
    relative = lambda x, way: lax.ppermute(x, "leaf", [(i, i ^ way) for i in range(devices)])
    message = lambda route: jax.ShapeDtypeStruct((route.depth, size), BF16)
    dense = lambda route: jax.ShapeDtypeStruct((route.dense_depth, size), BF16)

    def stacked(count, like_this):
        return pltpu.VMEM((count, *like_this.shape), like_this.dtype)

    dest, leaf = near_dest.T, near_leaf.T
    sent = call(
        functools.partial(products_kernel, routes, devices),
        [message(by_low)] * low + [message(by_high)] * high,
        ([ANY] * 6, [ANY] * (low + high)),
        (dest, leaf, probes, basis, transfer, remote_blocks),
        numbers(dest, leaf)
        + like(probes, basis, transfer, remote_blocks)
        + [
            stacked(low, message(by_low)),
            stacked(high, message(by_high)),
            pltpu.VMEM((high, by_high.meta - by_high.tails, size), F32),
            pltpu.SMEM((devices,), I32),
        ]
        + sems(7 + low + high),
        blocks * unit,
    )
    came_low, came_high = list(sent[:low]), list(sent[low:])
    planes = across_first(high)
    for k in range(1, low):
        came_low[k] = relative(came_low[k], k)
    for k in planes[1:]:
        came_high[k] = relative(came_high[k], k * low)
    came_low[0], came_low[1], came_high[0] = call(
        keep_kernel,
        (message(by_low), message(by_low), message(by_high)),
        ([VMEM] * 3, (VMEM,) * 3),
        (came_low[0], came_low[1], came_high[0]),
        [],
        0,
        0,
    )

    total = lambda route: jax.ShapeDtypeStruct((route.fan, (leaves + 1) * route.rows, size), F32)
    tails = jax.ShapeDtypeStruct((low, by_high.dense_box - by_high.dense_tails, size), F32)
    sums = call(
        functools.partial(sum_kernel, routes, devices),
        [dense(by_low)] * high + [dense(by_high)] * low,
        ([VMEM] * (low + high), [VMEM] * (low + high)),
        (*came_low, *(came_high[k] for k in planes)),
        [pltpu.VMEM((low + high, size), I32), pltpu.SMEM((low + high, size), I32)]
        + like(total(by_low), total(by_high), tails)
        + [pltpu.SemaphoreType.DMA(())],
        devices * CAP * columns * size,
        4 * (total(by_low).size + total(by_high).size + tails.size),
    )
    to_high, to_low = list(sums[:high]), list(sums[high:])
    probes_then, to_low[0] = lax.optimization_barrier((probes, to_low[0]))
    for k in planes[1:]:
        to_high[k] = relative(to_high[k], k * low)
    for k in range(1, low):
        to_low[k] = relative(to_low[k], k)

    base_shape = jax.ShapeDtypeStruct((columns, points), F32)
    base = call(
        local_kernel, base_shape, ([VMEM] * 2, VMEM), (probes_then, local_blocks), [], leaves * leaves * unit, 0
    )
    boxes = jax.ShapeDtypeStruct((devices, columns, rank), BF16)
    base = call(
        functools.partial(far_kernel, by_high, low),
        base_shape,
        ([SMEM] + [VMEM] * (4 + low), VMEM),
        (far_list, base, couplings, transfer, basis, *to_low),
        like(boxes),
        4 * leaves * unit,
        4 * boxes.size,
    )
    return call(
        functools.partial(last_kernel, routes, devices),
        base_shape,
        ([VMEM] * (1 + high + low), VMEM),
        (base, *(to_high[k] for k in planes), *to_low),
        [],
        devices * columns * size,
        0,
    )


def solution(mesh):
    placed = (
        P(None, ("grp", "leaf")),
        P(("grp", "leaf"), None, None),
        P(("grp", "leaf"), None, None),
        P(("grp", "leaf"), None, None, None),
        P(("grp", "leaf"), None, None, None),
        P(("grp", "leaf"), None),
        P(("grp", "leaf"), None),
        P(("grp", "leaf"), None, None, None),
        P(("grp", "leaf"), None),
    )
    return jax.shard_map(
        per_device, mesh=mesh, in_specs=placed, out_specs=P(None, ("grp", "leaf")), check_vma=False
    )
```

```python
import functools

import jax
import jax.numpy as jnp
from jax import lax
from jax.experimental import pallas as pl
from jax.experimental.pallas import tpu as pltpu
from jax.sharding import PartitionSpec as P

CAP = 4
TILE = 16
HEAVY = 4 * 10**9

F32 = jnp.float32
BF16 = jnp.bfloat16
I32 = jnp.int32

ANY = pl.BlockSpec(memory_space=pl.ANY)
VMEM = pl.BlockSpec(memory_space=pltpu.VMEM)
SMEM = pl.BlockSpec(memory_space=pltpu.SMEM)


def dot_t(lhs, rhs):
    return lax.dot_general(lhs, rhs, (((1,), (1,)), ((), ())), preferred_element_type=F32)


def dot(lhs, rhs):
    return lax.dot_general(lhs, rhs, (((1,), (0,)), ((), ())), preferred_element_type=F32)


class Copies:
    def __init__(self, sems):
        self.sems, self.used = sems, 0

    def start(self, src, dst):
        copy = pltpu.make_async_copy(src, dst, self.sems.at[self.used])
        self.used += 1
        copy.start()
        return copy


def grid_of(devices):
    low = 1 << (devices.bit_length() // 2)
    return devices // low, low


def up(rows):
    return -(-rows // TILE) * TILE


class Route:
    def __init__(self, first, last, fan, extra, main, columns, leaves, sources):
        self.first, self.rows, self.fan, self.extra, self.main = first, last - first, fan, extra, main
        self.leaves, self.half = leaves, main // 2
        slots = fan * CAP
        self.tails = slots * self.rows
        self.meta = self.tails + (up(slots) if extra else 0)
        self.box = self.meta + TILE
        self.depth = self.box + (self.half if extra else 0)
        self.dense_tails = leaves * self.rows
        self.dense_box = self.dense_tails + (up(leaves + sources) if extra else 0)
        self.dense_depth = self.dense_box + (sources * self.half if extra else 0)


def routes_of(devices, main, columns, leaves):
    high, low = grid_of(devices)
    split = up(main * 3 // 4)
    return (
        Route(0, split, high, False, main, columns, leaves, low),
        Route(split, main, low, True, main, columns, leaves, high),
    )


def products_kernel(routes, devices, *refs):
    dest_hbm, leaf_hbm, probes_hbm, basis_hbm, transfer_hbm, blocks_hbm = refs[:6]
    outs = refs[6:-11]
    (
        dest_ref, leaf_ref, probes_ref, basis_ref, transfer_ref, blocks_ref,
        send_low, send_high, tails, count, sems,
    ) = refs[-11:]
    by_low, by_high = routes
    high, low = grid_of(devices)
    me = lax.axis_index("leaf")
    main = by_high.main
    leaves, per_leaf, size = blocks_ref.shape[:3]
    columns, rank = probes_ref.shape[0], basis_ref.shape[1]
    copies = Copies(sems)
    chunk = leaves // 2
    arrivals = []
    early = [
        copies.start(probes_hbm, probes_ref),
        copies.start(dest_hbm, dest_ref),
        copies.start(leaf_hbm, leaf_ref),
    ]
    for j in range(0, leaves, chunk):
        arrivals.append(copies.start(blocks_hbm.at[pl.ds(j, chunk)], blocks_ref.at[pl.ds(j, chunk)]))
        if j == 0:
            early += [copies.start(basis_hbm, basis_ref), copies.start(transfer_hbm, transfer_ref)]

    @pl.loop(0, devices)
    def _(i):
        count[i] = 0

    tails[...] = jnp.zeros(tails.shape, F32)
    for copy in early:
        copy.wait()
    box = jnp.zeros((columns, rank), F32)

    numbers = jnp.full((-(-(low + high) // 8) * 8, size), leaves, I32)
    row = lax.broadcasted_iota(I32, numbers.shape, 0)
    lane = lax.broadcasted_iota(I32, numbers.shape, 1)
    for j in range(leaves):
        if j % chunk == 0:
            arrivals[j // chunk].wait()
        x = probes_ref[:, j * size : (j + 1) * size]
        box += dot_t(dot_t(x, basis_ref[j]).astype(BF16), transfer_ref[j])
        for first in range(0, per_leaf, 4):
            many = min(4, per_leaf - first)
            rhs = blocks_ref[j, first : first + many].reshape(many * size, size)
            product = dot_t(x, rhs)
            for b in range(many):
                target = jnp.bitwise_xor(dest_ref[first + b, j], me)
                slot = count[target]
                count[target] = slot + 1
                to_high = lax.shift_right_logical(target, low.bit_length() - 1)
                to_low = jnp.bitwise_and(target, low - 1)
                block = product[:, b * size : (b + 1) * size]
                piece = block[:main].astype(BF16)
                number = leaf_ref[first + b, j]

                at = to_high * CAP + slot
                rows = pl.ds(pl.multiple_of(at * by_low.rows, TILE), by_low.rows)
                send_low[to_low, rows, :] = piece[: by_low.rows]
                numbers = jnp.where((row == to_low) & (lane == at), number, numbers)

                at = to_low * CAP + slot
                rows = pl.ds(pl.multiple_of(at * by_high.rows, TILE), by_high.rows)
                send_high[to_high, rows, :] = piece[by_low.rows :]
                tails[to_high, pl.ds(at, 1), :] = block[main:]
                numbers = jnp.where((row == low + to_high) & (lane == at), number, numbers)

    half = by_high.half
    packed = jnp.concatenate([box[:half], box[half:main]], axis=1).astype(BF16)
    last = jnp.concatenate([box[main:], jnp.zeros_like(box[main:])], axis=1)
    numbers = numbers.astype(F32)
    blank = jnp.zeros((TILE - 2, size), F32)
    for i in range(low):
        tile = jnp.concatenate([numbers[i : i + 1], last, blank], axis=0)
        send_low[i, by_low.meta : by_low.box, :] = tile.astype(BF16)
    for i in range(high):
        tile = jnp.concatenate([numbers[low + i : low + i + 1], last, blank], axis=0)
        send_high[i, by_high.tails : by_high.meta, :] = tails[i].astype(BF16)
        send_high[i, by_high.meta : by_high.box, :] = tile.astype(BF16)
        send_high[i, by_high.box :, :] = packed
    leaving = [copies.start(send_low.at[i], outs[i]) for i in range(low)]
    leaving += [copies.start(send_high.at[i], outs[low + i]) for i in range(high)]
    for copy in leaving:
        copy.wait()


def sum_route(route, came, planes, outs, base, leaf_ref, total, tails):
    leaves, half, ways = route.leaves, route.half, len(came)
    for i in range(ways):
        if route.extra:
            tail = came[i][route.tails : route.meta, :].astype(F32)
        for k in range(route.fan):
            for slot in range(CAP):
                at = k * CAP + slot
                leaf = leaf_ref[base + i, at]
                rows = pl.ds(pl.multiple_of(leaf * route.rows, TILE), route.rows)
                total[k, rows, :] += came[i][at * route.rows : (at + 1) * route.rows, :].astype(F32)
                if route.extra:
                    tails[k, pl.ds(leaf, 1), :] += tail[at : at + 1]

    for k in range(route.fan):
        outs[k][: route.dense_tails, :] = total[k, : route.dense_tails, :].astype(BF16)
        if route.extra:
            for i in range(ways):
                last = came[i][route.meta : route.box, :].astype(F32)[1:2]
                at = planes[i]
                tails[k, leaves + at : leaves + at + 1, :] = last
                start = route.dense_box + at * half
                outs[k][start : start + half, :] = came[i][route.box :, :]
            outs[k][route.dense_tails : route.dense_box, :] = tails[k].astype(BF16)


def across_first(high):
    return [0, *range(2, high), 1]


def sum_kernel(route, planes, ways, *refs):
    came, outs = refs[:ways], refs[ways:-5]
    meta, leaf_ref, total, tails, late = refs[-5:]
    for i, ref in enumerate(came):
        meta[i : i + 1, :] = ref[route.meta : route.box, :].astype(F32)[:1].astype(I32)
    numbers = pltpu.make_async_copy(meta, leaf_ref, late)
    numbers.start()
    for ref in (total, tails):
        ref[...] = jnp.zeros(ref.shape, F32)
    numbers.wait()
    sum_route(route, came, planes, outs, 0, leaf_ref, total, tails)


def keep_kernel(*refs):
    half = len(refs) // 2
    for came, kept in zip(refs[:half], refs[half:]):
        kept[...] = came[...]


def local_kernel(probes_ref, local_ref, out_ref):
    leaves, size = local_ref.shape[0], local_ref.shape[2]
    for i in range(leaves):
        total = dot_t(probes_ref[:, :size], local_ref[i, 0])
        for c in range(1, leaves):
            total += dot_t(probes_ref[:, c * size : (c + 1) * size], local_ref[i, c])
        out_ref[:, i * size : (i + 1) * size] = total


def far_kernel(by_high, low, partner_ref, base_ref, couplings_ref, transfer_ref, basis_ref, *refs):
    came, out_ref, boxes = refs[:low], refs[low], refs[low + 1]
    columns = out_ref.shape[0]
    leaves, rank, size = basis_ref.shape
    high = boxes.shape[0] // low
    me = lax.axis_index("leaf")
    for k in range(low):
        tile = came[k][by_high.dense_tails : by_high.dense_box, :].astype(F32)
        for i in range(high):
            start = by_high.dense_box + i * by_high.half
            packed = came[k][start : start + by_high.half, :]
            last = tile[leaves + i : leaves + i + 1, :rank]
            boxes[i * low + k] = jnp.concatenate(
                [packed[:, :rank].astype(F32), packed[:, rank:].astype(F32), last], axis=0
            ).astype(BF16)
    far = jnp.zeros((columns, rank), F32)
    for f in range(couplings_ref.shape[1]):
        source = jnp.bitwise_xor(partner_ref[0, f], me)
        far += dot_t(boxes[source], couplings_ref[0, f])
    far = far.astype(BF16)
    down = [dot(far, transfer_ref[j]).astype(BF16) for j in range(leaves)]
    for j in range(leaves):
        cols = slice(j * size, (j + 1) * size)
        out_ref[:, cols] = base_ref[:, cols] + dot(down[j], basis_ref[j])


def across_kernel(came_own, *refs):
    out_ref = refs[-1]
    out_ref[...] = sum(ref[...].astype(F32) for ref in (came_own, *refs[:-1]))


def last_kernel(routes, devices, base_ref, *refs):
    by_low, by_high = routes
    high, low = grid_of(devices)
    came_high, came_low, out_ref = refs[: -low - 1], refs[-low - 1 : -1], refs[-1]
    leaves, split, main = by_low.leaves, by_low.rows, by_low.main
    size = base_ref.shape[1] // leaves
    tails = sum(came_low[k][by_high.dense_tails : by_high.dense_box, :].astype(F32) for k in range(low))
    for j in range(leaves):
        cols = slice(j * size, (j + 1) * size)
        upper = sum(ref[j * by_low.rows : (j + 1) * by_low.rows, :].astype(F32) for ref in came_high)
        lower = sum(came_low[k][j * by_high.rows : (j + 1) * by_high.rows, :].astype(F32) for k in range(low))
        out_ref[:split, cols] = base_ref[:split, cols] + upper
        out_ref[split:main, cols] = base_ref[split:main, cols] + lower
        out_ref[main:, cols] = base_ref[main:, cols] + tails[j : j + 1]


def call(kernel, out_shape, specs, operands, scratch, flops, room=None):
    outs = jax.tree.leaves(out_shape)
    nbytes = sum(a.size * a.dtype.itemsize for a in (*operands, *outs))
    limit = None if room is None else nbytes + room + 2**21
    return pl.pallas_call(
        kernel,
        out_shape=out_shape,
        in_specs=specs[0],
        out_specs=specs[1],
        scratch_shapes=scratch,
        compiler_params=pltpu.CompilerParams(vmem_limit_bytes=limit),
        cost_estimate=pl.CostEstimate(flops=flops, bytes_accessed=nbytes, transcendentals=0),
    )(*operands)


def per_device(
    probes, basis, transfer, local_blocks, remote_blocks, near_dest, near_leaf, couplings, far_list
):
    columns, points = probes.shape
    leaves, rank, size = basis.shape
    devices = lax.axis_size("leaf")
    main = columns // TILE * TILE
    routes = by_low, by_high = routes_of(devices, main, columns, leaves)
    high, low = grid_of(devices)
    blocks = remote_blocks.shape[0] * remote_blocks.shape[1]
    unit = 2 * columns * size * size
    like = lambda *arrays: [pltpu.VMEM(a.shape, a.dtype) for a in arrays]
    numbers = lambda *arrays: [pltpu.SMEM(a.shape, a.dtype) for a in arrays]
    sems = lambda count: [pltpu.SemaphoreType.DMA((count,))]
    relative = lambda x, way: lax.ppermute(x, "leaf", [(i, i ^ way) for i in range(devices)])
    message = lambda route: jax.ShapeDtypeStruct((route.depth, size), BF16)
    dense = lambda route: jax.ShapeDtypeStruct((route.dense_depth, size), BF16)

    def stacked(count, like_this):
        return pltpu.VMEM((count, *like_this.shape), like_this.dtype)

    dest, leaf = near_dest.T, near_leaf.T
    sent = call(
        functools.partial(products_kernel, routes, devices),
        [message(by_low)] * low + [message(by_high)] * high,
        ([ANY] * 6, [ANY] * (low + high)),
        (dest, leaf, probes, basis, transfer, remote_blocks),
        numbers(dest, leaf)
        + like(probes, basis, transfer, remote_blocks)
        + [
            stacked(low, message(by_low)),
            stacked(high, message(by_high)),
            pltpu.VMEM((high, by_high.meta - by_high.tails, size), F32),
            pltpu.SMEM((devices,), I32),
        ]
        + sems(7 + low + high),
        blocks * unit,
    )
    came_low, came_high = list(sent[:low]), list(sent[low:])
    planes = across_first(high)
    for k in range(1, low):
        came_low[k] = relative(came_low[k], k)
    for k in planes[1:]:
        came_high[k] = relative(came_high[k], k * low)
    came_low[0], came_low[1], came_high[0] = call(
        keep_kernel,
        (message(by_low), message(by_low), message(by_high)),
        ([VMEM] * 3, (VMEM,) * 3),
        (came_low[0], came_low[1], came_high[0]),
        [],
        0,
        0,
    )

    def summed(route, planes, came):
        total = jax.ShapeDtypeStruct((route.fan, (leaves + 1) * route.rows, size), F32)
        tails = jax.ShapeDtypeStruct((route.fan, max(TILE, route.dense_box - route.dense_tails), size), F32)
        ways = len(came)
        return list(
            call(
                functools.partial(sum_kernel, route, planes, ways),
                [dense(route)] * route.fan,
                ([VMEM] * ways, [VMEM] * route.fan),
                came,
                [pltpu.VMEM((ways, size), I32), pltpu.SMEM((ways, size), I32)]
                + like(total, tails)
                + [pltpu.SemaphoreType.DMA(())],
                devices * CAP * route.rows * size,
                4 * (total.size + tails.size),
            )
        )

    to_high = summed(by_low, None, came_low)
    came_high[0], to_high[0] = lax.optimization_barrier((came_high[0], to_high[0]))
    to_low = summed(by_high, planes, [came_high[k] for k in planes])
    base_shape = jax.ShapeDtypeStruct((columns, points), F32)
    probes_then, to_low[0] = lax.optimization_barrier((probes, to_low[0]))
    base = call(
        local_kernel, base_shape, ([VMEM] * 2, VMEM), (probes_then, local_blocks), [], leaves * leaves * unit, 0
    )
    for k in planes[1:]:
        to_high[k] = relative(to_high[k], k * low)
    for k in range(1, low):
        to_low[k] = relative(to_low[k], k)

    boxes = jax.ShapeDtypeStruct((devices, columns, rank), BF16)
    base = call(
        functools.partial(far_kernel, by_high, low),
        base_shape,
        ([SMEM] + [VMEM] * (4 + low), VMEM),
        (far_list, base, couplings, transfer, basis, *to_low),
        like(boxes),
        4 * leaves * unit,
        4 * boxes.size,
    )
    across = call(
        across_kernel,
        jax.ShapeDtypeStruct((by_low.dense_depth, size), F32),
        ([VMEM] * (high - 1), VMEM),
        [to_high[k] for k in planes[:-1]],
        [],
        HEAVY,
        0,
    )
    return call(
        functools.partial(last_kernel, routes, devices),
        base_shape,
        ([VMEM] * (3 + low), VMEM),
        (base, across, to_high[1], *to_low),
        [],
        devices * columns * size,
        0,
    )


def solution(mesh):
    placed = (
        P(None, ("grp", "leaf")),
        P(("grp", "leaf"), None, None),
        P(("grp", "leaf"), None, None),
        P(("grp", "leaf"), None, None, None),
        P(("grp", "leaf"), None, None, None),
        P(("grp", "leaf"), None),
        P(("grp", "leaf"), None),
        P(("grp", "leaf"), None, None, None),
        P(("grp", "leaf"), None),
    )
    return jax.shard_map(
        per_device, mesh=mesh, in_specs=placed, out_specs=P(None, ("grp", "leaf")), check_vma=False
    )
```

```python
import functools

import jax
import jax.numpy as jnp
from jax import lax
from jax.experimental import pallas as pl
from jax.experimental.pallas import tpu as pltpu
from jax.sharding import PartitionSpec as P

CAP = 4
TILE = 16
HEAVY = 4 * 10**9

F32 = jnp.float32
BF16 = jnp.bfloat16
I32 = jnp.int32

ANY = pl.BlockSpec(memory_space=pl.ANY)
VMEM = pl.BlockSpec(memory_space=pltpu.VMEM)
SMEM = pl.BlockSpec(memory_space=pltpu.SMEM)


def dot_t(lhs, rhs):
    return lax.dot_general(lhs, rhs, (((1,), (1,)), ((), ())), preferred_element_type=F32)


def dot(lhs, rhs):
    return lax.dot_general(lhs, rhs, (((1,), (0,)), ((), ())), preferred_element_type=F32)


class Copies:
    def __init__(self, sems):
        self.sems, self.used = sems, 0

    def start(self, src, dst):
        copy = pltpu.make_async_copy(src, dst, self.sems.at[self.used])
        self.used += 1
        copy.start()
        return copy


def grid_of(devices):
    low = 1 << (devices.bit_length() // 2)
    return devices // low, low


def up(rows):
    return -(-rows // TILE) * TILE


class Route:
    def __init__(self, first, last, fan, extra, main, columns, leaves, sources):
        self.first, self.rows, self.fan, self.extra, self.main = first, last - first, fan, extra, main
        self.leaves, self.half = leaves, main // 2
        slots = fan * CAP
        self.tails = slots * self.rows
        self.meta = self.tails + (up(slots) if extra else 0)
        self.box = self.meta + TILE
        self.depth = self.box + (self.half if extra else 0)
        self.dense_tails = leaves * self.rows
        self.dense_box = self.dense_tails + (up(leaves + sources) if extra else 0)
        self.dense_depth = self.dense_box + (sources * self.half if extra else 0)


def routes_of(devices, main, columns, leaves):
    high, low = grid_of(devices)
    split = up(main * 3 // 4)
    return (
        Route(0, split, high, False, main, columns, leaves, low),
        Route(split, main, low, True, main, columns, leaves, high),
    )


def products_kernel(routes, devices, *refs):
    dest_hbm, leaf_hbm, probes_hbm, basis_hbm, transfer_hbm, blocks_hbm = refs[:6]
    outs = refs[6:-11]
    (
        dest_ref, leaf_ref, probes_ref, basis_ref, transfer_ref, blocks_ref,
        send_low, send_high, tails, count, sems,
    ) = refs[-11:]
    by_low, by_high = routes
    high, low = grid_of(devices)
    me = lax.axis_index("leaf")
    main = by_high.main
    leaves, per_leaf, size = blocks_ref.shape[:3]
    columns, rank = probes_ref.shape[0], basis_ref.shape[1]
    copies = Copies(sems)
    chunk = leaves // 2
    arrivals = []
    early = [
        copies.start(probes_hbm, probes_ref),
        copies.start(dest_hbm, dest_ref),
        copies.start(leaf_hbm, leaf_ref),
    ]
    for j in range(0, leaves, chunk):
        arrivals.append(copies.start(blocks_hbm.at[pl.ds(j, chunk)], blocks_ref.at[pl.ds(j, chunk)]))
        if j == 0:
            early += [copies.start(basis_hbm, basis_ref), copies.start(transfer_hbm, transfer_ref)]

    @pl.loop(0, devices)
    def _(i):
        count[i] = 0

    tails[...] = jnp.zeros(tails.shape, F32)
    for copy in early:
        copy.wait()
    box = jnp.zeros((columns, rank), F32)

    numbers = jnp.full((-(-(low + high) // 8) * 8, size), leaves, I32)
    row = lax.broadcasted_iota(I32, numbers.shape, 0)
    lane = lax.broadcasted_iota(I32, numbers.shape, 1)
    for j in range(leaves):
        if j % chunk == 0:
            arrivals[j // chunk].wait()
        x = probes_ref[:, j * size : (j + 1) * size]
        box += dot_t(dot_t(x, basis_ref[j]).astype(BF16), transfer_ref[j])
        for first in range(0, per_leaf, 4):
            many = min(4, per_leaf - first)
            rhs = blocks_ref[j, first : first + many].reshape(many * size, size)
            product = dot_t(x, rhs)
            for b in range(many):
                target = jnp.bitwise_xor(dest_ref[first + b, j], me)
                slot = count[target]
                count[target] = slot + 1
                to_high = lax.shift_right_logical(target, low.bit_length() - 1)
                to_low = jnp.bitwise_and(target, low - 1)
                block = product[:, b * size : (b + 1) * size]
                piece = block[:main].astype(BF16)
                number = leaf_ref[first + b, j]

                at = to_high * CAP + slot
                rows = pl.ds(pl.multiple_of(at * by_low.rows, TILE), by_low.rows)
                send_low[to_low, rows, :] = piece[: by_low.rows]
                numbers = jnp.where((row == to_low) & (lane == at), number, numbers)

                at = to_low * CAP + slot
                rows = pl.ds(pl.multiple_of(at * by_high.rows, TILE), by_high.rows)
                send_high[to_high, rows, :] = piece[by_low.rows :]
                tails[to_high, pl.ds(at, 1), :] = block[main:]
                numbers = jnp.where((row == low + to_high) & (lane == at), number, numbers)

    half = by_high.half
    packed = jnp.concatenate([box[:half], box[half:main]], axis=1).astype(BF16)
    last = jnp.concatenate([box[main:], jnp.zeros_like(box[main:])], axis=1)
    numbers = numbers.astype(F32)
    blank = jnp.zeros((TILE - 2, size), F32)
    for i in range(low):
        tile = jnp.concatenate([numbers[i : i + 1], last, blank], axis=0)
        send_low[i, by_low.meta : by_low.box, :] = tile.astype(BF16)
    for i in range(high):
        tile = jnp.concatenate([numbers[low + i : low + i + 1], last, blank], axis=0)
        send_high[i, by_high.tails : by_high.meta, :] = tails[i].astype(BF16)
        send_high[i, by_high.meta : by_high.box, :] = tile.astype(BF16)
        send_high[i, by_high.box :, :] = packed
    leaving = [copies.start(send_low.at[i], outs[i]) for i in range(low)]
    leaving += [copies.start(send_high.at[i], outs[low + i]) for i in range(high)]
    for copy in leaving:
        copy.wait()


def sum_route(route, came, planes, outs, base, leaf_ref, total, tails):
    leaves, half, ways = route.leaves, route.half, len(came)
    for i in range(ways):
        if route.extra:
            tail = came[i][route.tails : route.meta, :].astype(F32)
        for k in range(route.fan):
            for slot in range(CAP):
                at = k * CAP + slot
                leaf = leaf_ref[base + i, at]
                rows = pl.ds(pl.multiple_of(leaf * route.rows, TILE), route.rows)
                total[k, rows, :] += came[i][at * route.rows : (at + 1) * route.rows, :].astype(F32)
                if route.extra:
                    tails[k, pl.ds(leaf, 1), :] += tail[at : at + 1]

    for k in range(route.fan):
        outs[k][: route.dense_tails, :] = total[k, : route.dense_tails, :].astype(BF16)
        if route.extra:
            for i in range(ways):
                last = came[i][route.meta : route.box, :].astype(F32)[1:2]
                at = planes[i]
                tails[k, leaves + at : leaves + at + 1, :] = last
                start = route.dense_box + at * half
                outs[k][start : start + half, :] = came[i][route.box :, :]
            outs[k][route.dense_tails : route.dense_box, :] = tails[k].astype(BF16)


def across_first(high):
    return [0, *range(2, high), 1]


def sum_kernel(route, planes, ways, *refs):
    came, outs = refs[:ways], refs[ways:-5]
    meta, leaf_ref, total, tails, late = refs[-5:]
    for i, ref in enumerate(came):
        meta[i : i + 1, :] = ref[route.meta : route.box, :].astype(F32)[:1].astype(I32)
    numbers = pltpu.make_async_copy(meta, leaf_ref, late)
    numbers.start()
    for ref in (total, tails):
        ref[...] = jnp.zeros(ref.shape, F32)
    numbers.wait()
    sum_route(route, came, planes, outs, 0, leaf_ref, total, tails)


def keep_kernel(*refs):
    half = len(refs) // 2
    for came, kept in zip(refs[:half], refs[half:]):
        kept[...] = came[...]


def local_kernel(probes_ref, local_ref, out_ref):
    leaves, size = local_ref.shape[0], local_ref.shape[2]
    for i in range(0, leaves, 2):
        total = 0.0
        for c in range(0, leaves, 2):
            square = jnp.concatenate(
                [jnp.concatenate([local_ref[r, c], local_ref[r, c + 1]], axis=1) for r in (i, i + 1)], axis=0
            )
            total += dot_t(probes_ref[:, c * size : (c + 2) * size], square)
        out_ref[:, i * size : (i + 2) * size] = total


def far_kernel(by_high, low, partner_ref, base_ref, couplings_ref, transfer_ref, basis_ref, *refs):
    came, out_ref, boxes = refs[:low], refs[low], refs[low + 1]
    columns = out_ref.shape[0]
    leaves, rank, size = basis_ref.shape
    high = boxes.shape[0] // low
    me = lax.axis_index("leaf")
    for k in range(low):
        tile = came[k][by_high.dense_tails : by_high.dense_box, :].astype(F32)
        for i in range(high):
            start = by_high.dense_box + i * by_high.half
            packed = came[k][start : start + by_high.half, :]
            last = tile[leaves + i : leaves + i + 1, :rank]
            boxes[i * low + k] = jnp.concatenate(
                [packed[:, :rank].astype(F32), packed[:, rank:].astype(F32), last], axis=0
            ).astype(BF16)
    far = jnp.zeros((columns, rank), F32)
    for f in range(couplings_ref.shape[1]):
        source = jnp.bitwise_xor(partner_ref[0, f], me)
        far += dot_t(boxes[source], couplings_ref[0, f])
    far = far.astype(BF16)
    down = [dot(far, transfer_ref[j]).astype(BF16) for j in range(leaves)]
    for j in range(leaves):
        cols = slice(j * size, (j + 1) * size)
        out_ref[:, cols] = base_ref[:, cols] + dot(down[j], basis_ref[j])


def across_kernel(came_own, *refs):
    out_ref = refs[-1]
    out_ref[...] = sum(ref[...].astype(F32) for ref in (came_own, *refs[:-1]))


def last_kernel(routes, devices, base_ref, *refs):
    by_low, by_high = routes
    high, low = grid_of(devices)
    came_high, came_low, out_ref = refs[: -low - 1], refs[-low - 1 : -1], refs[-1]
    leaves, split, main = by_low.leaves, by_low.rows, by_low.main
    size = base_ref.shape[1] // leaves
    tails = sum(came_low[k][by_high.dense_tails : by_high.dense_box, :].astype(F32) for k in range(low))
    for j in range(leaves):
        cols = slice(j * size, (j + 1) * size)
        upper = sum(ref[j * by_low.rows : (j + 1) * by_low.rows, :].astype(F32) for ref in came_high)
        lower = sum(came_low[k][j * by_high.rows : (j + 1) * by_high.rows, :].astype(F32) for k in range(low))
        out_ref[:split, cols] = base_ref[:split, cols] + upper
        out_ref[split:main, cols] = base_ref[split:main, cols] + lower
        out_ref[main:, cols] = base_ref[main:, cols] + tails[j : j + 1]


def call(kernel, out_shape, specs, operands, scratch, flops, room=None):
    outs = jax.tree.leaves(out_shape)
    nbytes = sum(a.size * a.dtype.itemsize for a in (*operands, *outs))
    limit = None if room is None else nbytes + room + 2**21
    return pl.pallas_call(
        kernel,
        out_shape=out_shape,
        in_specs=specs[0],
        out_specs=specs[1],
        scratch_shapes=scratch,
        compiler_params=pltpu.CompilerParams(vmem_limit_bytes=limit),
        cost_estimate=pl.CostEstimate(flops=flops, bytes_accessed=nbytes, transcendentals=0),
    )(*operands)


def per_device(
    probes, basis, transfer, local_blocks, remote_blocks, near_dest, near_leaf, couplings, far_list
):
    columns, points = probes.shape
    leaves, rank, size = basis.shape
    devices = lax.axis_size("leaf")
    main = columns // TILE * TILE
    routes = by_low, by_high = routes_of(devices, main, columns, leaves)
    high, low = grid_of(devices)
    blocks = remote_blocks.shape[0] * remote_blocks.shape[1]
    unit = 2 * columns * size * size
    like = lambda *arrays: [pltpu.VMEM(a.shape, a.dtype) for a in arrays]
    numbers = lambda *arrays: [pltpu.SMEM(a.shape, a.dtype) for a in arrays]
    sems = lambda count: [pltpu.SemaphoreType.DMA((count,))]
    relative = lambda x, way: lax.ppermute(x, "leaf", [(i, i ^ way) for i in range(devices)])
    message = lambda route: jax.ShapeDtypeStruct((route.depth, size), BF16)
    dense = lambda route: jax.ShapeDtypeStruct((route.dense_depth, size), BF16)

    def stacked(count, like_this):
        return pltpu.VMEM((count, *like_this.shape), like_this.dtype)

    dest, leaf = near_dest.T, near_leaf.T
    sent = call(
        functools.partial(products_kernel, routes, devices),
        [message(by_low)] * low + [message(by_high)] * high,
        ([ANY] * 6, [ANY] * (low + high)),
        (dest, leaf, probes, basis, transfer, remote_blocks),
        numbers(dest, leaf)
        + like(probes, basis, transfer, remote_blocks)
        + [
            stacked(low, message(by_low)),
            stacked(high, message(by_high)),
            pltpu.VMEM((high, by_high.meta - by_high.tails, size), F32),
            pltpu.SMEM((devices,), I32),
        ]
        + sems(7 + low + high),
        blocks * unit,
    )
    came_low, came_high = list(sent[:low]), list(sent[low:])
    planes = across_first(high)
    for k in range(1, low):
        came_low[k] = relative(came_low[k], k)
    for k in planes[1:]:
        came_high[k] = relative(came_high[k], k * low)
    came_low[0], came_low[1], came_high[0] = call(
        keep_kernel,
        (message(by_low), message(by_low), message(by_high)),
        ([VMEM] * 3, (VMEM,) * 3),
        (came_low[0], came_low[1], came_high[0]),
        [],
        0,
        0,
    )

    def summed(route, planes, came):
        total = jax.ShapeDtypeStruct((route.fan, (leaves + 1) * route.rows, size), F32)
        tails = jax.ShapeDtypeStruct((route.fan, max(TILE, route.dense_box - route.dense_tails), size), F32)
        ways = len(came)
        return list(
            call(
                functools.partial(sum_kernel, route, planes, ways),
                [dense(route)] * route.fan,
                ([VMEM] * ways, [VMEM] * route.fan),
                came,
                [pltpu.VMEM((ways, size), I32), pltpu.SMEM((ways, size), I32)]
                + like(total, tails)
                + [pltpu.SemaphoreType.DMA(())],
                devices * CAP * route.rows * size,
                4 * (total.size + tails.size),
            )
        )

    to_high = summed(by_low, None, came_low)
    came_high[0], to_high[0] = lax.optimization_barrier((came_high[0], to_high[0]))
    to_low = summed(by_high, planes, [came_high[k] for k in planes])
    base_shape = jax.ShapeDtypeStruct((columns, points), F32)
    for k in planes[1:]:
        to_high[k] = relative(to_high[k], k * low)
    for k in range(1, low):
        to_low[k] = relative(to_low[k], k)

    probes_then, to_low[1] = lax.optimization_barrier((probes, to_low[1]))
    base = call(
        local_kernel, base_shape, ([VMEM] * 2, VMEM), (probes_then, local_blocks), [], leaves * leaves * unit, 0
    )
    boxes = jax.ShapeDtypeStruct((devices, columns, rank), BF16)
    base = call(
        functools.partial(far_kernel, by_high, low),
        base_shape,
        ([SMEM] + [VMEM] * (4 + low), VMEM),
        (far_list, base, couplings, transfer, basis, *to_low),
        like(boxes),
        4 * leaves * unit,
        4 * boxes.size,
    )
    across = call(
        across_kernel,
        jax.ShapeDtypeStruct((by_low.dense_depth, size), F32),
        ([VMEM] * (high - 1), VMEM),
        [to_high[k] for k in planes[:-1]],
        [],
        HEAVY,
        0,
    )
    return call(
        functools.partial(last_kernel, routes, devices),
        base_shape,
        ([VMEM] * (3 + low), VMEM),
        (base, across, to_high[1], *to_low),
        [],
        devices * columns * size,
        0,
    )


def solution(mesh):
    placed = (
        P(None, ("grp", "leaf")),
        P(("grp", "leaf"), None, None),
        P(("grp", "leaf"), None, None),
        P(("grp", "leaf"), None, None, None),
        P(("grp", "leaf"), None, None, None),
        P(("grp", "leaf"), None),
        P(("grp", "leaf"), None),
        P(("grp", "leaf"), None, None, None),
        P(("grp", "leaf"), None),
    )
    return jax.shard_map(
        per_device, mesh=mesh, in_specs=placed, out_specs=P(None, ("grp", "leaf")), check_vma=False
    )
```

```python
import functools

import jax
import jax.numpy as jnp
from jax import lax
from jax.experimental import pallas as pl
from jax.experimental.pallas import tpu as pltpu
from jax.sharding import PartitionSpec as P

CAP = 4
TILE = 16
HEAVY = 4 * 10**9

F32 = jnp.float32
BF16 = jnp.bfloat16
I32 = jnp.int32

ANY = pl.BlockSpec(memory_space=pl.ANY)
VMEM = pl.BlockSpec(memory_space=pltpu.VMEM)
SMEM = pl.BlockSpec(memory_space=pltpu.SMEM)


def dot_t(lhs, rhs):
    return lax.dot_general(lhs, rhs, (((1,), (1,)), ((), ())), preferred_element_type=F32)


def dot(lhs, rhs):
    return lax.dot_general(lhs, rhs, (((1,), (0,)), ((), ())), preferred_element_type=F32)


class Copies:
    def __init__(self, sems):
        self.sems, self.used = sems, 0

    def start(self, src, dst):
        copy = pltpu.make_async_copy(src, dst, self.sems.at[self.used])
        self.used += 1
        copy.start()
        return copy


def grid_of(devices):
    low = 1 << (devices.bit_length() // 2)
    return devices // low, low


def up(rows):
    return -(-rows // TILE) * TILE


class Route:
    def __init__(self, first, last, fan, extra, main, columns, leaves, sources):
        self.first, self.rows, self.fan, self.extra, self.main = first, last - first, fan, extra, main
        self.leaves, self.half = leaves, main // 2
        slots = fan * CAP
        self.tails = slots * self.rows
        self.meta = self.tails + (up(slots) if extra else 0)
        self.box = self.meta + TILE
        self.depth = self.box + (self.half if extra else 0)
        self.dense_tails = leaves * self.rows
        self.dense_box = self.dense_tails + (up(leaves + sources) if extra else 0)
        self.dense_depth = self.dense_box + (sources * self.half if extra else 0)


def routes_of(devices, main, columns, leaves):
    high, low = grid_of(devices)
    split = up(main * 3 // 4)
    return (
        Route(0, split, high, False, main, columns, leaves, low),
        Route(split, main, low, True, main, columns, leaves, high),
    )


def products_kernel(routes, devices, *refs):
    dest_hbm, leaf_hbm, probes_hbm, basis_hbm, transfer_hbm, blocks_hbm = refs[:6]
    outs = refs[6:-11]
    (
        dest_ref, leaf_ref, probes_ref, basis_ref, transfer_ref, blocks_ref,
        send_low, send_high, tails, count, sems,
    ) = refs[-11:]
    by_low, by_high = routes
    high, low = grid_of(devices)
    me = lax.axis_index("leaf")
    main = by_high.main
    leaves, per_leaf, size = blocks_ref.shape[:3]
    columns, rank = probes_ref.shape[0], basis_ref.shape[1]
    copies = Copies(sems)
    cuts = (0, leaves // 4, leaves)
    arrivals = {}
    early = [
        copies.start(probes_hbm, probes_ref),
        copies.start(dest_hbm, dest_ref),
        copies.start(leaf_hbm, leaf_ref),
    ]
    for j, after in zip(cuts, cuts[1:]):
        part = pl.ds(j, after - j)
        arrivals[j] = copies.start(blocks_hbm.at[part], blocks_ref.at[part])
        if j == 0:
            early += [copies.start(basis_hbm, basis_ref), copies.start(transfer_hbm, transfer_ref)]

    @pl.loop(0, devices)
    def _(i):
        count[i] = 0

    tails[...] = jnp.zeros(tails.shape, F32)
    for copy in early:
        copy.wait()
    box = jnp.zeros((columns, rank), F32)

    numbers = jnp.full((-(-(low + high) // 8) * 8, size), leaves, I32)
    row = lax.broadcasted_iota(I32, numbers.shape, 0)
    lane = lax.broadcasted_iota(I32, numbers.shape, 1)
    for j in range(leaves):
        if j in arrivals:
            arrivals[j].wait()
        x = probes_ref[:, j * size : (j + 1) * size]
        box += dot_t(dot_t(x, basis_ref[j]).astype(BF16), transfer_ref[j])
        for first in range(0, per_leaf, 4):
            many = min(4, per_leaf - first)
            rhs = blocks_ref[j, first : first + many].reshape(many * size, size)
            product = dot_t(x, rhs)
            for b in range(many):
                target = jnp.bitwise_xor(dest_ref[first + b, j], me)
                slot = count[target]
                count[target] = slot + 1
                to_high = lax.shift_right_logical(target, low.bit_length() - 1)
                to_low = jnp.bitwise_and(target, low - 1)
                block = product[:, b * size : (b + 1) * size]
                piece = block[:main].astype(BF16)
                number = leaf_ref[first + b, j]

                at = to_high * CAP + slot
                rows = pl.ds(pl.multiple_of(at * by_low.rows, TILE), by_low.rows)
                send_low[to_low, rows, :] = piece[: by_low.rows]
                numbers = jnp.where((row == to_low) & (lane == at), number, numbers)

                at = to_low * CAP + slot
                rows = pl.ds(pl.multiple_of(at * by_high.rows, TILE), by_high.rows)
                send_high[to_high, rows, :] = piece[by_low.rows :]
                tails[to_high, pl.ds(at, 1), :] = block[main:]
                numbers = jnp.where((row == low + to_high) & (lane == at), number, numbers)

    half = by_high.half
    packed = jnp.concatenate([box[:half], box[half:main]], axis=1).astype(BF16)
    last = jnp.concatenate([box[main:], jnp.zeros_like(box[main:])], axis=1)
    numbers = numbers.astype(F32)
    blank = jnp.zeros((TILE - 2, size), F32)
    for i in range(low):
        tile = jnp.concatenate([numbers[i : i + 1], last, blank], axis=0)
        send_low[i, by_low.meta : by_low.box, :] = tile.astype(BF16)
    for i in range(high):
        tile = jnp.concatenate([numbers[low + i : low + i + 1], last, blank], axis=0)
        send_high[i, by_high.tails : by_high.meta, :] = tails[i].astype(BF16)
        send_high[i, by_high.meta : by_high.box, :] = tile.astype(BF16)
        send_high[i, by_high.box :, :] = packed
    leaving = [copies.start(send_low.at[i], outs[i]) for i in range(low)]
    leaving += [copies.start(send_high.at[i], outs[low + i]) for i in range(high)]
    for copy in leaving:
        copy.wait()


def sum_route(route, came, planes, outs, base, leaf_ref, total, tails):
    leaves, half, ways = route.leaves, route.half, len(came)
    for i in range(ways):
        if route.extra:
            tail = came[i][route.tails : route.meta, :].astype(F32)
        for k in range(route.fan):
            for slot in range(CAP):
                at = k * CAP + slot
                leaf = leaf_ref[base + i, at]
                rows = pl.ds(pl.multiple_of(leaf * route.rows, TILE), route.rows)
                total[k, rows, :] += came[i][at * route.rows : (at + 1) * route.rows, :].astype(F32)
                if route.extra:
                    tails[k, pl.ds(leaf, 1), :] += tail[at : at + 1]

    for k in range(route.fan):
        outs[k][: route.dense_tails, :] = total[k, : route.dense_tails, :].astype(BF16)
        if route.extra:
            for i in range(ways):
                last = came[i][route.meta : route.box, :].astype(F32)[1:2]
                at = planes[i]
                tails[k, leaves + at : leaves + at + 1, :] = last
                start = route.dense_box + at * half
                outs[k][start : start + half, :] = came[i][route.box :, :]
            outs[k][route.dense_tails : route.dense_box, :] = tails[k].astype(BF16)


def across_first(high):
    return [0, *range(2, high), 1]


def sum_kernel(route, planes, ways, *refs):
    came, outs = refs[:ways], refs[ways:-5]
    meta, leaf_ref, total, tails, late = refs[-5:]
    for i, ref in enumerate(came):
        meta[i : i + 1, :] = ref[route.meta : route.box, :].astype(F32)[:1].astype(I32)
    numbers = pltpu.make_async_copy(meta, leaf_ref, late)
    numbers.start()
    for ref in (total, tails):
        ref[...] = jnp.zeros(ref.shape, F32)
    numbers.wait()
    sum_route(route, came, planes, outs, 0, leaf_ref, total, tails)


def keep_kernel(*refs):
    half = len(refs) // 2
    for came, kept in zip(refs[:half], refs[half:]):
        kept[...] = came[...]


def local_kernel(probes_ref, local_ref, out_ref):
    leaves, size = local_ref.shape[0], local_ref.shape[2]
    for i in range(0, leaves, 2):
        total = 0.0
        for c in range(0, leaves, 2):
            square = jnp.concatenate(
                [jnp.concatenate([local_ref[r, c], local_ref[r, c + 1]], axis=1) for r in (i, i + 1)], axis=0
            )
            total += dot_t(probes_ref[:, c * size : (c + 2) * size], square)
        out_ref[:, i * size : (i + 2) * size] = total


def far_kernel(by_high, low, partner_ref, base_ref, couplings_ref, transfer_ref, basis_ref, *refs):
    came, out_ref, boxes = refs[:low], refs[low], refs[low + 1]
    columns = out_ref.shape[0]
    leaves, rank, size = basis_ref.shape
    high = boxes.shape[0] // low
    me = lax.axis_index("leaf")
    for k in range(low):
        tile = came[k][by_high.dense_tails : by_high.dense_box, :].astype(F32)
        for i in range(high):
            start = by_high.dense_box + i * by_high.half
            packed = came[k][start : start + by_high.half, :]
            last = tile[leaves + i : leaves + i + 1, :rank]
            boxes[i * low + k] = jnp.concatenate(
                [packed[:, :rank].astype(F32), packed[:, rank:].astype(F32), last], axis=0
            ).astype(BF16)
    far = jnp.zeros((columns, rank), F32)
    for f in range(couplings_ref.shape[1]):
        source = jnp.bitwise_xor(partner_ref[0, f], me)
        far += dot_t(boxes[source], couplings_ref[0, f])
    far = far.astype(BF16)
    down = [dot(far, transfer_ref[j]).astype(BF16) for j in range(leaves)]
    for j in range(leaves):
        cols = slice(j * size, (j + 1) * size)
        out_ref[:, cols] = base_ref[:, cols] + dot(down[j], basis_ref[j])


def across_kernel(came_own, *refs):
    out_ref = refs[-1]
    out_ref[...] = sum(ref[...].astype(F32) for ref in (came_own, *refs[:-1]))


def last_kernel(routes, devices, base_ref, *refs):
    by_low, by_high = routes
    high, low = grid_of(devices)
    came_high, came_low, out_ref = refs[: -low - 1], refs[-low - 1 : -1], refs[-1]
    leaves, split, main = by_low.leaves, by_low.rows, by_low.main
    size = base_ref.shape[1] // leaves
    tails = sum(came_low[k][by_high.dense_tails : by_high.dense_box, :].astype(F32) for k in range(low))
    for j in range(leaves):
        cols = slice(j * size, (j + 1) * size)
        upper = sum(ref[j * by_low.rows : (j + 1) * by_low.rows, :].astype(F32) for ref in came_high)
        lower = sum(came_low[k][j * by_high.rows : (j + 1) * by_high.rows, :].astype(F32) for k in range(low))
        out_ref[:split, cols] = base_ref[:split, cols] + upper
        out_ref[split:main, cols] = base_ref[split:main, cols] + lower
        out_ref[main:, cols] = base_ref[main:, cols] + tails[j : j + 1]


def call(kernel, out_shape, specs, operands, scratch, flops, room=None):
    outs = jax.tree.leaves(out_shape)
    nbytes = sum(a.size * a.dtype.itemsize for a in (*operands, *outs))
    limit = None if room is None else nbytes + room + 2**21
    return pl.pallas_call(
        kernel,
        out_shape=out_shape,
        in_specs=specs[0],
        out_specs=specs[1],
        scratch_shapes=scratch,
        compiler_params=pltpu.CompilerParams(vmem_limit_bytes=limit),
        cost_estimate=pl.CostEstimate(flops=flops, bytes_accessed=nbytes, transcendentals=0),
    )(*operands)


def per_device(
    probes, basis, transfer, local_blocks, remote_blocks, near_dest, near_leaf, couplings, far_list
):
    columns, points = probes.shape
    leaves, rank, size = basis.shape
    devices = lax.axis_size("leaf")
    main = columns // TILE * TILE
    routes = by_low, by_high = routes_of(devices, main, columns, leaves)
    high, low = grid_of(devices)
    blocks = remote_blocks.shape[0] * remote_blocks.shape[1]
    unit = 2 * columns * size * size
    like = lambda *arrays: [pltpu.VMEM(a.shape, a.dtype) for a in arrays]
    numbers = lambda *arrays: [pltpu.SMEM(a.shape, a.dtype) for a in arrays]
    sems = lambda count: [pltpu.SemaphoreType.DMA((count,))]
    relative = lambda x, way: lax.ppermute(x, "leaf", [(i, i ^ way) for i in range(devices)])
    message = lambda route: jax.ShapeDtypeStruct((route.depth, size), BF16)
    dense = lambda route: jax.ShapeDtypeStruct((route.dense_depth, size), BF16)

    def stacked(count, like_this):
        return pltpu.VMEM((count, *like_this.shape), like_this.dtype)

    dest, leaf = near_dest.T, near_leaf.T
    sent = call(
        functools.partial(products_kernel, routes, devices),
        [message(by_low)] * low + [message(by_high)] * high,
        ([ANY] * 6, [ANY] * (low + high)),
        (dest, leaf, probes, basis, transfer, remote_blocks),
        numbers(dest, leaf)
        + like(probes, basis, transfer, remote_blocks)
        + [
            stacked(low, message(by_low)),
            stacked(high, message(by_high)),
            pltpu.VMEM((high, by_high.meta - by_high.tails, size), F32),
            pltpu.SMEM((devices,), I32),
        ]
        + sems(7 + low + high),
        blocks * unit,
    )
    came_low, came_high = list(sent[:low]), list(sent[low:])
    planes = across_first(high)
    for k in range(1, low):
        came_low[k] = relative(came_low[k], k)
    came_low[0], came_high[0] = call(
        keep_kernel,
        (message(by_low), message(by_high)),
        ([VMEM] * 2, (VMEM,) * 2),
        (came_low[0], came_high[0]),
        [],
        0,
        0,
    )

    came_high[1], came_low[0] = lax.optimization_barrier((came_high[1], came_low[0]))
    for k in planes[1:]:
        came_high[k] = relative(came_high[k], k * low)

    def summed(route, planes, came):
        total = jax.ShapeDtypeStruct((route.fan, (leaves + 1) * route.rows, size), F32)
        tails = jax.ShapeDtypeStruct((route.fan, max(TILE, route.dense_box - route.dense_tails), size), F32)
        ways = len(came)
        return list(
            call(
                functools.partial(sum_kernel, route, planes, ways),
                [dense(route)] * route.fan,
                ([VMEM] * ways, [VMEM] * route.fan),
                came,
                [pltpu.VMEM((ways, size), I32), pltpu.SMEM((ways, size), I32)]
                + like(total, tails)
                + [pltpu.SemaphoreType.DMA(())],
                devices * CAP * route.rows * size,
                4 * (total.size + tails.size),
            )
        )

    to_high = summed(by_low, None, [came_low[k] for k in (0, *range(2, low), 1)])
    came_high[0], to_high[0] = lax.optimization_barrier((came_high[0], to_high[0]))
    to_low = summed(by_high, planes, [came_high[k] for k in planes])
    base_shape = jax.ShapeDtypeStruct((columns, points), F32)
    for k in planes[1:]:
        to_high[k] = relative(to_high[k], k * low)
    for k in range(1, low):
        to_low[k] = relative(to_low[k], k)

    probes_then, to_low[1] = lax.optimization_barrier((probes, to_low[1]))
    base = call(
        local_kernel, base_shape, ([VMEM] * 2, VMEM), (probes_then, local_blocks), [], leaves * leaves * unit, 0
    )
    boxes = jax.ShapeDtypeStruct((devices, columns, rank), BF16)
    base = call(
        functools.partial(far_kernel, by_high, low),
        base_shape,
        ([SMEM] + [VMEM] * (4 + low), VMEM),
        (far_list, base, couplings, transfer, basis, *to_low),
        like(boxes),
        4 * leaves * unit,
        4 * boxes.size,
    )
    across = call(
        across_kernel,
        jax.ShapeDtypeStruct((by_low.dense_depth, size), F32),
        ([VMEM] * (high - 1), VMEM),
        [to_high[k] for k in planes[:-1]],
        [],
        HEAVY,
        0,
    )
    return call(
        functools.partial(last_kernel, routes, devices),
        base_shape,
        ([VMEM] * (3 + low), VMEM),
        (base, across, to_high[1], *to_low),
        [],
        devices * columns * size,
        0,
    )


def solution(mesh):
    placed = (
        P(None, ("grp", "leaf")),
        P(("grp", "leaf"), None, None),
        P(("grp", "leaf"), None, None),
        P(("grp", "leaf"), None, None, None),
        P(("grp", "leaf"), None, None, None),
        P(("grp", "leaf"), None),
        P(("grp", "leaf"), None),
        P(("grp", "leaf"), None, None, None),
        P(("grp", "leaf"), None),
    )
    return jax.shard_map(
        per_device, mesh=mesh, in_specs=placed, out_specs=P(None, ("grp", "leaf")), check_vma=False
    )
```

```python
import functools

import jax
import jax.numpy as jnp
from jax import lax
from jax.experimental import pallas as pl
from jax.experimental.pallas import tpu as pltpu
from jax.sharding import PartitionSpec as P

CAP = 4
TILE = 16
HEAVY = 4 * 10**9

F32 = jnp.float32
BF16 = jnp.bfloat16
I32 = jnp.int32

ANY = pl.BlockSpec(memory_space=pl.ANY)
VMEM = pl.BlockSpec(memory_space=pltpu.VMEM)
SMEM = pl.BlockSpec(memory_space=pltpu.SMEM)


def dot_t(lhs, rhs):
    return lax.dot_general(lhs, rhs, (((1,), (1,)), ((), ())), preferred_element_type=F32)


def dot(lhs, rhs):
    return lax.dot_general(lhs, rhs, (((1,), (0,)), ((), ())), preferred_element_type=F32)


class Copies:
    def __init__(self, sems):
        self.sems, self.used = sems, 0

    def start(self, src, dst):
        copy = pltpu.make_async_copy(src, dst, self.sems.at[self.used])
        self.used += 1
        copy.start()
        return copy


def grid_of(devices):
    low = 1 << (devices.bit_length() // 2)
    return devices // low, low


def up(rows):
    return -(-rows // TILE) * TILE


class Route:
    def __init__(self, first, last, fan, extra, main, columns, leaves, sources):
        self.first, self.rows, self.fan, self.extra, self.main = first, last - first, fan, extra, main
        self.leaves, self.half = leaves, main // 2
        slots = fan * CAP
        self.tails = slots * self.rows
        self.meta = self.tails + (up(slots) if extra else 0)
        self.box = self.meta + TILE
        self.depth = self.box + (self.half if extra else 0)
        self.dense_tails = leaves * self.rows
        self.dense_box = self.dense_tails + (up(leaves + sources) if extra else 0)
        self.dense_depth = self.dense_box + (sources * self.half if extra else 0)


def routes_of(devices, main, columns, leaves):
    high, low = grid_of(devices)
    split = up(main * 3 // 4)
    return (
        Route(0, split, high, False, main, columns, leaves, low),
        Route(split, main, low, True, main, columns, leaves, high),
    )


def products_kernel(routes, devices, *refs):
    dest_hbm, leaf_hbm, probes_hbm, basis_hbm, transfer_hbm, blocks_hbm = refs[:6]
    outs = refs[6:-11]
    (
        dest_ref, leaf_ref, probes_ref, basis_ref, transfer_ref, blocks_ref,
        send_low, send_high, tails, count, sems,
    ) = refs[-11:]
    by_low, by_high = routes
    high, low = grid_of(devices)
    me = lax.axis_index("leaf")
    main = by_high.main
    leaves, per_leaf, size = blocks_ref.shape[:3]
    columns, rank = probes_ref.shape[0], basis_ref.shape[1]
    copies = Copies(sems)
    cuts = (0, leaves // 4, leaves)
    arrivals = {}
    early = [
        copies.start(probes_hbm, probes_ref),
        copies.start(dest_hbm, dest_ref),
        copies.start(leaf_hbm, leaf_ref),
    ]
    for j, after in zip(cuts, cuts[1:]):
        part = pl.ds(j, after - j)
        arrivals[j] = copies.start(blocks_hbm.at[part], blocks_ref.at[part])
        if j == 0:
            early += [copies.start(basis_hbm, basis_ref), copies.start(transfer_hbm, transfer_ref)]

    @pl.loop(0, devices)
    def _(i):
        count[i] = 0

    tails[...] = jnp.zeros(tails.shape, F32)
    for copy in early:
        copy.wait()
    box = jnp.zeros((columns, rank), F32)

    numbers = jnp.full((-(-(low + high) // 8) * 8, size), leaves, I32)
    row = lax.broadcasted_iota(I32, numbers.shape, 0)
    lane = lax.broadcasted_iota(I32, numbers.shape, 1)
    for j in range(leaves):
        if j in arrivals:
            arrivals[j].wait()
        x = probes_ref[:, j * size : (j + 1) * size]
        box += dot_t(dot_t(x, basis_ref[j]).astype(BF16), transfer_ref[j])
        for first in range(0, per_leaf, 4):
            many = min(4, per_leaf - first)
            rhs = blocks_ref[j, first : first + many].reshape(many * size, size)
            product = dot_t(x, rhs)
            for b in range(many):
                target = jnp.bitwise_xor(dest_ref[first + b, j], me)
                slot = count[target]
                count[target] = slot + 1
                to_high = lax.shift_right_logical(target, low.bit_length() - 1)
                to_low = jnp.bitwise_and(target, low - 1)
                block = product[:, b * size : (b + 1) * size]
                piece = block[:main].astype(BF16)
                number = leaf_ref[first + b, j]

                at = to_high * CAP + slot
                rows = pl.ds(pl.multiple_of(at * by_low.rows, TILE), by_low.rows)
                send_low[to_low, rows, :] = piece[: by_low.rows]
                numbers = jnp.where((row == to_low) & (lane == at), number, numbers)

                at = to_low * CAP + slot
                rows = pl.ds(pl.multiple_of(at * by_high.rows, TILE), by_high.rows)
                send_high[to_high, rows, :] = piece[by_low.rows :]
                tails[to_high, pl.ds(at, 1), :] = block[main:]
                numbers = jnp.where((row == low + to_high) & (lane == at), number, numbers)

    half = by_high.half
    packed = jnp.concatenate([box[:half], box[half:main]], axis=1).astype(BF16)
    last = jnp.concatenate([box[main:], jnp.zeros_like(box[main:])], axis=1)
    numbers = numbers.astype(F32)
    blank = jnp.zeros((TILE - 2, size), F32)
    for i in range(low):
        tile = jnp.concatenate([numbers[i : i + 1], last, blank], axis=0)
        send_low[i, by_low.meta : by_low.box, :] = tile.astype(BF16)
    for i in range(high):
        tile = jnp.concatenate([numbers[low + i : low + i + 1], last, blank], axis=0)
        send_high[i, by_high.tails : by_high.meta, :] = tails[i].astype(BF16)
        send_high[i, by_high.meta : by_high.box, :] = tile.astype(BF16)
        send_high[i, by_high.box :, :] = packed
    leaving = [copies.start(send_low.at[i], outs[i]) for i in range(low)]
    leaving += [copies.start(send_high.at[i], outs[low + i]) for i in range(high)]
    for copy in leaving:
        copy.wait()


def sum_route(route, came, planes, outs, base, leaf_ref, total, tails):
    leaves, half, ways = route.leaves, route.half, len(came)
    for i in range(ways):
        if route.extra:
            tail = came[i][route.tails : route.meta, :].astype(F32)
        for k in range(route.fan):
            for slot in range(CAP):
                at = k * CAP + slot
                leaf = leaf_ref[base + i, at]
                rows = pl.ds(pl.multiple_of(leaf * route.rows, TILE), route.rows)
                total[k, rows, :] += came[i][at * route.rows : (at + 1) * route.rows, :].astype(F32)
                if route.extra:
                    tails[k, pl.ds(leaf, 1), :] += tail[at : at + 1]

    for k in range(route.fan):
        outs[k][: route.dense_tails, :] = total[k, : route.dense_tails, :].astype(BF16)
        if route.extra:
            for i in range(ways):
                last = came[i][route.meta : route.box, :].astype(F32)[1:2]
                at = planes[i]
                tails[k, leaves + at : leaves + at + 1, :] = last
                start = route.dense_box + at * half
                outs[k][start : start + half, :] = came[i][route.box :, :]
            outs[k][route.dense_tails : route.dense_box, :] = tails[k].astype(BF16)


def across_first(high):
    return [0, *range(2, high), 1]


def sum_kernel(route, planes, ways, *refs):
    came, outs = refs[:ways], refs[ways:-5]
    meta, leaf_ref, total, tails, late = refs[-5:]
    for i, ref in enumerate(came):
        meta[i : i + 1, :] = ref[route.meta : route.box, :].astype(F32)[:1].astype(I32)
    numbers = pltpu.make_async_copy(meta, leaf_ref, late)
    numbers.start()
    for ref in (total, tails):
        ref[...] = jnp.zeros(ref.shape, F32)
    numbers.wait()
    sum_route(route, came, planes, outs, 0, leaf_ref, total, tails)


def keep_kernel(*refs):
    half = len(refs) // 2
    for came, kept in zip(refs[:half], refs[half:]):
        kept[...] = came[...]


def local_kernel(probes_ref, local_ref, out_ref):
    leaves, size = local_ref.shape[0], local_ref.shape[2]
    for i in range(0, leaves, 2):
        total = 0.0
        for c in range(0, leaves, 2):
            square = jnp.concatenate(
                [jnp.concatenate([local_ref[r, c], local_ref[r, c + 1]], axis=1) for r in (i, i + 1)], axis=0
            )
            total += dot_t(probes_ref[:, c * size : (c + 2) * size], square)
        out_ref[:, i * size : (i + 2) * size] = total


def far_kernel(by_high, low, partner_ref, base_ref, couplings_ref, transfer_ref, basis_ref, *refs):
    came, out_ref, boxes = refs[:low], refs[low], refs[low + 1]
    columns = out_ref.shape[0]
    leaves, rank, size = basis_ref.shape
    high = boxes.shape[0] // low
    me = lax.axis_index("leaf")
    for k in range(low):
        tile = came[k][by_high.dense_tails : by_high.dense_box, :].astype(F32)
        for i in range(high):
            start = by_high.dense_box + i * by_high.half
            packed = came[k][start : start + by_high.half, :]
            last = tile[leaves + i : leaves + i + 1, :rank]
            boxes[i * low + k] = jnp.concatenate(
                [packed[:, :rank].astype(F32), packed[:, rank:].astype(F32), last], axis=0
            ).astype(BF16)
    far = jnp.zeros((columns, rank), F32)
    for f in range(couplings_ref.shape[1]):
        source = jnp.bitwise_xor(partner_ref[0, f], me)
        far += dot_t(boxes[source], couplings_ref[0, f])
    far = far.astype(BF16)
    down = [dot(far, transfer_ref[j]).astype(BF16) for j in range(leaves)]
    for j in range(leaves):
        cols = slice(j * size, (j + 1) * size)
        out_ref[:, cols] = base_ref[:, cols] + dot(down[j], basis_ref[j])


def across_kernel(came_own, *refs):
    out_ref = refs[-1]
    out_ref[...] = sum(ref[...].astype(F32) for ref in (came_own, *refs[:-1]))


def last_kernel(routes, devices, base_ref, *refs):
    by_low, by_high = routes
    high, low = grid_of(devices)
    came_high, came_low, out_ref = refs[: -low - 1], refs[-low - 1 : -1], refs[-1]
    leaves, split, main = by_low.leaves, by_low.rows, by_low.main
    size = base_ref.shape[1] // leaves
    tails = sum(came_low[k][by_high.dense_tails : by_high.dense_box, :].astype(F32) for k in range(low))
    for j in range(leaves):
        cols = slice(j * size, (j + 1) * size)
        upper = sum(ref[j * by_low.rows : (j + 1) * by_low.rows, :].astype(F32) for ref in came_high)
        lower = sum(came_low[k][j * by_high.rows : (j + 1) * by_high.rows, :].astype(F32) for k in range(low))
        out_ref[:split, cols] = base_ref[:split, cols] + upper
        out_ref[split:main, cols] = base_ref[split:main, cols] + lower
        out_ref[main:, cols] = base_ref[main:, cols] + tails[j : j + 1]


def call(kernel, out_shape, specs, operands, scratch, flops, room=None):
    outs = jax.tree.leaves(out_shape)
    nbytes = sum(a.size * a.dtype.itemsize for a in (*operands, *outs))
    limit = None if room is None else nbytes + room + 2**21
    return pl.pallas_call(
        kernel,
        out_shape=out_shape,
        in_specs=specs[0],
        out_specs=specs[1],
        scratch_shapes=scratch,
        compiler_params=pltpu.CompilerParams(vmem_limit_bytes=limit),
        cost_estimate=pl.CostEstimate(flops=flops, bytes_accessed=nbytes, transcendentals=0),
    )(*operands)


def per_device(
    probes, basis, transfer, local_blocks, remote_blocks, near_dest, near_leaf, couplings, far_list
):
    columns, points = probes.shape
    leaves, rank, size = basis.shape
    devices = lax.axis_size("leaf")
    main = columns // TILE * TILE
    routes = by_low, by_high = routes_of(devices, main, columns, leaves)
    high, low = grid_of(devices)
    blocks = remote_blocks.shape[0] * remote_blocks.shape[1]
    unit = 2 * columns * size * size
    like = lambda *arrays: [pltpu.VMEM(a.shape, a.dtype) for a in arrays]
    numbers = lambda *arrays: [pltpu.SMEM(a.shape, a.dtype) for a in arrays]
    sems = lambda count: [pltpu.SemaphoreType.DMA((count,))]
    relative = lambda x, way: lax.ppermute(x, "leaf", [(i, i ^ way) for i in range(devices)])
    message = lambda route: jax.ShapeDtypeStruct((route.depth, size), BF16)
    dense = lambda route: jax.ShapeDtypeStruct((route.dense_depth, size), BF16)

    def stacked(count, like_this):
        return pltpu.VMEM((count, *like_this.shape), like_this.dtype)

    dest, leaf = near_dest.T, near_leaf.T
    sent = call(
        functools.partial(products_kernel, routes, devices),
        [message(by_low)] * low + [message(by_high)] * high,
        ([ANY] * 6, [ANY] * (low + high)),
        (dest, leaf, probes, basis, transfer, remote_blocks),
        numbers(dest, leaf)
        + like(probes, basis, transfer, remote_blocks)
        + [
            stacked(low, message(by_low)),
            stacked(high, message(by_high)),
            pltpu.VMEM((high, by_high.meta - by_high.tails, size), F32),
            pltpu.SMEM((devices,), I32),
        ]
        + sems(7 + low + high),
        blocks * unit,
    )
    came_low, came_high = list(sent[:low]), list(sent[low:])
    planes = across_first(high)
    for k in range(1, low):
        came_low[k] = relative(came_low[k], k)
    came_low[0], came_high[0] = call(
        keep_kernel,
        (message(by_low), message(by_high)),
        ([VMEM] * 2, (VMEM,) * 2),
        (came_low[0], came_high[0]),
        [],
        0,
        0,
    )

    for k in planes[1:]:
        came_high[k] = relative(came_high[k], k * low)

    def summed(route, planes, came):
        total = jax.ShapeDtypeStruct((route.fan, (leaves + 1) * route.rows, size), F32)
        tails = jax.ShapeDtypeStruct((route.fan, max(TILE, route.dense_box - route.dense_tails), size), F32)
        ways = len(came)
        return list(
            call(
                functools.partial(sum_kernel, route, planes, ways),
                [dense(route)] * route.fan,
                ([VMEM] * ways, [VMEM] * route.fan),
                came,
                [pltpu.VMEM((ways, size), I32), pltpu.SMEM((ways, size), I32)]
                + like(total, tails)
                + [pltpu.SemaphoreType.DMA(())],
                HEAVY if route is by_low else devices * CAP * route.rows * size,
                4 * (total.size + tails.size),
            )
        )

    to_high = summed(by_low, None, [came_low[k] for k in (0, *range(2, low), 1)])
    came_high[0], to_high[0] = lax.optimization_barrier((came_high[0], to_high[0]))
    to_low = summed(by_high, planes, [came_high[k] for k in planes])
    base_shape = jax.ShapeDtypeStruct((columns, points), F32)
    for k in planes[1:]:
        to_high[k] = relative(to_high[k], k * low)
    for k in range(1, low):
        to_low[k] = relative(to_low[k], k)

    probes_then, to_low[1] = lax.optimization_barrier((probes, to_low[1]))
    base = call(
        local_kernel, base_shape, ([VMEM] * 2, VMEM), (probes_then, local_blocks), [], leaves * leaves * unit, 0
    )
    boxes = jax.ShapeDtypeStruct((devices, columns, rank), BF16)
    base = call(
        functools.partial(far_kernel, by_high, low),
        base_shape,
        ([SMEM] + [VMEM] * (4 + low), VMEM),
        (far_list, base, couplings, transfer, basis, *to_low),
        like(boxes),
        4 * leaves * unit,
        4 * boxes.size,
    )
    across = call(
        across_kernel,
        jax.ShapeDtypeStruct((by_low.dense_depth, size), F32),
        ([VMEM] * (high - 1), VMEM),
        [to_high[k] for k in planes[:-1]],
        [],
        HEAVY,
        0,
    )
    return call(
        functools.partial(last_kernel, routes, devices),
        base_shape,
        ([VMEM] * (3 + low), VMEM),
        (base, across, to_high[1], *to_low),
        [],
        devices * columns * size,
        0,
    )


def solution(mesh):
    placed = (
        P(None, ("grp", "leaf")),
        P(("grp", "leaf"), None, None),
        P(("grp", "leaf"), None, None),
        P(("grp", "leaf"), None, None, None),
        P(("grp", "leaf"), None, None, None),
        P(("grp", "leaf"), None),
        P(("grp", "leaf"), None),
        P(("grp", "leaf"), None, None, None),
        P(("grp", "leaf"), None),
    )
    return jax.shard_map(
        per_device, mesh=mesh, in_specs=placed, out_specs=P(None, ("grp", "leaf")), check_vma=False
    )
```

```python
import functools

import jax
import jax.numpy as jnp
from jax import lax
from jax.experimental import pallas as pl
from jax.experimental.pallas import tpu as pltpu
from jax.sharding import PartitionSpec as P

CAP = 4
TILE = 16
HEAVY = 4 * 10**9

F32 = jnp.float32
BF16 = jnp.bfloat16
I32 = jnp.int32

ANY = pl.BlockSpec(memory_space=pl.ANY)
VMEM = pl.BlockSpec(memory_space=pltpu.VMEM)
SMEM = pl.BlockSpec(memory_space=pltpu.SMEM)


def dot_t(lhs, rhs):
    return lax.dot_general(lhs, rhs, (((1,), (1,)), ((), ())), preferred_element_type=F32)


def dot(lhs, rhs):
    return lax.dot_general(lhs, rhs, (((1,), (0,)), ((), ())), preferred_element_type=F32)


class Copies:
    def __init__(self, sems):
        self.sems, self.used = sems, 0

    def start(self, src, dst):
        copy = pltpu.make_async_copy(src, dst, self.sems.at[self.used])
        self.used += 1
        copy.start()
        return copy


def grid_of(devices):
    low = 1 << (devices.bit_length() // 2)
    return devices // low, low


def up(rows):
    return -(-rows // TILE) * TILE


class Route:
    def __init__(self, first, last, fan, extra, main, columns, leaves, sources):
        self.first, self.rows, self.fan, self.extra, self.main = first, last - first, fan, extra, main
        self.leaves, self.half = leaves, main // 2
        slots = fan * CAP
        self.tails = slots * self.rows
        self.meta = self.tails + (up(slots) if extra else 0)
        self.box = self.meta + TILE
        self.depth = self.box + (self.half if extra else 0)
        self.dense_tails = leaves * self.rows
        self.dense_box = self.dense_tails + (up(leaves + sources) if extra else 0)
        self.dense_depth = self.dense_box + (sources * self.half if extra else 0)


def routes_of(devices, main, columns, leaves):
    high, low = grid_of(devices)
    split = up(main * 3 // 4)
    return (
        Route(0, split, high, False, main, columns, leaves, low),
        Route(split, main, low, True, main, columns, leaves, high),
    )


def products_kernel(routes, devices, *refs):
    dest_hbm, leaf_hbm, probes_hbm, basis_hbm, transfer_hbm, blocks_hbm = refs[:6]
    outs = refs[6:-11]
    (
        dest_ref, leaf_ref, probes_ref, basis_ref, transfer_ref, blocks_ref,
        send_low, send_high, tails, count, sems,
    ) = refs[-11:]
    by_low, by_high = routes
    high, low = grid_of(devices)
    me = lax.axis_index("leaf")
    main = by_high.main
    leaves, per_leaf, size = blocks_ref.shape[:3]
    columns, rank = probes_ref.shape[0], basis_ref.shape[1]
    copies = Copies(sems)
    cuts = (0, leaves // 4, leaves)
    arrivals = {}
    early = [
        copies.start(probes_hbm, probes_ref),
        copies.start(dest_hbm, dest_ref),
        copies.start(leaf_hbm, leaf_ref),
    ]
    for j, after in zip(cuts, cuts[1:]):
        part = pl.ds(j, after - j)
        arrivals[j] = copies.start(blocks_hbm.at[part], blocks_ref.at[part])
        if j == 0:
            early += [copies.start(basis_hbm, basis_ref), copies.start(transfer_hbm, transfer_ref)]

    @pl.loop(0, devices)
    def _(i):
        count[i] = 0

    tails[...] = jnp.zeros(tails.shape, F32)
    for copy in early:
        copy.wait()
    box = jnp.zeros((columns, rank), F32)

    numbers = jnp.full((-(-(low + high) // 8) * 8, size), leaves, I32)
    row = lax.broadcasted_iota(I32, numbers.shape, 0)
    lane = lax.broadcasted_iota(I32, numbers.shape, 1)
    for j in range(leaves):
        if j in arrivals:
            arrivals[j].wait()
        x = probes_ref[:, j * size : (j + 1) * size]
        box += dot_t(dot_t(x, basis_ref[j]).astype(BF16), transfer_ref[j])
        for first in range(0, per_leaf, 4):
            many = min(4, per_leaf - first)
            rhs = blocks_ref[j, first : first + many].reshape(many * size, size)
            product = dot_t(x, rhs)
            for b in range(many):
                target = jnp.bitwise_xor(dest_ref[first + b, j], me)
                slot = count[target]
                count[target] = slot + 1
                to_high = lax.shift_right_logical(target, low.bit_length() - 1)
                to_low = jnp.bitwise_and(target, low - 1)
                block = product[:, b * size : (b + 1) * size]
                piece = block[:main].astype(BF16)
                number = leaf_ref[first + b, j]

                at = to_high * CAP + slot
                rows = pl.ds(pl.multiple_of(at * by_low.rows, TILE), by_low.rows)
                send_low[to_low, rows, :] = piece[: by_low.rows]
                numbers = jnp.where((row == to_low) & (lane == at), number, numbers)

                at = to_low * CAP + slot
                rows = pl.ds(pl.multiple_of(at * by_high.rows, TILE), by_high.rows)
                send_high[to_high, rows, :] = piece[by_low.rows :]
                tails[to_high, pl.ds(at, 1), :] = block[main:]
                numbers = jnp.where((row == low + to_high) & (lane == at), number, numbers)

    half = by_high.half
    packed = jnp.concatenate([box[:half], box[half:main]], axis=1).astype(BF16)
    last = jnp.concatenate([box[main:], jnp.zeros_like(box[main:])], axis=1)
    numbers = numbers.astype(F32)
    blank = jnp.zeros((TILE - 2, size), F32)
    for i in range(low):
        tile = jnp.concatenate([numbers[i : i + 1], last, blank], axis=0)
        send_low[i, by_low.meta : by_low.box, :] = tile.astype(BF16)
    for i in range(high):
        tile = jnp.concatenate([numbers[low + i : low + i + 1], last, blank], axis=0)
        send_high[i, by_high.tails : by_high.meta, :] = tails[i].astype(BF16)
        send_high[i, by_high.meta : by_high.box, :] = tile.astype(BF16)
        send_high[i, by_high.box :, :] = packed
    leaving = [copies.start(send_low.at[i], outs[i]) for i in range(low)]
    leaving += [copies.start(send_high.at[i], outs[low + i]) for i in range(high)]
    for copy in leaving:
        copy.wait()


def sum_route(route, came, planes, outs, base, leaf_ref, total, tails):
    leaves, half, ways = route.leaves, route.half, len(came)
    for i in range(ways):
        if route.extra:
            tail = came[i][route.tails : route.meta, :].astype(F32)
        for k in range(route.fan):
            for slot in range(CAP):
                at = k * CAP + slot
                leaf = leaf_ref[base + i, at]
                rows = pl.ds(pl.multiple_of(leaf * route.rows, TILE), route.rows)
                total[k, rows, :] += came[i][at * route.rows : (at + 1) * route.rows, :].astype(F32)
                if route.extra:
                    tails[k, pl.ds(leaf, 1), :] += tail[at : at + 1]

    for k in range(route.fan):
        outs[k][: route.dense_tails, :] = total[k, : route.dense_tails, :].astype(BF16)
        if route.extra:
            for i in range(ways):
                last = came[i][route.meta : route.box, :].astype(F32)[1:2]
                at = planes[i]
                tails[k, leaves + at : leaves + at + 1, :] = last
                start = route.dense_box + at * half
                outs[k][start : start + half, :] = came[i][route.box :, :]
            outs[k][route.dense_tails : route.dense_box, :] = tails[k].astype(BF16)


def across_first(high):
    return [0, *range(2, high), 1]


def sum_kernel(route, planes, ways, *refs):
    came, outs = refs[:ways], refs[ways:-5]
    meta, leaf_ref, total, tails, late = refs[-5:]
    for i, ref in enumerate(came):
        meta[i : i + 1, :] = ref[route.meta : route.box, :].astype(F32)[:1].astype(I32)
    numbers = pltpu.make_async_copy(meta, leaf_ref, late)
    numbers.start()
    for ref in (total, tails):
        ref[...] = jnp.zeros(ref.shape, F32)
    numbers.wait()
    sum_route(route, came, planes, outs, 0, leaf_ref, total, tails)


def keep_kernel(*refs):
    half = len(refs) // 2
    for came, kept in zip(refs[:half], refs[half:]):
        kept[...] = came[...]


def local_kernel(
    probes_ref, local_ref, couplings_ref, transfer_ref, basis_ref, out_ref, pairs_ref, across_ref, twos_ref
):
    rank = basis_ref.shape[1]
    blank = jnp.zeros((rank, rank), BF16)
    for f in range(couplings_ref.shape[1]):
        cols = slice(2 * f * rank, 2 * (f + 1) * rank)
        pairs_ref[:rank, cols] = jnp.concatenate([couplings_ref[0, f], blank], axis=1)
        pairs_ref[rank:, cols] = jnp.concatenate([blank, couplings_ref[0, f]], axis=1)
    for i in range(0, basis_ref.shape[0], 2):
        across_ref[:, i * rank : (i + 2) * rank] = jnp.concatenate([transfer_ref[i], transfer_ref[i + 1]], axis=1)
        none = jnp.zeros_like(basis_ref[i])
        twos_ref[i // 2, :rank, :] = jnp.concatenate([basis_ref[i], none], axis=1)
        twos_ref[i // 2, rank:, :] = jnp.concatenate([none, basis_ref[i + 1]], axis=1)
    leaves, size = local_ref.shape[0], local_ref.shape[2]
    for i in range(0, leaves, 2):
        total = 0.0
        for c in range(0, leaves, 2):
            square = jnp.concatenate(
                [jnp.concatenate([local_ref[r, c], local_ref[r, c + 1]], axis=1) for r in (i, i + 1)], axis=0
            )
            total += dot_t(probes_ref[:, c * size : (c + 2) * size], square)
        out_ref[:, i * size : (i + 2) * size] = total


def far_kernel(by_high, low, partner_ref, base_ref, pairs_ref, across_ref, twos_ref, *refs):
    came, out_ref, boxes, lasts = refs[:low], refs[low], refs[low + 1], refs[low + 2]
    leaves, half = by_high.leaves, by_high.half
    rank = across_ref.shape[0]
    high = boxes.shape[0] // low
    me = lax.axis_index("leaf")
    for k in range(low):
        tile = came[k][by_high.dense_tails : by_high.dense_box, :].astype(F32)
        for i in range(high):
            start = by_high.dense_box + i * half
            boxes[i * low + k] = came[k][start : start + half, :]
            lasts[i * low + k : i * low + k + 1, :] = tile[leaves + i : leaves + i + 1, :]
    chosen = []
    for f in range(partner_ref.shape[1]):
        source = jnp.bitwise_xor(partner_ref[0, f], me)
        rows = jnp.concatenate([boxes[source].astype(F32), lasts[pl.ds(source, 1), :]], axis=0)
        chosen.append(rows.astype(BF16))
    far = 0.0
    for f in range(0, len(chosen), 2):
        cols = slice(2 * f * rank, 2 * (f + 2) * rank)
        far += dot_t(jnp.concatenate(chosen[f : f + 2], axis=1), pairs_ref[:, cols])
    far = jnp.concatenate([far[:half, :rank], far[:half, rank:], far[half:, :rank]], axis=0).astype(BF16)
    down = dot(far, across_ref[...]).astype(BF16)
    size = twos_ref.shape[2]
    for i in range(leaves // 2):
        cols = slice(i * size, (i + 1) * size)
        out_ref[:, cols] = base_ref[:, cols] + dot(down[:, 2 * i * rank : 2 * (i + 1) * rank], twos_ref[i])


def across_kernel(came_own, *refs):
    out_ref = refs[-1]
    out_ref[...] = sum(ref[...].astype(F32) for ref in (came_own, *refs[:-1]))


def last_kernel(routes, devices, base_ref, *refs):
    by_low, by_high = routes
    high, low = grid_of(devices)
    came_high, came_low, out_ref = refs[: -low - 1], refs[-low - 1 : -1], refs[-1]
    leaves, split, main = by_low.leaves, by_low.rows, by_low.main
    size = base_ref.shape[1] // leaves
    tails = sum(came_low[k][by_high.dense_tails : by_high.dense_box, :].astype(F32) for k in range(low))
    for j in range(leaves):
        cols = slice(j * size, (j + 1) * size)
        upper = sum(ref[j * by_low.rows : (j + 1) * by_low.rows, :].astype(F32) for ref in came_high)
        lower = sum(came_low[k][j * by_high.rows : (j + 1) * by_high.rows, :].astype(F32) for k in range(low))
        out_ref[:split, cols] = base_ref[:split, cols] + upper
        out_ref[split:main, cols] = base_ref[split:main, cols] + lower
        out_ref[main:, cols] = base_ref[main:, cols] + tails[j : j + 1]


def call(kernel, out_shape, specs, operands, scratch, flops, room=None):
    outs = jax.tree.leaves(out_shape)
    nbytes = sum(a.size * a.dtype.itemsize for a in (*operands, *outs))
    limit = None if room is None else nbytes + room + 2**21
    return pl.pallas_call(
        kernel,
        out_shape=out_shape,
        in_specs=specs[0],
        out_specs=specs[1],
        scratch_shapes=scratch,
        compiler_params=pltpu.CompilerParams(vmem_limit_bytes=limit),
        cost_estimate=pl.CostEstimate(flops=flops, bytes_accessed=nbytes, transcendentals=0),
    )(*operands)


def per_device(
    probes, basis, transfer, local_blocks, remote_blocks, near_dest, near_leaf, couplings, far_list
):
    columns, points = probes.shape
    leaves, rank, size = basis.shape
    devices = lax.axis_size("leaf")
    main = columns // TILE * TILE
    routes = by_low, by_high = routes_of(devices, main, columns, leaves)
    high, low = grid_of(devices)
    blocks = remote_blocks.shape[0] * remote_blocks.shape[1]
    unit = 2 * columns * size * size
    like = lambda *arrays: [pltpu.VMEM(a.shape, a.dtype) for a in arrays]
    numbers = lambda *arrays: [pltpu.SMEM(a.shape, a.dtype) for a in arrays]
    sems = lambda count: [pltpu.SemaphoreType.DMA((count,))]
    relative = lambda x, way: lax.ppermute(x, "leaf", [(i, i ^ way) for i in range(devices)])
    message = lambda route: jax.ShapeDtypeStruct((route.depth, size), BF16)
    dense = lambda route: jax.ShapeDtypeStruct((route.dense_depth, size), BF16)

    def stacked(count, like_this):
        return pltpu.VMEM((count, *like_this.shape), like_this.dtype)

    dest, leaf = near_dest.T, near_leaf.T
    sent = call(
        functools.partial(products_kernel, routes, devices),
        [message(by_low)] * low + [message(by_high)] * high,
        ([ANY] * 6, [ANY] * (low + high)),
        (dest, leaf, probes, basis, transfer, remote_blocks),
        numbers(dest, leaf)
        + like(probes, basis, transfer, remote_blocks)
        + [
            stacked(low, message(by_low)),
            stacked(high, message(by_high)),
            pltpu.VMEM((high, by_high.meta - by_high.tails, size), F32),
            pltpu.SMEM((devices,), I32),
        ]
        + sems(7 + low + high),
        blocks * unit,
    )
    came_low, came_high = list(sent[:low]), list(sent[low:])
    planes = across_first(high)
    for k in range(1, low):
        came_low[k] = relative(came_low[k], k)
    came_low[0], came_high[0] = call(
        keep_kernel,
        (message(by_low), message(by_high)),
        ([VMEM] * 2, (VMEM,) * 2),
        (came_low[0], came_high[0]),
        [],
        0,
        0,
    )

    for k in planes[1:]:
        came_high[k] = relative(came_high[k], k * low)

    def summed(route, planes, came):
        total = jax.ShapeDtypeStruct((route.fan, (leaves + 1) * route.rows, size), F32)
        tails = jax.ShapeDtypeStruct((route.fan, max(TILE, route.dense_box - route.dense_tails), size), F32)
        ways = len(came)
        return list(
            call(
                functools.partial(sum_kernel, route, planes, ways),
                [dense(route)] * route.fan,
                ([VMEM] * ways, [VMEM] * route.fan),
                came,
                [pltpu.VMEM((ways, size), I32), pltpu.SMEM((ways, size), I32)]
                + like(total, tails)
                + [pltpu.SemaphoreType.DMA(())],
                HEAVY if route is by_low else devices * CAP * route.rows * size,
                4 * (total.size + tails.size),
            )
        )

    to_high = summed(by_low, None, [came_low[k] for k in (0, *range(2, low), 1)])
    came_high[0], to_high[0] = lax.optimization_barrier((came_high[0], to_high[0]))
    to_low = summed(by_high, planes, [came_high[k] for k in planes])
    base_shape = jax.ShapeDtypeStruct((columns, points), F32)
    for k in planes[1:]:
        to_high[k] = relative(to_high[k], k * low)
    for k in range(1, low):
        to_low[k] = relative(to_low[k], k)

    probes_then, to_low[1] = lax.optimization_barrier((probes, to_low[1]))
    base, *ready = call(
        local_kernel,
        (
            base_shape,
            jax.ShapeDtypeStruct((2 * rank, 2 * rank * couplings.shape[1]), BF16),
            jax.ShapeDtypeStruct((rank, leaves * rank), BF16),
            jax.ShapeDtypeStruct((leaves // 2, 2 * rank, 2 * size), BF16),
        ),
        ([VMEM] * 5, (VMEM,) * 4),
        (probes_then, local_blocks, couplings, transfer, basis),
        [],
        leaves * leaves * unit,
        0,
    )
    boxes = jax.ShapeDtypeStruct((devices, main // 2, size), BF16)
    base = call(
        functools.partial(far_kernel, by_high, low),
        base_shape,
        ([SMEM] + [VMEM] * (4 + low), VMEM),
        (far_list, base, *ready, *to_low),
        like(boxes, jax.ShapeDtypeStruct((devices, size), F32)),
        4 * leaves * unit,
        4 * boxes.size,
    )
    across = call(
        across_kernel,
        jax.ShapeDtypeStruct((by_low.dense_depth, size), F32),
        ([VMEM] * (high - 1), VMEM),
        [to_high[k] for k in planes[:-1]],
        [],
        HEAVY,
        0,
    )
    return call(
        functools.partial(last_kernel, routes, devices),
        base_shape,
        ([VMEM] * (3 + low), VMEM),
        (base, across, to_high[1], *to_low),
        [],
        devices * columns * size,
        0,
    )


def solution(mesh):
    placed = (
        P(None, ("grp", "leaf")),
        P(("grp", "leaf"), None, None),
        P(("grp", "leaf"), None, None),
        P(("grp", "leaf"), None, None, None),
        P(("grp", "leaf"), None, None, None),
        P(("grp", "leaf"), None),
        P(("grp", "leaf"), None),
        P(("grp", "leaf"), None, None, None),
        P(("grp", "leaf"), None),
    )
    return jax.shard_map(
        per_device, mesh=mesh, in_specs=placed, out_specs=P(None, ("grp", "leaf")), check_vma=False
    )
```

```python
import functools

import jax
import jax.numpy as jnp
from jax import lax
from jax.experimental import pallas as pl
from jax.experimental.pallas import tpu as pltpu
from jax.sharding import PartitionSpec as P

CAP = 4
TILE = 16
HEAVY = 4 * 10**9

F32 = jnp.float32
BF16 = jnp.bfloat16
I32 = jnp.int32

ANY = pl.BlockSpec(memory_space=pl.ANY)
VMEM = pl.BlockSpec(memory_space=pltpu.VMEM)
SMEM = pl.BlockSpec(memory_space=pltpu.SMEM)


def dot_t(lhs, rhs):
    return lax.dot_general(lhs, rhs, (((1,), (1,)), ((), ())), preferred_element_type=F32)


def dot(lhs, rhs):
    return lax.dot_general(lhs, rhs, (((1,), (0,)), ((), ())), preferred_element_type=F32)


class Copies:
    def __init__(self, sems):
        self.sems, self.used = sems, 0

    def start(self, src, dst):
        copy = pltpu.make_async_copy(src, dst, self.sems.at[self.used])
        self.used += 1
        copy.start()
        return copy


def grid_of(devices):
    low = 1 << (devices.bit_length() // 2)
    return devices // low, low


def up(rows):
    return -(-rows // TILE) * TILE


class Route:
    def __init__(self, first, last, fan, extra, main, columns, leaves, sources):
        self.first, self.rows, self.fan, self.extra, self.main = first, last - first, fan, extra, main
        self.leaves, self.half = leaves, main // 2
        slots = fan * CAP
        self.tails = slots * self.rows
        self.meta = self.tails + (up(slots) if extra else 0)
        self.box = self.meta + TILE
        self.depth = self.box + (self.half if extra else 0)
        self.dense_tails = leaves * self.rows
        self.dense_box = self.dense_tails + (up(leaves + sources) if extra else 0)
        self.dense_depth = self.dense_box + (sources * self.half if extra else 0)


def routes_of(devices, main, columns, leaves):
    high, low = grid_of(devices)
    split = up(main * 3 // 4)
    return (
        Route(0, split, high, False, main, columns, leaves, low),
        Route(split, main, low, True, main, columns, leaves, high),
    )


def products_kernel(routes, devices, *refs):
    dest_hbm, leaf_hbm, probes_hbm, basis_hbm, transfer_hbm, blocks_hbm = refs[:6]
    outs = refs[6:-11]
    (
        dest_ref, leaf_ref, probes_ref, basis_ref, transfer_ref, blocks_ref,
        send_low, send_high, tails, count, sems,
    ) = refs[-11:]
    by_low, by_high = routes
    high, low = grid_of(devices)
    me = lax.axis_index("leaf")
    main = by_high.main
    leaves, per_leaf, size = blocks_ref.shape[:3]
    columns, rank = probes_ref.shape[0], basis_ref.shape[1]
    copies = Copies(sems)
    cuts = (0, leaves // 4, leaves)
    arrivals = {}
    early = [
        copies.start(probes_hbm, probes_ref),
        copies.start(dest_hbm, dest_ref),
        copies.start(leaf_hbm, leaf_ref),
    ]
    for j, after in zip(cuts, cuts[1:]):
        part = pl.ds(j, after - j)
        arrivals[j] = copies.start(blocks_hbm.at[part], blocks_ref.at[part])
        if j == 0:
            early += [copies.start(basis_hbm, basis_ref), copies.start(transfer_hbm, transfer_ref)]

    @pl.loop(0, devices)
    def _(i):
        count[i] = 0

    tails[...] = jnp.zeros(tails.shape, F32)
    for copy in early:
        copy.wait()
    box = jnp.zeros((columns, rank), F32)

    numbers = jnp.full((-(-(low + high) // 8) * 8, size), leaves, I32)
    row = lax.broadcasted_iota(I32, numbers.shape, 0)
    lane = lax.broadcasted_iota(I32, numbers.shape, 1)
    for j in range(leaves):
        if j in arrivals:
            arrivals[j].wait()
        x = probes_ref[:, j * size : (j + 1) * size]
        box += dot_t(dot_t(x, basis_ref[j]).astype(BF16), transfer_ref[j])
        for first in range(0, per_leaf, 4):
            many = min(4, per_leaf - first)
            rhs = blocks_ref[j, first : first + many].reshape(many * size, size)
            product = dot_t(x, rhs)
            for b in range(many):
                target = jnp.bitwise_xor(dest_ref[first + b, j], me)
                slot = count[target]
                count[target] = slot + 1
                to_high = lax.shift_right_logical(target, low.bit_length() - 1)
                to_low = jnp.bitwise_and(target, low - 1)
                block = product[:, b * size : (b + 1) * size]
                piece = block[:main].astype(BF16)
                number = leaf_ref[first + b, j]

                at = to_high * CAP + slot
                rows = pl.ds(pl.multiple_of(at * by_low.rows, TILE), by_low.rows)
                send_low[to_low, rows, :] = piece[: by_low.rows]
                numbers = jnp.where((row == to_low) & (lane == at), number, numbers)

                at = to_low * CAP + slot
                rows = pl.ds(pl.multiple_of(at * by_high.rows, TILE), by_high.rows)
                send_high[to_high, rows, :] = piece[by_low.rows :]
                tails[to_high, pl.ds(at, 1), :] = block[main:]
                numbers = jnp.where((row == low + to_high) & (lane == at), number, numbers)

    half = by_high.half
    packed = jnp.concatenate([box[:half], box[half:main]], axis=1).astype(BF16)
    last = jnp.concatenate([box[main:], jnp.zeros_like(box[main:])], axis=1)
    numbers = numbers.astype(F32)
    blank = jnp.zeros((TILE - 2, size), F32)
    for i in range(low):
        tile = jnp.concatenate([numbers[i : i + 1], last, blank], axis=0)
        send_low[i, by_low.meta : by_low.box, :] = tile.astype(BF16)
    for i in range(high):
        tile = jnp.concatenate([numbers[low + i : low + i + 1], last, blank], axis=0)
        send_high[i, by_high.tails : by_high.meta, :] = tails[i].astype(BF16)
        send_high[i, by_high.meta : by_high.box, :] = tile.astype(BF16)
        send_high[i, by_high.box :, :] = packed
    leaving = [copies.start(send_low.at[i], outs[i]) for i in range(low)]
    leaving += [copies.start(send_high.at[i], outs[low + i]) for i in range(high)]
    for copy in leaving:
        copy.wait()


def sum_route(route, came, planes, outs, base, leaf_ref, total, tails):
    leaves, half, ways = route.leaves, route.half, len(came)
    for i in range(ways):
        if route.extra:
            tail = came[i][route.tails : route.meta, :].astype(F32)
        for k in range(route.fan):
            for slot in range(CAP):
                at = k * CAP + slot
                leaf = leaf_ref[base + i, at]
                rows = pl.ds(pl.multiple_of(leaf * route.rows, TILE), route.rows)
                total[k, rows, :] += came[i][at * route.rows : (at + 1) * route.rows, :].astype(F32)
                if route.extra:
                    tails[k, pl.ds(leaf, 1), :] += tail[at : at + 1]

    for k in range(route.fan):
        outs[k][: route.dense_tails, :] = total[k, : route.dense_tails, :].astype(BF16)
        if route.extra:
            for i in range(ways):
                last = came[i][route.meta : route.box, :].astype(F32)[1:2]
                at = planes[i]
                tails[k, leaves + at : leaves + at + 1, :] = last
                start = route.dense_box + at * half
                outs[k][start : start + half, :] = came[i][route.box :, :]
            outs[k][route.dense_tails : route.dense_box, :] = tails[k].astype(BF16)


def across_first(high):
    return [0, *range(2, high), 1]


def sum_kernel(route, planes, ways, *refs):
    came, outs = refs[:ways], refs[ways:-5]
    meta, leaf_ref, total, tails, late = refs[-5:]
    for i, ref in enumerate(came):
        meta[i : i + 1, :] = ref[route.meta : route.box, :].astype(F32)[:1].astype(I32)
    numbers = pltpu.make_async_copy(meta, leaf_ref, late)
    numbers.start()
    for ref in (total, tails):
        ref[...] = jnp.zeros(ref.shape, F32)
    numbers.wait()
    sum_route(route, came, planes, outs, 0, leaf_ref, total, tails)


def keep_kernel(*refs):
    half = len(refs) // 2
    for came, kept in zip(refs[:half], refs[half:]):
        kept[...] = came[...]


def local_kernel(
    probes_ref, local_ref, couplings_ref, transfer_ref, basis_ref, out_ref, pairs_ref, across_ref, twos_ref
):
    rank = basis_ref.shape[1]
    blank = jnp.zeros((rank, rank), BF16)
    for f in range(couplings_ref.shape[1]):
        cols = slice(2 * f * rank, 2 * (f + 1) * rank)
        pairs_ref[:rank, cols] = jnp.concatenate([couplings_ref[0, f], blank], axis=1)
        pairs_ref[rank:, cols] = jnp.concatenate([blank, couplings_ref[0, f]], axis=1)
    for i in range(0, basis_ref.shape[0], 2):
        across_ref[:, i * rank : (i + 2) * rank] = jnp.concatenate([transfer_ref[i], transfer_ref[i + 1]], axis=1)
        none = jnp.zeros_like(basis_ref[i])
        twos_ref[i // 2, :rank, :] = jnp.concatenate([basis_ref[i], none], axis=1)
        twos_ref[i // 2, rank:, :] = jnp.concatenate([none, basis_ref[i + 1]], axis=1)
    leaves, size = local_ref.shape[0], local_ref.shape[2]
    for i in range(0, leaves, 2):
        total = 0.0
        for c in range(0, leaves, 2):
            square = jnp.concatenate(
                [jnp.concatenate([local_ref[r, c], local_ref[r, c + 1]], axis=1) for r in (i, i + 1)], axis=0
            )
            total += dot_t(probes_ref[:, c * size : (c + 2) * size], square)
        out_ref[:, i * size : (i + 2) * size] = total


def far_kernel(by_high, low, partner_ref, base_ref, pairs_ref, across_ref, twos_ref, *refs):
    came, out_ref, boxes, lasts = refs[:low], refs[low], refs[low + 1], refs[low + 2]
    leaves, half = by_high.leaves, by_high.half
    rank = across_ref.shape[0]
    high = boxes.shape[0] // low
    me = lax.axis_index("leaf")
    for k in range(low):
        tile = came[k][by_high.dense_tails : by_high.dense_box, :].astype(F32)
        for i in range(high):
            start = by_high.dense_box + i * half
            boxes[i * low + k] = came[k][start : start + half, :]
            lasts[i * low + k : i * low + k + 1, :] = tile[leaves + i : leaves + i + 1, :]
    chosen = []
    for f in range(partner_ref.shape[1]):
        source = jnp.bitwise_xor(partner_ref[0, f], me)
        rows = jnp.concatenate([boxes[source].astype(F32), lasts[pl.ds(source, 1), :]], axis=0)
        chosen.append(rows.astype(BF16))
    far = 0.0
    for f in range(0, len(chosen), 2):
        cols = slice(2 * f * rank, 2 * (f + 2) * rank)
        far += dot_t(jnp.concatenate(chosen[f : f + 2], axis=1), pairs_ref[:, cols])
    far = jnp.concatenate([far[:half, :rank], far[:half, rank:], far[half:, :rank]], axis=0).astype(BF16)
    down = dot(far, across_ref[...]).astype(BF16)
    size = twos_ref.shape[2]
    for i in range(leaves // 2):
        cols = slice(i * size, (i + 1) * size)
        out_ref[:, cols] = base_ref[:, cols] + dot(down[:, 2 * i * rank : 2 * (i + 1) * rank], twos_ref[i])


def across_kernel(came_own, *refs):
    out_ref = refs[-1]
    out_ref[...] = sum(ref[...].astype(F32) for ref in (came_own, *refs[:-1]))


def last_kernel(routes, devices, base_ref, *refs):
    by_low, by_high = routes
    high, low = grid_of(devices)
    came_high, came_low, out_ref = refs[: -low - 1], refs[-low - 1 : -1], refs[-1]
    leaves, split, main = by_low.leaves, by_low.rows, by_low.main
    size = base_ref.shape[1] // leaves
    tails = sum(came_low[k][by_high.dense_tails : by_high.dense_box, :].astype(F32) for k in range(low))
    for j in range(leaves):
        cols = slice(j * size, (j + 1) * size)
        upper = sum(ref[j * by_low.rows : (j + 1) * by_low.rows, :].astype(F32) for ref in came_high)
        lower = sum(came_low[k][j * by_high.rows : (j + 1) * by_high.rows, :].astype(F32) for k in range(low))
        out_ref[:split, cols] = base_ref[:split, cols] + upper
        out_ref[split:main, cols] = base_ref[split:main, cols] + lower
        out_ref[main:, cols] = base_ref[main:, cols] + tails[j : j + 1]


def call(kernel, out_shape, specs, operands, scratch, flops, room=None):
    outs = jax.tree.leaves(out_shape)
    nbytes = sum(a.size * a.dtype.itemsize for a in (*operands, *outs))
    limit = None if room is None else nbytes + room + 2**21
    return pl.pallas_call(
        kernel,
        out_shape=out_shape,
        in_specs=specs[0],
        out_specs=specs[1],
        scratch_shapes=scratch,
        compiler_params=pltpu.CompilerParams(vmem_limit_bytes=limit),
        cost_estimate=pl.CostEstimate(flops=flops, bytes_accessed=nbytes, transcendentals=0),
    )(*operands)


def per_device(
    probes, basis, transfer, local_blocks, remote_blocks, near_dest, near_leaf, couplings, far_list
):
    columns, points = probes.shape
    leaves, rank, size = basis.shape
    devices = lax.axis_size("leaf")
    main = columns // TILE * TILE
    routes = by_low, by_high = routes_of(devices, main, columns, leaves)
    high, low = grid_of(devices)
    blocks = remote_blocks.shape[0] * remote_blocks.shape[1]
    unit = 2 * columns * size * size
    like = lambda *arrays: [pltpu.VMEM(a.shape, a.dtype) for a in arrays]
    numbers = lambda *arrays: [pltpu.SMEM(a.shape, a.dtype) for a in arrays]
    sems = lambda count: [pltpu.SemaphoreType.DMA((count,))]
    relative = lambda x, way: lax.ppermute(x, "leaf", [(i, i ^ way) for i in range(devices)])
    message = lambda route: jax.ShapeDtypeStruct((route.depth, size), BF16)
    dense = lambda route: jax.ShapeDtypeStruct((route.dense_depth, size), BF16)

    def stacked(count, like_this):
        return pltpu.VMEM((count, *like_this.shape), like_this.dtype)

    dest, leaf = near_dest.T, near_leaf.T
    sent = call(
        functools.partial(products_kernel, routes, devices),
        [message(by_low)] * low + [message(by_high)] * high,
        ([ANY] * 6, [ANY] * (low + high)),
        (dest, leaf, probes, basis, transfer, remote_blocks),
        numbers(dest, leaf)
        + like(probes, basis, transfer, remote_blocks)
        + [
            stacked(low, message(by_low)),
            stacked(high, message(by_high)),
            pltpu.VMEM((high, by_high.meta - by_high.tails, size), F32),
            pltpu.SMEM((devices,), I32),
        ]
        + sems(7 + low + high),
        blocks * unit,
    )
    came_low, came_high = list(sent[:low]), list(sent[low:])
    planes = across_first(high)
    for k in range(1, low):
        came_low[k] = relative(came_low[k], k)
    came_low[0], came_high[0] = call(
        keep_kernel,
        (message(by_low), message(by_high)),
        ([VMEM] * 2, (VMEM,) * 2),
        (came_low[0], came_high[0]),
        [],
        0,
        0,
    )

    for k in planes[1:]:
        came_high[k] = relative(came_high[k], k * low)

    def summed(route, planes, came):
        total = jax.ShapeDtypeStruct((route.fan, (leaves + 1) * route.rows, size), F32)
        tails = jax.ShapeDtypeStruct((route.fan, max(TILE, route.dense_box - route.dense_tails), size), F32)
        ways = len(came)
        return list(
            call(
                functools.partial(sum_kernel, route, planes, ways),
                [dense(route)] * route.fan,
                ([VMEM] * ways, [VMEM] * route.fan),
                came,
                [pltpu.VMEM((ways, size), I32), pltpu.SMEM((ways, size), I32)]
                + like(total, tails)
                + [pltpu.SemaphoreType.DMA(())],
                HEAVY if route is by_low else devices * CAP * route.rows * size,
                4 * (total.size + tails.size),
            )
        )

    to_high = summed(by_low, None, [came_low[k] for k in (0, *range(2, low), 1)])
    came_high[0], to_high[0] = lax.optimization_barrier((came_high[0], to_high[0]))
    to_low = summed(by_high, planes, [came_high[k] for k in planes])
    base_shape = jax.ShapeDtypeStruct((columns, points), F32)
    to_high[3], to_low[0] = lax.optimization_barrier((to_high[3], to_low[0]))
    for k in planes[1:]:
        to_high[k] = relative(to_high[k], k * low)
    for k in range(1, low):
        to_low[k] = relative(to_low[k], k)

    probes_then, to_low[1] = lax.optimization_barrier((probes, to_low[1]))
    base, *ready = call(
        local_kernel,
        (
            base_shape,
            jax.ShapeDtypeStruct((2 * rank, 2 * rank * couplings.shape[1]), BF16),
            jax.ShapeDtypeStruct((rank, leaves * rank), BF16),
            jax.ShapeDtypeStruct((leaves // 2, 2 * rank, 2 * size), BF16),
        ),
        ([VMEM] * 5, (VMEM,) * 4),
        (probes_then, local_blocks, couplings, transfer, basis),
        [],
        leaves * leaves * unit,
        0,
    )
    boxes = jax.ShapeDtypeStruct((devices, main // 2, size), BF16)
    base = call(
        functools.partial(far_kernel, by_high, low),
        base_shape,
        ([SMEM] + [VMEM] * (4 + low), VMEM),
        (far_list, base, *ready, *to_low),
        like(boxes, jax.ShapeDtypeStruct((devices, size), F32)),
        4 * leaves * unit,
        4 * boxes.size,
    )
    across = to_high[0]
    for came, work in ((to_high[2:3], devices * size), (to_high[3:], HEAVY)):
        across = call(
            across_kernel,
            jax.ShapeDtypeStruct((by_low.dense_depth, size), F32),
            ([VMEM] * (1 + len(came)), VMEM),
            (across, *came),
            [],
            work,
            0,
        )
    return call(
        functools.partial(last_kernel, routes, devices),
        base_shape,
        ([VMEM] * (3 + low), VMEM),
        (base, across, to_high[1], *to_low),
        [],
        devices * columns * size,
        0,
    )


def solution(mesh):
    placed = (
        P(None, ("grp", "leaf")),
        P(("grp", "leaf"), None, None),
        P(("grp", "leaf"), None, None),
        P(("grp", "leaf"), None, None, None),
        P(("grp", "leaf"), None, None, None),
        P(("grp", "leaf"), None),
        P(("grp", "leaf"), None),
        P(("grp", "leaf"), None, None, None),
        P(("grp", "leaf"), None),
    )
    return jax.shard_map(
        per_device, mesh=mesh, in_specs=placed, out_specs=P(None, ("grp", "leaf")), check_vma=False
    )
```

```python
import functools

import jax
import jax.numpy as jnp
from jax import lax
from jax.experimental import pallas as pl
from jax.experimental.pallas import tpu as pltpu
from jax.sharding import PartitionSpec as P

CAP = 4
TILE = 16
HEAVY = 4 * 10**9

F32 = jnp.float32
BF16 = jnp.bfloat16
I32 = jnp.int32

ANY = pl.BlockSpec(memory_space=pl.ANY)
VMEM = pl.BlockSpec(memory_space=pltpu.VMEM)
SMEM = pl.BlockSpec(memory_space=pltpu.SMEM)


def dot_t(lhs, rhs):
    return lax.dot_general(lhs, rhs, (((1,), (1,)), ((), ())), preferred_element_type=F32)


def dot(lhs, rhs):
    return lax.dot_general(lhs, rhs, (((1,), (0,)), ((), ())), preferred_element_type=F32)


class Copies:
    def __init__(self, sems):
        self.sems, self.used = sems, 0

    def start(self, src, dst):
        copy = pltpu.make_async_copy(src, dst, self.sems.at[self.used])
        self.used += 1
        copy.start()
        return copy


def grid_of(devices):
    low = 1 << (devices.bit_length() // 2)
    return devices // low, low


def up(rows):
    return -(-rows // TILE) * TILE


class Route:
    def __init__(self, first, last, fan, extra, main, columns, leaves, sources):
        self.first, self.rows, self.fan, self.extra, self.main = first, last - first, fan, extra, main
        self.leaves, self.half = leaves, main // 2
        slots = fan * CAP
        self.tails = slots * self.rows
        self.meta = self.tails + (up(slots) if extra else 0)
        self.box = self.meta + TILE
        self.depth = self.box + (self.half if extra else 0)
        self.dense_tails = leaves * self.rows
        self.dense_box = self.dense_tails + (up(leaves + sources) if extra else 0)
        self.dense_depth = self.dense_box + (sources * self.half if extra else 0)


def routes_of(devices, main, columns, leaves):
    high, low = grid_of(devices)
    split = up(main * 3 // 4)
    return (
        Route(0, split, high, False, main, columns, leaves, low),
        Route(split, main, low, True, main, columns, leaves, high),
    )


def products_kernel(routes, devices, *refs):
    dest_hbm, leaf_hbm, probes_hbm, basis_hbm, transfer_hbm, blocks_hbm = refs[:6]
    outs = refs[6:-11]
    (
        dest_ref, leaf_ref, probes_ref, basis_ref, transfer_ref, blocks_ref,
        send_low, send_high, tails, count, sems,
    ) = refs[-11:]
    by_low, by_high = routes
    high, low = grid_of(devices)
    me = lax.axis_index("leaf")
    main = by_high.main
    leaves, per_leaf, size = blocks_ref.shape[:3]
    columns, rank = probes_ref.shape[0], basis_ref.shape[1]
    copies = Copies(sems)
    cuts = (0, leaves // 4, leaves)
    arrivals = {}
    early = [
        copies.start(probes_hbm, probes_ref),
        copies.start(dest_hbm, dest_ref),
        copies.start(leaf_hbm, leaf_ref),
    ]
    for j, after in zip(cuts, cuts[1:]):
        part = pl.ds(j, after - j)
        arrivals[j] = copies.start(blocks_hbm.at[part], blocks_ref.at[part])
        if j == 0:
            early += [copies.start(basis_hbm, basis_ref), copies.start(transfer_hbm, transfer_ref)]

    @pl.loop(0, devices)
    def _(i):
        count[i] = 0

    tails[...] = jnp.zeros(tails.shape, F32)
    for copy in early:
        copy.wait()
    box = jnp.zeros((columns, rank), F32)

    numbers = jnp.full((-(-(low + high) // 8) * 8, size), leaves, I32)
    row = lax.broadcasted_iota(I32, numbers.shape, 0)
    lane = lax.broadcasted_iota(I32, numbers.shape, 1)
    for j in range(leaves):
        if j in arrivals:
            arrivals[j].wait()
        x = probes_ref[:, j * size : (j + 1) * size]
        box += dot_t(dot_t(x, basis_ref[j]).astype(BF16), transfer_ref[j])
        for first in range(0, per_leaf, 4):
            many = min(4, per_leaf - first)
            rhs = blocks_ref[j, first : first + many].reshape(many * size, size)
            product = dot_t(x, rhs)
            for b in range(many):
                target = jnp.bitwise_xor(dest_ref[first + b, j], me)
                slot = count[target]
                count[target] = slot + 1
                to_high = lax.shift_right_logical(target, low.bit_length() - 1)
                to_low = jnp.bitwise_and(target, low - 1)
                block = product[:, b * size : (b + 1) * size]
                piece = block[:main].astype(BF16)
                number = leaf_ref[first + b, j]

                at = to_high * CAP + slot
                rows = pl.ds(pl.multiple_of(at * by_low.rows, TILE), by_low.rows)
                send_low[to_low, rows, :] = piece[: by_low.rows]
                numbers = jnp.where((row == to_low) & (lane == at), number, numbers)

                at = to_low * CAP + slot
                rows = pl.ds(pl.multiple_of(at * by_high.rows, TILE), by_high.rows)
                send_high[to_high, rows, :] = piece[by_low.rows :]
                tails[to_high, pl.ds(at, 1), :] = block[main:]
                numbers = jnp.where((row == low + to_high) & (lane == at), number, numbers)

    half = by_high.half
    packed = jnp.concatenate([box[:half], box[half:main]], axis=1).astype(BF16)
    last = jnp.concatenate([box[main:], jnp.zeros_like(box[main:])], axis=1)
    numbers = numbers.astype(F32)
    blank = jnp.zeros((TILE - 2, size), F32)
    for i in range(low):
        tile = jnp.concatenate([numbers[i : i + 1], last, blank], axis=0)
        send_low[i, by_low.meta : by_low.box, :] = tile.astype(BF16)
    for i in range(high):
        tile = jnp.concatenate([numbers[low + i : low + i + 1], last, blank], axis=0)
        send_high[i, by_high.tails : by_high.meta, :] = tails[i].astype(BF16)
        send_high[i, by_high.meta : by_high.box, :] = tile.astype(BF16)
        send_high[i, by_high.box :, :] = packed
    leaving = [copies.start(send_low.at[i], outs[i]) for i in range(low)]
    leaving += [copies.start(send_high.at[i], outs[low + i]) for i in range(high)]
    for copy in leaving:
        copy.wait()


def sum_route(route, came, planes, outs, total, tails):
    leaves, half, ways = route.leaves, route.half, len(came)
    for i in range(ways):
        numbers = came[i][route.meta : route.box, :].astype(F32)[:1].astype(I32)
        if route.extra:
            tail = came[i][route.tails : route.meta, :].astype(F32)
        for k in range(route.fan):
            for slot in range(CAP):
                at = k * CAP + slot
                leaf = numbers[0, at]
                rows = pl.ds(pl.multiple_of(leaf * route.rows, TILE), route.rows)
                total[k, rows, :] += came[i][at * route.rows : (at + 1) * route.rows, :].astype(F32)
                if route.extra:
                    tails[k, pl.ds(leaf, 1), :] += tail[at : at + 1]

    for k in range(route.fan):
        outs[k][: route.dense_tails, :] = total[k, : route.dense_tails, :].astype(BF16)
        if route.extra:
            for i in range(ways):
                last = came[i][route.meta : route.box, :].astype(F32)[1:2]
                at = planes[i]
                tails[k, leaves + at : leaves + at + 1, :] = last
                start = route.dense_box + at * half
                outs[k][start : start + half, :] = came[i][route.box :, :]
            outs[k][route.dense_tails : route.dense_box, :] = tails[k].astype(BF16)


def across_first(high):
    return [0, *range(2, high), 1]


def sum_kernel(route, planes, ways, *refs):
    came, outs = refs[:ways], refs[ways:-2]
    total, tails = refs[-2:]
    for ref in (total, tails):
        ref[...] = jnp.zeros(ref.shape, F32)
    sum_route(route, came, planes, outs, total, tails)


def keep_kernel(*refs):
    half = len(refs) // 2
    for came, kept in zip(refs[:half], refs[half:]):
        kept[...] = came[...]


def local_kernel(
    probes_ref, local_ref, couplings_ref, transfer_ref, basis_ref, out_ref, pairs_ref, across_ref, twos_ref
):
    rank = basis_ref.shape[1]
    blank = jnp.zeros((rank, rank), BF16)
    for f in range(couplings_ref.shape[1]):
        cols = slice(2 * f * rank, 2 * (f + 1) * rank)
        pairs_ref[:rank, cols] = jnp.concatenate([couplings_ref[0, f], blank], axis=1)
        pairs_ref[rank:, cols] = jnp.concatenate([blank, couplings_ref[0, f]], axis=1)
    for i in range(0, basis_ref.shape[0], 2):
        across_ref[:, i * rank : (i + 2) * rank] = jnp.concatenate([transfer_ref[i], transfer_ref[i + 1]], axis=1)
        none = jnp.zeros_like(basis_ref[i])
        twos_ref[i // 2, :rank, :] = jnp.concatenate([basis_ref[i], none], axis=1)
        twos_ref[i // 2, rank:, :] = jnp.concatenate([none, basis_ref[i + 1]], axis=1)
    leaves, size = local_ref.shape[0], local_ref.shape[2]
    for i in range(0, leaves, 2):
        total = 0.0
        for c in range(0, leaves, 2):
            square = jnp.concatenate(
                [jnp.concatenate([local_ref[r, c], local_ref[r, c + 1]], axis=1) for r in (i, i + 1)], axis=0
            )
            total += dot_t(probes_ref[:, c * size : (c + 2) * size], square)
        out_ref[:, i * size : (i + 2) * size] = total


def far_kernel(by_high, low, partner_ref, base_ref, pairs_ref, across_ref, twos_ref, *refs):
    came, out_ref, boxes, lasts = refs[:low], refs[low], refs[low + 1], refs[low + 2]
    leaves, half = by_high.leaves, by_high.half
    rank = across_ref.shape[0]
    high = boxes.shape[0] // low
    me = lax.axis_index("leaf")
    for k in range(low):
        tile = came[k][by_high.dense_tails : by_high.dense_box, :].astype(F32)
        for i in range(high):
            start = by_high.dense_box + i * half
            boxes[i * low + k] = came[k][start : start + half, :]
            lasts[i * low + k : i * low + k + 1, :] = tile[leaves + i : leaves + i + 1, :]
    chosen = []
    for f in range(partner_ref.shape[1]):
        source = jnp.bitwise_xor(partner_ref[0, f], me)
        rows = jnp.concatenate([boxes[source].astype(F32), lasts[pl.ds(source, 1), :]], axis=0)
        chosen.append(rows.astype(BF16))
    far = 0.0
    for f in range(0, len(chosen), 2):
        cols = slice(2 * f * rank, 2 * (f + 2) * rank)
        far += dot_t(jnp.concatenate(chosen[f : f + 2], axis=1), pairs_ref[:, cols])
    far = jnp.concatenate([far[:half, :rank], far[:half, rank:], far[half:, :rank]], axis=0).astype(BF16)
    down = dot(far, across_ref[...]).astype(BF16)
    size = twos_ref.shape[2]
    for i in range(leaves // 2):
        cols = slice(i * size, (i + 1) * size)
        out_ref[:, cols] = base_ref[:, cols] + dot(down[:, 2 * i * rank : 2 * (i + 1) * rank], twos_ref[i])


def across_kernel(came_own, *refs):
    out_ref = refs[-1]
    out_ref[...] = sum(ref[...].astype(F32) for ref in (came_own, *refs[:-1]))


def last_kernel(routes, devices, base_ref, *refs):
    by_low, by_high = routes
    high, low = grid_of(devices)
    came_high, came_low, out_ref = refs[: -low - 1], refs[-low - 1 : -1], refs[-1]
    leaves, split, main = by_low.leaves, by_low.rows, by_low.main
    size = base_ref.shape[1] // leaves
    tails = sum(came_low[k][by_high.dense_tails : by_high.dense_box, :].astype(F32) for k in range(low))
    for j in range(leaves):
        cols = slice(j * size, (j + 1) * size)
        upper = sum(ref[j * by_low.rows : (j + 1) * by_low.rows, :].astype(F32) for ref in came_high)
        lower = sum(came_low[k][j * by_high.rows : (j + 1) * by_high.rows, :].astype(F32) for k in range(low))
        out_ref[:split, cols] = base_ref[:split, cols] + upper
        out_ref[split:main, cols] = base_ref[split:main, cols] + lower
        out_ref[main:, cols] = base_ref[main:, cols] + tails[j : j + 1]


def call(kernel, out_shape, specs, operands, scratch, flops, room=None):
    outs = jax.tree.leaves(out_shape)
    nbytes = sum(a.size * a.dtype.itemsize for a in (*operands, *outs))
    limit = None if room is None else nbytes + room + 2**21
    return pl.pallas_call(
        kernel,
        out_shape=out_shape,
        in_specs=specs[0],
        out_specs=specs[1],
        scratch_shapes=scratch,
        compiler_params=pltpu.CompilerParams(vmem_limit_bytes=limit),
        cost_estimate=pl.CostEstimate(flops=flops, bytes_accessed=nbytes, transcendentals=0),
    )(*operands)


def per_device(
    probes, basis, transfer, local_blocks, remote_blocks, near_dest, near_leaf, couplings, far_list
):
    columns, points = probes.shape
    leaves, rank, size = basis.shape
    devices = lax.axis_size("leaf")
    main = columns // TILE * TILE
    routes = by_low, by_high = routes_of(devices, main, columns, leaves)
    high, low = grid_of(devices)
    blocks = remote_blocks.shape[0] * remote_blocks.shape[1]
    unit = 2 * columns * size * size
    like = lambda *arrays: [pltpu.VMEM(a.shape, a.dtype) for a in arrays]
    numbers = lambda *arrays: [pltpu.SMEM(a.shape, a.dtype) for a in arrays]
    sems = lambda count: [pltpu.SemaphoreType.DMA((count,))]
    relative = lambda x, way: lax.ppermute(x, "leaf", [(i, i ^ way) for i in range(devices)])
    message = lambda route: jax.ShapeDtypeStruct((route.depth, size), BF16)
    dense = lambda route: jax.ShapeDtypeStruct((route.dense_depth, size), BF16)

    def stacked(count, like_this):
        return pltpu.VMEM((count, *like_this.shape), like_this.dtype)

    dest, leaf = near_dest.T, near_leaf.T
    sent = call(
        functools.partial(products_kernel, routes, devices),
        [message(by_low)] * low + [message(by_high)] * high,
        ([ANY] * 6, [ANY] * (low + high)),
        (dest, leaf, probes, basis, transfer, remote_blocks),
        numbers(dest, leaf)
        + like(probes, basis, transfer, remote_blocks)
        + [
            stacked(low, message(by_low)),
            stacked(high, message(by_high)),
            pltpu.VMEM((high, by_high.meta - by_high.tails, size), F32),
            pltpu.SMEM((devices,), I32),
        ]
        + sems(7 + low + high),
        blocks * unit,
    )
    came_low, came_high = list(sent[:low]), list(sent[low:])
    planes = across_first(high)
    for k in range(1, low):
        came_low[k] = relative(came_low[k], k)
    came_low[0], came_high[0] = call(
        keep_kernel,
        (message(by_low), message(by_high)),
        ([VMEM] * 2, (VMEM,) * 2),
        (came_low[0], came_high[0]),
        [],
        0,
        0,
    )

    for k in planes[1:]:
        came_high[k] = relative(came_high[k], k * low)

    def summed(route, planes, came):
        total = jax.ShapeDtypeStruct((route.fan, (leaves + 1) * route.rows, size), F32)
        tails = jax.ShapeDtypeStruct((route.fan, max(TILE, route.dense_box - route.dense_tails), size), F32)
        ways = len(came)
        return list(
            call(
                functools.partial(sum_kernel, route, planes, ways),
                [dense(route)] * route.fan,
                ([VMEM] * ways, [VMEM] * route.fan),
                came,
                like(total, tails),
                HEAVY if route is by_low else devices * CAP * route.rows * size,
                4 * (total.size + tails.size),
            )
        )

    to_high = summed(by_low, None, [came_low[k] for k in (0, *range(2, low), 1)])
    came_high[0], to_high[0] = lax.optimization_barrier((came_high[0], to_high[0]))
    to_low = summed(by_high, planes, [came_high[k] for k in planes])
    base_shape = jax.ShapeDtypeStruct((columns, points), F32)
    for k in planes[1:]:
        to_high[k] = relative(to_high[k], k * low)
    for k in range(1, low):
        to_low[k] = relative(to_low[k], k)

    probes_then, to_low[1] = lax.optimization_barrier((probes, to_low[1]))
    base, *ready = call(
        local_kernel,
        (
            base_shape,
            jax.ShapeDtypeStruct((2 * rank, 2 * rank * couplings.shape[1]), BF16),
            jax.ShapeDtypeStruct((rank, leaves * rank), BF16),
            jax.ShapeDtypeStruct((leaves // 2, 2 * rank, 2 * size), BF16),
        ),
        ([VMEM] * 5, (VMEM,) * 4),
        (probes_then, local_blocks, couplings, transfer, basis),
        [],
        leaves * leaves * unit,
        0,
    )
    boxes = jax.ShapeDtypeStruct((devices, main // 2, size), BF16)
    base = call(
        functools.partial(far_kernel, by_high, low),
        base_shape,
        ([SMEM] + [VMEM] * (4 + low), VMEM),
        (far_list, base, *ready, *to_low),
        like(boxes, jax.ShapeDtypeStruct((devices, size), F32)),
        4 * leaves * unit,
        4 * boxes.size,
    )
    across = call(
        across_kernel,
        jax.ShapeDtypeStruct((by_low.dense_depth, size), F32),
        ([VMEM] * (high - 1), VMEM),
        [to_high[k] for k in planes[:-1]],
        [],
        HEAVY,
        0,
    )
    return call(
        functools.partial(last_kernel, routes, devices),
        base_shape,
        ([VMEM] * (3 + low), VMEM),
        (base, across, to_high[1], *to_low),
        [],
        devices * columns * size,
        0,
    )


def solution(mesh):
    placed = (
        P(None, ("grp", "leaf")),
        P(("grp", "leaf"), None, None),
        P(("grp", "leaf"), None, None),
        P(("grp", "leaf"), None, None, None),
        P(("grp", "leaf"), None, None, None),
        P(("grp", "leaf"), None),
        P(("grp", "leaf"), None),
        P(("grp", "leaf"), None, None, None),
        P(("grp", "leaf"), None),
    )
    return jax.shard_map(
        per_device, mesh=mesh, in_specs=placed, out_specs=P(None, ("grp", "leaf")), check_vma=False
    )
```

```python
import functools

import jax
import jax.numpy as jnp
from jax import lax
from jax.experimental import pallas as pl
from jax.experimental.pallas import tpu as pltpu
from jax.sharding import PartitionSpec as P

CAP = 4
TILE = 16
HEAVY = 4 * 10**9

F32 = jnp.float32
BF16 = jnp.bfloat16
I32 = jnp.int32

ANY = pl.BlockSpec(memory_space=pl.ANY)
VMEM = pl.BlockSpec(memory_space=pltpu.VMEM)
SMEM = pl.BlockSpec(memory_space=pltpu.SMEM)


def dot_t(lhs, rhs):
    return lax.dot_general(lhs, rhs, (((1,), (1,)), ((), ())), preferred_element_type=F32)


def dot(lhs, rhs):
    return lax.dot_general(lhs, rhs, (((1,), (0,)), ((), ())), preferred_element_type=F32)


class Copies:
    def __init__(self, sems):
        self.sems, self.used = sems, 0

    def start(self, src, dst):
        copy = pltpu.make_async_copy(src, dst, self.sems.at[self.used])
        self.used += 1
        copy.start()
        return copy


def grid_of(devices):
    low = 1 << (devices.bit_length() // 2)
    return devices // low, low


def up(rows):
    return -(-rows // TILE) * TILE


class Route:
    def __init__(self, first, last, fan, extra, main, columns, leaves, sources):
        self.first, self.rows, self.fan, self.extra, self.main = first, last - first, fan, extra, main
        self.leaves, self.half = leaves, main // 2
        slots = fan * CAP
        self.tails = slots * self.rows
        self.meta = self.tails + (up(slots) if extra else 0)
        self.box = self.meta + TILE
        self.depth = self.box + (self.half if extra else 0)
        self.dense_tails = leaves * self.rows
        self.dense_box = self.dense_tails + (up(leaves + sources) if extra else 0)
        self.dense_depth = self.dense_box + (sources * self.half if extra else 0)


def routes_of(devices, main, columns, leaves):
    high, low = grid_of(devices)
    split = up(main * 3 // 4)
    return (
        Route(0, split, high, False, main, columns, leaves, low),
        Route(split, main, low, True, main, columns, leaves, high),
    )


def products_kernel(routes, devices, *refs):
    dest_hbm, leaf_hbm, probes_hbm, basis_hbm, transfer_hbm, blocks_hbm = refs[:6]
    outs = refs[6:-11]
    (
        dest_ref, leaf_ref, probes_ref, basis_ref, transfer_ref, blocks_ref,
        send_low, send_high, tails, count, sems,
    ) = refs[-11:]
    by_low, by_high = routes
    high, low = grid_of(devices)
    me = lax.axis_index("leaf")
    main = by_high.main
    leaves, per_leaf, size = blocks_ref.shape[:3]
    columns, rank = probes_ref.shape[0], basis_ref.shape[1]
    copies = Copies(sems)
    cuts = (0, leaves // 4, leaves)
    arrivals = {}
    early = [
        copies.start(probes_hbm, probes_ref),
        copies.start(dest_hbm, dest_ref),
        copies.start(leaf_hbm, leaf_ref),
    ]
    for j, after in zip(cuts, cuts[1:]):
        part = pl.ds(j, after - j)
        arrivals[j] = copies.start(blocks_hbm.at[part], blocks_ref.at[part])
        if j == 0:
            early += [copies.start(basis_hbm, basis_ref), copies.start(transfer_hbm, transfer_ref)]

    @pl.loop(0, devices)
    def _(i):
        count[i] = 0

    tails[...] = jnp.zeros(tails.shape, F32)
    for copy in early:
        copy.wait()
    box = jnp.zeros((columns, rank), F32)

    numbers = jnp.full((-(-(low + high) // 8) * 8, size), leaves, I32)
    row = lax.broadcasted_iota(I32, numbers.shape, 0)
    lane = lax.broadcasted_iota(I32, numbers.shape, 1)
    for j in range(leaves):
        if j in arrivals:
            arrivals[j].wait()
        x = probes_ref[:, j * size : (j + 1) * size]
        box += dot_t(dot_t(x, basis_ref[j]).astype(BF16), transfer_ref[j])
        for first in range(0, per_leaf, 4):
            many = min(4, per_leaf - first)
            rhs = blocks_ref[j, first : first + many].reshape(many * size, size)
            product = dot_t(x, rhs)
            for b in range(many):
                target = jnp.bitwise_xor(dest_ref[first + b, j], me)
                slot = count[target]
                count[target] = slot + 1
                to_high = lax.shift_right_logical(target, low.bit_length() - 1)
                to_low = jnp.bitwise_and(target, low - 1)
                block = product[:, b * size : (b + 1) * size]
                piece = block[:main].astype(BF16)
                number = leaf_ref[first + b, j]

                at = to_high * CAP + slot
                rows = pl.ds(pl.multiple_of(at * by_low.rows, TILE), by_low.rows)
                send_low[to_low, rows, :] = piece[: by_low.rows]
                numbers = jnp.where((row == to_low) & (lane == at), number, numbers)

                at = to_low * CAP + slot
                rows = pl.ds(pl.multiple_of(at * by_high.rows, TILE), by_high.rows)
                send_high[to_high, rows, :] = piece[by_low.rows :]
                tails[to_high, pl.ds(at, 1), :] = block[main:]
                numbers = jnp.where((row == low + to_high) & (lane == at), number, numbers)

    half = by_high.half
    packed = jnp.concatenate([box[:half], box[half:main]], axis=1).astype(BF16)
    last = jnp.concatenate([box[main:], jnp.zeros_like(box[main:])], axis=1)
    numbers = numbers.astype(F32)
    blank = jnp.zeros((TILE - 2, size), F32)
    for i in range(low):
        tile = jnp.concatenate([numbers[i : i + 1], last, blank], axis=0)
        send_low[i, by_low.meta : by_low.box, :] = tile.astype(BF16)
    for i in range(high):
        tile = jnp.concatenate([numbers[low + i : low + i + 1], last, blank], axis=0)
        send_high[i, by_high.tails : by_high.meta, :] = tails[i].astype(BF16)
        send_high[i, by_high.meta : by_high.box, :] = tile.astype(BF16)
        send_high[i, by_high.box :, :] = packed
    leaving = [copies.start(send_low.at[i], outs[i]) for i in range(low)]
    leaving += [copies.start(send_high.at[i], outs[low + i]) for i in range(high)]
    for copy in leaving:
        copy.wait()


def sum_route(route, came, planes, outs, total, tails):
    leaves, half, ways = route.leaves, route.half, len(came)
    for i in range(ways):
        numbers = came[i][route.meta : route.box, :].astype(F32)[:1].astype(I32)
        if route.extra:
            tail = came[i][route.tails : route.meta, :].astype(F32)
        for k in range(route.fan):
            for slot in range(CAP):
                at = k * CAP + slot
                leaf = numbers[0, at]
                rows = pl.ds(pl.multiple_of(leaf * route.rows, TILE), route.rows)
                total[k, rows, :] += came[i][at * route.rows : (at + 1) * route.rows, :].astype(F32)
                if route.extra:
                    tails[k, pl.ds(leaf, 1), :] += tail[at : at + 1]

    for k in range(route.fan):
        outs[k][: route.dense_tails, :] = total[k, : route.dense_tails, :].astype(BF16)
        if route.extra:
            for i in range(ways):
                last = came[i][route.meta : route.box, :].astype(F32)[1:2]
                at = planes[i]
                tails[k, leaves + at : leaves + at + 1, :] = last
                start = route.dense_box + at * half
                outs[k][start : start + half, :] = came[i][route.box :, :]
            outs[k][route.dense_tails : route.dense_box, :] = tails[k].astype(BF16)


def across_first(high):
    return [0, *range(2, high), 1]


def split(keys, bit):
    return [k for k in keys if k & bit], [k for k in keys if not k & bit]


def sum_kernel(route, planes, ways, places, *refs):
    came, given = refs[:ways], refs[ways:-2]
    total, tails = refs[-2:]
    outs = [given[n] if at is None else given[n].at[at] for n, at in places]
    for ref in (total, tails):
        ref[...] = jnp.zeros(ref.shape, F32)
    sum_route(route, came, planes, outs, total, tails)


def fold_kernel(terms, *refs):
    inputs, outs = refs[: -len(terms)], refs[-len(terms) :]
    for out, entries in zip(outs, terms):
        for i, entry in enumerate(entries):
            out[i] = sum(inputs[n][at].astype(F32) for n, at in entry).astype(BF16)


def keep_kernel(*refs):
    half = len(refs) // 2
    for came, kept in zip(refs[:half], refs[half:]):
        kept[...] = came[...]


def local_kernel(
    probes_ref, local_ref, couplings_ref, transfer_ref, basis_ref, out_ref, pairs_ref, across_ref, twos_ref
):
    rank = basis_ref.shape[1]
    blank = jnp.zeros((rank, rank), BF16)
    for f in range(couplings_ref.shape[1]):
        cols = slice(2 * f * rank, 2 * (f + 1) * rank)
        pairs_ref[:rank, cols] = jnp.concatenate([couplings_ref[0, f], blank], axis=1)
        pairs_ref[rank:, cols] = jnp.concatenate([blank, couplings_ref[0, f]], axis=1)
    for i in range(0, basis_ref.shape[0], 2):
        across_ref[:, i * rank : (i + 2) * rank] = jnp.concatenate([transfer_ref[i], transfer_ref[i + 1]], axis=1)
        none = jnp.zeros_like(basis_ref[i])
        twos_ref[i // 2, :rank, :] = jnp.concatenate([basis_ref[i], none], axis=1)
        twos_ref[i // 2, rank:, :] = jnp.concatenate([none, basis_ref[i + 1]], axis=1)
    leaves, size = local_ref.shape[0], local_ref.shape[2]
    for i in range(0, leaves, 2):
        total = 0.0
        for c in range(0, leaves, 2):
            square = jnp.concatenate(
                [jnp.concatenate([local_ref[r, c], local_ref[r, c + 1]], axis=1) for r in (i, i + 1)], axis=0
            )
            total += dot_t(probes_ref[:, c * size : (c + 2) * size], square)
        out_ref[:, i * size : (i + 2) * size] = total


def far_kernel(by_high, low, partner_ref, base_ref, pairs_ref, across_ref, twos_ref, *refs):
    came, out_ref, boxes, lasts = refs[:low], refs[low], refs[low + 1], refs[low + 2]
    leaves, half = by_high.leaves, by_high.half
    rank = across_ref.shape[0]
    high = boxes.shape[0] // low
    me = lax.axis_index("leaf")
    for k in range(low):
        tile = came[k][by_high.dense_tails : by_high.dense_box, :].astype(F32)
        for i in range(high):
            start = by_high.dense_box + i * half
            boxes[i * low + k] = came[k][start : start + half, :]
            lasts[i * low + k : i * low + k + 1, :] = tile[leaves + i : leaves + i + 1, :]
    chosen = []
    for f in range(partner_ref.shape[1]):
        source = jnp.bitwise_xor(partner_ref[0, f], me)
        rows = jnp.concatenate([boxes[source].astype(F32), lasts[pl.ds(source, 1), :]], axis=0)
        chosen.append(rows.astype(BF16))
    far = 0.0
    for f in range(0, len(chosen), 2):
        cols = slice(2 * f * rank, 2 * (f + 2) * rank)
        far += dot_t(jnp.concatenate(chosen[f : f + 2], axis=1), pairs_ref[:, cols])
    far = jnp.concatenate([far[:half, :rank], far[:half, rank:], far[half:, :rank]], axis=0).astype(BF16)
    down = dot(far, across_ref[...]).astype(BF16)
    size = twos_ref.shape[2]
    for i in range(leaves // 2):
        cols = slice(i * size, (i + 1) * size)
        out_ref[:, cols] = base_ref[:, cols] + dot(down[:, 2 * i * rank : 2 * (i + 1) * rank], twos_ref[i])


def last_kernel(routes, devices, picks, base_ref, *refs):
    by_low, by_high = routes
    high, low = grid_of(devices)
    came_low, out_ref = refs[:low], refs[-1]
    came_high = [ref if at is None else ref.at[at] for ref, at in zip(refs[low:-1], picks)]
    leaves, split, main = by_low.leaves, by_low.rows, by_low.main
    size = base_ref.shape[1] // leaves
    tails = sum(came_low[k][by_high.dense_tails : by_high.dense_box, :].astype(F32) for k in range(low))
    for j in range(leaves):
        cols = slice(j * size, (j + 1) * size)
        upper = sum(ref[j * by_low.rows : (j + 1) * by_low.rows, :].astype(F32) for ref in came_high)
        lower = sum(came_low[k][j * by_high.rows : (j + 1) * by_high.rows, :].astype(F32) for k in range(low))
        out_ref[:split, cols] = base_ref[:split, cols] + upper
        out_ref[split:main, cols] = base_ref[split:main, cols] + lower
        out_ref[main:, cols] = base_ref[main:, cols] + tails[j : j + 1]


def call(kernel, out_shape, specs, operands, scratch, flops, room=None):
    outs = jax.tree.leaves(out_shape)
    nbytes = sum(a.size * a.dtype.itemsize for a in (*operands, *outs))
    limit = None if room is None else nbytes + room + 2**21
    return pl.pallas_call(
        kernel,
        out_shape=out_shape,
        in_specs=specs[0],
        out_specs=specs[1],
        scratch_shapes=scratch,
        compiler_params=pltpu.CompilerParams(vmem_limit_bytes=limit),
        cost_estimate=pl.CostEstimate(flops=flops, bytes_accessed=nbytes, transcendentals=0),
    )(*operands)


def per_device(
    probes, basis, transfer, local_blocks, remote_blocks, near_dest, near_leaf, couplings, far_list
):
    columns, points = probes.shape
    leaves, rank, size = basis.shape
    devices = lax.axis_size("leaf")
    main = columns // TILE * TILE
    routes = by_low, by_high = routes_of(devices, main, columns, leaves)
    high, low = grid_of(devices)
    blocks = remote_blocks.shape[0] * remote_blocks.shape[1]
    unit = 2 * columns * size * size
    like = lambda *arrays: [pltpu.VMEM(a.shape, a.dtype) for a in arrays]
    numbers = lambda *arrays: [pltpu.SMEM(a.shape, a.dtype) for a in arrays]
    sems = lambda count: [pltpu.SemaphoreType.DMA((count,))]
    relative = lambda x, way: lax.ppermute(x, "leaf", [(i, i ^ way) for i in range(devices)])
    message = lambda route: jax.ShapeDtypeStruct((route.depth, size), BF16)
    dense = lambda route: jax.ShapeDtypeStruct((route.dense_depth, size), BF16)

    def stacked(count, like_this):
        return pltpu.VMEM((count, *like_this.shape), like_this.dtype)

    dest, leaf = near_dest.T, near_leaf.T
    sent = call(
        functools.partial(products_kernel, routes, devices),
        [message(by_low)] * low + [message(by_high)] * high,
        ([ANY] * 6, [ANY] * (low + high)),
        (dest, leaf, probes, basis, transfer, remote_blocks),
        numbers(dest, leaf)
        + like(probes, basis, transfer, remote_blocks)
        + [
            stacked(low, message(by_low)),
            stacked(high, message(by_high)),
            pltpu.VMEM((high, by_high.meta - by_high.tails, size), F32),
            pltpu.SMEM((devices,), I32),
        ]
        + sems(7 + low + high),
        blocks * unit,
    )
    came_low, came_high = list(sent[:low]), list(sent[low:])
    planes = across_first(high)
    for k in range(1, low):
        came_low[k] = relative(came_low[k], k)
    came_low[0], came_high[0] = call(
        keep_kernel,
        (message(by_low), message(by_high)),
        ([VMEM] * 2, (VMEM,) * 2),
        (came_low[0], came_high[0]),
        [],
        0,
        0,
    )

    for k in planes[1:]:
        came_high[k] = relative(came_high[k], k * low)

    def summed(route, planes, came, outs, places):
        total = jax.ShapeDtypeStruct((route.fan, (leaves + 1) * route.rows, size), F32)
        tails = jax.ShapeDtypeStruct((route.fan, max(TILE, route.dense_box - route.dense_tails), size), F32)
        ways = len(came)
        return list(
            call(
                functools.partial(sum_kernel, route, planes, ways, places),
                outs,
                ([VMEM] * ways, [VMEM] * len(outs)),
                came,
                like(total, tails),
                HEAVY,
                4 * (total.size + tails.size),
            )
        )

    stack = lambda keys: jax.ShapeDtypeStruct((len(keys), by_low.dense_depth, size), BF16)
    leaving, staying = split(range(2, high), 1)
    places = [(0, None), (1, None)]
    places += [(2, leaving.index(k)) if k in leaving else (3, staying.index(k)) for k in range(2, high)]
    own, beside, going, kept = summed(
        by_low,
        None,
        [came_low[k] for k in (0, *range(2, low), 1)],
        [dense(by_low), dense(by_low), stack(leaving), stack(staying)],
        places,
    )
    came_high[0], own = lax.optimization_barrier((came_high[0], own))
    to_low = summed(
        by_high,
        planes,
        [came_high[k] for k in planes],
        [dense(by_high)] * low,
        [(p, None) for p in range(low)],
    )
    across, bit = [], 1
    while True:
        came = relative(going, bit * low)
        arrived = [k ^ bit for k in leaving]
        across += [(came, arrived.index(0))] if 0 in arrived else []
        bit *= 2
        if bit >= high:
            break
        leaving, rest = split(staying, bit)
        entry = lambda k: [(0, staying.index(k))] + ([(1, arrived.index(k))] if k in arrived else [])
        groups = [group for group in (leaving, rest) if group]
        going, *kept_next = call(
            functools.partial(fold_kernel, [[entry(k) for k in group] for group in groups]),
            [stack(group) for group in groups],
            ([VMEM] * 2, [VMEM] * len(groups)),
            (kept, came),
            [],
            going.size,
            0,
        )
        kept, staying = (kept_next[0] if kept_next else None), rest
    beside = relative(beside, low)
    base_shape = jax.ShapeDtypeStruct((columns, points), F32)
    for k in range(1, low):
        to_low[k] = relative(to_low[k], k)

    probes_then, to_low[1] = lax.optimization_barrier((probes, to_low[1]))
    base, *ready = call(
        local_kernel,
        (
            base_shape,
            jax.ShapeDtypeStruct((2 * rank, 2 * rank * couplings.shape[1]), BF16),
            jax.ShapeDtypeStruct((rank, leaves * rank), BF16),
            jax.ShapeDtypeStruct((leaves // 2, 2 * rank, 2 * size), BF16),
        ),
        ([VMEM] * 5, (VMEM,) * 4),
        (probes_then, local_blocks, couplings, transfer, basis),
        [],
        leaves * leaves * unit,
        0,
    )
    boxes = jax.ShapeDtypeStruct((devices, main // 2, size), BF16)
    base = call(
        functools.partial(far_kernel, by_high, low),
        base_shape,
        ([SMEM] + [VMEM] * (4 + low), VMEM),
        (far_list, base, *ready, *to_low),
        like(boxes, jax.ShapeDtypeStruct((devices, size), F32)),
        HEAVY,
        4 * boxes.size,
    )
    came = [(own, None), (beside, None), *across]
    return call(
        functools.partial(last_kernel, routes, devices, [at for _, at in came]),
        base_shape,
        ([VMEM] * (1 + low + len(came)), VMEM),
        (base, *to_low, *(ref for ref, _ in came)),
        [],
        devices * columns * size,
        0,
    )


def solution(mesh):
    placed = (
        P(None, ("grp", "leaf")),
        P(("grp", "leaf"), None, None),
        P(("grp", "leaf"), None, None),
        P(("grp", "leaf"), None, None, None),
        P(("grp", "leaf"), None, None, None),
        P(("grp", "leaf"), None),
        P(("grp", "leaf"), None),
        P(("grp", "leaf"), None, None, None),
        P(("grp", "leaf"), None),
    )
    return jax.shard_map(
        per_device, mesh=mesh, in_specs=placed, out_specs=P(None, ("grp", "leaf")), check_vma=False
    )
```

```python
import functools

import jax
import jax.numpy as jnp
from jax import lax
from jax.experimental import pallas as pl
from jax.experimental.pallas import tpu as pltpu
from jax.sharding import PartitionSpec as P

CAP = 4
TILE = 16
HEAVY = 4 * 10**9

F32 = jnp.float32
BF16 = jnp.bfloat16
I32 = jnp.int32

ANY = pl.BlockSpec(memory_space=pl.ANY)
VMEM = pl.BlockSpec(memory_space=pltpu.VMEM)
SMEM = pl.BlockSpec(memory_space=pltpu.SMEM)


def dot_t(lhs, rhs):
    return lax.dot_general(lhs, rhs, (((1,), (1,)), ((), ())), preferred_element_type=F32)


def dot(lhs, rhs):
    return lax.dot_general(lhs, rhs, (((1,), (0,)), ((), ())), preferred_element_type=F32)


class Copies:
    def __init__(self, sems):
        self.sems, self.used = sems, 0

    def start(self, src, dst):
        copy = pltpu.make_async_copy(src, dst, self.sems.at[self.used])
        self.used += 1
        copy.start()
        return copy


def grid_of(devices):
    low = 1 << (devices.bit_length() // 2)
    return devices // low, low


def up(rows):
    return -(-rows // TILE) * TILE


class Route:
    def __init__(self, first, last, fan, extra, main, columns, leaves, sources):
        self.first, self.rows, self.fan, self.extra, self.main = first, last - first, fan, extra, main
        self.leaves, self.half = leaves, main // 2
        slots = fan * CAP
        self.tails = slots * self.rows
        self.meta = self.tails + (up(slots) if extra else 0)
        self.box = self.meta + TILE
        self.depth = self.box + (self.half if extra else 0)
        self.dense_tails = leaves * self.rows
        self.dense_box = self.dense_tails + (up(leaves + sources) if extra else 0)
        self.dense_depth = self.dense_box + (sources * self.half if extra else 0)


def routes_of(devices, main, columns, leaves):
    high, low = grid_of(devices)
    split = up(main * 3 // 4)
    return (
        Route(0, split, high, False, main, columns, leaves, low),
        Route(split, main, low, True, main, columns, leaves, high),
    )


def products_kernel(routes, devices, *refs):
    dest_hbm, leaf_hbm, probes_hbm, basis_hbm, transfer_hbm, blocks_hbm = refs[:6]
    outs = refs[6:-11]
    (
        dest_ref, leaf_ref, probes_ref, basis_ref, transfer_ref, blocks_ref,
        send_low, send_high, tails, count, sems,
    ) = refs[-11:]
    by_low, by_high = routes
    high, low = grid_of(devices)
    me = lax.axis_index("leaf")
    main = by_high.main
    leaves, per_leaf, size = blocks_ref.shape[:3]
    columns, rank = probes_ref.shape[0], basis_ref.shape[1]
    copies = Copies(sems)
    cuts = (0, leaves // 4, leaves)
    arrivals = {}
    early = [
        copies.start(probes_hbm, probes_ref),
        copies.start(dest_hbm, dest_ref),
        copies.start(leaf_hbm, leaf_ref),
    ]
    for j, after in zip(cuts, cuts[1:]):
        part = pl.ds(j, after - j)
        arrivals[j] = copies.start(blocks_hbm.at[part], blocks_ref.at[part])
        if j == 0:
            early += [copies.start(basis_hbm, basis_ref), copies.start(transfer_hbm, transfer_ref)]

    @pl.loop(0, devices)
    def _(i):
        count[i] = 0

    tails[...] = jnp.zeros(tails.shape, F32)
    for copy in early:
        copy.wait()
    box = jnp.zeros((columns, rank), F32)

    numbers = jnp.full((-(-(low + high) // 8) * 8, size), leaves, I32)
    row = lax.broadcasted_iota(I32, numbers.shape, 0)
    lane = lax.broadcasted_iota(I32, numbers.shape, 1)
    for j in range(leaves):
        if j in arrivals:
            arrivals[j].wait()
        x = probes_ref[:, j * size : (j + 1) * size]
        box += dot_t(dot_t(x, basis_ref[j]).astype(BF16), transfer_ref[j])
        for first in range(0, per_leaf, 4):
            many = min(4, per_leaf - first)
            rhs = blocks_ref[j, first : first + many].reshape(many * size, size)
            product = dot_t(x, rhs)
            for b in range(many):
                target = jnp.bitwise_xor(dest_ref[first + b, j], me)
                slot = count[target]
                count[target] = slot + 1
                to_high = lax.shift_right_logical(target, low.bit_length() - 1)
                to_low = jnp.bitwise_and(target, low - 1)
                block = product[:, b * size : (b + 1) * size]
                piece = block[:main].astype(BF16)
                number = leaf_ref[first + b, j]

                at = to_high * CAP + slot
                rows = pl.ds(pl.multiple_of(at * by_low.rows, TILE), by_low.rows)
                send_low[to_low, rows, :] = piece[: by_low.rows]
                numbers = jnp.where((row == to_low) & (lane == at), number, numbers)

                at = to_low * CAP + slot
                rows = pl.ds(pl.multiple_of(at * by_high.rows, TILE), by_high.rows)
                send_high[to_high, rows, :] = piece[by_low.rows :]
                tails[to_high, pl.ds(at, 1), :] = block[main:]
                numbers = jnp.where((row == low + to_high) & (lane == at), number, numbers)

    half = by_high.half
    packed = jnp.concatenate([box[:half], box[half:main]], axis=1).astype(BF16)
    last = jnp.concatenate([box[main:], jnp.zeros_like(box[main:])], axis=1)
    numbers = numbers.astype(F32)
    blank = jnp.zeros((TILE - 2, size), F32)
    for i in range(low):
        tile = jnp.concatenate([numbers[i : i + 1], last, blank], axis=0)
        send_low[i, by_low.meta : by_low.box, :] = tile.astype(BF16)
    for i in range(high):
        tile = jnp.concatenate([numbers[low + i : low + i + 1], last, blank], axis=0)
        send_high[i, by_high.tails : by_high.meta, :] = tails[i].astype(BF16)
        send_high[i, by_high.meta : by_high.box, :] = tile.astype(BF16)
        send_high[i, by_high.box :, :] = packed
    leaving = [copies.start(send_low.at[i], outs[i]) for i in range(low)]
    leaving += [copies.start(send_high.at[i], outs[low + i]) for i in range(high)]
    for copy in leaving:
        copy.wait()


def sum_route(route, came, planes, outs, total, tails):
    leaves, half, ways = route.leaves, route.half, len(came)
    for i in range(ways):
        numbers = came[i][route.meta : route.box, :].astype(F32)[:1].astype(I32)
        if route.extra:
            tail = came[i][route.tails : route.meta, :].astype(F32)
        for k in range(route.fan):
            for slot in range(CAP):
                at = k * CAP + slot
                leaf = numbers[0, at]
                rows = pl.ds(pl.multiple_of(leaf * route.rows, TILE), route.rows)
                total[k, rows, :] += came[i][at * route.rows : (at + 1) * route.rows, :].astype(F32)
                if route.extra:
                    tails[k, pl.ds(leaf, 1), :] += tail[at : at + 1]

    for k in range(route.fan):
        outs[k][: route.dense_tails, :] = total[k, : route.dense_tails, :].astype(BF16)
        if route.extra:
            for i in range(ways):
                last = came[i][route.meta : route.box, :].astype(F32)[1:2]
                at = planes[i]
                tails[k, leaves + at : leaves + at + 1, :] = last
                start = route.dense_box + at * half
                outs[k][start : start + half, :] = came[i][route.box :, :]
            outs[k][route.dense_tails : route.dense_box, :] = tails[k].astype(BF16)


def across_first(high):
    return [0, *range(2, high), 1]


def split(keys, bit):
    return [k for k in keys if k & bit], [k for k in keys if not k & bit]


def sum_kernel(route, planes, ways, places, *refs):
    came, given = refs[:ways], refs[ways:-2]
    total, tails = refs[-2:]
    outs = [given[n] if at is None else given[n].at[at] for n, at in places]
    for ref in (total, tails):
        ref[...] = jnp.zeros(ref.shape, F32)
    sum_route(route, came, planes, outs, total, tails)


def fold_kernel(terms, *refs):
    inputs, outs = refs[: -len(terms)], refs[-len(terms) :]
    for out, entries in zip(outs, terms):
        for i, entry in enumerate(entries):
            out[i] = sum(inputs[n][at].astype(F32) for n, at in entry).astype(BF16)


def keep_kernel(*refs):
    half = len(refs) // 2
    for came, kept in zip(refs[:half], refs[half:]):
        kept[...] = came[...]


def local_kernel(
    probes_ref, local_ref, couplings_ref, transfer_ref, basis_ref, out_ref, pairs_ref, across_ref, twos_ref
):
    rank = basis_ref.shape[1]
    blank = jnp.zeros((rank, rank), BF16)
    for f in range(couplings_ref.shape[1]):
        cols = slice(2 * f * rank, 2 * (f + 1) * rank)
        pairs_ref[:rank, cols] = jnp.concatenate([couplings_ref[0, f], blank], axis=1)
        pairs_ref[rank:, cols] = jnp.concatenate([blank, couplings_ref[0, f]], axis=1)
    for i in range(0, basis_ref.shape[0], 2):
        across_ref[:, i * rank : (i + 2) * rank] = jnp.concatenate([transfer_ref[i], transfer_ref[i + 1]], axis=1)
        none = jnp.zeros_like(basis_ref[i])
        twos_ref[i // 2, :rank, :] = jnp.concatenate([basis_ref[i], none], axis=1)
        twos_ref[i // 2, rank:, :] = jnp.concatenate([none, basis_ref[i + 1]], axis=1)
    leaves, size = local_ref.shape[0], local_ref.shape[2]
    for i in range(0, leaves, 2):
        total = 0.0
        for c in range(0, leaves, 2):
            square = jnp.concatenate(
                [jnp.concatenate([local_ref[r, c], local_ref[r, c + 1]], axis=1) for r in (i, i + 1)], axis=0
            )
            total += dot_t(probes_ref[:, c * size : (c + 2) * size], square)
        out_ref[:, i * size : (i + 2) * size] = total


def far_kernel(by_high, low, partner_ref, base_ref, pairs_ref, across_ref, twos_ref, *refs):
    came, out_ref, boxes, lasts = refs[:low], refs[low], refs[low + 1], refs[low + 2]
    leaves, half = by_high.leaves, by_high.half
    rank = across_ref.shape[0]
    high = boxes.shape[0] // low
    me = lax.axis_index("leaf")
    for k in range(low):
        tile = came[k][by_high.dense_tails : by_high.dense_box, :].astype(F32)
        for i in range(high):
            start = by_high.dense_box + i * half
            boxes[i * low + k] = came[k][start : start + half, :]
            lasts[i * low + k : i * low + k + 1, :] = tile[leaves + i : leaves + i + 1, :]
    chosen = []
    for f in range(partner_ref.shape[1]):
        source = jnp.bitwise_xor(partner_ref[0, f], me)
        rows = jnp.concatenate([boxes[source].astype(F32), lasts[pl.ds(source, 1), :]], axis=0)
        chosen.append(rows.astype(BF16))
    far = 0.0
    for f in range(0, len(chosen), 2):
        cols = slice(2 * f * rank, 2 * (f + 2) * rank)
        far += dot_t(jnp.concatenate(chosen[f : f + 2], axis=1), pairs_ref[:, cols])
    far = jnp.concatenate([far[:half, :rank], far[:half, rank:], far[half:, :rank]], axis=0).astype(BF16)
    down = dot(far, across_ref[...]).astype(BF16)
    size = twos_ref.shape[2]
    for i in range(leaves // 2):
        cols = slice(i * size, (i + 1) * size)
        out_ref[:, cols] = base_ref[:, cols] + dot(down[:, 2 * i * rank : 2 * (i + 1) * rank], twos_ref[i])


def last_kernel(routes, devices, picks, base_ref, *refs):
    by_low, by_high = routes
    high, low = grid_of(devices)
    came_low, out_ref = refs[:low], refs[-1]
    came_high = [ref if at is None else ref.at[at] for ref, at in zip(refs[low:-1], picks)]
    leaves, split, main = by_low.leaves, by_low.rows, by_low.main
    size = base_ref.shape[1] // leaves
    tails = sum(came_low[k][by_high.dense_tails : by_high.dense_box, :].astype(F32) for k in range(low))
    for j in range(leaves):
        cols = slice(j * size, (j + 1) * size)
        upper = sum(ref[j * by_low.rows : (j + 1) * by_low.rows, :].astype(F32) for ref in came_high)
        lower = sum(came_low[k][j * by_high.rows : (j + 1) * by_high.rows, :].astype(F32) for k in range(low))
        out_ref[:split, cols] = base_ref[:split, cols] + upper
        out_ref[split:main, cols] = base_ref[split:main, cols] + lower
        out_ref[main:, cols] = base_ref[main:, cols] + tails[j : j + 1]


def call(kernel, out_shape, specs, operands, scratch, flops, room=None):
    outs = jax.tree.leaves(out_shape)
    nbytes = sum(a.size * a.dtype.itemsize for a in (*operands, *outs))
    limit = None if room is None else nbytes + room + 2**21
    return pl.pallas_call(
        kernel,
        out_shape=out_shape,
        in_specs=specs[0],
        out_specs=specs[1],
        scratch_shapes=scratch,
        compiler_params=pltpu.CompilerParams(vmem_limit_bytes=limit),
        cost_estimate=pl.CostEstimate(flops=flops, bytes_accessed=nbytes, transcendentals=0),
    )(*operands)


def per_device(
    probes, basis, transfer, local_blocks, remote_blocks, near_dest, near_leaf, couplings, far_list
):
    columns, points = probes.shape
    leaves, rank, size = basis.shape
    devices = lax.axis_size("leaf")
    main = columns // TILE * TILE
    routes = by_low, by_high = routes_of(devices, main, columns, leaves)
    high, low = grid_of(devices)
    blocks = remote_blocks.shape[0] * remote_blocks.shape[1]
    unit = 2 * columns * size * size
    like = lambda *arrays: [pltpu.VMEM(a.shape, a.dtype) for a in arrays]
    numbers = lambda *arrays: [pltpu.SMEM(a.shape, a.dtype) for a in arrays]
    sems = lambda count: [pltpu.SemaphoreType.DMA((count,))]
    relative = lambda x, way: lax.ppermute(x, "leaf", [(i, i ^ way) for i in range(devices)])
    message = lambda route: jax.ShapeDtypeStruct((route.depth, size), BF16)
    dense = lambda route: jax.ShapeDtypeStruct((route.dense_depth, size), BF16)

    def stacked(count, like_this):
        return pltpu.VMEM((count, *like_this.shape), like_this.dtype)

    dest, leaf = near_dest.T, near_leaf.T
    sent = call(
        functools.partial(products_kernel, routes, devices),
        [message(by_low)] * low + [message(by_high)] * high,
        ([ANY] * 6, [ANY] * (low + high)),
        (dest, leaf, probes, basis, transfer, remote_blocks),
        numbers(dest, leaf)
        + like(probes, basis, transfer, remote_blocks)
        + [
            stacked(low, message(by_low)),
            stacked(high, message(by_high)),
            pltpu.VMEM((high, by_high.meta - by_high.tails, size), F32),
            pltpu.SMEM((devices,), I32),
        ]
        + sems(7 + low + high),
        blocks * unit,
    )
    came_low, came_high = list(sent[:low]), list(sent[low:])
    planes = across_first(high)
    for k in range(1, low):
        came_low[k] = relative(came_low[k], k)
    came_low[0], came_high[0] = call(
        keep_kernel,
        (message(by_low), message(by_high)),
        ([VMEM] * 2, (VMEM,) * 2),
        (came_low[0], came_high[0]),
        [],
        0,
        0,
    )

    for k in planes[1:]:
        came_high[k] = relative(came_high[k], k * low)

    def summed(route, planes, came, outs, places):
        total = jax.ShapeDtypeStruct((route.fan, (leaves + 1) * route.rows, size), F32)
        tails = jax.ShapeDtypeStruct((route.fan, max(TILE, route.dense_box - route.dense_tails), size), F32)
        ways = len(came)
        return list(
            call(
                functools.partial(sum_kernel, route, planes, ways, places),
                outs,
                ([VMEM] * ways, [VMEM] * len(outs)),
                came,
                like(total, tails),
                HEAVY,
                4 * (total.size + tails.size),
            )
        )

    stack = lambda keys: jax.ShapeDtypeStruct((len(keys), by_low.dense_depth, size), BF16)
    leaving, staying = split(range(2, high), 1)
    places = [(0, None), (1, None)]
    places += [(2, leaving.index(k)) if k in leaving else (3, staying.index(k)) for k in range(2, high)]
    own, beside, going, kept = summed(
        by_low,
        None,
        [came_low[k] for k in (0, *range(2, low), 1)],
        [dense(by_low), dense(by_low), stack(leaving), stack(staying)],
        places,
    )
    came_high[0], own = lax.optimization_barrier((came_high[0], own))
    to_low = summed(
        by_high,
        planes,
        [came_high[k] for k in planes],
        [dense(by_high)] * low,
        [(p, None) for p in range(low)],
    )
    across, bit = [], 1
    while True:
        came = relative(going, bit * low)
        arrived = [k ^ bit for k in leaving]
        across += [(came, arrived.index(0))] if 0 in arrived else []
        bit *= 2
        if bit >= high:
            break
        leaving, rest = split(staying, bit)
        entry = lambda k: [(0, staying.index(k))] + ([(1, arrived.index(k))] if k in arrived else [])
        groups = [group for group in (leaving, rest) if group]
        going, *kept_next = call(
            functools.partial(fold_kernel, [[entry(k) for k in group] for group in groups]),
            [stack(group) for group in groups],
            ([VMEM] * 2, [VMEM] * len(groups)),
            (kept, came),
            [],
            going.size,
            0,
        )
        kept, staying = (kept_next[0] if kept_next else None), rest
        beside, probes_then, going = lax.optimization_barrier((beside, probes, going))
    beside = relative(beside, low)
    base_shape = jax.ShapeDtypeStruct((columns, points), F32)
    for k in range(1, low):
        to_low[k] = relative(to_low[k], k)

    base, *ready = call(
        local_kernel,
        (
            base_shape,
            jax.ShapeDtypeStruct((2 * rank, 2 * rank * couplings.shape[1]), BF16),
            jax.ShapeDtypeStruct((rank, leaves * rank), BF16),
            jax.ShapeDtypeStruct((leaves // 2, 2 * rank, 2 * size), BF16),
        ),
        ([VMEM] * 5, (VMEM,) * 4),
        (probes_then, local_blocks, couplings, transfer, basis),
        [],
        leaves * leaves * unit,
        0,
    )
    boxes = jax.ShapeDtypeStruct((devices, main // 2, size), BF16)
    base = call(
        functools.partial(far_kernel, by_high, low),
        base_shape,
        ([SMEM] + [VMEM] * (4 + low), VMEM),
        (far_list, base, *ready, *to_low),
        like(boxes, jax.ShapeDtypeStruct((devices, size), F32)),
        HEAVY,
        4 * boxes.size,
    )
    came = [(own, None), *across, (beside, None)]
    return call(
        functools.partial(last_kernel, routes, devices, [at for _, at in came]),
        base_shape,
        ([VMEM] * (1 + low + len(came)), VMEM),
        (base, *to_low, *(ref for ref, _ in came)),
        [],
        devices * columns * size,
        0,
    )


def solution(mesh):
    placed = (
        P(None, ("grp", "leaf")),
        P(("grp", "leaf"), None, None),
        P(("grp", "leaf"), None, None),
        P(("grp", "leaf"), None, None, None),
        P(("grp", "leaf"), None, None, None),
        P(("grp", "leaf"), None),
        P(("grp", "leaf"), None),
        P(("grp", "leaf"), None, None, None),
        P(("grp", "leaf"), None),
    )
    return jax.shard_map(
        per_device, mesh=mesh, in_specs=placed, out_specs=P(None, ("grp", "leaf")), check_vma=False
    )
```

```python
import functools

import jax
import jax.numpy as jnp
from jax import lax
from jax.experimental import pallas as pl
from jax.experimental.pallas import tpu as pltpu
from jax.sharding import PartitionSpec as P

CAP = 4
TILE = 16
HEAVY = 4 * 10**9

F32 = jnp.float32
BF16 = jnp.bfloat16
I32 = jnp.int32

ANY = pl.BlockSpec(memory_space=pl.ANY)
VMEM = pl.BlockSpec(memory_space=pltpu.VMEM)
SMEM = pl.BlockSpec(memory_space=pltpu.SMEM)


def dot_t(lhs, rhs):
    return lax.dot_general(lhs, rhs, (((1,), (1,)), ((), ())), preferred_element_type=F32)


def dot(lhs, rhs):
    return lax.dot_general(lhs, rhs, (((1,), (0,)), ((), ())), preferred_element_type=F32)


class Copies:
    def __init__(self, sems):
        self.sems, self.used = sems, 0

    def start(self, src, dst):
        copy = pltpu.make_async_copy(src, dst, self.sems.at[self.used])
        self.used += 1
        copy.start()
        return copy


def grid_of(devices):
    low = 1 << (devices.bit_length() // 2)
    return devices // low, low


def up(rows):
    return -(-rows // TILE) * TILE


class Route:
    def __init__(self, first, last, fan, extra, main, columns, leaves, sources):
        self.first, self.rows, self.fan, self.extra, self.main = first, last - first, fan, extra, main
        self.leaves, self.half = leaves, main // 2
        slots = fan * CAP
        self.tails = slots * self.rows
        self.meta = self.tails + (up(slots) if extra else 0)
        self.box = self.meta + TILE
        self.depth = self.box + (self.half if extra else 0)
        self.dense_tails = leaves * self.rows
        self.dense_box = self.dense_tails + (up(leaves + sources) if extra else 0)
        self.dense_depth = self.dense_box + (sources * self.half if extra else 0)


def routes_of(devices, main, columns, leaves):
    high, low = grid_of(devices)
    split = up(main * 3 // 4)
    return (
        Route(0, split, high, False, main, columns, leaves, low),
        Route(split, main, low, True, main, columns, leaves, high),
    )


def products_kernel(routes, devices, *refs):
    dest_hbm, leaf_hbm, probes_hbm, basis_hbm, transfer_hbm, blocks_hbm = refs[:6]
    outs = refs[6:-11]
    (
        dest_ref, leaf_ref, probes_ref, basis_ref, transfer_ref, blocks_ref,
        send_low, send_high, tails, count, sems,
    ) = refs[-11:]
    by_low, by_high = routes
    high, low = grid_of(devices)
    me = lax.axis_index("leaf")
    main = by_high.main
    leaves, per_leaf, size = blocks_ref.shape[:3]
    columns, rank = probes_ref.shape[0], basis_ref.shape[1]
    copies = Copies(sems)
    first_leaves = leaves // 4
    early = [
        copies.start(probes_hbm, probes_ref),
        copies.start(dest_hbm, dest_ref),
        copies.start(leaf_hbm, leaf_ref),
    ]
    early += [copies.start(blocks_hbm.at[j], blocks_ref.at[j]) for j in range(first_leaves)]
    later = [copies.start(blocks_hbm.at[j], blocks_ref.at[j]) for j in range(first_leaves, leaves)]
    later += [copies.start(basis_hbm, basis_ref), copies.start(transfer_hbm, transfer_ref)]

    @pl.loop(0, devices)
    def _(i):
        count[i] = 0

    tails[...] = jnp.zeros(tails.shape, F32)
    for copy in early:
        copy.wait()
    box = jnp.zeros((columns, rank), F32)

    numbers = jnp.full((-(-(low + high) // 8) * 8, size), leaves, I32)
    row = lax.broadcasted_iota(I32, numbers.shape, 0)
    lane = lax.broadcasted_iota(I32, numbers.shape, 1)
    for j in range(leaves):
        if j == first_leaves:
            for copy in later:
                copy.wait()
        x = probes_ref[:, j * size : (j + 1) * size]
        for i in [j - first_leaves, *([j] if j >= leaves - first_leaves else [])] if j >= first_leaves else []:
            coef = dot_t(probes_ref[:, i * size : (i + 1) * size], basis_ref[i]).astype(BF16)
            box += dot_t(coef, transfer_ref[i])
        for first in range(0, per_leaf, 4):
            many = min(4, per_leaf - first)
            rhs = blocks_ref[j, first : first + many].reshape(many * size, size)
            product = dot_t(x, rhs)
            for b in range(many):
                target = jnp.bitwise_xor(dest_ref[first + b, j], me)
                slot = count[target]
                count[target] = slot + 1
                to_high = lax.shift_right_logical(target, low.bit_length() - 1)
                to_low = jnp.bitwise_and(target, low - 1)
                block = product[:, b * size : (b + 1) * size]
                piece = block[:main].astype(BF16)
                number = leaf_ref[first + b, j]

                at = to_high * CAP + slot
                rows = pl.ds(pl.multiple_of(at * by_low.rows, TILE), by_low.rows)
                send_low[to_low, rows, :] = piece[: by_low.rows]
                numbers = jnp.where((row == to_low) & (lane == at), number, numbers)

                at = to_low * CAP + slot
                rows = pl.ds(pl.multiple_of(at * by_high.rows, TILE), by_high.rows)
                send_high[to_high, rows, :] = piece[by_low.rows :]
                tails[to_high, pl.ds(at, 1), :] = block[main:]
                numbers = jnp.where((row == low + to_high) & (lane == at), number, numbers)

    half = by_high.half
    packed = jnp.concatenate([box[:half], box[half:main]], axis=1).astype(BF16)
    last = jnp.concatenate([box[main:], jnp.zeros_like(box[main:])], axis=1)
    numbers = numbers.astype(F32)
    blank = jnp.zeros((TILE - 2, size), F32)
    for i in range(low):
        tile = jnp.concatenate([numbers[i : i + 1], last, blank], axis=0)
        send_low[i, by_low.meta : by_low.box, :] = tile.astype(BF16)
    for i in range(high):
        tile = jnp.concatenate([numbers[low + i : low + i + 1], last, blank], axis=0)
        send_high[i, by_high.tails : by_high.meta, :] = tails[i].astype(BF16)
        send_high[i, by_high.meta : by_high.box, :] = tile.astype(BF16)
        send_high[i, by_high.box :, :] = packed
    leaving = [copies.start(send_low.at[i], outs[i]) for i in range(low)]
    leaving += [copies.start(send_high.at[i], outs[low + i]) for i in range(high)]
    for copy in leaving:
        copy.wait()


def sum_route(route, came, planes, outs, total, tails):
    leaves, half, ways = route.leaves, route.half, len(came)
    for i in range(ways):
        numbers = came[i][route.meta : route.box, :].astype(F32)[:1].astype(I32)
        if route.extra:
            tail = came[i][route.tails : route.meta, :].astype(F32)
        for k in range(route.fan):
            for slot in range(CAP):
                at = k * CAP + slot
                leaf = numbers[0, at]
                rows = pl.ds(pl.multiple_of(leaf * route.rows, TILE), route.rows)
                total[k, rows, :] += came[i][at * route.rows : (at + 1) * route.rows, :].astype(F32)
                if route.extra:
                    tails[k, pl.ds(leaf, 1), :] += tail[at : at + 1]

    for k in range(route.fan):
        outs[k][: route.dense_tails, :] = total[k, : route.dense_tails, :].astype(BF16)
        if route.extra:
            for i in range(ways):
                last = came[i][route.meta : route.box, :].astype(F32)[1:2]
                at = planes[i]
                tails[k, leaves + at : leaves + at + 1, :] = last
                start = route.dense_box + at * half
                outs[k][start : start + half, :] = came[i][route.box :, :]
            outs[k][route.dense_tails : route.dense_box, :] = tails[k].astype(BF16)


def across_first(high):
    return [0, *range(2, high), 1]


def sum_kernel(route, planes, ways, *refs):
    came, outs = refs[:ways], refs[ways:-2]
    total, tails = refs[-2:]
    for ref in (total, tails):
        ref[...] = jnp.zeros(ref.shape, F32)
    sum_route(route, came, planes, outs, total, tails)


def keep_kernel(*refs):
    half = len(refs) // 2
    for came, kept in zip(refs[:half], refs[half:]):
        kept[...] = came[...]


def local_kernel(
    probes_ref, local_ref, couplings_ref, transfer_ref, basis_ref, out_ref, pairs_ref, across_ref, twos_ref
):
    rank = basis_ref.shape[1]
    blank = jnp.zeros((rank, rank), BF16)
    for f in range(couplings_ref.shape[1]):
        cols = slice(2 * f * rank, 2 * (f + 1) * rank)
        pairs_ref[:rank, cols] = jnp.concatenate([couplings_ref[0, f], blank], axis=1)
        pairs_ref[rank:, cols] = jnp.concatenate([blank, couplings_ref[0, f]], axis=1)
    for i in range(0, basis_ref.shape[0], 2):
        across_ref[:, i * rank : (i + 2) * rank] = jnp.concatenate([transfer_ref[i], transfer_ref[i + 1]], axis=1)
        none = jnp.zeros_like(basis_ref[i])
        twos_ref[i // 2, :rank, :] = jnp.concatenate([basis_ref[i], none], axis=1)
        twos_ref[i // 2, rank:, :] = jnp.concatenate([none, basis_ref[i + 1]], axis=1)
    leaves, size = local_ref.shape[0], local_ref.shape[2]
    for i in range(0, leaves, 2):
        total = 0.0
        for c in range(0, leaves, 2):
            square = jnp.concatenate(
                [jnp.concatenate([local_ref[r, c], local_ref[r, c + 1]], axis=1) for r in (i, i + 1)], axis=0
            )
            total += dot_t(probes_ref[:, c * size : (c + 2) * size], square)
        out_ref[:, i * size : (i + 2) * size] = total


def far_kernel(by_high, low, partner_ref, base_ref, pairs_ref, across_ref, twos_ref, *refs):
    came, out_ref, boxes, lasts = refs[:low], refs[low], refs[low + 1], refs[low + 2]
    leaves, half = by_high.leaves, by_high.half
    rank = across_ref.shape[0]
    high = boxes.shape[0] // low
    me = lax.axis_index("leaf")
    for k in range(low):
        tile = came[k][by_high.dense_tails : by_high.dense_box, :].astype(F32)
        for i in range(high):
            start = by_high.dense_box + i * half
            boxes[i * low + k] = came[k][start : start + half, :]
            lasts[i * low + k : i * low + k + 1, :] = tile[leaves + i : leaves + i + 1, :]
    chosen = []
    for f in range(partner_ref.shape[1]):
        source = jnp.bitwise_xor(partner_ref[0, f], me)
        rows = jnp.concatenate([boxes[source].astype(F32), lasts[pl.ds(source, 1), :]], axis=0)
        chosen.append(rows.astype(BF16))
    far = 0.0
    for f in range(0, len(chosen), 2):
        cols = slice(2 * f * rank, 2 * (f + 2) * rank)
        far += dot_t(jnp.concatenate(chosen[f : f + 2], axis=1), pairs_ref[:, cols])
    far = jnp.concatenate([far[:half, :rank], far[:half, rank:], far[half:, :rank]], axis=0).astype(BF16)
    down = dot(far, across_ref[...]).astype(BF16)
    size = twos_ref.shape[2]
    for i in range(leaves // 2):
        cols = slice(i * size, (i + 1) * size)
        out_ref[:, cols] = base_ref[:, cols] + dot(down[:, 2 * i * rank : 2 * (i + 1) * rank], twos_ref[i])


def across_kernel(came_own, *refs):
    out_ref = refs[-1]
    out_ref[...] = sum(ref[...].astype(F32) for ref in (came_own, *refs[:-1]))


def last_kernel(routes, devices, base_ref, *refs):
    by_low, by_high = routes
    high, low = grid_of(devices)
    came_high, came_low, out_ref = refs[: -low - 1], refs[-low - 1 : -1], refs[-1]
    leaves, split, main = by_low.leaves, by_low.rows, by_low.main
    size = base_ref.shape[1] // leaves
    tails = sum(came_low[k][by_high.dense_tails : by_high.dense_box, :].astype(F32) for k in range(low))
    for j in range(leaves):
        cols = slice(j * size, (j + 1) * size)
        upper = sum(ref[j * by_low.rows : (j + 1) * by_low.rows, :].astype(F32) for ref in came_high)
        lower = sum(came_low[k][j * by_high.rows : (j + 1) * by_high.rows, :].astype(F32) for k in range(low))
        out_ref[:split, cols] = base_ref[:split, cols] + upper
        out_ref[split:main, cols] = base_ref[split:main, cols] + lower
        out_ref[main:, cols] = base_ref[main:, cols] + tails[j : j + 1]


def call(kernel, out_shape, specs, operands, scratch, flops, room=None):
    outs = jax.tree.leaves(out_shape)
    nbytes = sum(a.size * a.dtype.itemsize for a in (*operands, *outs))
    limit = None if room is None else nbytes + room + 2**21
    return pl.pallas_call(
        kernel,
        out_shape=out_shape,
        in_specs=specs[0],
        out_specs=specs[1],
        scratch_shapes=scratch,
        compiler_params=pltpu.CompilerParams(vmem_limit_bytes=limit),
        cost_estimate=pl.CostEstimate(flops=flops, bytes_accessed=nbytes, transcendentals=0),
    )(*operands)


def per_device(
    probes, basis, transfer, local_blocks, remote_blocks, near_dest, near_leaf, couplings, far_list
):
    columns, points = probes.shape
    leaves, rank, size = basis.shape
    devices = lax.axis_size("leaf")
    main = columns // TILE * TILE
    routes = by_low, by_high = routes_of(devices, main, columns, leaves)
    high, low = grid_of(devices)
    blocks = remote_blocks.shape[0] * remote_blocks.shape[1]
    unit = 2 * columns * size * size
    like = lambda *arrays: [pltpu.VMEM(a.shape, a.dtype) for a in arrays]
    numbers = lambda *arrays: [pltpu.SMEM(a.shape, a.dtype) for a in arrays]
    sems = lambda count: [pltpu.SemaphoreType.DMA((count,))]
    relative = lambda x, way: lax.ppermute(x, "leaf", [(i, i ^ way) for i in range(devices)])
    message = lambda route: jax.ShapeDtypeStruct((route.depth, size), BF16)
    dense = lambda route: jax.ShapeDtypeStruct((route.dense_depth, size), BF16)

    def stacked(count, like_this):
        return pltpu.VMEM((count, *like_this.shape), like_this.dtype)

    dest, leaf = near_dest.T, near_leaf.T
    sent = call(
        functools.partial(products_kernel, routes, devices),
        [message(by_low)] * low + [message(by_high)] * high,
        ([ANY] * 6, [ANY] * (low + high)),
        (dest, leaf, probes, basis, transfer, remote_blocks),
        numbers(dest, leaf)
        + like(probes, basis, transfer, remote_blocks)
        + [
            stacked(low, message(by_low)),
            stacked(high, message(by_high)),
            pltpu.VMEM((high, by_high.meta - by_high.tails, size), F32),
            pltpu.SMEM((devices,), I32),
        ]
        + sems(5 + leaves + low + high),
        blocks * unit,
    )
    came_low, came_high = list(sent[:low]), list(sent[low:])
    planes = across_first(high)
    for k in range(1, low):
        came_low[k] = relative(came_low[k], k)
    came_low[0], came_high[0] = call(
        keep_kernel,
        (message(by_low), message(by_high)),
        ([VMEM] * 2, (VMEM,) * 2),
        (came_low[0], came_high[0]),
        [],
        0,
        0,
    )

    for k in planes[1:]:
        came_high[k] = relative(came_high[k], k * low)

    def summed(route, planes, came):
        total = jax.ShapeDtypeStruct((route.fan, (leaves + 1) * route.rows, size), F32)
        tails = jax.ShapeDtypeStruct((route.fan, max(TILE, route.dense_box - route.dense_tails), size), F32)
        ways = len(came)
        return list(
            call(
                functools.partial(sum_kernel, route, planes, ways),
                [dense(route)] * route.fan,
                ([VMEM] * ways, [VMEM] * route.fan),
                came,
                like(total, tails),
                HEAVY if route is by_low else devices * CAP * route.rows * size,
                4 * (total.size + tails.size),
            )
        )

    to_high = summed(by_low, None, [came_low[k] for k in (0, *range(2, low), 1)])
    came_high[0], to_high[0] = lax.optimization_barrier((came_high[0], to_high[0]))
    to_low = summed(by_high, planes, [came_high[k] for k in planes])
    base_shape = jax.ShapeDtypeStruct((columns, points), F32)
    for k in planes[1:]:
        to_high[k] = relative(to_high[k], k * low)
    for k in range(1, low):
        to_low[k] = relative(to_low[k], k)

    probes_then, to_low[1] = lax.optimization_barrier((probes, to_low[1]))
    base, *ready = call(
        local_kernel,
        (
            base_shape,
            jax.ShapeDtypeStruct((2 * rank, 2 * rank * couplings.shape[1]), BF16),
            jax.ShapeDtypeStruct((rank, leaves * rank), BF16),
            jax.ShapeDtypeStruct((leaves // 2, 2 * rank, 2 * size), BF16),
        ),
        ([VMEM] * 5, (VMEM,) * 4),
        (probes_then, local_blocks, couplings, transfer, basis),
        [],
        leaves * leaves * unit,
        0,
    )
    boxes = jax.ShapeDtypeStruct((devices, main // 2, size), BF16)
    base = call(
        functools.partial(far_kernel, by_high, low),
        base_shape,
        ([SMEM] + [VMEM] * (4 + low), VMEM),
        (far_list, base, *ready, *to_low),
        like(boxes, jax.ShapeDtypeStruct((devices, size), F32)),
        4 * leaves * unit,
        4 * boxes.size,
    )
    across = call(
        across_kernel,
        jax.ShapeDtypeStruct((by_low.dense_depth, size), F32),
        ([VMEM] * (high - 1), VMEM),
        [to_high[k] for k in planes[:-1]],
        [],
        HEAVY,
        0,
    )
    return call(
        functools.partial(last_kernel, routes, devices),
        base_shape,
        ([VMEM] * (3 + low), VMEM),
        (base, across, to_high[1], *to_low),
        [],
        devices * columns * size,
        0,
    )


def solution(mesh):
    placed = (
        P(None, ("grp", "leaf")),
        P(("grp", "leaf"), None, None),
        P(("grp", "leaf"), None, None),
        P(("grp", "leaf"), None, None, None),
        P(("grp", "leaf"), None, None, None),
        P(("grp", "leaf"), None),
        P(("grp", "leaf"), None),
        P(("grp", "leaf"), None, None, None),
        P(("grp", "leaf"), None),
    )
    return jax.shard_map(
        per_device, mesh=mesh, in_specs=placed, out_specs=P(None, ("grp", "leaf")), check_vma=False
    )
```

```python
import functools

import jax
import jax.numpy as jnp
from jax import lax
from jax.experimental import pallas as pl
from jax.experimental.pallas import tpu as pltpu
from jax.sharding import PartitionSpec as P

CAP = 4
TILE = 16
HEAVY = 4 * 10**9

F32 = jnp.float32
BF16 = jnp.bfloat16
I32 = jnp.int32

ANY = pl.BlockSpec(memory_space=pl.ANY)
VMEM = pl.BlockSpec(memory_space=pltpu.VMEM)
SMEM = pl.BlockSpec(memory_space=pltpu.SMEM)


def dot_t(lhs, rhs):
    return lax.dot_general(lhs, rhs, (((1,), (1,)), ((), ())), preferred_element_type=F32)


def dot(lhs, rhs):
    return lax.dot_general(lhs, rhs, (((1,), (0,)), ((), ())), preferred_element_type=F32)


class Copies:
    def __init__(self, sems):
        self.sems, self.used = sems, 0

    def start(self, src, dst):
        copy = pltpu.make_async_copy(src, dst, self.sems.at[self.used])
        self.used += 1
        copy.start()
        return copy


def grid_of(devices):
    low = 1 << (devices.bit_length() // 2)
    return devices // low, low


def up(rows):
    return -(-rows // TILE) * TILE


class Route:
    def __init__(self, first, last, fan, extra, main, columns, leaves, sources):
        self.first, self.rows, self.fan, self.extra, self.main = first, last - first, fan, extra, main
        self.leaves, self.half = leaves, main // 2
        slots = fan * CAP
        self.tails = slots * self.rows
        self.meta = self.tails + (up(slots) if extra else 0)
        self.box = self.meta + TILE
        self.depth = self.box + (self.half if extra else 0)
        self.dense_tails = leaves * self.rows
        self.dense_box = self.dense_tails + (up(leaves + sources) if extra else 0)
        self.dense_depth = self.dense_box + (sources * self.half if extra else 0)


def routes_of(devices, main, columns, leaves):
    high, low = grid_of(devices)
    split = up(main * 3 // 4)
    return (
        Route(0, split, high, False, main, columns, leaves, low),
        Route(split, main, low, True, main, columns, leaves, high),
    )


def products_kernel(routes, devices, *refs):
    dest_hbm, leaf_hbm, probes_hbm, basis_hbm, transfer_hbm, blocks_hbm = refs[:6]
    outs = refs[6:-11]
    (
        dest_ref, leaf_ref, probes_ref, basis_ref, transfer_ref, blocks_ref,
        send_low, send_high, tails, count, sems,
    ) = refs[-11:]
    by_low, by_high = routes
    high, low = grid_of(devices)
    me = lax.axis_index("leaf")
    main = by_high.main
    leaves, per_leaf, size = blocks_ref.shape[:3]
    columns, rank = probes_ref.shape[0], basis_ref.shape[1]
    copies = Copies(sems)
    cuts = (0, leaves // 4, leaves)
    arrivals = {}
    early = [
        copies.start(probes_hbm, probes_ref),
        copies.start(dest_hbm, dest_ref),
        copies.start(leaf_hbm, leaf_ref),
    ]
    for j, after in zip(cuts, cuts[1:]):
        part = pl.ds(j, after - j)
        arrivals[j] = copies.start(blocks_hbm.at[part], blocks_ref.at[part])
        if j == 0:
            early += [copies.start(basis_hbm, basis_ref), copies.start(transfer_hbm, transfer_ref)]

    @pl.loop(0, devices)
    def _(i):
        count[i] = 0

    tails[...] = jnp.zeros(tails.shape, F32)
    for copy in early:
        copy.wait()
    box = jnp.zeros((columns, rank), F32)

    numbers = jnp.full((-(-(low + high) // 8) * 8, size), leaves, I32)
    row = lax.broadcasted_iota(I32, numbers.shape, 0)
    lane = lax.broadcasted_iota(I32, numbers.shape, 1)
    for j in range(leaves):
        if j in arrivals:
            arrivals[j].wait()
        x = probes_ref[:, j * size : (j + 1) * size]
        box += dot_t(dot_t(x, basis_ref[j]).astype(BF16), transfer_ref[j])
        for first in range(0, per_leaf, 4):
            many = min(4, per_leaf - first)
            rhs = blocks_ref[j, first : first + many].reshape(many * size, size)
            product = dot_t(x, rhs)
            for b in range(many):
                target = jnp.bitwise_xor(dest_ref[first + b, j], me)
                slot = count[target]
                count[target] = slot + 1
                to_high = lax.shift_right_logical(target, low.bit_length() - 1)
                to_low = jnp.bitwise_and(target, low - 1)
                block = product[:, b * size : (b + 1) * size]
                piece = block[:main].astype(BF16)
                number = leaf_ref[first + b, j]

                at = to_high * CAP + slot
                rows = pl.ds(pl.multiple_of(at * by_low.rows, TILE), by_low.rows)
                send_low[to_low, rows, :] = piece[: by_low.rows]
                numbers = jnp.where((row == to_low) & (lane == at), number, numbers)

                at = to_low * CAP + slot
                rows = pl.ds(pl.multiple_of(at * by_high.rows, TILE), by_high.rows)
                send_high[to_high, rows, :] = piece[by_low.rows :]
                tails[to_high, pl.ds(at, 1), :] = block[main:]
                numbers = jnp.where((row == low + to_high) & (lane == at), number, numbers)

    numbers = numbers.astype(F32)
    leaving = []
    blank = jnp.zeros((TILE - 1, size), F32)
    for i in (*range(2, low), 1, 0):
        tile = jnp.concatenate([numbers[i : i + 1], blank], axis=0)
        send_low[i, by_low.meta : by_low.box, :] = tile.astype(BF16)
        leaving.append(copies.start(send_low.at[i], outs[i]))
    half = by_high.half
    packed = jnp.concatenate([box[:half], box[half:main]], axis=1).astype(BF16)
    last = jnp.concatenate([box[main:], jnp.zeros_like(box[main:])], axis=1)
    blank = jnp.zeros((TILE - 2, size), F32)
    for i in range(high):
        tile = jnp.concatenate([numbers[low + i : low + i + 1], last, blank], axis=0)
        send_high[i, by_high.tails : by_high.meta, :] = tails[i].astype(BF16)
        send_high[i, by_high.meta : by_high.box, :] = tile.astype(BF16)
        send_high[i, by_high.box :, :] = packed
        leaving.append(copies.start(send_high.at[i], outs[low + i]))
    for copy in leaving:
        copy.wait()


def sum_route(route, came, planes, outs, total, tails):
    leaves, half, ways = route.leaves, route.half, len(came)
    for i in range(ways):
        numbers = came[i][route.meta : route.box, :].astype(F32)[:1].astype(I32)
        if route.extra:
            tail = came[i][route.tails : route.meta, :].astype(F32)
        for k in range(route.fan):
            for slot in range(CAP):
                at = k * CAP + slot
                leaf = numbers[0, at]
                rows = pl.ds(pl.multiple_of(leaf * route.rows, TILE), route.rows)
                total[k, rows, :] += came[i][at * route.rows : (at + 1) * route.rows, :].astype(F32)
                if route.extra:
                    tails[k, pl.ds(leaf, 1), :] += tail[at : at + 1]

    for k in range(route.fan):
        outs[k][: route.dense_tails, :] = total[k, : route.dense_tails, :].astype(BF16)
        if route.extra:
            for i in range(ways):
                last = came[i][route.meta : route.box, :].astype(F32)[1:2]
                at = planes[i]
                tails[k, leaves + at : leaves + at + 1, :] = last
                start = route.dense_box + at * half
                outs[k][start : start + half, :] = came[i][route.box :, :]
            outs[k][route.dense_tails : route.dense_box, :] = tails[k].astype(BF16)


def across_first(high):
    return [0, *range(2, high), 1]


def sum_kernel(route, planes, ways, *refs):
    came, outs = refs[:ways], refs[ways:-2]
    total, tails = refs[-2:]
    for ref in (total, tails):
        ref[...] = jnp.zeros(ref.shape, F32)
    sum_route(route, came, planes, outs, total, tails)


def keep_kernel(*refs):
    half = len(refs) // 2
    for came, kept in zip(refs[:half], refs[half:]):
        kept[...] = came[...]


def local_kernel(
    probes_ref, local_ref, couplings_ref, transfer_ref, basis_ref, out_ref, pairs_ref, across_ref, twos_ref
):
    rank = basis_ref.shape[1]
    blank = jnp.zeros((rank, rank), BF16)
    for f in range(couplings_ref.shape[1]):
        cols = slice(2 * f * rank, 2 * (f + 1) * rank)
        pairs_ref[:rank, cols] = jnp.concatenate([couplings_ref[0, f], blank], axis=1)
        pairs_ref[rank:, cols] = jnp.concatenate([blank, couplings_ref[0, f]], axis=1)
    for i in range(0, basis_ref.shape[0], 2):
        across_ref[:, i * rank : (i + 2) * rank] = jnp.concatenate([transfer_ref[i], transfer_ref[i + 1]], axis=1)
        none = jnp.zeros_like(basis_ref[i])
        twos_ref[i // 2, :rank, :] = jnp.concatenate([basis_ref[i], none], axis=1)
        twos_ref[i // 2, rank:, :] = jnp.concatenate([none, basis_ref[i + 1]], axis=1)
    leaves, size = local_ref.shape[0], local_ref.shape[2]
    for i in range(0, leaves, 2):
        total = 0.0
        for c in range(0, leaves, 2):
            square = jnp.concatenate(
                [jnp.concatenate([local_ref[r, c], local_ref[r, c + 1]], axis=1) for r in (i, i + 1)], axis=0
            )
            total += dot_t(probes_ref[:, c * size : (c + 2) * size], square)
        out_ref[:, i * size : (i + 2) * size] = total


def far_kernel(by_high, low, partner_ref, base_ref, pairs_ref, across_ref, twos_ref, *refs):
    came, out_ref, boxes, lasts = refs[:low], refs[low], refs[low + 1], refs[low + 2]
    leaves, half = by_high.leaves, by_high.half
    rank = across_ref.shape[0]
    high = boxes.shape[0] // low
    me = lax.axis_index("leaf")
    for k in range(low):
        tile = came[k][by_high.dense_tails : by_high.dense_box, :].astype(F32)
        for i in range(high):
            start = by_high.dense_box + i * half
            boxes[i * low + k] = came[k][start : start + half, :]
            lasts[i * low + k : i * low + k + 1, :] = tile[leaves + i : leaves + i + 1, :]
    chosen = []
    for f in range(partner_ref.shape[1]):
        source = jnp.bitwise_xor(partner_ref[0, f], me)
        rows = jnp.concatenate([boxes[source].astype(F32), lasts[pl.ds(source, 1), :]], axis=0)
        chosen.append(rows.astype(BF16))
    far = 0.0
    for f in range(0, len(chosen), 2):
        cols = slice(2 * f * rank, 2 * (f + 2) * rank)
        far += dot_t(jnp.concatenate(chosen[f : f + 2], axis=1), pairs_ref[:, cols])
    far = jnp.concatenate([far[:half, :rank], far[:half, rank:], far[half:, :rank]], axis=0).astype(BF16)
    down = dot(far, across_ref[...]).astype(BF16)
    size = twos_ref.shape[2]
    for i in range(leaves // 2):
        cols = slice(i * size, (i + 1) * size)
        out_ref[:, cols] = base_ref[:, cols] + dot(down[:, 2 * i * rank : 2 * (i + 1) * rank], twos_ref[i])


def across_kernel(came_own, *refs):
    out_ref = refs[-1]
    out_ref[...] = sum(ref[...].astype(F32) for ref in (came_own, *refs[:-1]))


def last_kernel(routes, devices, base_ref, *refs):
    by_low, by_high = routes
    high, low = grid_of(devices)
    came_high, came_low, out_ref = refs[: -low - 1], refs[-low - 1 : -1], refs[-1]
    leaves, split, main = by_low.leaves, by_low.rows, by_low.main
    size = base_ref.shape[1] // leaves
    tails = sum(came_low[k][by_high.dense_tails : by_high.dense_box, :].astype(F32) for k in range(low))
    for j in range(leaves):
        cols = slice(j * size, (j + 1) * size)
        upper = sum(ref[j * by_low.rows : (j + 1) * by_low.rows, :].astype(F32) for ref in came_high)
        lower = sum(came_low[k][j * by_high.rows : (j + 1) * by_high.rows, :].astype(F32) for k in range(low))
        out_ref[:split, cols] = base_ref[:split, cols] + upper
        out_ref[split:main, cols] = base_ref[split:main, cols] + lower
        out_ref[main:, cols] = base_ref[main:, cols] + tails[j : j + 1]


def call(kernel, out_shape, specs, operands, scratch, flops, room=None):
    outs = jax.tree.leaves(out_shape)
    nbytes = sum(a.size * a.dtype.itemsize for a in (*operands, *outs))
    limit = None if room is None else nbytes + room + 2**21
    return pl.pallas_call(
        kernel,
        out_shape=out_shape,
        in_specs=specs[0],
        out_specs=specs[1],
        scratch_shapes=scratch,
        compiler_params=pltpu.CompilerParams(vmem_limit_bytes=limit),
        cost_estimate=pl.CostEstimate(flops=flops, bytes_accessed=nbytes, transcendentals=0),
    )(*operands)


def per_device(
    probes, basis, transfer, local_blocks, remote_blocks, near_dest, near_leaf, couplings, far_list
):
    columns, points = probes.shape
    leaves, rank, size = basis.shape
    devices = lax.axis_size("leaf")
    main = columns // TILE * TILE
    routes = by_low, by_high = routes_of(devices, main, columns, leaves)
    high, low = grid_of(devices)
    blocks = remote_blocks.shape[0] * remote_blocks.shape[1]
    unit = 2 * columns * size * size
    like = lambda *arrays: [pltpu.VMEM(a.shape, a.dtype) for a in arrays]
    numbers = lambda *arrays: [pltpu.SMEM(a.shape, a.dtype) for a in arrays]
    sems = lambda count: [pltpu.SemaphoreType.DMA((count,))]
    relative = lambda x, way: lax.ppermute(x, "leaf", [(i, i ^ way) for i in range(devices)])
    message = lambda route: jax.ShapeDtypeStruct((route.depth, size), BF16)
    dense = lambda route: jax.ShapeDtypeStruct((route.dense_depth, size), BF16)

    def stacked(count, like_this):
        return pltpu.VMEM((count, *like_this.shape), like_this.dtype)

    dest, leaf = near_dest.T, near_leaf.T
    sent = call(
        functools.partial(products_kernel, routes, devices),
        [message(by_low)] * low + [message(by_high)] * high,
        ([ANY] * 6, [ANY] * (low + high)),
        (dest, leaf, probes, basis, transfer, remote_blocks),
        numbers(dest, leaf)
        + like(probes, basis, transfer, remote_blocks)
        + [
            stacked(low, message(by_low)),
            stacked(high, message(by_high)),
            pltpu.VMEM((high, by_high.meta - by_high.tails, size), F32),
            pltpu.SMEM((devices,), I32),
        ]
        + sems(7 + low + high),
        blocks * unit,
    )
    came_low, came_high = list(sent[:low]), list(sent[low:])
    planes = across_first(high)
    for k in range(1, low):
        came_low[k] = relative(came_low[k], k)
    came_low[0], came_high[0] = call(
        keep_kernel,
        (message(by_low), message(by_high)),
        ([VMEM] * 2, (VMEM,) * 2),
        (came_low[0], came_high[0]),
        [],
        0,
        0,
    )

    for k in planes[1:]:
        came_high[k] = relative(came_high[k], k * low)

    def summed(route, planes, came):
        total = jax.ShapeDtypeStruct((route.fan, (leaves + 1) * route.rows, size), F32)
        tails = jax.ShapeDtypeStruct((route.fan, max(TILE, route.dense_box - route.dense_tails), size), F32)
        ways = len(came)
        return list(
            call(
                functools.partial(sum_kernel, route, planes, ways),
                [dense(route)] * route.fan,
                ([VMEM] * ways, [VMEM] * route.fan),
                came,
                like(total, tails),
                HEAVY if route is by_low else devices * CAP * route.rows * size,
                4 * (total.size + tails.size),
            )
        )

    to_high = summed(by_low, None, [came_low[k] for k in (0, *range(2, low), 1)])
    came_high[0], to_high[0] = lax.optimization_barrier((came_high[0], to_high[0]))
    to_low = summed(by_high, planes, [came_high[k] for k in planes])
    base_shape = jax.ShapeDtypeStruct((columns, points), F32)
    for k in planes[1:]:
        to_high[k] = relative(to_high[k], k * low)
    for k in range(1, low):
        to_low[k] = relative(to_low[k], k)

    probes_then, to_low[1] = lax.optimization_barrier((probes, to_low[1]))
    base, *ready = call(
        local_kernel,
        (
            base_shape,
            jax.ShapeDtypeStruct((2 * rank, 2 * rank * couplings.shape[1]), BF16),
            jax.ShapeDtypeStruct((rank, leaves * rank), BF16),
            jax.ShapeDtypeStruct((leaves // 2, 2 * rank, 2 * size), BF16),
        ),
        ([VMEM] * 5, (VMEM,) * 4),
        (probes_then, local_blocks, couplings, transfer, basis),
        [],
        leaves * leaves * unit,
        0,
    )
    boxes = jax.ShapeDtypeStruct((devices, main // 2, size), BF16)
    base = call(
        functools.partial(far_kernel, by_high, low),
        base_shape,
        ([SMEM] + [VMEM] * (4 + low), VMEM),
        (far_list, base, *ready, *to_low),
        like(boxes, jax.ShapeDtypeStruct((devices, size), F32)),
        4 * leaves * unit,
        4 * boxes.size,
    )
    across = call(
        across_kernel,
        jax.ShapeDtypeStruct((by_low.dense_depth, size), F32),
        ([VMEM] * (high - 1), VMEM),
        [to_high[k] for k in planes[:-1]],
        [],
        HEAVY,
        0,
    )
    return call(
        functools.partial(last_kernel, routes, devices),
        base_shape,
        ([VMEM] * (3 + low), VMEM),
        (base, across, to_high[1], *to_low),
        [],
        devices * columns * size,
        0,
    )


def solution(mesh):
    placed = (
        P(None, ("grp", "leaf")),
        P(("grp", "leaf"), None, None),
        P(("grp", "leaf"), None, None),
        P(("grp", "leaf"), None, None, None),
        P(("grp", "leaf"), None, None, None),
        P(("grp", "leaf"), None),
        P(("grp", "leaf"), None),
        P(("grp", "leaf"), None, None, None),
        P(("grp", "leaf"), None),
    )
    return jax.shard_map(
        per_device, mesh=mesh, in_specs=placed, out_specs=P(None, ("grp", "leaf")), check_vma=False
    )
```

```python
import functools

import jax
import jax.numpy as jnp
from jax import lax
from jax.experimental import pallas as pl
from jax.experimental.pallas import tpu as pltpu
from jax.sharding import PartitionSpec as P

CAP = 4
TILE = 16
HEAVY = 4 * 10**9

F32 = jnp.float32
BF16 = jnp.bfloat16
I32 = jnp.int32

ANY = pl.BlockSpec(memory_space=pl.ANY)
VMEM = pl.BlockSpec(memory_space=pltpu.VMEM)
SMEM = pl.BlockSpec(memory_space=pltpu.SMEM)


def dot_t(lhs, rhs):
    return lax.dot_general(lhs, rhs, (((1,), (1,)), ((), ())), preferred_element_type=F32)


def dot(lhs, rhs):
    return lax.dot_general(lhs, rhs, (((1,), (0,)), ((), ())), preferred_element_type=F32)


class Copies:
    def __init__(self, sems):
        self.sems, self.used = sems, 0

    def start(self, src, dst):
        copy = pltpu.make_async_copy(src, dst, self.sems.at[self.used])
        self.used += 1
        copy.start()
        return copy


def grid_of(devices):
    low = 1 << (devices.bit_length() // 2)
    return devices // low, low


def up(rows):
    return -(-rows // TILE) * TILE


class Route:
    def __init__(self, first, last, fan, extra, main, columns, leaves, sources):
        self.first, self.rows, self.fan, self.extra, self.main = first, last - first, fan, extra, main
        self.leaves, self.half = leaves, main // 2
        slots = fan * CAP
        self.tails = slots * self.rows
        self.meta = self.tails + (up(slots) if extra else 0)
        self.box = self.meta + TILE
        self.depth = self.box + (self.half if extra else 0)
        self.dense_tails = leaves * self.rows
        self.dense_box = self.dense_tails + (up(leaves + sources) if extra else 0)
        self.dense_depth = self.dense_box + (sources * self.half if extra else 0)


def routes_of(devices, main, columns, leaves):
    high, low = grid_of(devices)
    split = up(main * 3 // 4)
    return (
        Route(0, split, high, False, main, columns, leaves, low),
        Route(split, main, low, True, main, columns, leaves, high),
    )


def products_kernel(routes, devices, *refs):
    dest_hbm, leaf_hbm, probes_hbm, basis_hbm, transfer_hbm, blocks_hbm = refs[:6]
    outs = refs[6:-11]
    (
        dest_ref, leaf_ref, probes_ref, basis_ref, transfer_ref, blocks_ref,
        send_low, send_high, tails, count, sems,
    ) = refs[-11:]
    by_low, by_high = routes
    high, low = grid_of(devices)
    me = lax.axis_index("leaf")
    main = by_high.main
    leaves, per_leaf, size = blocks_ref.shape[:3]
    columns, rank = probes_ref.shape[0], basis_ref.shape[1]
    copies = Copies(sems)
    cuts = (0, leaves // 4, leaves)
    arrivals = {}
    early = [
        copies.start(probes_hbm, probes_ref),
        copies.start(dest_hbm, dest_ref),
        copies.start(leaf_hbm, leaf_ref),
    ]
    for j, after in zip(cuts, cuts[1:]):
        part = pl.ds(j, after - j)
        arrivals[j] = copies.start(blocks_hbm.at[part], blocks_ref.at[part])
        if j == 0:
            early += [copies.start(basis_hbm, basis_ref), copies.start(transfer_hbm, transfer_ref)]

    @pl.loop(0, devices)
    def _(i):
        count[i] = 0

    tails[...] = jnp.zeros(tails.shape, F32)
    for copy in early:
        copy.wait()
    box = jnp.zeros((columns, rank), F32)

    numbers = jnp.full((-(-(low + high) // 8) * 8, size), leaves, I32)
    row = lax.broadcasted_iota(I32, numbers.shape, 0)
    lane = lax.broadcasted_iota(I32, numbers.shape, 1)
    for j in range(leaves):
        if j in arrivals:
            arrivals[j].wait()
        x = probes_ref[:, j * size : (j + 1) * size]
        box += dot_t(dot_t(x, basis_ref[j]).astype(BF16), transfer_ref[j])
        for first in range(0, per_leaf, 4):
            many = min(4, per_leaf - first)
            rhs = blocks_ref[j, first : first + many].reshape(many * size, size)
            product = dot_t(x, rhs)
            for b in range(many):
                target = jnp.bitwise_xor(dest_ref[first + b, j], me)
                slot = count[target]
                count[target] = slot + 1
                to_high = lax.shift_right_logical(target, low.bit_length() - 1)
                to_low = jnp.bitwise_and(target, low - 1)
                block = product[:, b * size : (b + 1) * size]
                piece = block[:main].astype(BF16)
                number = leaf_ref[first + b, j]

                at = to_high * CAP + slot
                rows = pl.ds(pl.multiple_of(at * by_low.rows, TILE), by_low.rows)
                send_low[to_low, rows, :] = piece[: by_low.rows]
                numbers = jnp.where((row == to_low) & (lane == at), number, numbers)

                at = to_low * CAP + slot
                rows = pl.ds(pl.multiple_of(at * by_high.rows, TILE), by_high.rows)
                send_high[to_high, rows, :] = piece[by_low.rows :]
                tails[to_high, pl.ds(at, 1), :] = block[main:]
                numbers = jnp.where((row == low + to_high) & (lane == at), number, numbers)

    numbers = numbers.astype(F32)
    leaving = []
    blank = jnp.zeros((TILE - 1, size), F32)
    for i in (*range(2, low), 1, 0):
        tile = jnp.concatenate([numbers[i : i + 1], blank], axis=0)
        send_low[i, by_low.meta : by_low.box, :] = tile.astype(BF16)
        leaving.append(copies.start(send_low.at[i], outs[i]))
    half = by_high.half
    packed = jnp.concatenate([box[:half], box[half:main]], axis=1).astype(BF16)
    last = jnp.concatenate([box[main:], jnp.zeros_like(box[main:])], axis=1)
    blank = jnp.zeros((TILE - 2, size), F32)
    for i in range(high):
        tile = jnp.concatenate([numbers[low + i : low + i + 1], last, blank], axis=0)
        send_high[i, by_high.tails : by_high.meta, :] = tails[i].astype(BF16)
        send_high[i, by_high.meta : by_high.box, :] = tile.astype(BF16)
        send_high[i, by_high.box :, :] = packed
        leaving.append(copies.start(send_high.at[i], outs[low + i]))
    for copy in leaving:
        copy.wait()


def sum_route(route, came, planes, outs, total, tails):
    leaves, half, ways = route.leaves, route.half, len(came)
    for i in range(ways):
        numbers = came[i][route.meta : route.box, :].astype(F32)[:1].astype(I32)
        if route.extra:
            tail = came[i][route.tails : route.meta, :].astype(F32)
        for k in range(route.fan):
            for slot in range(CAP):
                at = k * CAP + slot
                leaf = numbers[0, at]
                rows = pl.ds(pl.multiple_of(leaf * route.rows, TILE), route.rows)
                total[k, rows, :] += came[i][at * route.rows : (at + 1) * route.rows, :].astype(F32)
                if route.extra:
                    tails[k, pl.ds(leaf, 1), :] += tail[at : at + 1]

    for k in range(route.fan):
        outs[k][: route.dense_tails, :] = total[k, : route.dense_tails, :].astype(BF16)
        if route.extra:
            for i in range(ways):
                last = came[i][route.meta : route.box, :].astype(F32)[1:2]
                at = planes[i]
                tails[k, leaves + at : leaves + at + 1, :] = last
                start = route.dense_box + at * half
                outs[k][start : start + half, :] = came[i][route.box :, :]
            outs[k][route.dense_tails : route.dense_box, :] = tails[k].astype(BF16)


def across_first(high):
    return [0, *range(2, high), 1]


def sum_kernel(route, planes, ways, *refs):
    came, outs = refs[:ways], refs[ways:-2]
    total, tails = refs[-2:]
    for ref in (total, tails):
        ref[...] = jnp.zeros(ref.shape, F32)
    sum_route(route, came, planes, outs, total, tails)


def keep_kernel(*refs):
    half = len(refs) // 2
    for came, kept in zip(refs[:half], refs[half:]):
        kept[...] = came[...]


def local_kernel(
    probes_ref, local_ref, couplings_ref, transfer_ref, basis_ref, out_ref, pairs_ref, across_ref, twos_ref
):
    rank = basis_ref.shape[1]
    blank = jnp.zeros((rank, rank), BF16)
    for f in range(couplings_ref.shape[1]):
        cols = slice(2 * f * rank, 2 * (f + 1) * rank)
        pairs_ref[:rank, cols] = jnp.concatenate([couplings_ref[0, f], blank], axis=1)
        pairs_ref[rank:, cols] = jnp.concatenate([blank, couplings_ref[0, f]], axis=1)
    for i in range(0, basis_ref.shape[0], 2):
        across_ref[:, i * rank : (i + 2) * rank] = jnp.concatenate([transfer_ref[i], transfer_ref[i + 1]], axis=1)
        none = jnp.zeros_like(basis_ref[i])
        twos_ref[i // 2, :rank, :] = jnp.concatenate([basis_ref[i], none], axis=1)
        twos_ref[i // 2, rank:, :] = jnp.concatenate([none, basis_ref[i + 1]], axis=1)
    leaves, size = local_ref.shape[0], local_ref.shape[2]
    for i in range(0, leaves, 2):
        total = 0.0
        for c in range(0, leaves, 2):
            square = jnp.concatenate(
                [jnp.concatenate([local_ref[r, c], local_ref[r, c + 1]], axis=1) for r in (i, i + 1)], axis=0
            )
            total += dot_t(probes_ref[:, c * size : (c + 2) * size], square)
        out_ref[:, i * size : (i + 2) * size] = total


def far_kernel(by_high, low, partner_ref, base_ref, pairs_ref, across_ref, twos_ref, *refs):
    came, out_ref, boxes, lasts = refs[:low], refs[low], refs[low + 1], refs[low + 2]
    leaves, half = by_high.leaves, by_high.half
    rank = across_ref.shape[0]
    high = boxes.shape[0] // low
    me = lax.axis_index("leaf")
    for k in range(low):
        tile = came[k][by_high.dense_tails : by_high.dense_box, :].astype(F32)
        for i in range(high):
            start = by_high.dense_box + i * half
            boxes[i * low + k] = came[k][start : start + half, :]
            lasts[i * low + k : i * low + k + 1, :] = tile[leaves + i : leaves + i + 1, :]
    chosen = []
    for f in range(partner_ref.shape[1]):
        source = jnp.bitwise_xor(partner_ref[0, f], me)
        rows = jnp.concatenate([boxes[source].astype(F32), lasts[pl.ds(source, 1), :]], axis=0)
        chosen.append(rows.astype(BF16))
    far = 0.0
    for f in range(0, len(chosen), 2):
        cols = slice(2 * f * rank, 2 * (f + 2) * rank)
        far += dot_t(jnp.concatenate(chosen[f : f + 2], axis=1), pairs_ref[:, cols])
    far = jnp.concatenate([far[:half, :rank], far[:half, rank:], far[half:, :rank]], axis=0).astype(BF16)
    down = dot(far, across_ref[...]).astype(BF16)
    size = twos_ref.shape[2]
    for i in range(leaves // 2):
        cols = slice(i * size, (i + 1) * size)
        out_ref[:, cols] = base_ref[:, cols] + dot(down[:, 2 * i * rank : 2 * (i + 1) * rank], twos_ref[i])


def across_kernel(came_own, *refs):
    out_ref = refs[-1]
    out_ref[...] = sum(ref[...].astype(F32) for ref in (came_own, *refs[:-1]))


def last_kernel(routes, devices, base_ref, *refs):
    by_low, by_high = routes
    high, low = grid_of(devices)
    came_high, came_low, out_ref = refs[: -low - 1], refs[-low - 1 : -1], refs[-1]
    leaves, split, main = by_low.leaves, by_low.rows, by_low.main
    size = base_ref.shape[1] // leaves
    tails = sum(came_low[k][by_high.dense_tails : by_high.dense_box, :].astype(F32) for k in range(low))
    for j in range(leaves):
        cols = slice(j * size, (j + 1) * size)
        upper = sum(ref[j * by_low.rows : (j + 1) * by_low.rows, :].astype(F32) for ref in came_high)
        lower = sum(came_low[k][j * by_high.rows : (j + 1) * by_high.rows, :].astype(F32) for k in range(low))
        out_ref[:split, cols] = base_ref[:split, cols] + upper
        out_ref[split:main, cols] = base_ref[split:main, cols] + lower
        out_ref[main:, cols] = base_ref[main:, cols] + tails[j : j + 1]


def call(kernel, out_shape, specs, operands, scratch, flops, room=None):
    outs = jax.tree.leaves(out_shape)
    nbytes = sum(a.size * a.dtype.itemsize for a in (*operands, *outs))
    limit = None if room is None else nbytes + room + 2**21
    return pl.pallas_call(
        kernel,
        out_shape=out_shape,
        in_specs=specs[0],
        out_specs=specs[1],
        scratch_shapes=scratch,
        compiler_params=pltpu.CompilerParams(vmem_limit_bytes=limit),
        cost_estimate=pl.CostEstimate(flops=flops, bytes_accessed=nbytes, transcendentals=0),
    )(*operands)


def per_device(
    probes, basis, transfer, local_blocks, remote_blocks, near_dest, near_leaf, couplings, far_list
):
    columns, points = probes.shape
    leaves, rank, size = basis.shape
    devices = lax.axis_size("leaf")
    main = columns // TILE * TILE
    routes = by_low, by_high = routes_of(devices, main, columns, leaves)
    high, low = grid_of(devices)
    blocks = remote_blocks.shape[0] * remote_blocks.shape[1]
    unit = 2 * columns * size * size
    like = lambda *arrays: [pltpu.VMEM(a.shape, a.dtype) for a in arrays]
    numbers = lambda *arrays: [pltpu.SMEM(a.shape, a.dtype) for a in arrays]
    sems = lambda count: [pltpu.SemaphoreType.DMA((count,))]
    relative = lambda x, way: lax.ppermute(x, "leaf", [(i, i ^ way) for i in range(devices)])
    message = lambda route: jax.ShapeDtypeStruct((route.depth, size), BF16)
    dense = lambda route: jax.ShapeDtypeStruct((route.dense_depth, size), BF16)

    def stacked(count, like_this):
        return pltpu.VMEM((count, *like_this.shape), like_this.dtype)

    dest, leaf = near_dest.T, near_leaf.T
    sent = call(
        functools.partial(products_kernel, routes, devices),
        [message(by_low)] * low + [message(by_high)] * high,
        ([ANY] * 6, [ANY] * (low + high)),
        (dest, leaf, probes, basis, transfer, remote_blocks),
        numbers(dest, leaf)
        + like(probes, basis, transfer, remote_blocks)
        + [
            stacked(low, message(by_low)),
            stacked(high, message(by_high)),
            pltpu.VMEM((high, by_high.meta - by_high.tails, size), F32),
            pltpu.SMEM((devices,), I32),
        ]
        + sems(7 + low + high),
        blocks * unit,
    )
    came_low, came_high = list(sent[:low]), list(sent[low:])
    planes = across_first(high)
    for k in range(1, low):
        came_low[k] = relative(came_low[k], k)
    came_low[0], came_high[0] = call(
        keep_kernel,
        (message(by_low), message(by_high)),
        ([VMEM] * 2, (VMEM,) * 2),
        (came_low[0], came_high[0]),
        [],
        0,
        0,
    )

    for k in planes[1:]:
        came_high[k] = relative(came_high[k], k * low)

    def summed(route, planes, came):
        total = jax.ShapeDtypeStruct((route.fan, (leaves + 1) * route.rows, size), F32)
        tails = jax.ShapeDtypeStruct((route.fan, max(TILE, route.dense_box - route.dense_tails), size), F32)
        ways = len(came)
        return list(
            call(
                functools.partial(sum_kernel, route, planes, ways),
                [dense(route)] * route.fan,
                ([VMEM] * ways, [VMEM] * route.fan),
                came,
                like(total, tails),
                HEAVY if route is by_low else devices * CAP * route.rows * size,
                4 * (total.size + tails.size),
            )
        )

    to_high = summed(by_low, None, [came_low[k] for k in (0, *range(2, low), 1)])
    came_high[0], to_high[0] = lax.optimization_barrier((came_high[0], to_high[0]))
    to_low = summed(by_high, planes, [came_high[k] for k in planes])
    base_shape = jax.ShapeDtypeStruct((columns, points), F32)
    for k in planes[1:]:
        to_high[k] = relative(to_high[k], k * low)
    for k in range(1, low):
        to_low[k] = relative(to_low[k], k)

    probes_then, to_low[1] = lax.optimization_barrier((probes, to_low[1]))
    base, *ready = call(
        local_kernel,
        (
            base_shape,
            jax.ShapeDtypeStruct((2 * rank, 2 * rank * couplings.shape[1]), BF16),
            jax.ShapeDtypeStruct((rank, leaves * rank), BF16),
            jax.ShapeDtypeStruct((leaves // 2, 2 * rank, 2 * size), BF16),
        ),
        ([VMEM] * 5, (VMEM,) * 4),
        (probes_then, local_blocks, couplings, transfer, basis),
        [],
        leaves * leaves * unit,
        0,
    )
    boxes = jax.ShapeDtypeStruct((devices, main // 2, size), BF16)
    base = call(
        functools.partial(far_kernel, by_high, low),
        base_shape,
        ([SMEM] + [VMEM] * (4 + low), VMEM),
        (far_list, base, *ready, *to_low),
        like(boxes, jax.ShapeDtypeStruct((devices, size), F32)),
        4 * leaves * unit,
        4 * boxes.size,
    )
    across = call(
        across_kernel,
        jax.ShapeDtypeStruct((by_low.dense_depth, size), F32),
        ([VMEM] * (high - 1), VMEM),
        [to_high[k] for k in (0, *range(2, high - 1), 1)],
        [],
        HEAVY,
        0,
    )
    return call(
        functools.partial(last_kernel, routes, devices),
        base_shape,
        ([VMEM] * (3 + low), VMEM),
        (base, across, to_high[high - 1], *to_low),
        [],
        devices * columns * size,
        0,
    )


def solution(mesh):
    placed = (
        P(None, ("grp", "leaf")),
        P(("grp", "leaf"), None, None),
        P(("grp", "leaf"), None, None),
        P(("grp", "leaf"), None, None, None),
        P(("grp", "leaf"), None, None, None),
        P(("grp", "leaf"), None),
        P(("grp", "leaf"), None),
        P(("grp", "leaf"), None, None, None),
        P(("grp", "leaf"), None),
    )
    return jax.shard_map(
        per_device, mesh=mesh, in_specs=placed, out_specs=P(None, ("grp", "leaf")), check_vma=False
    )
```

```python
import functools

import jax
import jax.numpy as jnp
from jax import lax
from jax.experimental import pallas as pl
from jax.experimental.pallas import tpu as pltpu
from jax.sharding import PartitionSpec as P

CAP = 4
TILE = 16
HEAVY = 4 * 10**9

F32 = jnp.float32
BF16 = jnp.bfloat16
I32 = jnp.int32

ANY = pl.BlockSpec(memory_space=pl.ANY)
VMEM = pl.BlockSpec(memory_space=pltpu.VMEM)
SMEM = pl.BlockSpec(memory_space=pltpu.SMEM)


def dot_t(lhs, rhs):
    return lax.dot_general(lhs, rhs, (((1,), (1,)), ((), ())), preferred_element_type=F32)


def dot(lhs, rhs):
    return lax.dot_general(lhs, rhs, (((1,), (0,)), ((), ())), preferred_element_type=F32)


class Copies:
    def __init__(self, sems):
        self.sems, self.used = sems, 0

    def start(self, src, dst):
        copy = pltpu.make_async_copy(src, dst, self.sems.at[self.used])
        self.used += 1
        copy.start()
        return copy


def grid_of(devices):
    low = 1 << (devices.bit_length() // 2)
    return devices // low, low


def up(rows):
    return -(-rows // TILE) * TILE


class Route:
    def __init__(self, first, last, fan, extra, main, columns, leaves, sources):
        self.first, self.rows, self.fan, self.extra, self.main = first, last - first, fan, extra, main
        self.leaves, self.half = leaves, main // 2
        slots = fan * CAP
        self.tails = slots * self.rows
        self.meta = self.tails + (up(slots) if extra else 0)
        self.box = self.meta + TILE
        self.depth = self.box + (self.half if extra else 0)
        self.dense_tails = leaves * self.rows
        self.dense_box = self.dense_tails + (up(leaves + sources) if extra else 0)
        self.dense_depth = self.dense_box + (sources * self.half if extra else 0)


def routes_of(devices, main, columns, leaves):
    high, low = grid_of(devices)
    split = up(main * 3 // 4)
    return (
        Route(0, split, high, False, main, columns, leaves, low),
        Route(split, main, low, True, main, columns, leaves, high),
    )


def products_kernel(routes, devices, *refs):
    dest_hbm, leaf_hbm, probes_hbm, basis_hbm, transfer_hbm, blocks_hbm = refs[:6]
    outs = refs[6:-11]
    (
        dest_ref, leaf_ref, probes_ref, basis_ref, transfer_ref, blocks_ref,
        send_low, send_high, tails, count, sems,
    ) = refs[-11:]
    by_low, by_high = routes
    high, low = grid_of(devices)
    me = lax.axis_index("leaf")
    main = by_high.main
    leaves, per_leaf, size = blocks_ref.shape[:3]
    columns, rank = probes_ref.shape[0], basis_ref.shape[1]
    copies = Copies(sems)
    cuts = (0, leaves // 4, leaves)
    arrivals = {}
    early = [
        copies.start(probes_hbm, probes_ref),
        copies.start(dest_hbm, dest_ref),
        copies.start(leaf_hbm, leaf_ref),
    ]
    for j, after in zip(cuts, cuts[1:]):
        part = pl.ds(j, after - j)
        arrivals[j] = copies.start(blocks_hbm.at[part], blocks_ref.at[part])
        if j == 0:
            early += [copies.start(basis_hbm, basis_ref), copies.start(transfer_hbm, transfer_ref)]

    @pl.loop(0, devices)
    def _(i):
        count[i] = 0

    tails[...] = jnp.zeros(tails.shape, F32)
    for copy in early:
        copy.wait()
    box = jnp.zeros((columns, rank), F32)

    numbers = jnp.full((-(-(low + high) // 8) * 8, size), leaves, I32)
    row = lax.broadcasted_iota(I32, numbers.shape, 0)
    lane = lax.broadcasted_iota(I32, numbers.shape, 1)
    for j in range(leaves):
        if j in arrivals:
            arrivals[j].wait()
        x = probes_ref[:, j * size : (j + 1) * size]
        box += dot_t(dot_t(x, basis_ref[j]).astype(BF16), transfer_ref[j])
        for first in range(0, per_leaf, 4):
            many = min(4, per_leaf - first)
            rhs = blocks_ref[j, first : first + many].reshape(many * size, size)
            product = dot_t(x, rhs)
            for b in range(many):
                target = jnp.bitwise_xor(dest_ref[first + b, j], me)
                slot = count[target]
                count[target] = slot + 1
                to_high = lax.shift_right_logical(target, low.bit_length() - 1)
                to_low = jnp.bitwise_and(target, low - 1)
                block = product[:, b * size : (b + 1) * size]
                piece = block[:main].astype(BF16)
                number = leaf_ref[first + b, j]

                at = to_high * CAP + slot
                rows = pl.ds(pl.multiple_of(at * by_low.rows, TILE), by_low.rows)
                send_low[to_low, rows, :] = piece[: by_low.rows]
                numbers = jnp.where((row == to_low) & (lane == at), number, numbers)

                at = to_low * CAP + slot
                rows = pl.ds(pl.multiple_of(at * by_high.rows, TILE), by_high.rows)
                send_high[to_high, rows, :] = piece[by_low.rows :]
                tails[to_high, pl.ds(at, 1), :] = block[main:]
                numbers = jnp.where((row == low + to_high) & (lane == at), number, numbers)

    numbers = numbers.astype(F32)
    leaving = []
    blank = jnp.zeros((TILE - 1, size), F32)
    for i in (*range(2, low), 1, 0):
        tile = jnp.concatenate([numbers[i : i + 1], blank], axis=0)
        send_low[i, by_low.meta : by_low.box, :] = tile.astype(BF16)
        leaving.append(copies.start(send_low.at[i], outs[i]))
    half = by_high.half
    packed = jnp.concatenate([box[:half], box[half:main]], axis=1).astype(BF16)
    last = jnp.concatenate([box[main:], jnp.zeros_like(box[main:])], axis=1)
    blank = jnp.zeros((TILE - 2, size), F32)
    for i in range(high):
        tile = jnp.concatenate([numbers[low + i : low + i + 1], last, blank], axis=0)
        send_high[i, by_high.tails : by_high.meta, :] = tails[i].astype(BF16)
        send_high[i, by_high.meta : by_high.box, :] = tile.astype(BF16)
        send_high[i, by_high.box :, :] = packed
        leaving.append(copies.start(send_high.at[i], outs[low + i]))
    for copy in leaving:
        copy.wait()


def sum_route(route, came, planes, outs, total, tails):
    leaves, half, ways = route.leaves, route.half, len(came)
    for i in range(ways):
        numbers = came[i][route.meta : route.box, :].astype(F32)[:1].astype(I32)
        if route.extra:
            tail = came[i][route.tails : route.meta, :].astype(F32)
        for k in range(route.fan):
            for slot in range(CAP):
                at = k * CAP + slot
                leaf = numbers[0, at]
                rows = pl.ds(pl.multiple_of(leaf * route.rows, TILE), route.rows)
                total[k, rows, :] += came[i][at * route.rows : (at + 1) * route.rows, :].astype(F32)
                if route.extra:
                    tails[k, pl.ds(leaf, 1), :] += tail[at : at + 1]

    for k in range(route.fan):
        outs[k][: route.dense_tails, :] = total[k, : route.dense_tails, :].astype(BF16)
        if route.extra:
            for i in range(ways):
                last = came[i][route.meta : route.box, :].astype(F32)[1:2]
                at = planes[i]
                tails[k, leaves + at : leaves + at + 1, :] = last
                start = route.dense_box + at * half
                outs[k][start : start + half, :] = came[i][route.box :, :]
            outs[k][route.dense_tails : route.dense_box, :] = tails[k].astype(BF16)


def across_first(high):
    return [0, *range(2, high), 1]


def sum_kernel(route, planes, ways, *refs):
    came, outs = refs[:ways], refs[ways:-2]
    total, tails = refs[-2:]
    for ref in (total, tails):
        ref[...] = jnp.zeros(ref.shape, F32)
    sum_route(route, came, planes, outs, total, tails)


def keep_kernel(*refs):
    half = len(refs) // 2
    for came, kept in zip(refs[:half], refs[half:]):
        kept[...] = came[...]


def local_kernel(
    probes_ref, local_ref, couplings_ref, transfer_ref, basis_ref, out_ref, pairs_ref, across_ref, twos_ref
):
    rank = basis_ref.shape[1]
    blank = jnp.zeros((rank, rank), BF16)
    for f in range(couplings_ref.shape[1]):
        cols = slice(2 * f * rank, 2 * (f + 1) * rank)
        pairs_ref[:rank, cols] = jnp.concatenate([couplings_ref[0, f], blank], axis=1)
        pairs_ref[rank:, cols] = jnp.concatenate([blank, couplings_ref[0, f]], axis=1)
    for i in range(0, basis_ref.shape[0], 2):
        across_ref[:, i * rank : (i + 2) * rank] = jnp.concatenate([transfer_ref[i], transfer_ref[i + 1]], axis=1)
        none = jnp.zeros_like(basis_ref[i])
        twos_ref[i // 2, :rank, :] = jnp.concatenate([basis_ref[i], none], axis=1)
        twos_ref[i // 2, rank:, :] = jnp.concatenate([none, basis_ref[i + 1]], axis=1)
    leaves, size = local_ref.shape[0], local_ref.shape[2]
    for i in range(0, leaves, 2):
        total = 0.0
        for c in range(0, leaves, 2):
            square = jnp.concatenate(
                [jnp.concatenate([local_ref[r, c], local_ref[r, c + 1]], axis=1) for r in (i, i + 1)], axis=0
            )
            total += dot_t(probes_ref[:, c * size : (c + 2) * size], square)
        out_ref[:, i * size : (i + 2) * size] = total


def far_kernel(by_high, low, partner_ref, base_ref, pairs_ref, across_ref, twos_ref, *refs):
    came, out_ref, boxes, lasts = refs[:low], refs[low], refs[low + 1], refs[low + 2]
    leaves, half = by_high.leaves, by_high.half
    rank = across_ref.shape[0]
    high = boxes.shape[0] // low
    me = lax.axis_index("leaf")
    for k in range(low):
        tile = came[k][by_high.dense_tails : by_high.dense_box, :].astype(F32)
        for i in range(high):
            start = by_high.dense_box + i * half
            boxes[i * low + k] = came[k][start : start + half, :]
            lasts[i * low + k : i * low + k + 1, :] = tile[leaves + i : leaves + i + 1, :]
    chosen = []
    for f in range(partner_ref.shape[1]):
        source = jnp.bitwise_xor(partner_ref[0, f], me)
        rows = jnp.concatenate([boxes[source].astype(F32), lasts[pl.ds(source, 1), :]], axis=0)
        chosen.append(rows.astype(BF16))
    far = 0.0
    for f in range(0, len(chosen), 2):
        cols = slice(2 * f * rank, 2 * (f + 2) * rank)
        far += dot_t(jnp.concatenate(chosen[f : f + 2], axis=1), pairs_ref[:, cols])
    far = jnp.concatenate([far[:half, :rank], far[:half, rank:], far[half:, :rank]], axis=0).astype(BF16)
    down = dot(far, across_ref[...]).astype(BF16)
    size = twos_ref.shape[2]
    for i in range(leaves // 2):
        cols = slice(i * size, (i + 1) * size)
        out_ref[:, cols] = base_ref[:, cols] + dot(down[:, 2 * i * rank : 2 * (i + 1) * rank], twos_ref[i])


def across_kernel(came_own, *refs):
    out_ref = refs[-1]
    out_ref[...] = sum(ref[...].astype(F32) for ref in (came_own, *refs[:-1]))


def last_kernel(routes, devices, base_ref, *refs):
    by_low, by_high = routes
    high, low = grid_of(devices)
    came_high, came_low, out_ref = refs[: -low - 1], refs[-low - 1 : -1], refs[-1]
    leaves, split, main = by_low.leaves, by_low.rows, by_low.main
    size = base_ref.shape[1] // leaves
    tails = sum(came_low[k][by_high.dense_tails : by_high.dense_box, :].astype(F32) for k in range(low))
    for j in range(leaves):
        cols = slice(j * size, (j + 1) * size)
        upper = sum(ref[j * by_low.rows : (j + 1) * by_low.rows, :].astype(F32) for ref in came_high)
        lower = sum(came_low[k][j * by_high.rows : (j + 1) * by_high.rows, :].astype(F32) for k in range(low))
        out_ref[:split, cols] = base_ref[:split, cols] + upper
        out_ref[split:main, cols] = base_ref[split:main, cols] + lower
        out_ref[main:, cols] = base_ref[main:, cols] + tails[j : j + 1]


def call(kernel, out_shape, specs, operands, scratch, flops, room=None):
    outs = jax.tree.leaves(out_shape)
    nbytes = sum(a.size * a.dtype.itemsize for a in (*operands, *outs))
    limit = None if room is None else nbytes + room + 2**21
    return pl.pallas_call(
        kernel,
        out_shape=out_shape,
        in_specs=specs[0],
        out_specs=specs[1],
        scratch_shapes=scratch,
        compiler_params=pltpu.CompilerParams(vmem_limit_bytes=limit),
        cost_estimate=pl.CostEstimate(flops=flops, bytes_accessed=nbytes, transcendentals=0),
    )(*operands)


def per_device(
    probes, basis, transfer, local_blocks, remote_blocks, near_dest, near_leaf, couplings, far_list
):
    columns, points = probes.shape
    leaves, rank, size = basis.shape
    devices = lax.axis_size("leaf")
    main = columns // TILE * TILE
    routes = by_low, by_high = routes_of(devices, main, columns, leaves)
    high, low = grid_of(devices)
    blocks = remote_blocks.shape[0] * remote_blocks.shape[1]
    unit = 2 * columns * size * size
    like = lambda *arrays: [pltpu.VMEM(a.shape, a.dtype) for a in arrays]
    numbers = lambda *arrays: [pltpu.SMEM(a.shape, a.dtype) for a in arrays]
    sems = lambda count: [pltpu.SemaphoreType.DMA((count,))]
    relative = lambda x, way: lax.ppermute(x, "leaf", [(i, i ^ way) for i in range(devices)])
    message = lambda route: jax.ShapeDtypeStruct((route.depth, size), BF16)
    dense = lambda route: jax.ShapeDtypeStruct((route.dense_depth, size), BF16)

    def stacked(count, like_this):
        return pltpu.VMEM((count, *like_this.shape), like_this.dtype)

    dest, leaf = near_dest.T, near_leaf.T
    sent = call(
        functools.partial(products_kernel, routes, devices),
        [message(by_low)] * low + [message(by_high)] * high,
        ([ANY] * 6, [ANY] * (low + high)),
        (dest, leaf, probes, basis, transfer, remote_blocks),
        numbers(dest, leaf)
        + like(probes, basis, transfer, remote_blocks)
        + [
            stacked(low, message(by_low)),
            stacked(high, message(by_high)),
            pltpu.VMEM((high, by_high.meta - by_high.tails, size), F32),
            pltpu.SMEM((devices,), I32),
        ]
        + sems(7 + low + high),
        blocks * unit,
    )
    came_low, came_high = list(sent[:low]), list(sent[low:])
    planes = across_first(high)
    for k in range(1, low):
        came_low[k] = relative(came_low[k], k)
    came_low[0], came_high[0] = call(
        keep_kernel,
        (message(by_low), message(by_high)),
        ([VMEM] * 2, (VMEM,) * 2),
        (came_low[0], came_high[0]),
        [],
        0,
        0,
    )

    for k in planes[1:]:
        came_high[k] = relative(came_high[k], k * low)

    def summed(route, planes, came):
        total = jax.ShapeDtypeStruct((route.fan, (leaves + 1) * route.rows, size), F32)
        tails = jax.ShapeDtypeStruct((route.fan, max(TILE, route.dense_box - route.dense_tails), size), F32)
        ways = len(came)
        return list(
            call(
                functools.partial(sum_kernel, route, planes, ways),
                [dense(route)] * route.fan,
                ([VMEM] * ways, [VMEM] * route.fan),
                came,
                like(total, tails),
                HEAVY if route is by_low else devices * CAP * route.rows * size,
                4 * (total.size + tails.size),
            )
        )

    to_high = summed(by_low, None, [came_low[k] for k in (0, *range(2, low), 1)])
    came_high[0], to_high[0] = lax.optimization_barrier((came_high[0], to_high[0]))
    to_low = summed(by_high, planes, [came_high[k] for k in planes])
    base_shape = jax.ShapeDtypeStruct((columns, points), F32)
    for k in planes[1:]:
        to_high[k] = relative(to_high[k], k * low)
    for k in range(1, low):
        to_low[k] = relative(to_low[k], k)

    probes_then, to_low[1] = lax.optimization_barrier((probes, to_low[1]))
    base, *ready = call(
        local_kernel,
        (
            base_shape,
            jax.ShapeDtypeStruct((2 * rank, 2 * rank * couplings.shape[1]), BF16),
            jax.ShapeDtypeStruct((rank, leaves * rank), BF16),
            jax.ShapeDtypeStruct((leaves // 2, 2 * rank, 2 * size), BF16),
        ),
        ([VMEM] * 5, (VMEM,) * 4),
        (probes_then, local_blocks, couplings, transfer, basis),
        [],
        leaves * leaves * unit,
        0,
    )
    boxes = jax.ShapeDtypeStruct((devices, main // 2, size), BF16)
    base = call(
        functools.partial(far_kernel, by_high, low),
        base_shape,
        ([SMEM] + [VMEM] * (4 + low), VMEM),
        (far_list, base, *ready, *to_low),
        like(boxes, jax.ShapeDtypeStruct((devices, size), F32)),
        4 * leaves * unit,
        4 * boxes.size,
    )
    across = call(
        across_kernel,
        jax.ShapeDtypeStruct((by_low.dense_depth, size), F32),
        ([VMEM] * (high - 1), VMEM),
        [to_high[k] for k in (0, *range(high - 1, 1, -1))],
        [],
        HEAVY,
        0,
    )
    return call(
        functools.partial(last_kernel, routes, devices),
        base_shape,
        ([VMEM] * (3 + low), VMEM),
        (base, across, to_high[1], *to_low),
        [],
        devices * columns * size,
        0,
    )


def solution(mesh):
    placed = (
        P(None, ("grp", "leaf")),
        P(("grp", "leaf"), None, None),
        P(("grp", "leaf"), None, None),
        P(("grp", "leaf"), None, None, None),
        P(("grp", "leaf"), None, None, None),
        P(("grp", "leaf"), None),
        P(("grp", "leaf"), None),
        P(("grp", "leaf"), None, None, None),
        P(("grp", "leaf"), None),
    )
    return jax.shard_map(
        per_device, mesh=mesh, in_specs=placed, out_specs=P(None, ("grp", "leaf")), check_vma=False
    )
```

```python
import functools

import jax
import jax.numpy as jnp
from jax import lax
from jax.experimental import pallas as pl
from jax.experimental.pallas import tpu as pltpu
from jax.sharding import PartitionSpec as P

CAP = 4
TILE = 16
HEAVY = 4 * 10**9

F32 = jnp.float32
BF16 = jnp.bfloat16
I32 = jnp.int32

ANY = pl.BlockSpec(memory_space=pl.ANY)
VMEM = pl.BlockSpec(memory_space=pltpu.VMEM)
SMEM = pl.BlockSpec(memory_space=pltpu.SMEM)


def dot_t(lhs, rhs):
    return lax.dot_general(lhs, rhs, (((1,), (1,)), ((), ())), preferred_element_type=F32)


def dot(lhs, rhs):
    return lax.dot_general(lhs, rhs, (((1,), (0,)), ((), ())), preferred_element_type=F32)


class Copies:
    def __init__(self, sems):
        self.sems, self.used = sems, 0

    def start(self, src, dst):
        copy = pltpu.make_async_copy(src, dst, self.sems.at[self.used])
        self.used += 1
        copy.start()
        return copy


def grid_of(devices):
    low = 1 << (devices.bit_length() // 2)
    return devices // low, low


def up(rows):
    return -(-rows // TILE) * TILE


class Route:
    def __init__(self, first, last, fan, extra, main, columns, leaves, sources):
        self.first, self.rows, self.fan, self.extra, self.main = first, last - first, fan, extra, main
        self.leaves, self.half = leaves, main // 2
        slots = fan * CAP
        self.tails = slots * self.rows
        self.meta = self.tails + (up(slots) if extra else 0)
        self.box = self.meta + TILE
        self.depth = self.box + (self.half if extra else 0)
        self.dense_tails = leaves * self.rows
        self.dense_box = self.dense_tails + (up(leaves + sources) if extra else 0)
        self.dense_depth = self.dense_box + (sources * self.half if extra else 0)


def routes_of(devices, main, columns, leaves):
    high, low = grid_of(devices)
    split = up(main * 3 // 4)
    return (
        Route(0, split, high, False, main, columns, leaves, low),
        Route(split, main, low, True, main, columns, leaves, high),
    )


def products_kernel(routes, devices, *refs):
    dest_hbm, leaf_hbm, probes_hbm, basis_hbm, transfer_hbm, blocks_hbm = refs[:6]
    outs = refs[6:-11]
    (
        dest_ref, leaf_ref, probes_ref, basis_ref, transfer_ref, blocks_ref,
        send_low, send_high, tails, count, sems,
    ) = refs[-11:]
    by_low, by_high = routes
    high, low = grid_of(devices)
    me = lax.axis_index("leaf")
    main = by_high.main
    leaves, per_leaf, size = blocks_ref.shape[:3]
    columns, rank = probes_ref.shape[0], basis_ref.shape[1]
    copies = Copies(sems)
    cuts = (0, leaves // 4, leaves)
    early = [copies.start(probes_hbm, probes_ref)]
    arrivals = {}
    for j, after in zip(cuts, cuts[1:]):
        part = pl.ds(j, after - j)
        arrivals[j] = copies.start(blocks_hbm.at[part], blocks_ref.at[part])
    early += [
        copies.start(basis_hbm, basis_ref),
        copies.start(transfer_hbm, transfer_ref),
        copies.start(dest_hbm, dest_ref),
        copies.start(leaf_hbm, leaf_ref),
    ]

    @pl.loop(0, devices)
    def _(i):
        count[i] = 0

    tails[...] = jnp.zeros(tails.shape, F32)
    for copy in early:
        copy.wait()
    box = jnp.zeros((columns, rank), F32)

    numbers = jnp.full((-(-(low + high) // 8) * 8, size), leaves, I32)
    row = lax.broadcasted_iota(I32, numbers.shape, 0)
    lane = lax.broadcasted_iota(I32, numbers.shape, 1)
    for j in range(leaves):
        if j in arrivals:
            arrivals[j].wait()
        x = probes_ref[:, j * size : (j + 1) * size]
        box += dot_t(dot_t(x, basis_ref[j]).astype(BF16), transfer_ref[j])
        for first in range(0, per_leaf, 4):
            many = min(4, per_leaf - first)
            rhs = blocks_ref[j, first : first + many].reshape(many * size, size)
            product = dot_t(x, rhs)
            for b in range(many):
                target = jnp.bitwise_xor(dest_ref[first + b, j], me)
                slot = count[target]
                count[target] = slot + 1
                to_high = lax.shift_right_logical(target, low.bit_length() - 1)
                to_low = jnp.bitwise_and(target, low - 1)
                block = product[:, b * size : (b + 1) * size]
                piece = block[:main].astype(BF16)
                number = leaf_ref[first + b, j]

                at = to_high * CAP + slot
                rows = pl.ds(pl.multiple_of(at * by_low.rows, TILE), by_low.rows)
                send_low[to_low, rows, :] = piece[: by_low.rows]
                numbers = jnp.where((row == to_low) & (lane == at), number, numbers)

                at = to_low * CAP + slot
                rows = pl.ds(pl.multiple_of(at * by_high.rows, TILE), by_high.rows)
                send_high[to_high, rows, :] = piece[by_low.rows :]
                tails[to_high, pl.ds(at, 1), :] = block[main:]
                numbers = jnp.where((row == low + to_high) & (lane == at), number, numbers)

    numbers = numbers.astype(F32)
    leaving = []
    blank = jnp.zeros((TILE - 1, size), F32)
    for i in (*range(2, low), 1, 0):
        tile = jnp.concatenate([numbers[i : i + 1], blank], axis=0)
        send_low[i, by_low.meta : by_low.box, :] = tile.astype(BF16)
        leaving.append(copies.start(send_low.at[i], outs[i]))
    half = by_high.half
    packed = jnp.concatenate([box[:half], box[half:main]], axis=1).astype(BF16)
    last = jnp.concatenate([box[main:], jnp.zeros_like(box[main:])], axis=1)
    blank = jnp.zeros((TILE - 2, size), F32)
    for i in range(high):
        tile = jnp.concatenate([numbers[low + i : low + i + 1], last, blank], axis=0)
        send_high[i, by_high.tails : by_high.meta, :] = tails[i].astype(BF16)
        send_high[i, by_high.meta : by_high.box, :] = tile.astype(BF16)
        send_high[i, by_high.box :, :] = packed
        leaving.append(copies.start(send_high.at[i], outs[low + i]))
    for copy in leaving:
        copy.wait()


def sum_route(route, came, planes, outs, total, tails):
    leaves, half, ways = route.leaves, route.half, len(came)
    for i in range(ways):
        numbers = came[i][route.meta : route.box, :].astype(F32)[:1].astype(I32)
        if route.extra:
            tail = came[i][route.tails : route.meta, :].astype(F32)
        for k in range(route.fan):
            for slot in range(CAP):
                at = k * CAP + slot
                leaf = numbers[0, at]
                rows = pl.ds(pl.multiple_of(leaf * route.rows, TILE), route.rows)
                total[k, rows, :] += came[i][at * route.rows : (at + 1) * route.rows, :].astype(F32)
                if route.extra:
                    tails[k, pl.ds(leaf, 1), :] += tail[at : at + 1]

    for k in range(route.fan):
        outs[k][: route.dense_tails, :] = total[k, : route.dense_tails, :].astype(BF16)
        if route.extra:
            for i in range(ways):
                last = came[i][route.meta : route.box, :].astype(F32)[1:2]
                at = planes[i]
                tails[k, leaves + at : leaves + at + 1, :] = last
                start = route.dense_box + at * half
                outs[k][start : start + half, :] = came[i][route.box :, :]
            outs[k][route.dense_tails : route.dense_box, :] = tails[k].astype(BF16)


def across_first(high):
    return [0, *range(2, high), 1]


def sum_kernel(route, planes, ways, *refs):
    came, outs = refs[:ways], refs[ways:-2]
    total, tails = refs[-2:]
    for ref in (total, tails):
        ref[...] = jnp.zeros(ref.shape, F32)
    sum_route(route, came, planes, outs, total, tails)


def keep_kernel(*refs):
    half = len(refs) // 2
    for came, kept in zip(refs[:half], refs[half:]):
        kept[...] = came[...]


def local_kernel(
    probes_ref, local_ref, couplings_ref, transfer_ref, basis_ref, out_ref, pairs_ref, across_ref, twos_ref
):
    rank = basis_ref.shape[1]
    blank = jnp.zeros((rank, rank), BF16)
    for f in range(couplings_ref.shape[1]):
        cols = slice(2 * f * rank, 2 * (f + 1) * rank)
        pairs_ref[:rank, cols] = jnp.concatenate([couplings_ref[0, f], blank], axis=1)
        pairs_ref[rank:, cols] = jnp.concatenate([blank, couplings_ref[0, f]], axis=1)
    for i in range(0, basis_ref.shape[0], 2):
        across_ref[:, i * rank : (i + 2) * rank] = jnp.concatenate([transfer_ref[i], transfer_ref[i + 1]], axis=1)
        none = jnp.zeros_like(basis_ref[i])
        twos_ref[i // 2, :rank, :] = jnp.concatenate([basis_ref[i], none], axis=1)
        twos_ref[i // 2, rank:, :] = jnp.concatenate([none, basis_ref[i + 1]], axis=1)
    leaves, size = local_ref.shape[0], local_ref.shape[2]
    for i in range(0, leaves, 2):
        total = 0.0
        for c in range(0, leaves, 2):
            square = jnp.concatenate(
                [jnp.concatenate([local_ref[r, c], local_ref[r, c + 1]], axis=1) for r in (i, i + 1)], axis=0
            )
            total += dot_t(probes_ref[:, c * size : (c + 2) * size], square)
        out_ref[:, i * size : (i + 2) * size] = total


def far_kernel(by_high, low, partner_ref, base_ref, pairs_ref, across_ref, twos_ref, *refs):
    came, out_ref, boxes, lasts = refs[:low], refs[low], refs[low + 1], refs[low + 2]
    leaves, half = by_high.leaves, by_high.half
    rank = across_ref.shape[0]
    high = boxes.shape[0] // low
    me = lax.axis_index("leaf")
    for k in range(low):
        tile = came[k][by_high.dense_tails : by_high.dense_box, :].astype(F32)
        for i in range(high):
            start = by_high.dense_box + i * half
            boxes[i * low + k] = came[k][start : start + half, :]
            lasts[i * low + k : i * low + k + 1, :] = tile[leaves + i : leaves + i + 1, :]
    chosen = []
    for f in range(partner_ref.shape[1]):
        source = jnp.bitwise_xor(partner_ref[0, f], me)
        rows = jnp.concatenate([boxes[source].astype(F32), lasts[pl.ds(source, 1), :]], axis=0)
        chosen.append(rows.astype(BF16))
    far = 0.0
    for f in range(0, len(chosen), 2):
        cols = slice(2 * f * rank, 2 * (f + 2) * rank)
        far += dot_t(jnp.concatenate(chosen[f : f + 2], axis=1), pairs_ref[:, cols])
    far = jnp.concatenate([far[:half, :rank], far[:half, rank:], far[half:, :rank]], axis=0).astype(BF16)
    down = dot(far, across_ref[...]).astype(BF16)
    size = twos_ref.shape[2]
    for i in range(leaves // 2):
        cols = slice(i * size, (i + 1) * size)
        out_ref[:, cols] = base_ref[:, cols] + dot(down[:, 2 * i * rank : 2 * (i + 1) * rank], twos_ref[i])


def across_kernel(came_own, *refs):
    out_ref = refs[-1]
    out_ref[...] = sum(ref[...].astype(F32) for ref in (came_own, *refs[:-1]))


def last_kernel(routes, devices, base_ref, *refs):
    by_low, by_high = routes
    high, low = grid_of(devices)
    came_high, came_low, out_ref = refs[: -low - 1], refs[-low - 1 : -1], refs[-1]
    leaves, split, main = by_low.leaves, by_low.rows, by_low.main
    size = base_ref.shape[1] // leaves
    tails = sum(came_low[k][by_high.dense_tails : by_high.dense_box, :].astype(F32) for k in range(low))
    for j in range(leaves):
        cols = slice(j * size, (j + 1) * size)
        upper = sum(ref[j * by_low.rows : (j + 1) * by_low.rows, :].astype(F32) for ref in came_high)
        lower = sum(came_low[k][j * by_high.rows : (j + 1) * by_high.rows, :].astype(F32) for k in range(low))
        out_ref[:split, cols] = base_ref[:split, cols] + upper
        out_ref[split:main, cols] = base_ref[split:main, cols] + lower
        out_ref[main:, cols] = base_ref[main:, cols] + tails[j : j + 1]


def call(kernel, out_shape, specs, operands, scratch, flops, room=None):
    outs = jax.tree.leaves(out_shape)
    nbytes = sum(a.size * a.dtype.itemsize for a in (*operands, *outs))
    limit = None if room is None else nbytes + room + 2**21
    return pl.pallas_call(
        kernel,
        out_shape=out_shape,
        in_specs=specs[0],
        out_specs=specs[1],
        scratch_shapes=scratch,
        compiler_params=pltpu.CompilerParams(vmem_limit_bytes=limit),
        cost_estimate=pl.CostEstimate(flops=flops, bytes_accessed=nbytes, transcendentals=0),
    )(*operands)


def per_device(
    probes, basis, transfer, local_blocks, remote_blocks, near_dest, near_leaf, couplings, far_list
):
    columns, points = probes.shape
    leaves, rank, size = basis.shape
    devices = lax.axis_size("leaf")
    main = columns // TILE * TILE
    routes = by_low, by_high = routes_of(devices, main, columns, leaves)
    high, low = grid_of(devices)
    blocks = remote_blocks.shape[0] * remote_blocks.shape[1]
    unit = 2 * columns * size * size
    like = lambda *arrays: [pltpu.VMEM(a.shape, a.dtype) for a in arrays]
    numbers = lambda *arrays: [pltpu.SMEM(a.shape, a.dtype) for a in arrays]
    sems = lambda count: [pltpu.SemaphoreType.DMA((count,))]
    relative = lambda x, way: lax.ppermute(x, "leaf", [(i, i ^ way) for i in range(devices)])
    message = lambda route: jax.ShapeDtypeStruct((route.depth, size), BF16)
    dense = lambda route: jax.ShapeDtypeStruct((route.dense_depth, size), BF16)

    def stacked(count, like_this):
        return pltpu.VMEM((count, *like_this.shape), like_this.dtype)

    dest, leaf = near_dest.T, near_leaf.T
    sent = call(
        functools.partial(products_kernel, routes, devices),
        [message(by_low)] * low + [message(by_high)] * high,
        ([ANY] * 6, [ANY] * (low + high)),
        (dest, leaf, probes, basis, transfer, remote_blocks),
        numbers(dest, leaf)
        + like(probes, basis, transfer, remote_blocks)
        + [
            stacked(low, message(by_low)),
            stacked(high, message(by_high)),
            pltpu.VMEM((high, by_high.meta - by_high.tails, size), F32),
            pltpu.SMEM((devices,), I32),
        ]
        + sems(7 + low + high),
        blocks * unit,
    )
    came_low, came_high = list(sent[:low]), list(sent[low:])
    planes = across_first(high)
    for k in range(1, low):
        came_low[k] = relative(came_low[k], k)
    came_low[0], came_high[0] = call(
        keep_kernel,
        (message(by_low), message(by_high)),
        ([VMEM] * 2, (VMEM,) * 2),
        (came_low[0], came_high[0]),
        [],
        0,
        0,
    )

    for k in planes[1:]:
        came_high[k] = relative(came_high[k], k * low)

    def summed(route, planes, came):
        total = jax.ShapeDtypeStruct((route.fan, (leaves + 1) * route.rows, size), F32)
        tails = jax.ShapeDtypeStruct((route.fan, max(TILE, route.dense_box - route.dense_tails), size), F32)
        ways = len(came)
        return list(
            call(
                functools.partial(sum_kernel, route, planes, ways),
                [dense(route)] * route.fan,
                ([VMEM] * ways, [VMEM] * route.fan),
                came,
                like(total, tails),
                HEAVY if route is by_low else devices * CAP * route.rows * size,
                4 * (total.size + tails.size),
            )
        )

    to_high = summed(by_low, None, [came_low[k] for k in (0, *range(2, low), 1)])
    came_high[0], to_high[0] = lax.optimization_barrier((came_high[0], to_high[0]))
    to_low = summed(by_high, planes, [came_high[k] for k in planes])
    base_shape = jax.ShapeDtypeStruct((columns, points), F32)
    for k in planes[1:]:
        to_high[k] = relative(to_high[k], k * low)
    for k in range(1, low):
        to_low[k] = relative(to_low[k], k)

    probes_then, to_low[1] = lax.optimization_barrier((probes, to_low[1]))
    base, *ready = call(
        local_kernel,
        (
            base_shape,
            jax.ShapeDtypeStruct((2 * rank, 2 * rank * couplings.shape[1]), BF16),
            jax.ShapeDtypeStruct((rank, leaves * rank), BF16),
            jax.ShapeDtypeStruct((leaves // 2, 2 * rank, 2 * size), BF16),
        ),
        ([VMEM] * 5, (VMEM,) * 4),
        (probes_then, local_blocks, couplings, transfer, basis),
        [],
        leaves * leaves * unit,
        0,
    )
    boxes = jax.ShapeDtypeStruct((devices, main // 2, size), BF16)
    base = call(
        functools.partial(far_kernel, by_high, low),
        base_shape,
        ([SMEM] + [VMEM] * (4 + low), VMEM),
        (far_list, base, *ready, *to_low),
        like(boxes, jax.ShapeDtypeStruct((devices, size), F32)),
        4 * leaves * unit,
        4 * boxes.size,
    )
    across = call(
        across_kernel,
        jax.ShapeDtypeStruct((by_low.dense_depth, size), F32),
        ([VMEM] * (high - 1), VMEM),
        [to_high[k] for k in planes[:-1]],
        [],
        HEAVY,
        0,
    )
    return call(
        functools.partial(last_kernel, routes, devices),
        base_shape,
        ([VMEM] * (3 + low), VMEM),
        (base, across, to_high[1], *to_low),
        [],
        devices * columns * size,
        0,
    )


def solution(mesh):
    placed = (
        P(None, ("grp", "leaf")),
        P(("grp", "leaf"), None, None),
        P(("grp", "leaf"), None, None),
        P(("grp", "leaf"), None, None, None),
        P(("grp", "leaf"), None, None, None),
        P(("grp", "leaf"), None),
        P(("grp", "leaf"), None),
        P(("grp", "leaf"), None, None, None),
        P(("grp", "leaf"), None),
    )
    return jax.shard_map(
        per_device, mesh=mesh, in_specs=placed, out_specs=P(None, ("grp", "leaf")), check_vma=False
    )
```
